32 devices in a mesh: dp: 4 (over x, core), blk: 8 (over z, y).
Axes of the slice: x: 2, y: 2, z: 4, core: 2. Of those that a mesh axis runs over, the one named last changes fastest.
Arguments:
- x_a: bfloat16 [8, 4096, 512], P('dp', 'blk'), may hold values from -6 to 6
- x_b: bfloat16 [16, 2048, 512], P('dp', 'blk'), may hold values from -6 to 6
- sel_a: int32 [8, 64], P('dp', 'blk'), may hold values from 0 to 63, as said below
- sel_b: int32 [16, 64], P('dp', 'blk'), may hold values from 0 to 63, as said below
- gain_one: bfloat16 [512], replicated, may hold values from 0.099609375 to 1.8984375
- w_qkv: bfloat16 [512, 1536], replicated, may hold values from -0.25 to 0.25
- w_out: bfloat16 [512, 512], replicated, may hold values from -2 to 2
- w_sort: bfloat16 [512, 64], replicated, may hold values from -0.125 to 0.125
- gain_two: bfloat16 [512], replicated, may hold values from 0.099609375 to 1.8984375
- w_up: bfloat16 [512, 2048], replicated, may hold values from -0.25 to 0.25
- w_down: bfloat16 [2048, 512], replicated, may hold values from -0.125 to 0.125
- cot_a: bfloat16 [8, 4096, 512], P('dp', 'blk'), may hold values from -6 to 6
- cot_b: bfloat16 [16, 2048, 512], P('dp', 'blk'), may hold values from -6 to 6
Outputs:
- out_a: bfloat16 [8, 4096, 512], P('dp', 'blk')
- out_b: bfloat16 [16, 2048, 512], P('dp', 'blk')
- grad_x_a: bfloat16 [8, 4096, 512], P('dp', 'blk')
- grad_x_b: bfloat16 [16, 2048, 512], P('dp', 'blk')
- grad_gain_one: float32 [512], replicated
- grad_qkv: float32 [512, 1536], replicated
- grad_w_out: float32 [512, 512], replicated
- grad_sort: float32 [512, 64], replicated
- grad_gain_two: float32 [512], replicated
- grad_up: float32 [512, 2048], replicated
- grad_down: float32 [2048, 512], replicated
The draws below stay inside these ranges and needn't reach their ends.
Inputs may be any that keep to these rules, and one draw needn't show every extreme that they name: `sel_a`: each entry is the block of the same sequence chosen as keys for that query block. Counting a chosen block of x_a as two units and one of x_b as one, the query blocks held by one device of blk choose at most 14 units among the blocks held by any one device of blk (block k is held by device k // 8), and in every draw exactly 14 from some device. `sel_b`: as for sel_a, the two counted together.
All inputs are finite; a program needn't handle non-finite values.
Results may differ from the reference program's by a relative error of at most 0.014.
Values may be sent and summed in bfloat16 or wider, within the bound.
No kernel may reach another device: no remote copies, remote signals or barrier semaphores. Data moves between devices by JAX's collectives and lax.ppermute only.
A program may use at most 320 MiB of HBM per device.

```python
import jax
import jax.numpy as jnp
from jax import lax

D = 512
HEADS = 8
FF = 2048
NB = 64
BLOCK_A = 64
BLOCK_B = 32
SINK_ITERS = 8
SEQ_A = 2
SEQ_B = 4
LEN_A = 4096
LEN_B = 2048
SEQS_A = 8
SEQS_B = 16
N_DP = 4
N_BLK = 8


def chosen_blocks(key):
    per_shard_rows = NB // N_BLK
    unit_count = per_shard_rows * (2 * SEQ_A + SEQ_B)
    capacity = 2 * max(1, (4 * unit_count + 5 * N_BLK - 1) // (5 * N_BLK))
    half_cap = capacity // 2
    cell_count = N_BLK * half_cap
    count_a = SEQ_A * per_shard_rows
    count_b = SEQ_B * per_shard_rows
    positions = jnp.arange(cell_count, dtype=jnp.int32)
    cell_source = positions // half_cap

    def one_receiver(subkey):
        keys_four = jax.random.split(subkey, 4)
        hottest = jax.random.randint(keys_four[0], (), 0, N_BLK, dtype=jnp.int32)
        shuffled = jax.random.permutation(keys_four[1], cell_count).astype(jnp.int32)
        ranking = jnp.where(cell_source == hottest, positions - cell_count, shuffled)
        ordering = jnp.argsort(ranking, stable=True)
        sources = cell_source[ordering]
        pick_a = jax.random.randint(keys_four[2], (count_a,), 0, per_shard_rows, dtype=jnp.int32)
        pick_b = jax.random.randint(keys_four[3], (count_b,), 0, per_shard_rows, dtype=jnp.int32)
        first = sources[:count_a] * per_shard_rows + pick_a
        second = sources[count_a:count_a + count_b] * per_shard_rows + pick_b
        return (first, second)
    receivers = jax.random.split(key, N_DP * N_BLK)
    picked_a, picked_b = jax.vmap(one_receiver)(receivers)
    table_a = picked_a.reshape(N_DP, N_BLK, SEQ_A, per_shard_rows).transpose(0, 2, 1, 3).reshape(N_DP * SEQ_A, NB)
    table_b = picked_b.reshape(N_DP, N_BLK, SEQ_B, per_shard_rows).transpose(0, 2, 1, 3).reshape(N_DP * SEQ_B, NB)
    return (table_a.astype(jnp.int32), table_b.astype(jnp.int32))


def draw_sel_a(key, part):
    return chosen_blocks(key)[0]


def draw_sel_b(key, part):
    return chosen_blocks(key)[1]


def level_of(rng, shape, pieces, least, high):
    def one(axis_at, parts):
        steps = jax.random.uniform(jax.random.fold_in(jax.random.fold_in(rng, 6), axis_at), (parts,), jnp.float32, least / len(pieces), high / len(pieces))
        return jnp.repeat(jnp.exp(steps), shape[axis_at] // parts).reshape((-1,) + (1,) * (len(shape) - axis_at - 1))

    level = one(*pieces[0])
    for cut in pieces[1:]:
        level = level * one(*cut)
    return level


def normal_values(own_key, dims, scale, most, cuts=(), kind=jnp.bfloat16):
    entries = jax.random.normal(own_key, dims, jnp.float32) * scale
    if len(cuts) > 0:
        entries = level_of(own_key, dims, cuts, -0.22, 0.18) * entries
    return jnp.clip(entries, min=-most, max=most).astype(kind)


def setup_inputs(seed: int = 0) -> dict:
    seeds = jax.random.split(jax.random.key(seed), 14)
    return {
        "x_a": normal_values(seeds[0], (SEQS_A, LEN_A, D), 1.0, 6.0, ((0, 4), (1, 8))),
        "x_b": normal_values(seeds[1], (SEQS_B, LEN_B, D), 1.0, 6.0, ((0, 4), (1, 8))),
        "sel_a": draw_sel_a(jax.random.fold_in(seeds[13], 71), 0),
        "sel_b": draw_sel_b(jax.random.fold_in(seeds[13], 71), 0),
        "gain_one": jnp.clip(1.0 + 0.18 * jax.random.normal(seeds[4], (D,), jnp.float32), 0.099609375, 1.8984375).astype(jnp.bfloat16),
        "w_qkv": normal_values(seeds[5], (D, 3 * D), D ** -0.5, 0.25),
        "w_out": normal_values(seeds[6], (D, D), (D // 64) ** -0.5, 2.0),
        "w_sort": normal_values(seeds[7], (D, NB), (4 * D) ** -0.5, 0.125),
        "gain_two": jnp.clip(1.0 + 0.18 * jax.random.normal(seeds[8], (D,), jnp.float32), 0.099609375, 1.8984375).astype(jnp.bfloat16),
        "w_up": normal_values(seeds[9], (D, FF), D ** -0.5, 0.25),
        "w_down": normal_values(seeds[10], (FF, D), FF ** -0.5, 0.125),
        "cot_a": normal_values(seeds[11], (SEQS_A, LEN_A, D), 1.0, 6.0, ((0, 4), (1, 8))),
        "cot_b": normal_values(seeds[12], (SEQS_B, LEN_B, D), 1.0, 6.0, ((0, 4), (1, 8))),
    }


EPSILON = 1e-05
SOFTMAX_HEAT = 0.75
PRECISE = lax.Precision.HIGHEST

@jax.custom_vjp
def low(v):
    return lax.optimization_barrier(v.astype(jnp.bfloat16)).astype(jnp.float32)

@jax.custom_vjp
def low_back(v):
    return v

def low_keep(v):
    return (low(v), None)

def low_pass(kept, grad):
    return (grad,)

def back_keep(v):
    return (v, None)

def back_low(kept, grad):
    return (low(grad),)
low.defvjp(low_keep, low_pass)
low_back.defvjp(back_keep, back_low)

def matrix_product(left_side, right_side):
    return jnp.dot(left_side, right_side, preferred_element_type=jnp.float32, precision=PRECISE)

def normalize(values, gain_row):
    return values * lax.rsqrt(lax.optimization_barrier(jnp.mean(values * values, axis=-1, keepdims=True)) + EPSILON) * gain_row

def doubly_stochastic_normalizer(unscaled_ranking_affinity):
    for repeat in range(SINK_ITERS):
        unscaled_ranking_affinity = unscaled_ranking_affinity - jax.nn.logsumexp(unscaled_ranking_affinity, axis=-1, keepdims=True)
        unscaled_ranking_affinity = unscaled_ranking_affinity - jax.nn.logsumexp(unscaled_ranking_affinity, axis=-2, keepdims=True)
    return jnp.exp(unscaled_ranking_affinity)

def one_sequence(inputs, chosen, params, block_size):
    gain_first, qkv_weight, out_weight, sorting_weight, gain_second, up_weight, down_weight = params
    length, features = inputs.shape
    block_count = length // block_size
    heads_shape = (block_count, block_size, HEADS, features // HEADS)
    normed = normalize(inputs, gain_first)
    projected = low(low_back(matrix_product(low(normed), qkv_weight)))
    queries = projected[:, :features].reshape(heads_shape)
    keys_all = projected[:, features:2 * features].reshape(heads_shape)
    values_all = projected[:, 2 * features:].reshape(heads_shape)
    summary = lax.optimization_barrier(jnp.mean(normed.reshape(block_count, block_size, features), axis=1))
    block_summary_rows = low(summary * lax.rsqrt(lax.optimization_barrier(jnp.mean(summary * summary, axis=-1, keepdims=True)) + EPSILON))
    unscaled_ranking_affinity = matrix_product(block_summary_rows, sorting_weight) / SOFTMAX_HEAT
    group_transport_plan = doubly_stochastic_normalizer(unscaled_ranking_affinity)
    picked = (chosen[:, None] == jnp.arange(block_count)[None, :]).astype(jnp.float32)
    weights = NB * lax.optimization_barrier(jnp.sum(group_transport_plan * picked, axis=1))
    keys_far = keys_all[chosen]
    values_far = values_all[chosen]
    head_scale = (features // HEADS) ** (-0.5)
    near_scores = jnp.einsum('nqhd,nkhd->nhqk', queries, keys_all, precision=PRECISE)
    far_scores = jnp.einsum('nqhd,nkhd->nhqk', queries, keys_far, precision=PRECISE)
    scores = low_back(jnp.concatenate([near_scores, far_scores], axis=-1) * head_scale)
    probabilities = low(jax.nn.softmax(scores, axis=-1))
    near_out = jnp.einsum('nhqk,nkhd->nqhd', probabilities[..., :block_size], values_all, precision=PRECISE)
    far_out = jnp.einsum('nhqk,nkhd->nqhd', probabilities[..., block_size:], values_far, precision=PRECISE)
    mixture = near_out + weights[:, None, None, None] * far_out
    attended = low(low_back(mixture.reshape(length, features)))
    branch = low_back(matrix_product(attended, out_weight))
    middle = inputs + branch
    normed_two = normalize(middle, gain_second)
    hidden = low_back(matrix_product(low(normed_two), up_weight))
    active = low(jax.nn.gelu(hidden))
    return middle + low_back(matrix_product(active, down_weight))

def reference(x_a, x_b, sel_a, sel_b, gain_one, w_qkv, w_out, w_sort, gain_two, w_up, w_down, cot_a, cot_b):
    params = (gain_one.astype(jnp.float32), w_qkv.astype(jnp.float32), w_out.astype(jnp.float32), w_sort.astype(jnp.float32), gain_two.astype(jnp.float32), w_up.astype(jnp.float32), w_down.astype(jnp.float32))

    def forward(inputs_a, inputs_b, *weights):

        def run_first(operands):
            return one_sequence(operands[0], operands[1], weights, BLOCK_A)

        def run_second(operands):
            return one_sequence(operands[0], operands[1], weights, BLOCK_B)
        result_a = lax.map(jax.checkpoint(run_first), (inputs_a, sel_a))
        result_b = lax.map(jax.checkpoint(run_second), (inputs_b, sel_b))
        return (result_a, result_b)
    primal, pullback = jax.vjp(forward, x_a.astype(jnp.float32), x_b.astype(jnp.float32), *params)
    grads = pullback((cot_a.astype(jnp.float32), cot_b.astype(jnp.float32)))
    return (primal[0].astype(jnp.bfloat16), primal[1].astype(jnp.bfloat16), grads[0].astype(jnp.bfloat16), grads[1].astype(jnp.bfloat16), grads[2], grads[3], grads[4], grads[5], grads[6], grads[7], grads[8])
```

```python
import functools

import jax
import jax.numpy as jnp
import numpy as np
from jax import lax
from jax.experimental import pallas as pl
from jax.experimental.pallas import tpu as pltpu
from jax.sharding import PartitionSpec as P

HEADS = 8
SINK_ITERS = 8
EPSILON = 1e-05
SOFTMAX_HEAT = 0.75
UNIT = 32
EXTRA = 256
GROUP = 64
TILE = 256
HALF = 256
PER_HALF = 4
VMEM_LIMIT = 58 * 1024 * 1024

F32 = jnp.float32
BF16 = jnp.bfloat16

NN = (((1,), (0,)), ((), ()))
NT = (((1,), (1,)), ((), ()))
TN = (((0,), (0,)), ((), ()))


def dot(a, b, dims=NN):
    return lax.dot_general(a, b, dims, preferred_element_type=F32)


def inverse_norm(values):
    return lax.rsqrt(jnp.mean(values * values, axis=-1, keepdims=True) + EPSILON)


def whole(shape):
    zeros = (0,) * len(shape)
    return pl.BlockSpec(shape, lambda *_: zeros, pipeline_mode=pl.Buffered(1))


def rows_of(tile, width):
    return pl.BlockSpec((tile, width), lambda i: (i, 0))


SMEM = pl.BlockSpec(memory_space=pltpu.SMEM)


def params():
    return pltpu.CompilerParams(
        dimension_semantics=("arbitrary",), vmem_limit_bytes=VMEM_LIMIT
    )


def cost(flops, nbytes):
    return pl.CostEstimate(flops=int(flops * 1e-3), bytes_accessed=int(nbytes * 1e-3), transcendentals=0)


ANY = pl.BlockSpec(memory_space=pl.ANY)
VMEM = pl.BlockSpec(memory_space=pltpu.VMEM)


def limit(mib):
    return pltpu.CompilerParams(vmem_limit_bytes=mib * 1024 * 1024)


def request_kernel(
    npl, seqs_a, seqs_b, devices, capacity, first, early, sizes, extra, spare_rows,
    sel_ref, table_ref, back_ref, far_ref, ret_ref, perm_ref, place_ref, kinds_ref, fill, begin, used,
):
    count_a = seqs_a * npl
    count_b = seqs_b * npl
    units_a = 2 * count_a
    width = sum(sizes)
    shift = npl.bit_length() - 1 if npl & (npl - 1) == 0 else -1

    def split(chosen):
        if shift >= 0:
            return lax.shift_right_logical(chosen, shift), lax.bitwise_and(chosen, npl - 1)
        return lax.div(chosen, npl), lax.rem(chosen, npl)

    def clear(ref):
        def body(i, carry):
            ref[i] = -1
            return carry

        return body

    lax.fori_loop(0, devices * capacity, clear(table_ref), 0)
    lax.fori_loop(0, devices * width, clear(back_ref), 0)
    for s in range(devices):
        fill[s] = 0
        used[s] = 0
        used[devices + s] = 0
    one = lambda flag: jnp.where(flag, 1, 0)
    ready_a, ready_b, must_a, must_b = (jnp.int32(0) for _ in range(4))
    for j in range(count_a + count_b):
        source, inner = split(sel_ref[j])
        slot = fill[source]
        begin[j] = slot
        size = 2 if j < count_a else 1
        fill[source] = slot + size
        if j < count_a:
            unit = inner * 2 + (j // npl) * npl * 2
            ready_a = ready_a + one(slot + 2 <= first)
            table_ref[source * capacity + slot + 1] = unit + 1
        else:
            unit = inner + (units_a + (j - count_a) // npl * npl)
            ready_b = ready_b + one(slot + 1 <= first)
        table_ref[source * capacity + slot] = unit

    two = early < count_a + count_b // 2

    def must(j):
        source, _ = split(sel_ref[j])
        if not two:
            return begin[j] < 0
        return begin[j] < fill[source] - 6

    for j in range(count_a):
        must_a = must_a + one(must(j))
    for j in range(count_b):
        must_b = must_b + one(must(count_a + j))
    even = jnp.logical_or(lax.bitwise_and(must_b, 1) == 0, ready_b > must_b)
    pairs = lax.shift_right_logical(must_b + one(even), 1)
    take_a = jnp.minimum(ready_a, early - pairs)
    if not two:
        take_a = jnp.int32(count_a)
    take_b = 2 * (early - take_a)
    late_b = 2 * (early + count_a - take_a)
    kinds_ref[0] = take_a
    kinds_ref[1] = early + count_a - take_a
    second = devices * first * UNIT

    def ret_row(phase, source, slot):
        chunks = list(enumerate(sizes))
        if two:
            chunks = chunks[:1] if phase == 0 else chunks[1:]
        row = jnp.int32(0)
        begin_slot, begin_row = 0, 0
        for index, size in chunks:
            height = size * UNIT + (extra if index == len(sizes) - 1 else 0)
            here = begin_row + source * height + (slot - begin_slot) * UNIT
            row = jnp.where(slot >= begin_slot, here, row)
            begin_slot += size
            begin_row += devices * height
        return row

    def put(pos, unit, inner, source, slot, late):
        near = (source * first + slot) * UNIT
        rest = second + source * ((capacity - first) * UNIT + spare_rows) + (slot - first) * UNIT
        far_ref[pos] = jnp.where(slot < first, near, rest)
        at = late * devices + source
        back = used[at]
        used[at] = back + 1
        if two:
            ret_ref[pos] = jnp.where(late == 0, ret_row(0, source, back), ret_row(1, source, back))
            back_ref[source * width + back + late * sizes[0]] = inner
        else:
            ret_ref[pos] = ret_row(0, source, back)
            back_ref[source * width + back] = inner
        perm_ref[pos] = unit
        place_ref[unit] = pos

    spare = take_a - must_a
    taken, other, free = (jnp.int32(0) for _ in range(3))
    for j in range(count_a):
        source, inner = split(sel_ref[j])
        slot = begin[j]
        need = must(j)
        pick = jnp.logical_and(jnp.logical_not(need), jnp.logical_and(slot + 2 <= first, free < spare))
        use = jnp.logical_or(need, pick)
        free = free + one(pick)
        pos = 2 * jnp.where(use, taken, early + other)
        inner = inner * 2 + (j // npl) * npl * 2
        put(pos, 2 * j, inner, source, slot, one(jnp.logical_not(use)))
        put(pos + 1, 2 * j + 1, inner + 1, source, slot + 1, one(jnp.logical_not(use)))
        taken = taken + one(use)
        other = other + one(jnp.logical_not(use))
    spare = take_b - must_b
    drop = one(spare < 0)
    taken, other, free = (jnp.int32(0) for _ in range(3))
    for j in range(count_b):
        source, inner = split(sel_ref[count_a + j])
        slot = begin[count_a + j]
        need = must(count_a + j)
        skip = jnp.logical_and(need, drop > 0)
        drop = drop - one(skip)
        pick = jnp.logical_and(jnp.logical_not(need), jnp.logical_and(slot + 1 <= first, free < spare))
        use = jnp.logical_or(jnp.logical_and(need, jnp.logical_not(skip)), pick)
        free = free + one(pick)
        pos = jnp.where(use, 2 * take_a + taken, late_b + other)
        inner = inner + (units_a + (j // npl) * npl)
        put(pos, units_a + j, inner, source, slot, one(jnp.logical_not(use)))
        taken = taken + one(use)
        other = other + one(jnp.logical_not(use))


def request(sel, npl, seqs_a, seqs_b, devices, capacity, first, early, sizes, extra, spare_rows):
    units = npl * (2 * seqs_a + seqs_b)
    counts = [devices * capacity, devices * sum(sizes), units, units, units, units, 2]
    return pl.pallas_call(
        functools.partial(
            request_kernel, npl, seqs_a, seqs_b, devices, capacity, first, early, sizes, extra,
            spare_rows,
        ),
        in_specs=[SMEM],
        out_specs=[SMEM] * len(counts),
        out_shape=[jax.ShapeDtypeStruct((n,), jnp.int32) for n in counts],
        scratch_shapes=[
            pltpu.SMEM((devices,), jnp.int32),
            pltpu.SMEM((npl * (seqs_a + seqs_b),), jnp.int32),
            pltpu.SMEM((2 * devices,), jnp.int32),
        ],
        cost_estimate=cost(1000, 2000),
        name="request",
    )(sel)


def digest_kernel(
    tiles_a, xa_ref, xb_ref, gain_ref, avg_ref, wsort_ref, x_ref, means_ref, logits_ref, sums
):
    step = pl.program_id(0)

    def take(src):
        x = src[...]
        x_ref[...] = x
        x = x.astype(F32)
        scaled = x * inverse_norm(x)
        units = x.shape[0] // UNIT
        at = pl.ds(pl.multiple_of(step * units, units), units)
        sums[at, :] = jnp.sum(scaled.reshape(units, UNIT, x.shape[1]), axis=1)

    pl.when(step < tiles_a)(lambda: take(xa_ref))
    pl.when(step >= tiles_a)(lambda: take(xb_ref))

    @pl.when(step == pl.num_programs(0) - 1)
    def _():
        means = lax.dot_general(
            avg_ref[...], sums[...], NN, precision=lax.Precision.HIGHEST, preferred_element_type=F32
        )
        means_ref[...] = means
        summary = means * gain_ref[...]
        unit = (summary * inverse_norm(summary)).astype(BF16)
        logits_ref[...] = dot(unit, wsort_ref[...]) * (1.0 / SOFTMAX_HEAT)


def digest(x_a, x_b, gain_row, average, w_sort):
    width = x_a.shape[1]
    tiles_a = x_a.shape[0] // TILE
    tiles_b = x_b.shape[0] // TILE
    rows = x_a.shape[0] + x_b.shape[0]
    picks = average.shape[0]
    return pl.pallas_call(
        functools.partial(digest_kernel, tiles_a),
        grid=(tiles_a + tiles_b,),
        in_specs=[
            pl.BlockSpec((TILE, width), lambda i: (jnp.minimum(i, tiles_a - 1), 0)),
            pl.BlockSpec((TILE, width), lambda i: (jnp.maximum(i - tiles_a, 0), 0)),
            whole((1, width)),
            whole(average.shape),
            whole(w_sort.shape),
        ],
        out_specs=[rows_of(TILE, width), whole((picks, width)), whole((picks, w_sort.shape[1]))],
        out_shape=[
            jax.ShapeDtypeStruct((rows, width), BF16),
            jax.ShapeDtypeStruct((picks, width), F32),
            jax.ShapeDtypeStruct((picks, w_sort.shape[1]), F32),
        ],
        scratch_shapes=[pltpu.VMEM((rows // UNIT, width), F32)],
        compiler_params=params(),
        cost_estimate=cost(rows * width * 10, rows * width * 4),
        name="digest",
    )(x_a, x_b, gain_row, average, w_sort)


def pack_kernel(devices, capacity, first, spare, table_ref, x_ref, *rest):
    outs = rest[: 1 if first == capacity else 2]
    held, sems = rest[len(outs) :]
    sizes = [first, capacity - first]
    copies = []
    for part, out_ref in enumerate(outs):
        size = sizes[part]
        base = part * devices * first
        for r in range(devices):
            for slot in range(size):
                unit = jnp.maximum(table_ref[r * capacity + part * first + slot], 0)
                src = pl.ds(pl.multiple_of(unit * UNIT, UNIT), UNIT)
                at = (base + r * size + slot) * UNIT
                held[at : at + UNIT, :] = x_ref[src, :]
            at = (base + r * size) * UNIT
            copy = pltpu.make_async_copy(
                held.at[pl.ds(at, size * UNIT)],
                out_ref.at[pl.ds(r * (size * UNIT + part * spare), size * UNIT)],
                sems.at[part * devices + r],
            )
            copy.start()
            copies.append(copy)
    for copy in copies:
        copy.wait()


def pack(table, x, devices, capacity, first, spare):
    width = x.shape[1]
    sizes = [first] if first == capacity else [first, capacity - first]
    return pl.pallas_call(
        functools.partial(pack_kernel, devices, capacity, first, spare),
        in_specs=[SMEM, VMEM],
        out_specs=[ANY] * len(sizes),
        out_shape=[
            jax.ShapeDtypeStruct((devices * (n * UNIT + i * spare), width), BF16)
            for i, n in enumerate(sizes)
        ],
        scratch_shapes=[
            pltpu.VMEM((devices * capacity * UNIT, width), BF16),
            pltpu.SemaphoreType.DMA((len(sizes) * devices,)),
        ],
        compiler_params=limit(12),
        cost_estimate=cost(0, x.size * 6),
        name="pack",
    )(table, x)


def arrange_kernel(units_a, perm_ref, x_ref, cota_ref, cotb_ref, xp_ref, cotp_ref):
    def body(pos, carry):
        unit = perm_ref[pos]
        at = pl.ds(pl.multiple_of(pos * UNIT, UNIT), UNIT)
        xp_ref[at, :] = x_ref[pl.ds(pl.multiple_of(unit * UNIT, UNIT), UNIT), :]

        @pl.when(unit < units_a)
        def _():
            cotp_ref[at, :] = cota_ref[pl.ds(pl.multiple_of(unit * UNIT, UNIT), UNIT), :]

        @pl.when(unit >= units_a)
        def _():
            src = pl.ds(pl.multiple_of((unit - units_a) * UNIT, UNIT), UNIT)
            cotp_ref[at, :] = cotb_ref[src, :]

        return carry

    lax.fori_loop(0, x_ref.shape[0] // UNIT, body, 0)


def arrange(perm, x, cot_a, cot_b):
    like = jax.ShapeDtypeStruct(x.shape, BF16)
    return pl.pallas_call(
        functools.partial(arrange_kernel, cot_a.shape[0] // UNIT),
        in_specs=[SMEM, VMEM, VMEM, VMEM],
        out_specs=[VMEM, VMEM],
        out_shape=[like, like],
        compiler_params=limit(16),
        cost_estimate=cost(0, x.size * 8),
        name="arrange",
    )(perm, x, cot_a, cot_b)


def restore_kernel(perm_ref, out_ref, outa_ref, outb_ref):
    units_a = outa_ref.shape[0] // UNIT

    def body(pos, carry):
        unit = perm_ref[pos]
        at = pl.ds(pl.multiple_of(pos * UNIT, UNIT), UNIT)

        @pl.when(unit < units_a)
        def _():
            outa_ref[pl.ds(pl.multiple_of(unit * UNIT, UNIT), UNIT), :] = out_ref[at, :]

        @pl.when(unit >= units_a)
        def _():
            dst = pl.ds(pl.multiple_of((unit - units_a) * UNIT, UNIT), UNIT)
            outb_ref[dst, :] = out_ref[at, :]

        return carry

    lax.fori_loop(0, out_ref.shape[0] // UNIT, body, 0)


def restore(perm, out, rows_a):
    rows, width = out.shape
    return pl.pallas_call(
        restore_kernel,
        in_specs=[SMEM, VMEM],
        out_specs=[VMEM, VMEM],
        out_shape=[
            jax.ShapeDtypeStruct((rows_a, width), BF16),
            jax.ShapeDtypeStruct((rows - rows_a, width), BF16),
        ],
        compiler_params=limit(16),
        cost_estimate=cost(0, out.size * 4),
        name="restore",
    )(perm, out)


def project_kernel(x_ref, gain_ref, w_ref, proj_ref):
    x = x_ref[...].astype(F32)
    proj_ref[...] = dot((x * inverse_norm(x) * gain_ref[...]).astype(BF16), w_ref[...]).astype(BF16)


def project(x, gain_row, w_qkv):
    rows, width = x.shape
    wide = w_qkv.shape[1]
    return pl.pallas_call(
        project_kernel,
        grid=(rows // TILE,),
        in_specs=[rows_of(TILE, width), whole((1, width)), whole((width, wide))],
        out_specs=rows_of(TILE, wide),
        out_shape=jax.ShapeDtypeStruct((rows, wide), BF16),
        compiler_params=params(),
        cost_estimate=cost(2 * rows * width * wide, rows * (width + wide) * 2),
        name="project",
    )(x, gain_row, w_qkv)


def log_sum(values, axis):
    top = jnp.max(values, axis=axis, keepdims=True)
    return top + jnp.log(jnp.sum(jnp.exp(values - top), axis=axis, keepdims=True))


def sinkhorn_kernel(logits_ref, picked_ref, weight_ref):
    state = logits_ref[...]
    for _ in range(SINK_ITERS):
        state = state - log_sum(state, 2)
        state = state - log_sum(state, 1)
    count = state.shape[1]
    weight = count * jnp.sum(jnp.exp(state) * picked_ref[...], axis=2, keepdims=True)
    weight_ref[...] = jnp.broadcast_to(weight, weight_ref.shape)


def sinkhorn(logits, picked):
    seqs, count, _ = logits.shape
    return pl.pallas_call(
        sinkhorn_kernel,
        out_shape=jax.ShapeDtypeStruct((seqs, count, 128), F32),
        cost_estimate=cost(logits.size * 100, logits.size * 32),
        name="sinkhorn",
    )(logits, picked)


def sinkhorn_back_kernel(logits_ref, picked_ref, gw_ref, out_ref, kept):
    state = logits_ref[...]
    for step in range(SINK_ITERS):
        state = state - log_sum(state, 2)
        kept[2 * step] = jnp.exp(state)
        state = state - log_sum(state, 1)
        kept[2 * step + 1] = jnp.exp(state)
    count = state.shape[1]
    grad = count * picked_ref[...] * gw_ref[...] * jnp.exp(state)
    for step in reversed(range(SINK_ITERS)):
        grad = grad - kept[2 * step + 1] * jnp.sum(grad, axis=1, keepdims=True)
        grad = grad - kept[2 * step] * jnp.sum(grad, axis=2, keepdims=True)
    out_ref[...] = grad


def sinkhorn_back(logits, picked, gw):
    return pl.pallas_call(
        sinkhorn_back_kernel,
        out_shape=jax.ShapeDtypeStruct(logits.shape, F32),
        scratch_shapes=[pltpu.VMEM((2 * SINK_ITERS,) + logits.shape, F32)],
        compiler_params=pltpu.CompilerParams(vmem_limit_bytes=VMEM_LIMIT),
        cost_estimate=cost(logits.size * 200, logits.size * 32),
        name="sinkhorn_back",
    )(logits, picked, gw)


def head_masks(rows):
    lane = lax.broadcasted_iota(jnp.int32, (rows, HALF), 1) // (HALF // PER_HALF)
    return [lane == h for h in range(PER_HALF)]


def stack_heads(values, masks):
    zero = jnp.zeros_like(values)
    return jnp.concatenate([jnp.where(m, values, zero) for m in masks], axis=0)


def unstack_heads(values, masks):
    total = None
    for h, m in enumerate(masks):
        part = jnp.where(m, values[h * GROUP : (h + 1) * GROUP], 0.0)
        total = part if total is None else total + part
    return total


def repeat_heads(values):
    return jnp.concatenate([values] * PER_HALF, axis=0)


def forward_kernel(first_group, recvs, prior, final, *refs):
    refs = list(refs)
    take = lambda n: [refs.pop(0) for _ in range(n)]
    far_ref, kinds_ref, core_ref = take(3)
    recv_refs = take(recvs)
    (
        x_ref, cot_ref, proj_ref, wrow_ref, mask_ref, gain1_ref, gain2_ref,
        wqkv_ref, wout_ref, wup_ref, wdown_ref,
    ) = take(11)
    take(1)
    prior_refs = take(3) if prior else []
    if prior:
        take(6)
    out_ref, gmid_ref, gatt_ref, prob_ref, farx_ref, farkv_ref = take(6)
    if final:
        keep_ref, give_ref, gain_ref = take(3)
    else:
        up_ref, down_ref, gain_ref = take(3)
    attended, up_acc, down_acc, wo_acc, gain_acc = take(5)
    if prior:
        up_prior, down_prior, sems = take(3)
    step = pl.program_id(0)
    steps = pl.num_programs(0)
    tile, width = x_ref.shape
    ff = wup_ref.shape[1]
    units = tile // UNIT
    groups = tile // GROUP
    base = first_group + step * groups
    rows_one = recv_refs[0].shape[0]
    for u in range(units):
        row = far_ref[2 * base + u]
        dst = pl.ds(u * UNIT, UNIT)
        if recvs == 1:
            farx_ref[dst, :] = recv_refs[0][pl.ds(pl.multiple_of(row, UNIT), UNIT), :]
        else:

            @pl.when(row < rows_one)
            def _():
                farx_ref[dst, :] = recv_refs[0][pl.ds(pl.multiple_of(row, 16), UNIT), :]

            @pl.when(row >= rows_one)
            def _():
                src = pl.ds(pl.multiple_of(row - rows_one, 16), UNIT)
                farx_ref[dst, :] = recv_refs[1][src, :]

    if prior:
        moves = [
            pltpu.make_async_copy(prior_refs[0], up_prior, sems.at[0]),
            pltpu.make_async_copy(prior_refs[1], down_prior, sems.at[1]),
        ]

        @pl.when(step == 0)
        def _():
            for move in moves:
                move.start()

    far = farx_ref[...].astype(F32)
    far = (far * inverse_norm(far) * gain1_ref[...]).astype(BF16)
    farkv_ref[...] = dot(far, wqkv_ref[:, width:]).astype(BF16)
    masks16 = head_masks(GROUP)
    head_scale = (width // HEADS) ** -0.5
    boundary = kinds_ref[1 if prior else 0]

    def group_step(i, carry):
        rows = pl.ds(pl.multiple_of(i * GROUP, GROUP), GROUP)
        which = jnp.where(base + i < boundary, 0, 1)
        barrier = repeat_heads(mask_ref[which])
        scale = repeat_heads(wrow_ref[rows, :])
        for half in range(width // HALF):
            lo = half * HALF
            q = proj_ref[rows, lo : lo + HALF] * jnp.asarray(head_scale, BF16)
            keys = jnp.concatenate(
                [proj_ref[rows, width + lo : width + lo + HALF], farkv_ref[rows, lo : lo + HALF]],
                axis=0,
            )
            vals = jnp.concatenate(
                [
                    proj_ref[rows, 2 * width + lo : 2 * width + lo + HALF],
                    farkv_ref[rows, width + lo : width + lo + HALF],
                ],
                axis=0,
            )
            scores = dot(stack_heads(q, masks16), keys, NT) + barrier
            top = jnp.max(scores, axis=1, keepdims=True)
            weight = jnp.exp(scores - top)
            prob = weight * (1.0 / jnp.sum(weight, axis=1, keepdims=True))
            prob_ref[i, half] = prob.astype(BF16)
            mixed = dot((prob * scale).astype(BF16), vals)
            attended[rows, lo : lo + HALF] = unstack_heads(mixed, masks16).astype(BF16)
        return carry

    lax.fori_loop(0, groups, group_step, 0, unroll=True)

    att = attended[...]
    middle = x_ref[...].astype(F32) + dot(att, wout_ref[...])
    r2 = inverse_norm(middle)
    scaled = middle * r2
    second = (scaled * gain2_ref[...]).astype(BF16)
    cot = cot_ref[...]
    cot_t = cot.T
    second_t = second.T

    @pl.when(step == 0)
    def _():
        up_acc[...] = jnp.zeros_like(up_acc)
        down_acc[...] = jnp.zeros_like(down_acc)
        wo_acc[...] = jnp.zeros_like(wo_acc)
        gain_acc[...] = prior_refs[2][...] if prior else jnp.zeros_like(gain_acc)

    result = middle
    back = jnp.zeros((tile, width), F32)
    c0 = 0.7978845608028654
    c1 = 0.044715
    chunk = 512
    for c in range(0, ff, chunk):
        hidden = dot(second, wup_ref[:, c : c + chunk])
        grad = dot(cot, wdown_ref[c : c + chunk, :], NT)
        square = hidden * hidden
        t = jnp.tanh(hidden * (c0 + (c0 * c1) * square))
        left = 0.5 + 0.5 * t
        active = (hidden * left).astype(BF16)
        slope = left + (0.5 * hidden) * (1.0 - t * t) * (c0 + (3.0 * c0 * c1) * square)
        grad = (grad * slope).astype(BF16)
        result = result + dot(active, wdown_ref[c : c + chunk, :])
        back = back + dot(grad, wup_ref[:, c : c + chunk], NT)
        down_acc[:, c : c + chunk] += dot(cot_t, active)
        up_acc[:, c : c + chunk] += dot(second_t, grad)
    out_ref[...] = result.astype(BF16)
    gain_acc[...] += jnp.sum(back * scaled, axis=0, keepdims=True)
    e = back * gain2_ref[...]
    inner = jnp.mean(e * scaled, axis=-1, keepdims=True)
    grad_middle = cot.astype(F32) + r2 * (e - scaled * inner)
    branch = grad_middle.astype(BF16)
    gmid_ref[...] = branch
    wo_acc[...] += dot(att.T, branch)
    gatt_ref[...] = dot(branch, wout_ref[...], NT).astype(BF16)

    @pl.when(step == steps - 1)
    def _():
        gain_ref[...] = gain_acc[...]
        if not final:
            up_ref[:, :ff] = up_acc[...].astype(BF16)
            up_ref[:, ff:] = wo_acc[...].astype(BF16)
            down_ref[...] = down_acc[...].astype(BF16)
            return
        if prior:
            for move in moves:
                move.wait()

        def total(acc, old, lanes):
            value = acc[:, lanes]
            return value + old[:, lanes].astype(F32) if prior else value

        def write(ref, half):
            at = 0
            for c in range(half * ff // 2, (half + 1) * ff // 2, width):
                value = total(up_acc, up_prior if prior else None, slice(c, c + width))
                ref[at : at + width, :] = value.astype(BF16)
                at += width
            lines = slice(half * width // 2, (half + 1) * width // 2)
            value = wo_acc[lines, :]
            if prior:
                value = value + up_prior[lines, ff:].astype(F32)
            ref[at : at + width // 2, :] = value.astype(BF16)
            at += width // 2
            for c in range(half * ff // 2, (half + 1) * ff // 2, width):
                value = total(down_acc, down_prior if prior else None, slice(c, c + width))
                ref[at : at + width, :] = value.T.astype(BF16)
                at += width

        @pl.when(core_ref[0] == 0)
        def _():
            write(keep_ref, 0)
            write(give_ref, 1)

        @pl.when(core_ref[0] == 1)
        def _():
            write(keep_ref, 1)
            write(give_ref, 0)


def forward(
    far_rows, kinds, core, recv, x, cot, proj, wrow, mask, gain1, gain2, w_qkv, w_out, w_up, w_down,
    first_group, groups, prior, final, token,
):
    rows, width = x.shape
    ff = w_up.shape[1]
    per = TILE // GROUP
    skip = first_group // per
    halves = width // HALF
    at = lambda wide: pl.BlockSpec((TILE, wide), lambda i: (i + skip, 0))
    like = lambda wide, kind=BF16: jax.ShapeDtypeStruct((rows, wide), kind)
    probs = jax.ShapeDtypeStruct((rows // GROUP, halves, PER_HALF * GROUP, 2 * GROUP), BF16)
    part = ff + width // 2
    if final:
        tail_shapes = [jax.ShapeDtypeStruct((part, width), BF16)] * 2
    else:
        tail_shapes = [
            jax.ShapeDtypeStruct((width, ff + width), BF16),
            jax.ShapeDtypeStruct((width, ff), BF16),
        ]
    tail_shapes = tail_shapes + [jax.ShapeDtypeStruct((1, width), F32)]
    in_specs = (
        [SMEM, SMEM, SMEM]
        + [whole(r.shape) for r in recv]
        + [at(width), at(width), at(3 * width), at(2 * GROUP)]
        + [whole(v.shape) for v in (mask, gain1, gain2, w_qkv, w_out, w_up, w_down)]
    )
    operands = [far_rows, kinds, core, *recv, x, cot, proj, wrow, mask, gain1, gain2]
    operands += [w_qkv, w_out, w_up, w_down]
    in_specs += [ANY]
    operands += [token]
    scratch = [
        pltpu.VMEM((TILE, width), BF16),
        pltpu.VMEM((width, ff), F32),
        pltpu.VMEM((width, ff), F32),
        pltpu.VMEM((width, width), F32),
        pltpu.VMEM((1, width), F32),
    ]
    aliases = {}
    if prior is not None:
        streams, sums = prior
        in_specs += [ANY, ANY, whole((1, width))] + [ANY] * 6
        operands += list(sums)
        aliases = {len(operands) + i: i for i in range(6)}
        operands += list(streams)
        scratch += [
            pltpu.VMEM((width, ff + width), BF16),
            pltpu.VMEM((width, ff), BF16),
            pltpu.SemaphoreType.DMA((2,)),
        ]
    out = pl.pallas_call(
        functools.partial(forward_kernel, first_group, len(recv), prior is not None, final),
        grid=(groups // per,),
        in_specs=in_specs,
        out_specs=[
            at(width),
            at(width),
            at(width),
            pl.BlockSpec((per,) + probs.shape[1:], lambda i: (i + skip, 0, 0, 0)),
            at(width),
            at(2 * width),
        ]
        + [whole(v.shape) for v in tail_shapes],
        out_shape=[like(width), like(width), like(width), probs, like(width), like(2 * width)]
        + tail_shapes,
        scratch_shapes=scratch,
        input_output_aliases=aliases,
        compiler_params=params(),
        cost_estimate=cost(1.0e9 * groups, 1e6 * groups),
        name="forward",
    )(*operands)
    return out[:6], out[6:]


def backward_kernel(first_group, prior, *refs):
    refs = list(refs)
    take = lambda n: [refs.pop(0) for _ in range(n)]
    (ret_rows,) = take(1)
    proj_ref, farx_ref, farkv_ref, gatt_ref, prob_ref, wrow_ref, wqkv_ref = take(7)
    if prior:
        (prior_gain,) = take(1)
        take(2)
    take(1)
    dproj_ref, dfar_ref, gw_ref, gain_ref = take(4)
    ret_refs = refs
    step = pl.program_id(0)
    tile, width = gatt_ref.shape
    units = tile // UNIT
    groups = tile // GROUP
    masks16 = head_masks(GROUP)
    head_scale = (width // HEADS) ** -0.5

    is_far = lax.broadcasted_iota(jnp.int32, (PER_HALF * GROUP, 2 * GROUP), 1) >= GROUP

    def group_step(i, carry):
        rows = pl.ds(pl.multiple_of(i * GROUP, GROUP), GROUP)
        scale = repeat_heads(wrow_ref[rows, :])
        weight_grad = jnp.zeros((GROUP, 1), F32)
        for half in range(width // HALF):
            lo = half * HALF
            q = proj_ref[rows, lo : lo + HALF] * jnp.asarray(head_scale, BF16)
            keys = jnp.concatenate(
                [proj_ref[rows, width + lo : width + lo + HALF], farkv_ref[rows, lo : lo + HALF]],
                axis=0,
            )
            vals = jnp.concatenate(
                [
                    proj_ref[rows, 2 * width + lo : 2 * width + lo + HALF],
                    farkv_ref[rows, width + lo : width + lo + HALF],
                ],
                axis=0,
            )
            q = stack_heads(q, masks16)
            up = stack_heads(gatt_ref[rows, lo : lo + HALF], masks16)
            prob = prob_ref[i, half].astype(F32)
            raw = dot(up, vals, NT)
            far_sum = jnp.sum(jnp.where(is_far, prob * raw, 0.0), axis=1, keepdims=True)
            mixed = prob * scale
            ds = mixed * raw
            total = jnp.sum(ds, axis=1, keepdims=True)
            ds = (ds - prob * total).astype(BF16)
            dq = unstack_heads(dot(ds, keys), masks16) * head_scale
            dk = dot(ds, q, TN).astype(BF16)
            dv = dot(mixed.astype(BF16), up, TN).astype(BF16)
            dproj_ref[rows, lo : lo + HALF] = dq.astype(BF16)
            dproj_ref[rows, width + lo : width + lo + HALF] = dk[:GROUP]
            dproj_ref[rows, 2 * width + lo : 2 * width + lo + HALF] = dv[:GROUP]
            dfar_ref[rows, lo : lo + HALF] = dk[GROUP:]
            dfar_ref[rows, width + lo : width + lo + HALF] = dv[GROUP:]
            for h in range(PER_HALF):
                weight_grad = weight_grad + far_sum[h * GROUP : (h + 1) * GROUP]
        pair = jnp.broadcast_to(weight_grad, (GROUP, 128)).reshape(GROUP // UNIT, UNIT, 128)
        gw_ref[i] = jnp.sum(pair, axis=1)
        return carry

    lax.fori_loop(0, groups, group_step, 0, unroll=True)

    def scatter(values, first_unit, count):
        for u in range(count):
            row = ret_rows[first_unit + u]
            edge = 0
            for ret_ref in ret_refs:
                inside = jnp.logical_and(row >= edge, row < edge + ret_ref.shape[0])

                @pl.when(inside)
                def _(ret_ref=ret_ref, edge=edge):
                    at = pl.ds(pl.multiple_of(row - edge, 16), UNIT)
                    ret_ref[at, :] = values(u)

                edge += ret_ref.shape[0]

    @pl.when(step == 0)
    def _():
        gain_ref[...] = prior_gain[...] if prior else jnp.zeros_like(gain_ref)

    grad = dot(dfar_ref[...], wqkv_ref[:, width:], NT)
    far = farx_ref[...].astype(F32)
    gain_ref[...] += jnp.sum(grad * (far * inverse_norm(far)), axis=0, keepdims=True)
    grad = grad.astype(BF16)
    scatter(
        lambda u: grad[u * UNIT : (u + 1) * UNIT],
        2 * first_group + step * units,
        units,
    )


def backward(
    ret_rows, proj, farx, farkv, gatt, prob, wrow, w_qkv, sizes, first_group, groups, prior, token
):
    rows, width = gatt.shape
    per = TILE // GROUP
    skip = first_group // per
    at = lambda wide: pl.BlockSpec((TILE, wide), lambda i: (i + skip, 0))
    in_specs = [
        SMEM,
        at(3 * width),
        at(width),
        at(2 * width),
        at(width),
        pl.BlockSpec((per,) + prob.shape[1:], lambda i: (i + skip, 0, 0, 0)),
        at(2 * GROUP),
        whole(w_qkv.shape),
    ]
    operands = [ret_rows, proj, farx, farkv, gatt, prob, wrow, w_qkv]
    aliases = {}
    if prior is not None:
        dproj, dfar, gain = prior
        in_specs += [whole(gain.shape), ANY, ANY]
        aliases = {len(operands) + 1: 0, len(operands) + 2: 1}
        operands += [gain, dproj, dfar]
    in_specs += [ANY]
    operands += [token]
    ret_specs = [whole((n, width)) for n in sizes]
    ret_shapes = [jax.ShapeDtypeStruct((n, width), BF16) for n in sizes]
    return pl.pallas_call(
        functools.partial(backward_kernel, first_group, prior is not None),
        grid=(groups // per,),
        in_specs=in_specs,
        out_specs=[
            at(3 * width),
            at(2 * width),
            pl.BlockSpec((per, GROUP // UNIT, 128), lambda i: (i, 0, 0)),
            whole((1, width)),
        ]
        + ret_specs,
        out_shape=[
            jax.ShapeDtypeStruct((rows, 3 * width), BF16),
            jax.ShapeDtypeStruct((rows, 2 * width), BF16),
            jax.ShapeDtypeStruct((groups, GROUP // UNIT, 128), F32),
            jax.ShapeDtypeStruct((1, width), F32),
        ]
        + ret_shapes,
        input_output_aliases=aliases,
        compiler_params=params(),
        cost_estimate=cost(0.4e9 * groups, 1e6 * groups),
        name="backward",
    )(*operands)


def qkv_kernel(
    extra, core_ref, x_ref, farx_ref, dproj_ref, dfar_ref, gain1_ref, wqkv_ref, gains_ref, token_ref,
    gn_ref, keep_ref, give_ref, acc, gain_acc,
):
    step = pl.program_id(0)
    steps = pl.num_programs(0)
    width = x_ref.shape[1]

    @pl.when(step == 0)
    def _():
        acc[...] = jnp.zeros_like(acc)
        gain_acc[...] = jnp.zeros_like(gain_acc)

    x = x_ref[...].astype(F32)
    scaled = x * inverse_norm(x)
    far = farx_ref[...].astype(F32)
    far = (far * inverse_norm(far) * gain1_ref[...]).astype(BF16)
    near = (scaled * gain1_ref[...]).astype(BF16)
    acc[...] += dot(near.T, dproj_ref[...])
    acc[:, width:] += dot(far.T, dfar_ref[...])
    grad = dot(dproj_ref[...], wqkv_ref[...], NT)
    gn_ref[...] = grad.astype(BF16)
    gain_acc[...] += jnp.sum(grad * scaled, axis=0, keepdims=True)

    @pl.when(step == steps - 1)
    def _():
        line = lax.broadcasted_iota(jnp.int32, (extra, width), 0)
        small = jnp.where(line == 0, gain_acc[...] + gains_ref[0:1, :], 0.0)
        small = jnp.where(line == 1, gains_ref[1:2, :], small)
        total = acc.shape[1] + extra
        half = total // 2

        def write(ref, which):
            at = which * half
            while at < (which + 1) * half:
                block, line = divmod(at, width)
                if at >= acc.shape[1]:
                    count = extra
                    value = small
                else:
                    count = min(width - line, (which + 1) * half - at)
                    value = acc[line : line + count, block * width : (block + 1) * width]
                ref[at - which * half : at - which * half + count, :] = value.astype(BF16)
                at += count

        @pl.when(core_ref[0] == 0)
        def _():
            write(keep_ref, 0)
            write(give_ref, 1)

        @pl.when(core_ref[0] == 1)
        def _():
            write(keep_ref, 1)
            write(give_ref, 0)


def qkv_grads(core, x, farx, dproj, dfar, gain1, w_qkv, gains, extra, token):
    rows, width = x.shape
    wide = w_qkv.shape[1]
    half = (wide + extra) // 2
    return pl.pallas_call(
        functools.partial(qkv_kernel, extra),
        grid=(rows // TILE,),
        in_specs=[
            SMEM,
            rows_of(TILE, width),
            rows_of(TILE, width),
            rows_of(TILE, wide),
            rows_of(TILE, 2 * width),
            whole((1, width)),
            whole(w_qkv.shape),
            whole(gains.shape),
            ANY,
        ],
        out_specs=[rows_of(TILE, width), whole((half, width)), whole((half, width))],
        out_shape=[
            jax.ShapeDtypeStruct((rows, width), BF16),
            jax.ShapeDtypeStruct((half, width), BF16),
            jax.ShapeDtypeStruct((half, width), BF16),
        ],
        scratch_shapes=[pltpu.VMEM((width, wide), F32), pltpu.VMEM((1, width), F32)],
        compiler_params=params(),
        cost_estimate=cost(10e9, 25e6),
        name="qkv_grads",
    )(core, x, farx, dproj, dfar, gain1, w_qkv, gains, token)


def row_gradient(f, x):
    r1 = inverse_norm(x)
    scaled = x * r1
    return r1 * (f - scaled * jnp.mean(f * scaled, axis=-1, keepdims=True))


def base_kernel(x_ref, gmid_ref, gn_ref, gs_ref, gain1_ref, out_ref):
    rows, width = x_ref.shape
    spread = jnp.broadcast_to(gs_ref[...][:, None, :], (rows // UNIT, UNIT, width))
    f = (gn_ref[...].astype(F32) + spread.reshape(rows, width)) * gain1_ref[...]
    grad = gmid_ref[...].astype(F32) + row_gradient(f, x_ref[...].astype(F32))
    out_ref[...] = grad.astype(BF16)


def base_rows(x, gmid, gn, gs, gain1):
    rows, width = x.shape
    return pl.pallas_call(
        base_kernel,
        grid=(rows // TILE,),
        in_specs=[
            rows_of(TILE, width),
            rows_of(TILE, width),
            rows_of(TILE, width),
            rows_of(TILE // UNIT, width),
            whole((1, width)),
        ],
        out_specs=rows_of(TILE, width),
        out_shape=jax.ShapeDtypeStruct((rows, width), BF16),
        compiler_params=params(),
        cost_estimate=cost(rows * width * 20, rows * width * 8),
        name="base",
    )(x, gmid, gn, gs, gain1)


def last_kernel(sizes, extra, capacity, table_ref, place_ref, *refs):
    ret_refs = refs[: len(sizes)]
    x_ref, base_ref, gain1_ref, outa_ref, outb_ref, acc = refs[len(sizes) :]
    rows_a = outa_ref.shape[0]
    acc[...] = jnp.zeros_like(acc)

    begin = 0
    for index, (size, ret_ref) in enumerate(zip(sizes, ret_refs)):
        height = size * UNIT + (extra if index == len(sizes) - 1 else 0)

        def add(r, carry, size=size, ret_ref=ret_ref, begin=begin, height=height):
            for slot in range(size):
                unit = table_ref[r * capacity + begin + slot]

                @pl.when(unit >= 0)
                def _():
                    at = pl.ds(pl.multiple_of(unit * UNIT, UNIT), UNIT)
                    src = pl.ds(pl.multiple_of(r * height + slot * UNIT, 16), UNIT)
                    acc[at, :] += ret_ref[src, :].astype(F32)

            return carry

        lax.fori_loop(0, ret_ref.shape[0] // height, add, 0)
        begin += size

    def finish(out_ref, first):
        def body(u, carry):
            at = pl.ds(pl.multiple_of(place_ref[first + u] * UNIT, UNIT), UNIT)
            own = pl.ds(pl.multiple_of((first + u) * UNIT, UNIT), UNIT)
            f = acc[own, :] * gain1_ref[...]
            grad = base_ref[at, :].astype(F32) + row_gradient(f, x_ref[own, :].astype(F32))
            out_ref[pl.ds(pl.multiple_of(u * UNIT, UNIT), UNIT), :] = grad.astype(BF16)
            return carry

        lax.fori_loop(0, out_ref.shape[0] // UNIT, body, 0, unroll=2)

    finish(outa_ref, 0)
    finish(outb_ref, rows_a // UNIT)


def last(table, place, ret, sizes, extra, capacity, x, base, gain1, rows_a):
    rows, width = x.shape
    return pl.pallas_call(
        functools.partial(last_kernel, sizes, extra, capacity),
        in_specs=[SMEM, SMEM] + [VMEM] * (len(ret) + 3),
        out_specs=[VMEM, VMEM],
        out_shape=[
            jax.ShapeDtypeStruct((rows_a, width), BF16),
            jax.ShapeDtypeStruct((rows - rows_a, width), BF16),
        ],
        scratch_shapes=[pltpu.VMEM((rows, width), F32)],
        compiler_params=limit(24),
        cost_estimate=cost(rows * width * 20, rows * width * 12),
        name="last",
    )(table, place, *ret, x, base, gain1)


def bits_of(size):
    count = 0
    while (1 << count) < size:
        count += 1
    return count


def bit_of(axis, bit):
    return (lax.axis_index(axis) >> bit) & 1


def swap(values, axis, bit):
    size = lax.axis_size(axis)
    return lax.ppermute(values, axis, [(i, i ^ (1 << bit)) for i in range(size)])


def halve(values, axis, bit):
    half = values.shape[0] // 2
    mine = bit_of(axis, bit)
    keep = lax.dynamic_slice_in_dim(values, mine * half, half, 0)
    give = lax.dynamic_slice_in_dim(values, (1 - mine) * half, half, 0)
    return keep, give


def double(values, axis, bit):
    got = swap(values, axis, bit)
    return jnp.where(
        bit_of(axis, bit) == 0,
        jnp.concatenate([values, got], axis=0),
        jnp.concatenate([got, values], axis=0),
    )


def add(one, two):
    return (one.astype(F32) + two.astype(F32)).astype(BF16)


def reduce_any(values, order):
    for axis, bit in order:
        keep, give = halve(values, axis, bit)
        values = add(keep, swap(give, axis, bit))
    for axis, bit in reversed(order):
        values = double(values, axis, bit)
    return values


def tie(values, *tokens):
    return pl.pallas_call(
        lambda *refs: None,
        in_specs=[ANY] * (1 + len(tokens)),
        out_specs=ANY,
        out_shape=jax.ShapeDtypeStruct(values.shape, values.dtype),
        input_output_aliases={0: 0},
        name="tie",
    )(values, *tokens)


def halve_kernel(ranges, sources, bits_ref, *refs):
    outs = refs[2 * sources + 1 :]
    for source, first, count, bit, out, there in ranges:
        own, came = refs[2 * source], refs[2 * source + 1]
        half = count // 2
        keep = pl.multiple_of(first + bits_ref[bit] * half, 16)
        give = pl.multiple_of(first + (1 - bits_ref[bit]) * half, 16)
        for ref, line in ((outs[2 * out], keep), (outs[2 * out + 1], give)):
            rows = pl.ds(line, half)
            total = own[rows, :].astype(F32) + came[rows, :].astype(F32)
            ref[there : there + half, :] = total.astype(BF16)


def halve_step(ranges, bits, pairs, token):
    width = pairs[0][0].shape[1]
    count = 1 + max(r[4] for r in ranges)
    heights = [max(r[5] + r[2] // 2 for r in ranges if r[4] == out) for out in range(count)]
    shapes = [jax.ShapeDtypeStruct((n, width), BF16) for n in heights for _ in range(2)]
    flat = [v for pair in pairs for v in pair]
    out = pl.pallas_call(
        functools.partial(halve_kernel, ranges, len(pairs)),
        in_specs=[SMEM] + [VMEM] * len(flat) + [ANY],
        out_specs=[VMEM] * len(shapes),
        out_shape=shapes,
        compiler_params=limit(24),
        cost_estimate=cost(0, 8 * sum(heights) * width),
        name="halve_step",
    )(jnp.stack([bit_of(*b) for b in bits]).astype(jnp.int32), *flat, token)
    return [(out[2 * i], out[2 * i + 1]) for i in range(count)]


def double_kernel(ranges, sources, tokens, bits_ref, *refs):
    outs = refs[2 * sources + tokens :]
    for source, first, count, bit, out, there in ranges:
        own, came = refs[2 * out], refs[2 * out + 1]
        half = count // 2
        keep = pl.multiple_of(first + bits_ref[bit] * half, 16)
        give = pl.multiple_of(first + (1 - bits_ref[bit]) * half, 16)
        outs[source][pl.ds(keep, half), :] = own[there : there + half, :]
        outs[source][pl.ds(give, half), :] = came[there : there + half, :]


def double_step(ranges, bits, pairs, *tokens):
    width = pairs[0][0].shape[1]
    count = 1 + max(r[0] for r in ranges)
    heights = [max(r[1] + r[2] for r in ranges if r[0] == source) for source in range(count)]
    flat = [v for pair in pairs for v in pair]
    return pl.pallas_call(
        functools.partial(double_kernel, ranges, len(pairs), len(tokens)),
        in_specs=[SMEM] + [VMEM] * len(flat) + [ANY] * len(tokens),
        out_specs=[VMEM] * count,
        out_shape=[jax.ShapeDtypeStruct((n, width), BF16) for n in heights],
        compiler_params=limit(24),
        cost_estimate=cost(0, 4 * sum(heights) * width),
        name="double_step",
    )(jnp.stack([bit_of(*b) for b in bits]).astype(jnp.int32), *flat, *tokens)


AXIS_X, AXIS_Y, AXIS_Z0, AXIS_Z1 = ("dp", 1), ("blk", 0), ("blk", 1), ("blk", 2)


def places(half, width, ff):
    up, down, out, qkv, gains = range(5)
    edge = ff // 2
    result = [
        (c, width, up, 0, half * edge + c) for c in range(0, edge, width)
    ]
    result.append((edge, width // 2, out, half * (width // 2), 0))
    result += [
        (edge + width // 2 + c, width, down, half * edge + c, 0) for c in range(0, edge, width)
    ]
    start = edge + width // 2 + edge
    total = 3 * width + EXTRA
    at = half * total // 2
    while at < (half + 1) * total // 2:
        block, line = divmod(at, width)
        if at >= 3 * width:
            result.append((start + at - half * total // 2, 16, gains, 0, 0))
            break
        count = min(width - line, (half + 1) * total // 2 - at)
        result.append((start + at - half * total // 2, count, qkv, line, block * width))
        at += count
    return result


def assemble_kernel(which, prior, width, ff, core_ref, values_ref, *refs):
    outs = refs[5 if prior else 0 :][:5]
    held, sems = refs[-2:]

    def write(half):
        copies = []
        for i, (first, count, out, line, column) in enumerate(places(half, width, ff)):
            held[first : first + count, :] = values_ref[first : first + count, :].astype(F32)
            copy = pltpu.make_async_copy(
                held.at[pl.ds(first, count)],
                outs[out].at[pl.ds(line, count), pl.ds(column, width)],
                sems.at[i],
            )
            copy.start()
            copies.append(copy)
        for copy in copies:
            copy.wait()

    @pl.when(core_ref[0] == which)
    def _():
        write(0)

    @pl.when(core_ref[0] != which)
    def _():
        write(1)


def assemble(core, which, values, width, ff, prior):
    shapes = [(width, ff), (ff, width), (width, width), (width, 3 * width), (16, width)]
    operands = [core, values] + (list(prior) if prior is not None else [])
    most = max(len(places(half, width, ff)) for half in (0, 1))
    return pl.pallas_call(
        functools.partial(assemble_kernel, which, prior is not None, width, ff),
        in_specs=[SMEM, VMEM] + [ANY] * (len(operands) - 2),
        out_specs=[ANY] * 5,
        out_shape=[jax.ShapeDtypeStruct(shape, F32) for shape in shapes],
        scratch_shapes=[pltpu.VMEM(values.shape, F32), pltpu.SemaphoreType.DMA((most,))],
        input_output_aliases={} if prior is None else {2 + i: i for i in range(5)},
        compiler_params=limit(16),
        cost_estimate=cost(0, values.size * 6),
        name="assemble",
    )(*operands)


def exchange(values, devices):
    shape = values.shape
    parts = values.reshape(devices, shape[0] // devices, *shape[1:])
    return lax.all_to_all(parts, "blk", split_axis=0, concat_axis=0, tiled=True).reshape(shape)


def per_device(
    x_a, x_b, sel_a, sel_b, gain_one, w_qkv, w_out, w_sort, gain_two, w_up, w_down, cot_a, cot_b
):
    devices = lax.axis_size("blk")
    me = lax.axis_index("blk")
    seqs_a, rows_a, width = x_a.shape
    seqs_b, rows_b, _ = x_b.shape
    npl = sel_a.shape[1]
    blocks = npl * devices
    len_a = rows_a // npl
    len_b = rows_b // npl
    total_a = seqs_a * rows_a
    total_b = seqs_b * rows_b
    rows = total_a + total_b
    units = rows // UNIT
    units_a = total_a // UNIT
    count_a = seqs_a * npl
    count_b = seqs_b * npl
    picks = count_a + count_b
    picks_up = -(-picks // 16) * 16
    groups = rows // GROUP
    per = TILE // GROUP
    capacity = 2 * max(1, (4 * units + 5 * devices - 1) // (5 * devices))
    send_rows = devices * capacity * UNIT
    ff = w_up.shape[1]
    gain1 = gain_one.astype(F32).reshape(1, width)
    gain2 = gain_two.astype(F32).reshape(1, width)

    first, early = capacity, groups
    if capacity > 8:
        full, left = divmod(units, capacity)
        sure = (full * 8 + min(left, 8)) // 2 // per * per
        if capacity == 14 and 0 < sure < groups:
            first, early = 8, sure

    sizes = [8, 7] if early < groups else [capacity]
    extra = 16
    sel = jnp.concatenate([sel_a.reshape(-1), sel_b.reshape(-1)])
    table, back_table, far_rows, ret_rows, perm, place, kinds = request(
        sel, npl, seqs_a, seqs_b, devices, capacity, first, early, sizes, extra, picks_up
    )

    average = np.zeros((picks, units), np.float32)
    for j in range(count_a):
        average[j, 2 * j : 2 * j + 2] = 1.0 / len_a
    for j in range(count_b):
        average[count_a + j, units_a + j] = 1.0 / len_b
    x, means, logits = digest(
        x_a.reshape(-1, width), x_b.reshape(-1, width), gain1, average, w_sort
    )
    spare = -(-picks // 8) * 8 + 8 - picks
    news = jnp.concatenate([logits, sel.astype(F32)[:, None]], axis=1)
    news = jnp.pad(news, ((0, spare), (0, 127 - blocks)))
    both = jnp.concatenate(
        [table.reshape(devices, capacity), back_table.reshape(devices, sum(sizes))], axis=1
    ).astype(F32)
    asked = jnp.pad(both[:, None], ((0, 0), (picks, spare - 1), (0, 128 - both.shape[1])))
    news = lax.all_to_all(news[None] + asked, "blk", split_axis=0, concat_axis=0, tiled=True)
    table = news[:, picks, :capacity].astype(jnp.int32).reshape(-1)
    back_table = news[:, picks, capacity : both.shape[1]].astype(jnp.int32).reshape(-1)
    news = news[:, :picks]
    parcels = pack(table, x, devices, capacity, first, picks_up)
    recv = [exchange(parcels[0], devices)]
    summary = means * gain1
    rs = inverse_norm(summary)
    unit_summary = (summary * rs).astype(BF16)
    all_summaries = jnp.broadcast_to(
        jnp.pad(unit_summary, ((0, picks_up - picks), (0, 0))), (devices, picks_up, width)
    )

    xp, cot = arrange(perm, x, cot_a.reshape(-1, width), cot_b.reshape(-1, width))
    proj = project(xp, gain1, w_qkv)

    def by_sequence(values):
        tail = values.shape[2:]
        one = values[:, :count_a].reshape((devices, seqs_a, npl) + tail)
        two = values[:, count_a:].reshape((devices, seqs_b, npl) + tail)
        both = jnp.concatenate([one, two], axis=1)
        return jnp.swapaxes(both, 0, 1).reshape((seqs_a + seqs_b, blocks) + tail)

    def own_rows(values):
        return lax.dynamic_slice_in_dim(values, me * npl, npl, 1).reshape((-1,) + values.shape[2:])

    def to_units(values):
        return jnp.concatenate(
            [jnp.repeat(values[:count_a], len_a // UNIT, axis=0), values[count_a:]], axis=0
        )

    news = by_sequence(news)
    logits = news[..., :blocks]
    picked = (news[..., blocks : blocks + 1] == jnp.arange(blocks, dtype=F32)).astype(F32)
    weights = jnp.take(to_units(own_rows(sinkhorn(logits, picked))), perm, axis=0)
    lane = jnp.arange(2 * GROUP) >= GROUP
    wrow = jnp.where(lane[None, :], jnp.repeat(weights, UNIT, axis=0), 1.0)
    if len(parcels) > 1:
        tall = (capacity - first) * UNIT
        parcel = lax.dynamic_update_slice(
            parcels[1].reshape(devices, -1, width), all_summaries, (0, tall, 0)
        )
        recv.append(exchange(tie(parcel.reshape(-1, width), wrow, proj), devices))
        units_all = recv[1].reshape(devices, -1, width)[:, tall:]
    else:
        units_all = exchange(all_summaries.reshape(-1, width), devices)
        units_all = units_all.reshape(devices, picks_up, width)
    units_all = by_sequence(units_all[:, :picks])
    block_of = np.arange(GROUP) // len_b
    cross = block_of[:, None] != block_of[None, :]
    mask = np.zeros((2, GROUP, 2 * GROUP), np.float32)
    mask[1] = np.where(np.concatenate([cross, cross], axis=1), -1e30, 0.0)

    core = bit_of("dp", 0).astype(jnp.int32).reshape(1)
    shared = (xp, cot, proj, wrow, mask, gain1, gain2, w_qkv, w_out, w_up, w_down)
    heights = [
        devices * (n * UNIT + (extra if i == len(sizes) - 1 else 0))
        for i, n in enumerate(sizes)
    ]

    def run_backward(streams, *rest):
        _, _, gatt, prob, farx, farkv = streams
        return backward(ret_rows, proj, farx, farkv, gatt, prob, wrow, w_qkv, *rest)

    fast = lax.axis_size("dp") == 4 and devices == 8 and early < groups
    part_x = ff // 2 + width // 2
    if early < groups:
        prior = forward(far_rows, kinds, core, recv[:1], *shared, 0, early, None, False, wrow)
        dproj, dfar, gw_one, gain, *ret = run_backward(
            prior[0], heights[:1], 0, early, None, prior[0][0]
        )
        back = [exchange(v, devices) for v in ret]
        streams, sums = forward(
            far_rows, kinds, core, recv, *shared, early, groups - early, prior, True, gain
        )
        keep, give, g_gain2 = sums
        out_a, out_b = restore(perm, streams[0], total_a)
        big_came = swap(give, "dp", 0)
        token = keep
        if fast:
            ranges_one = [(0, 0, part_x, 0, 0, 0), (0, part_x, keep.shape[0] - part_x, 1, 1, 0)]
            (bx, gx), (by, gy) = halve_step(
                ranges_one, [AXIS_X, AXIS_Y], [(keep, big_came)], out_a
            )
            bx_came, by_came = swap(gx, *AXIS_X), swap(gy, *AXIS_Y)
            token = bx
        dproj, dfar, gw_two, g_gain1_far, *ret = run_backward(
            streams, heights[1:], early, groups - early, (dproj, dfar, gain), token
        )
        gw = jnp.concatenate([gw_one, gw_two])
    else:
        streams, sums = forward(far_rows, kinds, core, recv, *shared, 0, groups, None, True, wrow)
        keep, give, g_gain2 = sums
        out_a, out_b = restore(perm, streams[0], total_a)
        big_came = swap(give, "dp", 0)
        back = []
        dproj, dfar, gw, g_gain1_far, *ret = run_backward(
            streams, heights, 0, groups, None, keep
        )
    _, gmid, _, _, farx, _ = streams

    gw = jnp.take(gw[:, :, 0].reshape(-1), place)
    gw = jnp.concatenate(
        [jnp.sum(gw[:units_a].reshape(-1, len_a // UNIT), axis=1), gw[units_a:]]
    )
    gw = jnp.pad(gw.astype(BF16)[None], ((0, extra - 1), (0, width - picks)))
    if fast:
        gw = tie(gw, bx_came, by_came, back[0])
    tall = sizes[len(back)] * UNIT
    parcel = lax.dynamic_update_slice(
        ret[0].reshape(devices, -1, width), jnp.broadcast_to(gw, (devices, extra, width)), (0, tall, 0)
    )
    arrived = exchange(parcel.reshape(-1, width), devices)
    back.append(arrived)
    gains = jnp.concatenate([g_gain1_far, g_gain2], axis=0)
    token = dproj
    gn, late_keep, late_give = qkv_grads(
        core, xp, farx, dproj, dfar, gain1, w_qkv, gains, EXTRA, token
    )
    late_came = swap(late_give, "dp", 0)
    part_late = 512
    gw = arrived.reshape(devices, -1, width)[:, tall:, :picks]
    if fast:
        late_rows = late_keep.shape[0]
        ranges_late = [(0, 0, part_late, 0, 0, 0), (0, part_late, late_rows - part_late, 1, 1, 0)]
        (lx, gx), (ly, gy) = halve_step(
            ranges_late, [AXIS_X, AXIS_Y], [(late_keep, late_came)], late_came
        )
        lx_came, ly_came = swap(gx, *AXIS_X), swap(gy, *AXIS_Y)
        nbx, nlx, nby, nly = (v.shape[0] for v in (bx, lx, by, ly))
        ranges_two = [
            (0, 0, nbx, 0, 0, 0),
            (1, 0, nlx, 0, 0, nbx // 2),
            (2, 0, nby, 1, 1, 0),
            (3, 0, nly, 1, 1, nby // 2),
        ]
        (vx, gx), (vy, gy) = halve_step(
            ranges_two,
            [AXIS_Y, AXIS_X],
            [(bx, bx_came), (lx, lx_came), (by, by_came), (ly, ly_came)],
            lx,
        )
        vx_came, vy_came = swap(gx, *AXIS_Y), swap(gy, *AXIS_X)
        cuts = [nbx // 2, nlx // 2, nby // 2, nly // 2]
        ranges_three = [
            (0, 0, cuts[0], 0, 0, 0),
            (0, cuts[0], cuts[1], 0, 0, cuts[0] // 2),
            (1, 0, cuts[2], 0, 0, (cuts[0] + cuts[1]) // 2),
            (1, cuts[2], cuts[3], 0, 0, (cuts[0] + cuts[1] + cuts[2]) // 2),
        ]
        ((total, gz),) = halve_step(
            ranges_three, [AXIS_Z0], [(vx, vx_came), (vy, vy_came)], arrived
        )
        gw = tie(gw, total)
        total = add(total, swap(gz, *AXIS_Z0))
    gw = by_sequence(gw[:, 0].astype(F32))
    g_logits = sinkhorn_back(logits, picked, jnp.broadcast_to(gw[..., None], logits.shape)) * (
        1.0 / SOFTMAX_HEAT
    )
    precise = lax.Precision.HIGHEST
    flat_logits = g_logits.reshape(-1, blocks)
    flat_units = units_all.reshape(-1, width).astype(F32)
    g_sort = lax.dot_general(
        flat_logits, flat_units, TN, precision=precise, preferred_element_type=F32
    )
    g_unit = lax.dot_general(
        flat_logits, w_sort.astype(F32), NT, precision=precise, preferred_element_type=F32
    )
    g_own = own_rows(g_unit.reshape(g_logits.shape[:2] + (width,)))
    g_summary = rs * (
        g_own - summary * rs * rs * jnp.mean(g_own * summary, axis=-1, keepdims=True)
    )
    both = g_unit * flat_units
    both = both - flat_units * flat_units * jnp.mean(both, axis=-1, keepdims=True)
    small = jnp.concatenate([g_sort, jnp.sum(both, axis=0, keepdims=True) / gain1], axis=0)
    spread = to_units(
        jnp.concatenate([g_summary[:count_a] / len_a, g_summary[count_a:] / len_b], axis=0)
    )
    base = base_rows(xp, gmid, gn, jnp.take(spread, perm, axis=0), gain1)

    gx_a, gx_b = last(back_table, place, back, sizes, extra, sum(sizes), x, base, gain1, total_a)
    if fast:
        for bit in (0, 1):
            small = small + swap(small, "dp", bit)
        total = add(total, tie(swap(total, *AXIS_Z1), gx_a, small))
        vx, vy = double_step(ranges_three, [AXIS_Z0], [(total, swap(total, *AXIS_Z0))])
        ranges_back = [
            (0, 0, nbx, 0, 0, 0),
            (0, nbx, nlx, 0, 0, cuts[0]),
            (1, 0, nby, 1, 1, 0),
            (1, nby, nly, 1, 1, cuts[2]),
        ]
        vx, vy = double_step(
            ranges_back,
            [AXIS_Y, AXIS_X],
            [(vx, swap(vx, *AXIS_Y)), (vy, swap(vy, *AXIS_X))],
        )
        big_rows = keep.shape[0]
        ranges_all = [
            (0, 0, part_x, 0, 0, 0),
            (0, big_rows, part_late, 0, 0, nbx),
            (0, part_x, big_rows - part_x, 1, 1, 0),
            (0, big_rows + part_late, late_rows - part_late, 1, 1, nby),
        ]
        (sums_own,) = double_step(
            ranges_all,
            [AXIS_X, AXIS_Y],
            [(vx, swap(vx, *AXIS_X)), (vy, swap(vy, *AXIS_Y))],
        )
    else:
        across = [("dp", bit) for bit in range(1, bits_of(lax.axis_size("dp")))]
        along = [("blk", bit) for bit in range(bits_of(devices))]
        sums_own = jnp.concatenate(
            [
                reduce_any(add(keep, big_came), across + along),
                reduce_any(add(late_keep, late_came), along + across),
            ],
            axis=0,
        )
    sums_came = swap(sums_own, "dp", 0)

    if not fast:
        small = lax.psum(small, "dp")
    written = assemble(core, 0, sums_own, width, ff, None)
    sum_up, sum_down, sum_out, sum_qkv, gains = assemble(core, 1, sums_came, width, ff, written)

    return (
        out_a.reshape(x_a.shape),
        out_b.reshape(x_b.shape),
        gx_a.reshape(x_a.shape),
        gx_b.reshape(x_b.shape),
        gains[0] + small[blocks],
        sum_qkv,
        sum_out,
        small[:blocks].T,
        gains[1],
        sum_up,
        sum_down,
    )


def solution(mesh):
    rows_spec = P("dp", "blk", None)
    in_specs = (
        (rows_spec, rows_spec, P("dp", "blk"), P("dp", "blk")) + (P(),) * 7 + (rows_spec, rows_spec)
    )
    out_specs = (rows_spec,) * 4 + (P(),) * 7
    return jax.shard_map(
        per_device, mesh=mesh, in_specs=in_specs, out_specs=out_specs, check_vma=False
    )
```

```python
import functools

import jax
import jax.numpy as jnp
import numpy as np
from jax import lax
from jax.experimental import pallas as pl
from jax.experimental.pallas import tpu as pltpu
from jax.sharding import PartitionSpec as P

HEADS = 8
SINK_ITERS = 8
EPSILON = 1e-05
SOFTMAX_HEAT = 0.75
UNIT = 32
EXTRA = 256
GROUP = 64
TILE = 256
HALF = 256
PER_HALF = 4
VMEM_LIMIT = 58 * 1024 * 1024

F32 = jnp.float32
BF16 = jnp.bfloat16

NN = (((1,), (0,)), ((), ()))
NT = (((1,), (1,)), ((), ()))
TN = (((0,), (0,)), ((), ()))


def dot(a, b, dims=NN):
    return lax.dot_general(a, b, dims, preferred_element_type=F32)


def inverse_norm(values):
    return lax.rsqrt(jnp.mean(values * values, axis=-1, keepdims=True) + EPSILON)


def whole(shape):
    zeros = (0,) * len(shape)
    return pl.BlockSpec(shape, lambda *_: zeros, pipeline_mode=pl.Buffered(1))


def rows_of(tile, width):
    return pl.BlockSpec((tile, width), lambda i: (i, 0))


SMEM = pl.BlockSpec(memory_space=pltpu.SMEM)


def params():
    return pltpu.CompilerParams(
        dimension_semantics=("arbitrary",), vmem_limit_bytes=VMEM_LIMIT
    )


def cost(flops, nbytes):
    return pl.CostEstimate(flops=int(flops * 1e-3), bytes_accessed=int(nbytes * 1e-3), transcendentals=0)


ANY = pl.BlockSpec(memory_space=pl.ANY)
VMEM = pl.BlockSpec(memory_space=pltpu.VMEM)
HBM = pl.BlockSpec(memory_space=pltpu.HBM)


def limit(mib):
    return pltpu.CompilerParams(vmem_limit_bytes=mib * 1024 * 1024)


def request_kernel(
    npl, seqs_a, seqs_b, devices, capacity, first, early, sizes, extra, spare_rows,
    sela_ref, selb_ref, table_ref, back_ref, far_ref, ret_ref, perm_ref, place_ref, kinds_ref, fill, begin, used,
):
    count_a = seqs_a * npl
    count_b = seqs_b * npl
    units_a = 2 * count_a
    width = sum(sizes)
    shift = npl.bit_length() - 1 if npl & (npl - 1) == 0 else -1

    def choice(j):
        ref, at = (sela_ref, j) if j < count_a else (selb_ref, j - count_a)
        return ref[at // npl, at % npl]

    def split(chosen):
        if shift >= 0:
            return lax.shift_right_logical(chosen, shift), lax.bitwise_and(chosen, npl - 1)
        return lax.div(chosen, npl), lax.rem(chosen, npl)

    def clear(ref):
        def body(i, carry):
            ref[i] = -1
            return carry

        return body

    lax.fori_loop(0, devices * capacity, clear(table_ref), 0)
    lax.fori_loop(0, devices * width, clear(back_ref), 0)
    for s in range(devices):
        fill[s] = 0
        used[s] = 0
        used[devices + s] = 0
    one = lambda flag: jnp.where(flag, 1, 0)
    ready_a, ready_b, must_a, must_b = (jnp.int32(0) for _ in range(4))
    for j in range(count_a + count_b):
        source, inner = split(choice(j))
        slot = fill[source]
        begin[j] = slot
        size = 2 if j < count_a else 1
        fill[source] = slot + size
        if j < count_a:
            unit = inner * 2 + (j // npl) * npl * 2
            ready_a = ready_a + one(slot + 2 <= first)
            table_ref[source * capacity + slot + 1] = unit + 1
        else:
            unit = inner + (units_a + (j - count_a) // npl * npl)
            ready_b = ready_b + one(slot + 1 <= first)
        table_ref[source * capacity + slot] = unit

    two = early < count_a + count_b // 2

    def must(j):
        source, _ = split(choice(j))
        if not two:
            return begin[j] < 0
        return begin[j] < fill[source] - 6

    for j in range(count_a):
        must_a = must_a + one(must(j))
    for j in range(count_b):
        must_b = must_b + one(must(count_a + j))
    even = jnp.logical_or(lax.bitwise_and(must_b, 1) == 0, ready_b > must_b)
    pairs = lax.shift_right_logical(must_b + one(even), 1)
    take_a = jnp.minimum(ready_a, early - pairs)
    if not two:
        take_a = jnp.int32(count_a)
    take_b = 2 * (early - take_a)
    late_b = 2 * (early + count_a - take_a)
    kinds_ref[0] = take_a
    kinds_ref[1] = early + count_a - take_a
    second = devices * first * UNIT

    def ret_row(phase, source, slot):
        chunks = list(enumerate(sizes))
        if two:
            chunks = chunks[:1] if phase == 0 else chunks[1:]
        row = jnp.int32(0)
        begin_slot, begin_row = 0, 0
        for index, size in chunks:
            height = size * UNIT + (extra if index == len(sizes) - 1 else 0)
            here = begin_row + source * height + (slot - begin_slot) * UNIT
            row = jnp.where(slot >= begin_slot, here, row)
            begin_slot += size
            begin_row += devices * height
        return row

    def put(pos, unit, inner, source, slot, late):
        near = (source * first + slot) * UNIT
        rest = second + source * ((capacity - first) * UNIT + spare_rows) + (slot - first) * UNIT
        far_ref[pos] = jnp.where(slot < first, near, rest)
        at = late * devices + source
        back = used[at]
        used[at] = back + 1
        if two:
            ret_ref[pos] = jnp.where(late == 0, ret_row(0, source, back), ret_row(1, source, back))
            back_ref[source * width + back + late * sizes[0]] = inner
        else:
            ret_ref[pos] = ret_row(0, source, back)
            back_ref[source * width + back] = inner
        perm_ref[pos] = unit
        place_ref[unit] = pos

    spare = take_a - must_a
    taken, other, free = (jnp.int32(0) for _ in range(3))
    for j in range(count_a):
        source, inner = split(choice(j))
        slot = begin[j]
        need = must(j)
        pick = jnp.logical_and(jnp.logical_not(need), jnp.logical_and(slot + 2 <= first, free < spare))
        use = jnp.logical_or(need, pick)
        free = free + one(pick)
        pos = 2 * jnp.where(use, taken, early + other)
        inner = inner * 2 + (j // npl) * npl * 2
        put(pos, 2 * j, inner, source, slot, one(jnp.logical_not(use)))
        put(pos + 1, 2 * j + 1, inner + 1, source, slot + 1, one(jnp.logical_not(use)))
        taken = taken + one(use)
        other = other + one(jnp.logical_not(use))
    spare = take_b - must_b
    drop = one(spare < 0)
    taken, other, free = (jnp.int32(0) for _ in range(3))
    for j in range(count_b):
        source, inner = split(choice(count_a + j))
        slot = begin[count_a + j]
        need = must(count_a + j)
        skip = jnp.logical_and(need, drop > 0)
        drop = drop - one(skip)
        pick = jnp.logical_and(jnp.logical_not(need), jnp.logical_and(slot + 1 <= first, free < spare))
        use = jnp.logical_or(jnp.logical_and(need, jnp.logical_not(skip)), pick)
        free = free + one(pick)
        pos = jnp.where(use, 2 * take_a + taken, late_b + other)
        inner = inner + (units_a + (j // npl) * npl)
        put(pos, units_a + j, inner, source, slot, one(jnp.logical_not(use)))
        taken = taken + one(use)
        other = other + one(jnp.logical_not(use))


def digest_kernel(
    tiles_a, settings, sela_ref, selb_ref, xa_ref, xb_ref, gain_ref, avg_ref, wsort_ref,
    x_ref, means_ref, news_ref, far_ref, ret_ref, perm_ref, place_ref, kinds_ref,
    sums, table_ref, back_ref, fill, begin, used,
):
    step = pl.program_id(0)

    @pl.when(step == 0)
    def _():
        request_kernel(
            *settings, sela_ref, selb_ref, table_ref, back_ref, far_ref, ret_ref, perm_ref, place_ref,
            kinds_ref, fill, begin, used,
        )

    def take(src):
        x = src[...]
        x_ref[...] = x
        x = x.astype(F32)
        scaled = x * inverse_norm(x)
        units = x.shape[0] // UNIT
        at = pl.ds(pl.multiple_of(step * units, units), units)
        sums[at, :] = jnp.sum(scaled.reshape(units, UNIT, x.shape[1]), axis=1)

    pl.when(step < tiles_a)(lambda: take(xa_ref))
    pl.when(step >= tiles_a)(lambda: take(xb_ref))

    @pl.when(step == pl.num_programs(0) - 1)
    def _():
        means = lax.dot_general(
            avg_ref[...], sums[...], NN, precision=lax.Precision.HIGHEST, preferred_element_type=F32
        )
        means_ref[...] = means
        summary = means * gain_ref[...]
        unit = (summary * inverse_norm(summary)).astype(BF16)
        logits = dot(unit, wsort_ref[...], NT) * (1.0 / SOFTMAX_HEAT)
        picks, blocks = logits.shape
        devices, height, lanes = news_ref.shape
        line = lax.broadcasted_iota(jnp.int32, (picks, lanes - blocks), 0)
        lane = lax.broadcasted_iota(jnp.int32, (picks, lanes - blocks), 1)
        chosen = jnp.zeros((picks, lanes - blocks), jnp.int32)
        count_a = sela_ref.shape[0] * sela_ref.shape[1]
        for j in range(picks):
            ref, at = (sela_ref, j) if j < count_a else (selb_ref, j - count_a)
            npl = ref.shape[1]
            chosen = jnp.where(line == j, ref[at // npl, at % npl], chosen)
        chosen = jnp.where(lane == 0, chosen, 0).astype(F32)
        message = jnp.concatenate([logits, chosen], axis=1)
        lane = lax.broadcasted_iota(jnp.int32, (1, lanes), 1)
        wanted = table_ref.shape[0] // devices
        order = back_ref.shape[0] // devices
        rest = lax.broadcasted_iota(jnp.int32, (height - picks, lanes), 0)
        for d in range(devices):
            row = jnp.zeros((1, lanes), jnp.int32)
            for k in range(wanted):
                row = jnp.where(lane == k, table_ref[d * wanted + k], row)
            for k in range(order):
                row = jnp.where(lane == wanted + k, back_ref[d * order + k], row)
            news_ref[d, :picks, :] = message
            news_ref[d, picks:, :] = jnp.where(rest == 0, row.astype(F32), 0.0)


def digest(x_a, x_b, sel_a, sel_b, gain_row, average, w_sort_t, settings):
    npl, seqs_a, seqs_b, devices, capacity, _, _, sizes, _, _ = settings
    width = x_a.shape[1]
    tiles_a = x_a.shape[0] // TILE
    tiles_b = x_b.shape[0] // TILE
    rows = x_a.shape[0] + x_b.shape[0]
    picks = average.shape[0]
    height = -(-picks // 8) * 8 + 8
    units = rows // UNIT
    ints = lambda n: jax.ShapeDtypeStruct((n,), jnp.int32)
    return pl.pallas_call(
        functools.partial(digest_kernel, tiles_a, settings),
        grid=(tiles_a + tiles_b,),
        in_specs=[
            SMEM,
            SMEM,
            pl.BlockSpec((TILE, width), lambda i: (jnp.minimum(i, tiles_a - 1), 0)),
            pl.BlockSpec((TILE, width), lambda i: (jnp.maximum(i - tiles_a, 0), 0)),
            whole((1, width)),
            whole(average.shape),
            whole(w_sort_t.shape),
        ],
        out_specs=[rows_of(TILE, width), whole((picks, width)), whole((devices, height, 128))]
        + [SMEM] * 5,
        out_shape=[
            jax.ShapeDtypeStruct((rows, width), BF16),
            jax.ShapeDtypeStruct((picks, width), F32),
            jax.ShapeDtypeStruct((devices, height, 128), F32),
        ]
        + [ints(n) for n in (units, units, units, units, 2)],
        scratch_shapes=[
            pltpu.VMEM((units, width), F32),
            pltpu.SMEM((devices * capacity,), jnp.int32),
            pltpu.SMEM((devices * sum(sizes),), jnp.int32),
            pltpu.SMEM((devices,), jnp.int32),
            pltpu.SMEM((picks,), jnp.int32),
            pltpu.SMEM((2 * devices,), jnp.int32),
        ],
        compiler_params=params(),
        cost_estimate=cost(rows * width * 10, rows * width * 4),
        name="digest",
    )(sel_a, sel_b, x_a, x_b, gain_row, average, w_sort_t)


def pack_kernel(devices, capacity, first, spare, table_ref, x_ref, *rest):
    outs = rest[: 1 if first == capacity else 2]
    held, sems = rest[len(outs) :]
    sizes = [first, capacity - first]
    copies = []
    for part, out_ref in enumerate(outs):
        size = sizes[part]
        base = part * devices * first
        for r in range(devices):
            for slot in range(size):
                unit = jnp.maximum(table_ref[r * capacity + part * first + slot], 0)
                src = pl.ds(pl.multiple_of(unit * UNIT, UNIT), UNIT)
                at = (base + r * size + slot) * UNIT
                held[at : at + UNIT, :] = x_ref[src, :]
            at = (base + r * size) * UNIT
            copy = pltpu.make_async_copy(
                held.at[pl.ds(at, size * UNIT)],
                out_ref.at[pl.ds(r * (size * UNIT + part * spare), size * UNIT)],
                sems.at[part * devices + r],
            )
            copy.start()
            copies.append(copy)
    for copy in copies:
        copy.wait()


def pack(table, x, devices, capacity, first, spare):
    width = x.shape[1]
    sizes = [first] if first == capacity else [first, capacity - first]
    return pl.pallas_call(
        functools.partial(pack_kernel, devices, capacity, first, spare),
        in_specs=[SMEM, VMEM],
        out_specs=[HBM] * len(sizes),
        out_shape=[
            jax.ShapeDtypeStruct((devices * (n * UNIT + i * spare), width), BF16)
            for i, n in enumerate(sizes)
        ],
        scratch_shapes=[
            pltpu.VMEM((devices * capacity * UNIT, width), BF16),
            pltpu.SemaphoreType.DMA((len(sizes) * devices,)),
        ],
        compiler_params=limit(12),
        cost_estimate=cost(0, x.size * 6),
        name="pack",
    )(table, x)


def arrange_kernel(units_a, perm_ref, x_ref, cota_ref, cotb_ref, xp_ref, cotp_ref):
    def body(pos, carry):
        unit = perm_ref[pos]
        at = pl.ds(pl.multiple_of(pos * UNIT, UNIT), UNIT)
        xp_ref[at, :] = x_ref[pl.ds(pl.multiple_of(unit * UNIT, UNIT), UNIT), :]

        @pl.when(unit < units_a)
        def _():
            cotp_ref[at, :] = cota_ref[pl.ds(pl.multiple_of(unit * UNIT, UNIT), UNIT), :]

        @pl.when(unit >= units_a)
        def _():
            src = pl.ds(pl.multiple_of((unit - units_a) * UNIT, UNIT), UNIT)
            cotp_ref[at, :] = cotb_ref[src, :]

        return carry

    lax.fori_loop(0, x_ref.shape[0] // UNIT, body, 0)


def arrange(perm, x, cot_a, cot_b):
    like = jax.ShapeDtypeStruct(x.shape, BF16)
    return pl.pallas_call(
        functools.partial(arrange_kernel, cot_a.shape[0] // UNIT),
        in_specs=[SMEM, VMEM, VMEM, VMEM],
        out_specs=[VMEM, VMEM],
        out_shape=[like, like],
        compiler_params=limit(16),
        cost_estimate=cost(0, x.size * 8),
        name="arrange",
    )(perm, x, cot_a, cot_b)


def restore_kernel(perm_ref, out_ref, outa_ref, outb_ref):
    units_a = outa_ref.shape[0] // UNIT

    def body(pos, carry):
        unit = perm_ref[pos]
        at = pl.ds(pl.multiple_of(pos * UNIT, UNIT), UNIT)

        @pl.when(unit < units_a)
        def _():
            outa_ref[pl.ds(pl.multiple_of(unit * UNIT, UNIT), UNIT), :] = out_ref[at, :]

        @pl.when(unit >= units_a)
        def _():
            dst = pl.ds(pl.multiple_of((unit - units_a) * UNIT, UNIT), UNIT)
            outb_ref[dst, :] = out_ref[at, :]

        return carry

    lax.fori_loop(0, out_ref.shape[0] // UNIT, body, 0)


def restore(perm, out, rows_a):
    rows, width = out.shape
    return pl.pallas_call(
        restore_kernel,
        in_specs=[SMEM, VMEM],
        out_specs=[VMEM, VMEM],
        out_shape=[
            jax.ShapeDtypeStruct((rows_a, width), BF16),
            jax.ShapeDtypeStruct((rows - rows_a, width), BF16),
        ],
        compiler_params=limit(16),
        cost_estimate=cost(0, out.size * 4),
        name="restore",
    )(perm, out)


def project_kernel(x_ref, gain_ref, w_ref, proj_ref):
    x = x_ref[...].astype(F32)
    proj_ref[...] = dot((x * inverse_norm(x) * gain_ref[...]).astype(BF16), w_ref[...]).astype(BF16)


def project(x, gain_row, w_qkv):
    rows, width = x.shape
    wide = w_qkv.shape[1]
    return pl.pallas_call(
        project_kernel,
        grid=(rows // TILE,),
        in_specs=[rows_of(TILE, width), whole((1, width)), whole((width, wide))],
        out_specs=rows_of(TILE, wide),
        out_shape=jax.ShapeDtypeStruct((rows, wide), BF16),
        compiler_params=params(),
        cost_estimate=cost(2 * rows * width * wide, rows * (width + wide) * 2),
        name="project",
    )(x, gain_row, w_qkv)


def log_sum(values, axis):
    top = jnp.max(values, axis=axis, keepdims=True)
    return top + jnp.log(jnp.sum(jnp.exp(values - top), axis=axis, keepdims=True))


def sinkhorn_kernel(logits_ref, picked_ref, weight_ref):
    state = logits_ref[...]
    for _ in range(SINK_ITERS):
        state = state - log_sum(state, 2)
        state = state - log_sum(state, 1)
    count = state.shape[1]
    weight = count * jnp.sum(jnp.exp(state) * picked_ref[...], axis=2, keepdims=True)
    weight_ref[...] = jnp.broadcast_to(weight, weight_ref.shape)


def sinkhorn(logits, picked):
    seqs, count, _ = logits.shape
    return pl.pallas_call(
        sinkhorn_kernel,
        out_shape=jax.ShapeDtypeStruct((seqs, count, 128), F32),
        cost_estimate=cost(logits.size * 100, logits.size * 32),
        name="sinkhorn",
    )(logits, picked)


def sinkhorn_back_kernel(logits_ref, picked_ref, gw_ref, out_ref, kept):
    state = logits_ref[...]
    for step in range(SINK_ITERS):
        state = state - log_sum(state, 2)
        kept[2 * step] = jnp.exp(state)
        state = state - log_sum(state, 1)
        kept[2 * step + 1] = jnp.exp(state)
    count = state.shape[1]
    grad = count * picked_ref[...] * gw_ref[...] * jnp.exp(state)
    for step in reversed(range(SINK_ITERS)):
        grad = grad - kept[2 * step + 1] * jnp.sum(grad, axis=1, keepdims=True)
        grad = grad - kept[2 * step] * jnp.sum(grad, axis=2, keepdims=True)
    out_ref[...] = grad


def sinkhorn_back(logits, picked, gw):
    return pl.pallas_call(
        sinkhorn_back_kernel,
        out_shape=jax.ShapeDtypeStruct(logits.shape, F32),
        scratch_shapes=[pltpu.VMEM((2 * SINK_ITERS,) + logits.shape, F32)],
        compiler_params=pltpu.CompilerParams(vmem_limit_bytes=VMEM_LIMIT),
        cost_estimate=cost(logits.size * 200, logits.size * 32),
        name="sinkhorn_back",
    )(logits, picked, gw)


def head_masks(rows):
    lane = lax.broadcasted_iota(jnp.int32, (rows, HALF), 1) // (HALF // PER_HALF)
    return [lane == h for h in range(PER_HALF)]


def stack_heads(values, masks):
    zero = jnp.zeros_like(values)
    return jnp.concatenate([jnp.where(m, values, zero) for m in masks], axis=0)


def unstack_heads(values, masks):
    total = None
    for h, m in enumerate(masks):
        part = jnp.where(m, values[h * GROUP : (h + 1) * GROUP], 0.0)
        total = part if total is None else total + part
    return total


def repeat_heads(values):
    return jnp.concatenate([values] * PER_HALF, axis=0)


class Mover:
    def __init__(self, sems):
        self.sems, self.used, self.out = sems, 0, []

    def start(self, source, target):
        copy = pltpu.make_async_copy(source, target, self.sems.at[self.used])
        self.used += 1
        copy.start()
        return copy

    def store(self, source, target):
        self.out.append(self.start(source, target))

    def finish(self):
        for copy in self.out:
            copy.wait()


BATCH = 4


def forward_kernel(first_group, groups, recvs, prior, final, *refs):
    refs = list(refs)
    take = lambda n: [refs.pop(0) for _ in range(n)]
    far_ref, kinds_ref, core_ref = take(3)
    recv_hbm = take(recvs)
    x_hbm, cot_hbm, proj_hbm, wrow_hbm, mask_ref, gain1_ref, gain2_ref = take(7)
    wqkv_hbm, wout_hbm, wup_hbm, wdown_hbm, _ = take(5)
    prior_refs = take(3) if prior else []
    if prior:
        take(6)
    out_hbm, gmid_hbm, gatt_hbm, prob_hbm, farx_hbm, farkv_hbm = take(6)
    if final:
        keep_hbm, give_hbm, gain_ref = take(3)
    else:
        up_hbm, down_hbm, gain_ref = take(3)
    recv_refs = take(recvs)
    x_ref, cot_ref, proj_ref, wrow_ref, wqkv_ref, wout_ref, wup_ref, wdown_ref = take(8)
    out_ref, gmid_ref, gatt_ref, prob_ref, farx_ref, farkv_ref, attended = take(7)
    one_ref, two_ref = take(2)
    if prior:
        up_prior, down_prior = take(2)
    (sems,) = take(1)
    move = Mover(sems)
    rows = groups * GROUP
    width = x_ref.shape[1]
    ff = wup_ref.shape[1]
    base = first_group
    here = pl.ds(first_group * GROUP, rows)
    got_recv = [move.start(a, b) for a, b in zip(recv_hbm, recv_refs)]
    got_wqkv = move.start(wqkv_hbm, wqkv_ref)
    got_proj = move.start(proj_hbm.at[here], proj_ref)
    got_wrow = move.start(wrow_hbm.at[here], wrow_ref)
    got_x = move.start(x_hbm.at[here], x_ref)
    got_wout = move.start(wout_hbm, wout_ref)
    got_cot = move.start(cot_hbm.at[here], cot_ref)
    got_up = move.start(wup_hbm, wup_ref)
    got_down = move.start(wdown_hbm, wdown_ref)
    if prior:
        got_prior = [
            move.start(prior_refs[0], up_prior),
            move.start(prior_refs[1], down_prior),
        ]

    for copy in got_recv:
        copy.wait()
    rows_one = recv_refs[0].shape[0]
    for u in range(rows // UNIT):
        row = far_ref[2 * base + u]
        dst = slice(u * UNIT, (u + 1) * UNIT)
        if recvs == 1:
            farx_ref[dst, :] = recv_refs[0][pl.ds(pl.multiple_of(row, UNIT), UNIT), :]
        else:

            @pl.when(row < rows_one)
            def _():
                farx_ref[dst, :] = recv_refs[0][pl.ds(pl.multiple_of(row, 16), UNIT), :]

            @pl.when(row >= rows_one)
            def _():
                src = pl.ds(pl.multiple_of(row - rows_one, 16), UNIT)
                farx_ref[dst, :] = recv_refs[1][src, :]

    move.store(farx_ref, farx_hbm.at[here])
    far = farx_ref[...].astype(F32)
    far = (far * inverse_norm(far) * gain1_ref[...]).astype(BF16)
    got_wqkv.wait()
    farkv_ref[...] = dot(far, wqkv_ref[:, width:]).astype(BF16)
    move.store(farkv_ref, farkv_hbm.at[here])
    masks16 = head_masks(GROUP)
    head_scale = (width // HEADS) ** -0.5
    boundary = kinds_ref[1 if prior else 0]
    got_proj.wait()
    got_wrow.wait()
    for first in range(0, groups, BATCH):
        work = [
            (i, half) for i in range(first, min(first + BATCH, groups)) for half in range(width // HALF)
        ]
        scores, vals = [], []
        for i, half in work:
            at = slice(i * GROUP, (i + 1) * GROUP)
            lo = half * HALF
            q = proj_ref[at, lo : lo + HALF] * jnp.asarray(head_scale, BF16)
            keys = jnp.concatenate(
                [proj_ref[at, width + lo : width + lo + HALF], farkv_ref[at, lo : lo + HALF]], axis=0
            )
            vals.append(
                jnp.concatenate(
                    [
                        proj_ref[at, 2 * width + lo : 2 * width + lo + HALF],
                        farkv_ref[at, width + lo : width + lo + HALF],
                    ],
                    axis=0,
                )
            )
            which = jnp.where(base + i < boundary, 0, 1)
            scores.append(dot(stack_heads(q, masks16), keys, NT) + repeat_heads(mask_ref[which]))
        tops = [jnp.max(v, axis=1, keepdims=True) for v in scores]
        weights = [jnp.exp(v - t) for v, t in zip(scores, tops)]
        sums = [jnp.sum(v, axis=1, keepdims=True) for v in weights]
        probs = [v * (1.0 / t) for v, t in zip(weights, sums)]
        mixed = []
        for (i, half), prob, value in zip(work, probs, vals):
            at = slice(i * GROUP, (i + 1) * GROUP)
            prob_ref[i, half] = prob.astype(BF16)
            mixed.append(dot((prob * repeat_heads(wrow_ref[at, :])).astype(BF16), value))
        for (i, half), value in zip(work, mixed):
            at = slice(i * GROUP, (i + 1) * GROUP)
            lo = half * HALF
            attended[at, lo : lo + HALF] = unstack_heads(value, masks16).astype(BF16)
    move.store(prob_ref, prob_hbm.at[pl.ds(first_group, groups)])

    got_x.wait()
    got_wout.wait()
    att = attended[...]
    middle = x_ref[...].astype(F32) + dot(att, wout_ref[...])
    r2 = inverse_norm(middle)
    scaled = middle * r2
    second = (scaled * gain2_ref[...]).astype(BF16)
    got_cot.wait()
    cot = cot_ref[...]
    cot_t = cot.T
    second_t = second.T
    got_up.wait()
    got_down.wait()
    if prior:
        for copy in got_prior:
            copy.wait()

    def total(value, old, lanes):
        return value + old[:, lanes].astype(F32) if prior else value

    edge = ff // 2

    def put_up(c, value):
        lanes = slice(c, c + width)
        if not final:
            one_ref[:, lanes] = value.astype(BF16)
            return
        ref, at = (one_ref, c) if c < edge else (two_ref, c - edge)
        ref[at : at + width, :] = total(value, up_prior if prior else None, lanes).astype(BF16)

    def put_down(c, value):
        lanes = slice(c, c + width)
        if not final:
            two_ref[:, lanes] = value.astype(BF16)
            return
        ref, at = (one_ref, c) if c < edge else (two_ref, c - edge)
        at += edge + width // 2
        ref[at : at + width, :] = total(value, down_prior if prior else None, lanes).T.astype(BF16)

    def put_out(value):
        if not final:
            one_ref[:, ff:] = value.astype(BF16)
            return
        value = total(value, up_prior if prior else None, slice(ff, ff + width)).astype(BF16)
        one_ref[edge : edge + width // 2, :] = value[: width // 2]
        two_ref[edge : edge + width // 2, :] = value[width // 2 :]

    result = middle
    back = jnp.zeros((rows, width), F32)
    c0 = 0.7978845608028654
    c1 = 0.044715
    for c in range(0, ff, width):
        hidden = dot(second, wup_ref[:, c : c + width])
        grad = dot(cot, wdown_ref[c : c + width, :], NT)
        square = hidden * hidden
        t = jnp.tanh(hidden * (c0 + (c0 * c1) * square))
        left = 0.5 + 0.5 * t
        active = (hidden * left).astype(BF16)
        slope = left + (0.5 * hidden) * (1.0 - t * t) * (c0 + (3.0 * c0 * c1) * square)
        grad = (grad * slope).astype(BF16)
        result = result + dot(active, wdown_ref[c : c + width, :])
        back = back + dot(grad, wup_ref[:, c : c + width], NT)
        put_down(c, dot(cot_t, active))
        put_up(c, dot(second_t, grad))
    out_ref[...] = result.astype(BF16)
    move.store(out_ref, out_hbm.at[here])
    gain = jnp.sum(back * scaled, axis=0, keepdims=True)
    gain_ref[...] = gain + prior_refs[2][...] if prior else gain
    e = back * gain2_ref[...]
    inner = jnp.mean(e * scaled, axis=-1, keepdims=True)
    grad_middle = cot.astype(F32) + r2 * (e - scaled * inner)
    branch = grad_middle.astype(BF16)
    gmid_ref[...] = branch
    move.store(gmid_ref, gmid_hbm.at[here])
    put_out(dot(att.T, branch))
    if not final:
        move.store(one_ref, up_hbm)
        move.store(two_ref, down_hbm)
    gatt_ref[...] = dot(branch, wout_ref[...], NT).astype(BF16)
    move.store(gatt_ref, gatt_hbm.at[here])
    if final:
        first, second_copy = move.used, move.used + 1
        for which, (mine, other) in enumerate(((one_ref, two_ref), (two_ref, one_ref))):

            @pl.when(core_ref[0] == which)
            def _():
                copies = [
                    pltpu.make_async_copy(mine, keep_hbm, sems.at[first]),
                    pltpu.make_async_copy(other, give_hbm, sems.at[second_copy]),
                ]
                for copy in copies:
                    copy.start()
                for copy in copies:
                    copy.wait()

    move.finish()


def forward(
    far_rows, kinds, core, recv, x, cot, proj, wrow, mask, gain1, gain2, w_qkv, w_out, w_up, w_down,
    first_group, groups, prior, final, token,
):
    rows, width = x.shape
    ff = w_up.shape[1]
    halves = width // HALF
    count = groups * GROUP
    like = lambda wide, kind=BF16: jax.ShapeDtypeStruct((rows, wide), kind)
    probs = jax.ShapeDtypeStruct((rows // GROUP, halves, PER_HALF * GROUP, 2 * GROUP), BF16)
    part = ff + width // 2
    if final:
        tails = [(part, width), (part, width)]
    else:
        tails = [(width, ff + width), (width, ff)]
    in_specs = [SMEM] * 3 + [ANY] * (len(recv) + 4) + [VMEM] * 3 + [ANY] * 5
    operands = [far_rows, kinds, core, *recv, x, cot, proj, wrow, mask, gain1, gain2]
    operands += [w_qkv, w_out, w_up, w_down, token]
    scratch = [pltpu.VMEM(r.shape, BF16) for r in recv]
    scratch += [
        pltpu.VMEM((count, width), BF16),
        pltpu.VMEM((count, width), BF16),
        pltpu.VMEM((count, 3 * width), BF16),
        pltpu.VMEM((count, 2 * GROUP), F32),
    ]
    scratch += [pltpu.VMEM(w.shape, BF16) for w in (w_qkv, w_out, w_up, w_down)]
    scratch += [pltpu.VMEM((count, width), BF16)] * 3
    scratch += [pltpu.VMEM((groups,) + probs.shape[1:], BF16)]
    scratch += [pltpu.VMEM((count, n * width), BF16) for n in (1, 2, 1)]
    scratch += [pltpu.VMEM(shape, BF16) for shape in tails]
    aliases = {}
    if prior is not None:
        streams, sums = prior
        in_specs += [ANY, ANY, VMEM] + [ANY] * 6
        operands += list(sums)
        aliases = {len(operands) + i: i for i in range(6)}
        operands += list(streams)
        scratch += [pltpu.VMEM((width, ff + width), BF16), pltpu.VMEM((width, ff), BF16)]
    scratch += [pltpu.SemaphoreType.DMA((24,))]
    out = pl.pallas_call(
        functools.partial(
            forward_kernel, first_group, groups, len(recv), prior is not None, final
        ),
        in_specs=in_specs,
        out_specs=[ANY] * 8 + [VMEM],
        out_shape=[like(width), like(width), like(width), probs, like(width), like(2 * width)]
        + [jax.ShapeDtypeStruct(shape, BF16) for shape in tails]
        + [jax.ShapeDtypeStruct((1, width), F32)],
        scratch_shapes=scratch,
        input_output_aliases=aliases,
        compiler_params=pltpu.CompilerParams(vmem_limit_bytes=VMEM_LIMIT),
        cost_estimate=cost(1.0e9 * groups, 1e6 * groups),
        name="forward",
    )(*operands)
    return out[:6], out[6:]


def backward_kernel(first_group, groups, prior, chunks, letter, *refs):
    refs = list(refs)
    take = lambda n: [refs.pop(0) for _ in range(n)]
    ret_rows, place_ref = take(2)
    proj_hbm, farx_hbm, farkv_hbm, gatt_hbm, prob_hbm, wrow_hbm, wqkv_hbm = take(7)
    if prior:
        prior_gain, prior_gw = take(2)
        take(2)
    take(1)
    dproj_hbm, dfar_hbm, gw_ref, gain_ref = take(4)
    ret_hbm = take(chunks)
    proj_ref, farx_ref, farkv_ref, gatt_ref, prob_ref, wrow_ref, wqkv_ref = take(7)
    dproj_ref, dfar_ref = take(2)
    ret_refs = take(chunks)
    (sems,) = take(1)
    move = Mover(sems)
    rows = groups * GROUP
    width = gatt_ref.shape[1]
    start = first_group * GROUP
    batches = [(first, min(first + BATCH, groups)) for first in range(0, groups, BATCH)]
    loads = []
    for low, high in batches:
        at = pl.ds(low * GROUP, (high - low) * GROUP)
        there = pl.ds(start + low * GROUP, (high - low) * GROUP)
        loads.append(
            [
                move.start(hbm.at[there], ref.at[at])
                for hbm, ref in (
                    (proj_hbm, proj_ref),
                    (farkv_hbm, farkv_ref),
                    (gatt_hbm, gatt_ref),
                    (wrow_hbm, wrow_ref),
                )
            ]
            + [
                move.start(
                    prob_hbm.at[pl.ds(first_group + low, high - low)],
                    prob_ref.at[pl.ds(low, high - low)],
                )
            ]
        )
    got_wqkv = move.start(wqkv_hbm, wqkv_ref)
    got_farx = move.start(farx_hbm.at[pl.ds(start, rows)], farx_ref)
    masks16 = head_masks(GROUP)
    head_scale = (width // HEADS) ** -0.5
    far_lane = lax.broadcasted_iota(jnp.int32, (GROUP // UNIT, 2 * GROUP), 1) >= GROUP
    for (low, high), copies in zip(batches, loads):
        for copy in copies:
            copy.wait()
        work = [(i, half) for i in range(low, high) for half in range(width // HALF)]
        stacks, products = [], []
        for i, half in work:
            at = slice(i * GROUP, (i + 1) * GROUP)
            lo = half * HALF
            vals = jnp.concatenate(
                [
                    proj_ref[at, 2 * width + lo : 2 * width + lo + HALF],
                    farkv_ref[at, width + lo : width + lo + HALF],
                ],
                axis=0,
            )
            up = stack_heads(gatt_ref[at, lo : lo + HALF], masks16)
            stacks.append(up)
            products.append(prob_ref[i, half].astype(F32) * dot(up, vals, NT))
        for i in range(low, high):
            summed = jnp.zeros((GROUP, 2 * GROUP), F32)
            for (j, _), prod in zip(work, products):
                if j == i:
                    for h in range(PER_HALF):
                        summed = summed + prod[h * GROUP : (h + 1) * GROUP]
            pair = jnp.sum(summed.reshape(GROUP // UNIT, UNIT, 2 * GROUP), axis=1)
            pair = jnp.sum(jnp.where(far_lane, pair, 0.0), axis=1, keepdims=True)
            gw_ref[i] = jnp.broadcast_to(pair, (GROUP // UNIT, 128))
        scales = [repeat_heads(wrow_ref[i * GROUP : (i + 1) * GROUP, :]) for i, _ in work]
        products = [v * s for v, s in zip(products, scales)]
        totals = [jnp.sum(v, axis=1, keepdims=True) for v in products]
        for (i, half), up, prod, scale, total in zip(work, stacks, products, scales, totals):
            at = slice(i * GROUP, (i + 1) * GROUP)
            lo = half * HALF
            prob = prob_ref[i, half].astype(F32)
            ds = (prod - prob * total).astype(BF16)
            mixed = (prob * scale).astype(BF16)
            q = stack_heads(
                proj_ref[at, lo : lo + HALF] * jnp.asarray(head_scale, BF16), masks16
            )
            keys = jnp.concatenate(
                [proj_ref[at, width + lo : width + lo + HALF], farkv_ref[at, lo : lo + HALF]], axis=0
            )
            dq = unstack_heads(dot(ds, keys), masks16) * head_scale
            dk = dot(ds, q, TN).astype(BF16)
            dv = dot(mixed, up, TN).astype(BF16)
            dproj_ref[at, lo : lo + HALF] = dq.astype(BF16)
            dproj_ref[at, width + lo : width + lo + HALF] = dk[:GROUP]
            dproj_ref[at, 2 * width + lo : 2 * width + lo + HALF] = dv[:GROUP]
            dfar_ref[at, lo : lo + HALF] = dk[GROUP:]
            dfar_ref[at, width + lo : width + lo + HALF] = dv[GROUP:]
        at = pl.ds(low * GROUP, (high - low) * GROUP)
        there = pl.ds(start + low * GROUP, (high - low) * GROUP)
        move.store(dproj_ref.at[at], dproj_hbm.at[there])
        move.store(dfar_ref.at[at], dfar_hbm.at[there])

    got_wqkv.wait()
    got_farx.wait()
    grad = dot(dfar_ref[...], wqkv_ref[:, width:], NT)
    far = farx_ref[...].astype(F32)
    gain = jnp.sum(grad * (far * inverse_norm(far)), axis=0, keepdims=True)
    gain_ref[...] = gain + prior_gain[...] if prior else gain
    grad = grad.astype(BF16)
    for u in range(rows // UNIT):
        row = ret_rows[2 * first_group + u]
        edge = 0
        for ret_ref in ret_refs:
            value = grad[u * UNIT : (u + 1) * UNIT]

            def put(ret_ref=ret_ref, edge=edge, value=value):
                ret_ref[pl.ds(pl.multiple_of(row - edge, 16), UNIT), :] = value

            if chunks == 1:
                put()
            else:
                pl.when(jnp.logical_and(row >= edge, row < edge + ret_ref.shape[0]))(put)
            edge += ret_ref.shape[0]
    if letter:
        count_a, count_b, devices, extra = letter
        lane = lax.broadcasted_iota(jnp.int32, (1, 128), 1)
        row = jnp.zeros((1, 128), F32)

        def pair_at(at):
            if not prior:
                return gw_ref[at]
            early = prior_gw.shape[0]
            one = prior_gw[jnp.minimum(at, early - 1)]
            two = gw_ref[jnp.maximum(at - early, 0)]
            return jnp.where(at < early, one, two)

        for j in range(count_a + count_b):
            if j < count_a:
                both = pair_at(lax.shift_right_logical(place_ref[2 * j], 1))
                value = both[0:1] + both[1:2]
            else:
                pos = place_ref[count_a + j]
                both = pair_at(lax.shift_right_logical(pos, 1))
                value = jnp.where(lax.bitwise_and(pos, 1) == 0, both[0:1], both[1:2])
            row = jnp.where(lane == j, value, row)
        page = jnp.concatenate([row, jnp.zeros((1, width - 128), F32)], axis=1)
        line = lax.broadcasted_iota(jnp.int32, (extra, width), 0)
        page = jnp.where(line == 0, page, 0.0).astype(BF16)
        ret_ref = ret_refs[-1]
        height = ret_ref.shape[0] // devices
        for d in range(devices):
            ret_ref[(d + 1) * height - extra : (d + 1) * height, :] = page
    for ret_ref, hbm in zip(ret_refs, ret_hbm):
        move.store(ret_ref, hbm)
    move.finish()


def backward(
    ret_rows, place, proj, farx, farkv, gatt, prob, wrow, w_qkv, sizes, first_group, groups, prior, letter,
    token,
):
    rows, width = gatt.shape
    count = groups * GROUP
    in_specs = [SMEM, SMEM] + [ANY] * 7
    operands = [ret_rows, place, proj, farx, farkv, gatt, prob, wrow, w_qkv]
    aliases = {}
    if prior is not None:
        dproj, dfar, gw, gain = prior
        in_specs += [VMEM, VMEM, ANY, ANY]
        aliases = {len(operands) + 2: 0, len(operands) + 3: 1}
        operands += [gain, gw, dproj, dfar]
    in_specs += [ANY]
    operands += [token]
    batches = -(-groups // BATCH)
    return pl.pallas_call(
        functools.partial(
            backward_kernel, first_group, groups, prior is not None, len(sizes), letter
        ),
        in_specs=in_specs,
        out_specs=[ANY, ANY, VMEM, VMEM] + [ANY] * len(sizes),
        out_shape=[
            jax.ShapeDtypeStruct((rows, 3 * width), BF16),
            jax.ShapeDtypeStruct((rows, 2 * width), BF16),
            jax.ShapeDtypeStruct((groups, GROUP // UNIT, 128), F32),
            jax.ShapeDtypeStruct((1, width), F32),
        ]
        + [jax.ShapeDtypeStruct((n, width), BF16) for n in sizes],
        scratch_shapes=[
            pltpu.VMEM((count, 3 * width), BF16),
            pltpu.VMEM((count, width), BF16),
            pltpu.VMEM((count, 2 * width), BF16),
            pltpu.VMEM((count, width), BF16),
            pltpu.VMEM((groups,) + prob.shape[1:], BF16),
            pltpu.VMEM((count, 2 * GROUP), F32),
            pltpu.VMEM(w_qkv.shape, BF16),
            pltpu.VMEM((count, 3 * width), BF16),
            pltpu.VMEM((count, 2 * width), BF16),
        ]
        + [pltpu.VMEM((n, width), BF16) for n in sizes]
        + [pltpu.SemaphoreType.DMA((7 * batches + 2 + len(sizes),))],
        input_output_aliases=aliases,
        compiler_params=pltpu.CompilerParams(vmem_limit_bytes=VMEM_LIMIT),
        cost_estimate=cost(0.4e9 * groups, 1e6 * groups),
        name="backward",
    )(*operands)


def qkv_kernel(
    extra, core_ref, x_ref, farx_ref, dproj_ref, dfar_ref, gain1_ref, wqkv_ref, gains_ref, token_ref,
    gn_ref, keep_ref, give_ref, acc, gain_acc,
):
    step = pl.program_id(0)
    steps = pl.num_programs(0)
    width = x_ref.shape[1]

    @pl.when(step == 0)
    def _():
        acc[...] = jnp.zeros_like(acc)
        gain_acc[...] = jnp.zeros_like(gain_acc)

    x = x_ref[...].astype(F32)
    scaled = x * inverse_norm(x)
    far = farx_ref[...].astype(F32)
    far = (far * inverse_norm(far) * gain1_ref[...]).astype(BF16)
    near = (scaled * gain1_ref[...]).astype(BF16)
    acc[...] += dot(near.T, dproj_ref[...])
    acc[:, width:] += dot(far.T, dfar_ref[...])
    grad = dot(dproj_ref[...], wqkv_ref[...], NT)
    gn_ref[...] = grad.astype(BF16)
    gain_acc[...] += jnp.sum(grad * scaled, axis=0, keepdims=True)

    @pl.when(step == steps - 1)
    def _():
        line = lax.broadcasted_iota(jnp.int32, (extra, width), 0)
        small = jnp.where(line == 0, gain_acc[...] + gains_ref[0:1, :], 0.0)
        small = jnp.where(line == 1, gains_ref[1:2, :], small)
        total = acc.shape[1] + extra
        half = total // 2

        def write(ref, which):
            at = which * half
            while at < (which + 1) * half:
                block, line = divmod(at, width)
                if at >= acc.shape[1]:
                    count = extra
                    value = small
                else:
                    count = min(width - line, (which + 1) * half - at)
                    value = acc[line : line + count, block * width : (block + 1) * width]
                ref[at - which * half : at - which * half + count, :] = value.astype(BF16)
                at += count

        @pl.when(core_ref[0] == 0)
        def _():
            write(keep_ref, 0)
            write(give_ref, 1)

        @pl.when(core_ref[0] == 1)
        def _():
            write(keep_ref, 1)
            write(give_ref, 0)


def qkv_grads(core, x, farx, dproj, dfar, gain1, w_qkv, gains, extra, token):
    rows, width = x.shape
    wide = w_qkv.shape[1]
    half = (wide + extra) // 2
    return pl.pallas_call(
        functools.partial(qkv_kernel, extra),
        grid=(rows // TILE,),
        in_specs=[
            SMEM,
            rows_of(TILE, width),
            rows_of(TILE, width),
            rows_of(TILE, wide),
            rows_of(TILE, 2 * width),
            whole((1, width)),
            whole(w_qkv.shape),
            whole(gains.shape),
            ANY,
        ],
        out_specs=[rows_of(TILE, width), whole((half, width)), whole((half, width))],
        out_shape=[
            jax.ShapeDtypeStruct((rows, width), BF16),
            jax.ShapeDtypeStruct((half, width), BF16),
            jax.ShapeDtypeStruct((half, width), BF16),
        ],
        scratch_shapes=[pltpu.VMEM((width, wide), F32), pltpu.VMEM((1, width), F32)],
        compiler_params=params(),
        cost_estimate=cost(10e9, 25e6),
        name="qkv_grads",
    )(core, x, farx, dproj, dfar, gain1, w_qkv, gains, token)


def row_gradient(f, x):
    r1 = inverse_norm(x)
    scaled = x * r1
    return r1 * (f - scaled * jnp.mean(f * scaled, axis=-1, keepdims=True))


def base_kernel(x_ref, gmid_ref, gn_ref, gs_ref, gain1_ref, out_ref):
    rows, width = x_ref.shape
    spread = jnp.broadcast_to(gs_ref[...][:, None, :], (rows // UNIT, UNIT, width))
    f = (gn_ref[...].astype(F32) + spread.reshape(rows, width)) * gain1_ref[...]
    grad = gmid_ref[...].astype(F32) + row_gradient(f, x_ref[...].astype(F32))
    out_ref[...] = grad.astype(BF16)


def base_rows(x, gmid, gn, gs, gain1):
    rows, width = x.shape
    return pl.pallas_call(
        base_kernel,
        grid=(rows // TILE,),
        in_specs=[
            rows_of(TILE, width),
            rows_of(TILE, width),
            rows_of(TILE, width),
            rows_of(TILE // UNIT, width),
            whole((1, width)),
        ],
        out_specs=rows_of(TILE, width),
        out_shape=jax.ShapeDtypeStruct((rows, width), BF16),
        compiler_params=params(),
        cost_estimate=cost(rows * width * 20, rows * width * 8),
        name="base",
    )(x, gmid, gn, gs, gain1)


def last_kernel(sizes, extra, capacity, table_ref, place_ref, *refs):
    ret_refs = refs[: len(sizes)]
    x_ref, base_ref, gain1_ref, outa_ref, outb_ref, acc = refs[len(sizes) :]
    rows_a = outa_ref.shape[0]
    acc[...] = jnp.zeros_like(acc)

    begin = 0
    for index, (size, ret_ref) in enumerate(zip(sizes, ret_refs)):
        height = size * UNIT + (extra if index == len(sizes) - 1 else 0)

        def add(r, carry, size=size, ret_ref=ret_ref, begin=begin, height=height):
            for slot in range(size):
                unit = table_ref[r * capacity + begin + slot]

                @pl.when(unit >= 0)
                def _():
                    at = pl.ds(pl.multiple_of(unit * UNIT, UNIT), UNIT)
                    src = pl.ds(pl.multiple_of(r * height + slot * UNIT, 16), UNIT)
                    acc[at, :] += ret_ref[src, :].astype(F32)

            return carry

        lax.fori_loop(0, ret_ref.shape[0] // height, add, 0)
        begin += size

    def finish(out_ref, first):
        def body(u, carry):
            at = pl.ds(pl.multiple_of(place_ref[first + u] * UNIT, UNIT), UNIT)
            own = pl.ds(pl.multiple_of((first + u) * UNIT, UNIT), UNIT)
            f = acc[own, :] * gain1_ref[...]
            grad = base_ref[at, :].astype(F32) + row_gradient(f, x_ref[own, :].astype(F32))
            out_ref[pl.ds(pl.multiple_of(u * UNIT, UNIT), UNIT), :] = grad.astype(BF16)
            return carry

        lax.fori_loop(0, out_ref.shape[0] // UNIT, body, 0, unroll=2)

    finish(outa_ref, 0)
    finish(outb_ref, rows_a // UNIT)


def last(table, place, ret, sizes, extra, capacity, x, base, gain1, rows_a):
    rows, width = x.shape
    return pl.pallas_call(
        functools.partial(last_kernel, sizes, extra, capacity),
        in_specs=[SMEM, SMEM] + [VMEM] * (len(ret) + 3),
        out_specs=[VMEM, VMEM],
        out_shape=[
            jax.ShapeDtypeStruct((rows_a, width), BF16),
            jax.ShapeDtypeStruct((rows - rows_a, width), BF16),
        ],
        scratch_shapes=[pltpu.VMEM((rows, width), F32)],
        compiler_params=limit(24),
        cost_estimate=cost(rows * width * 20, rows * width * 12),
        name="last",
    )(table, place, *ret, x, base, gain1)


def bits_of(size):
    count = 0
    while (1 << count) < size:
        count += 1
    return count


def bit_of(axis, bit):
    return (lax.axis_index(axis) >> bit) & 1


def swap(values, axis, bit):
    size = lax.axis_size(axis)
    return lax.ppermute(values, axis, [(i, i ^ (1 << bit)) for i in range(size)])


def halve(values, axis, bit):
    half = values.shape[0] // 2
    mine = bit_of(axis, bit)
    keep = lax.dynamic_slice_in_dim(values, mine * half, half, 0)
    give = lax.dynamic_slice_in_dim(values, (1 - mine) * half, half, 0)
    return keep, give


def double(values, axis, bit):
    got = swap(values, axis, bit)
    return jnp.where(
        bit_of(axis, bit) == 0,
        jnp.concatenate([values, got], axis=0),
        jnp.concatenate([got, values], axis=0),
    )


def add(one, two):
    return (one.astype(F32) + two.astype(F32)).astype(BF16)


def reduce_any(values, order):
    for axis, bit in order:
        keep, give = halve(values, axis, bit)
        values = add(keep, swap(give, axis, bit))
    for axis, bit in reversed(order):
        values = double(values, axis, bit)
    return values


def tie(values, *tokens):
    return pl.pallas_call(
        lambda *refs: None,
        in_specs=[ANY] * (1 + len(tokens)),
        out_specs=ANY,
        out_shape=jax.ShapeDtypeStruct(values.shape, values.dtype),
        input_output_aliases={0: 0},
        name="tie",
    )(values, *tokens)


def fetch(sources, targets, sems):
    copies = [
        pltpu.make_async_copy(source, target, sems.at[i])
        for i, (source, target) in enumerate(zip(sources, targets))
    ]
    for copy in copies:
        copy.start()
    for copy in copies:
        copy.wait()


def halve_kernel(ranges, sources, bits_ref, *refs):
    count = 2 * (1 + max(r[4] for r in ranges))
    outs = refs[2 * sources + 1 : 2 * sources + 1 + count]
    held = refs[2 * sources + 1 + count : -1]
    fetch(refs[: 2 * sources], held, refs[-1])
    refs = held
    for source, first, count, bit, out, there in ranges:
        own, came = refs[2 * source], refs[2 * source + 1]
        half = count // 2
        keep = pl.multiple_of(first + bits_ref[bit] * half, 16)
        give = pl.multiple_of(first + (1 - bits_ref[bit]) * half, 16)
        for ref, line in ((outs[2 * out], keep), (outs[2 * out + 1], give)):
            rows = pl.ds(line, half)
            total = own[rows, :].astype(F32) + came[rows, :].astype(F32)
            ref[there : there + half, :] = total.astype(BF16)


def halve_step(ranges, bits, pairs, token):
    width = pairs[0][0].shape[1]
    count = 1 + max(r[4] for r in ranges)
    heights = [max(r[5] + r[2] // 2 for r in ranges if r[4] == out) for out in range(count)]
    shapes = [jax.ShapeDtypeStruct((n, width), BF16) for n in heights for _ in range(2)]
    flat = [v for pair in pairs for v in pair]
    out = pl.pallas_call(
        functools.partial(halve_kernel, ranges, len(pairs)),
        in_specs=[SMEM] + [ANY] * len(flat) + [ANY],
        out_specs=[VMEM] * len(shapes),
        out_shape=shapes,
        scratch_shapes=[pltpu.VMEM(v.shape, BF16) for v in flat]
        + [pltpu.SemaphoreType.DMA((len(flat),))],
        compiler_params=limit(24),
        cost_estimate=cost(0, 8 * sum(heights) * width),
        name="halve_step",
    )(jnp.stack([bit_of(*b) for b in bits]).astype(jnp.int32), *flat, token)
    return [(out[2 * i], out[2 * i + 1]) for i in range(count)]


def double_kernel(ranges, sources, tokens, bits_ref, *refs):
    count = 1 + max(r[0] for r in ranges)
    outs = refs[2 * sources + tokens : 2 * sources + tokens + count]
    held = refs[2 * sources + tokens + count : -1]
    fetch(refs[: 2 * sources], held, refs[-1])
    refs = held
    for source, first, count, bit, out, there in ranges:
        own, came = refs[2 * out], refs[2 * out + 1]
        half = count // 2
        keep = pl.multiple_of(first + bits_ref[bit] * half, 16)
        give = pl.multiple_of(first + (1 - bits_ref[bit]) * half, 16)
        outs[source][pl.ds(keep, half), :] = own[there : there + half, :]
        outs[source][pl.ds(give, half), :] = came[there : there + half, :]


def double_step(ranges, bits, pairs, *tokens):
    width = pairs[0][0].shape[1]
    count = 1 + max(r[0] for r in ranges)
    heights = [max(r[1] + r[2] for r in ranges if r[0] == source) for source in range(count)]
    flat = [v for pair in pairs for v in pair]
    return pl.pallas_call(
        functools.partial(double_kernel, ranges, len(pairs), len(tokens)),
        in_specs=[SMEM] + [ANY] * len(flat) + [ANY] * len(tokens),
        out_specs=[VMEM] * count,
        out_shape=[jax.ShapeDtypeStruct((n, width), BF16) for n in heights],
        scratch_shapes=[pltpu.VMEM(v.shape, BF16) for v in flat]
        + [pltpu.SemaphoreType.DMA((len(flat),))],
        compiler_params=limit(24),
        cost_estimate=cost(0, 4 * sum(heights) * width),
        name="double_step",
    )(jnp.stack([bit_of(*b) for b in bits]).astype(jnp.int32), *flat, *tokens)


AXIS_X, AXIS_Y, AXIS_Z0, AXIS_Z1 = ("dp", 1), ("blk", 0), ("blk", 1), ("blk", 2)


def places(half, width, ff):
    up, down, out, qkv, gains = range(5)
    edge = ff // 2
    result = [
        (c, width, up, 0, half * edge + c) for c in range(0, edge, width)
    ]
    result.append((edge, width // 2, out, half * (width // 2), 0))
    result += [
        (edge + width // 2 + c, width, down, half * edge + c, 0) for c in range(0, edge, width)
    ]
    start = edge + width // 2 + edge
    total = 3 * width + EXTRA
    at = half * total // 2
    while at < (half + 1) * total // 2:
        block, line = divmod(at, width)
        if at >= 3 * width:
            result.append((start + at - half * total // 2, 16, gains, 0, 0))
            break
        count = min(width - line, (half + 1) * total // 2 - at)
        result.append((start + at - half * total // 2, count, qkv, line, block * width))
        at += count
    return result


def assemble_kernel(which, prior, width, ff, core_ref, values_ref, *refs):
    outs = refs[5 if prior else 0 :][:5]
    held, sems = refs[-2:]

    def write(half):
        copies = []
        for i, (first, count, out, line, column) in enumerate(places(half, width, ff)):
            held[first : first + count, :] = values_ref[first : first + count, :].astype(F32)
            copy = pltpu.make_async_copy(
                held.at[pl.ds(first, count)],
                outs[out].at[pl.ds(line, count), pl.ds(column, width)],
                sems.at[i],
            )
            copy.start()
            copies.append(copy)
        for copy in copies:
            copy.wait()

    @pl.when(core_ref[0] == which)
    def _():
        write(0)

    @pl.when(core_ref[0] != which)
    def _():
        write(1)


def assemble(core, which, values, width, ff, prior):
    shapes = [(width, ff), (ff, width), (width, width), (width, 3 * width), (16, width)]
    operands = [core, values] + (list(prior) if prior is not None else [])
    most = max(len(places(half, width, ff)) for half in (0, 1))
    return pl.pallas_call(
        functools.partial(assemble_kernel, which, prior is not None, width, ff),
        in_specs=[SMEM, VMEM] + [ANY] * (len(operands) - 2),
        out_specs=[ANY] * 5,
        out_shape=[jax.ShapeDtypeStruct(shape, F32) for shape in shapes],
        scratch_shapes=[pltpu.VMEM(values.shape, F32), pltpu.SemaphoreType.DMA((most,))],
        input_output_aliases={} if prior is None else {2 + i: i for i in range(5)},
        compiler_params=limit(16),
        cost_estimate=cost(0, values.size * 6),
        name="assemble",
    )(*operands)


def exchange(values, devices):
    shape = values.shape
    parts = values.reshape(devices, shape[0] // devices, *shape[1:])
    return lax.all_to_all(parts, "blk", split_axis=0, concat_axis=0, tiled=True).reshape(shape)


def per_device(
    x_a, x_b, sel_a, sel_b, gain_one, w_qkv, w_out, w_sort, gain_two, w_up, w_down, cot_a, cot_b
):
    devices = lax.axis_size("blk")
    me = lax.axis_index("blk")
    seqs_a, rows_a, width = x_a.shape
    seqs_b, rows_b, _ = x_b.shape
    npl = sel_a.shape[1]
    blocks = npl * devices
    len_a = rows_a // npl
    len_b = rows_b // npl
    total_a = seqs_a * rows_a
    total_b = seqs_b * rows_b
    rows = total_a + total_b
    units = rows // UNIT
    units_a = total_a // UNIT
    count_a = seqs_a * npl
    count_b = seqs_b * npl
    picks = count_a + count_b
    picks_up = -(-picks // 16) * 16
    groups = rows // GROUP
    per = TILE // GROUP
    capacity = 2 * max(1, (4 * units + 5 * devices - 1) // (5 * devices))
    send_rows = devices * capacity * UNIT
    ff = w_up.shape[1]
    gain1 = gain_one.astype(F32).reshape(1, width)
    gain2 = gain_two.astype(F32).reshape(1, width)

    first, early = capacity, groups
    if capacity > 8:
        full, left = divmod(units, capacity)
        sure = (full * 8 + min(left, 8)) // 2 // per * per
        if capacity == 14 and 0 < sure < groups:
            first, early = 8, sure

    sizes = [8, 7] if early < groups else [capacity]
    extra = 16
    average = np.zeros((picks, units), np.float32)
    for j in range(count_a):
        average[j, 2 * j : 2 * j + 2] = 1.0 / len_a
    for j in range(count_b):
        average[count_a + j, units_a + j] = 1.0 / len_b
    settings = (npl, seqs_a, seqs_b, devices, capacity, first, early, sizes, extra, picks_up)
    w_sort_t = w_sort.T
    x, means, news, far_rows, ret_rows, perm, place, kinds = digest(
        x_a.reshape(-1, width), x_b.reshape(-1, width), sel_a, sel_b, gain1, average, w_sort_t, settings
    )
    news = lax.all_to_all(news, "blk", split_axis=0, concat_axis=0, tiled=True)
    table = news[:, picks, :capacity].astype(jnp.int32).reshape(-1)
    back_table = news[:, picks, capacity : capacity + sum(sizes)].astype(jnp.int32).reshape(-1)
    news = news[:, :picks]
    parcels = pack(table, x, devices, capacity, first, picks_up)
    recv = [exchange(parcels[0], devices)]
    summary = means * gain1
    rs = inverse_norm(summary)
    unit_summary = (summary * rs).astype(BF16)
    all_summaries = jnp.broadcast_to(
        jnp.pad(unit_summary, ((0, picks_up - picks), (0, 0))), (devices, picks_up, width)
    )

    xp, cot = arrange(perm, x, cot_a.reshape(-1, width), cot_b.reshape(-1, width))
    proj = project(xp, gain1, w_qkv)

    def by_sequence(values):
        tail = values.shape[2:]
        one = values[:, :count_a].reshape((devices, seqs_a, npl) + tail)
        two = values[:, count_a:].reshape((devices, seqs_b, npl) + tail)
        both = jnp.concatenate([one, two], axis=1)
        return jnp.swapaxes(both, 0, 1).reshape((seqs_a + seqs_b, blocks) + tail)

    def own_rows(values):
        return lax.dynamic_slice_in_dim(values, me * npl, npl, 1).reshape((-1,) + values.shape[2:])

    def to_units(values):
        return jnp.concatenate(
            [jnp.repeat(values[:count_a], len_a // UNIT, axis=0), values[count_a:]], axis=0
        )

    news = by_sequence(news)
    logits = news[..., :blocks]
    picked = (news[..., blocks : blocks + 1] == jnp.arange(blocks, dtype=F32)).astype(F32)
    weights = jnp.take(to_units(own_rows(sinkhorn(logits, picked))), perm, axis=0)
    lane = jnp.arange(2 * GROUP) >= GROUP
    wrow = jnp.where(lane[None, :], jnp.repeat(weights, UNIT, axis=0), 1.0)
    if len(parcels) > 1:
        tall = (capacity - first) * UNIT
        parcel = lax.dynamic_update_slice(
            parcels[1].reshape(devices, -1, width), all_summaries, (0, tall, 0)
        )
        recv.append(exchange(tie(parcel.reshape(-1, width), wrow, proj), devices))
        units_all = recv[1].reshape(devices, -1, width)[:, tall:]
    else:
        units_all = exchange(all_summaries.reshape(-1, width), devices)
        units_all = units_all.reshape(devices, picks_up, width)
    units_all = by_sequence(units_all[:, :picks])
    block_of = np.arange(GROUP) // len_b
    cross = block_of[:, None] != block_of[None, :]
    mask = np.zeros((2, GROUP, 2 * GROUP), np.float32)
    mask[1] = np.where(np.concatenate([cross, cross], axis=1), -1e30, 0.0)

    core = bit_of("dp", 0).astype(jnp.int32).reshape(1)
    shared = (xp, cot, proj, wrow, mask, gain1, gain2, w_qkv, w_out, w_up, w_down)
    heights = [
        devices * (n * UNIT + (extra if i == len(sizes) - 1 else 0))
        for i, n in enumerate(sizes)
    ]

    letter = (count_a, count_b, devices, extra)

    def run_backward(streams, *rest):
        _, _, gatt, prob, farx, farkv = streams
        return backward(ret_rows, place, proj, farx, farkv, gatt, prob, wrow, w_qkv, *rest)

    fast = lax.axis_size("dp") == 4 and devices == 8 and early < groups
    part_x = ff // 2 + width // 2
    if early < groups:
        prior = forward(far_rows, kinds, core, recv[:1], *shared, 0, early, None, False, wrow)
        dproj, dfar, gw_one, gain, *ret = run_backward(
            prior[0], heights[:1], 0, early, None, None, prior[0][0]
        )
        back = [exchange(v, devices) for v in ret]
        streams, sums = forward(
            far_rows, kinds, core, recv, *shared, early, groups - early, prior, True, gain
        )
        keep, give, g_gain2 = sums
        out_a, out_b = restore(perm, streams[0], total_a)
        big_came = swap(give, "dp", 0)
        token = keep
        if fast:
            ranges_one = [(0, 0, part_x, 0, 0, 0), (0, part_x, keep.shape[0] - part_x, 1, 1, 0)]
            (bx, gx), (by, gy) = halve_step(
                ranges_one, [AXIS_X, AXIS_Y], [(keep, big_came)], out_a
            )
            bx_came, by_came = swap(gx, *AXIS_X), swap(gy, *AXIS_Y)
            token = bx
        dproj, dfar, _, g_gain1_far, *ret = run_backward(
            streams, heights[1:], early, groups - early, (dproj, dfar, gw_one, gain), letter, token
        )
    else:
        streams, sums = forward(far_rows, kinds, core, recv, *shared, 0, groups, None, True, wrow)
        keep, give, g_gain2 = sums
        out_a, out_b = restore(perm, streams[0], total_a)
        big_came = swap(give, "dp", 0)
        back = []
        dproj, dfar, _, g_gain1_far, *ret = run_backward(
            streams, heights, 0, groups, None, letter, keep
        )
    _, gmid, _, _, farx, _ = streams

    parcel = tie(ret[0], bx_came, by_came, back[0]) if fast else ret[0]
    tall = sizes[-1] * UNIT
    arrived = exchange(parcel, devices)
    back.append(arrived)
    gains = jnp.concatenate([g_gain1_far, g_gain2], axis=0)
    token = dproj
    gn, late_keep, late_give = qkv_grads(
        core, xp, farx, dproj, dfar, gain1, w_qkv, gains, EXTRA, token
    )
    late_came = swap(late_give, "dp", 0)
    part_late = 512
    gw = arrived.reshape(devices, -1, width)[:, tall:, :picks]
    if fast:
        late_rows = late_keep.shape[0]
        ranges_late = [(0, 0, part_late, 0, 0, 0), (0, part_late, late_rows - part_late, 1, 1, 0)]
        (lx, gx), (ly, gy) = halve_step(
            ranges_late, [AXIS_X, AXIS_Y], [(late_keep, late_came)], late_came
        )
        lx_came, ly_came = swap(gx, *AXIS_X), swap(gy, *AXIS_Y)
        nbx, nlx, nby, nly = (v.shape[0] for v in (bx, lx, by, ly))
        ranges_two = [
            (0, 0, nbx, 0, 0, 0),
            (1, 0, nlx, 0, 0, nbx // 2),
            (2, 0, nby, 1, 1, 0),
            (3, 0, nly, 1, 1, nby // 2),
        ]
        (vx, gx), (vy, gy) = halve_step(
            ranges_two,
            [AXIS_Y, AXIS_X],
            [(bx, bx_came), (lx, lx_came), (by, by_came), (ly, ly_came)],
            lx,
        )
        vx_came, vy_came = swap(gx, *AXIS_Y), swap(gy, *AXIS_X)
        cuts = [nbx // 2, nlx // 2, nby // 2, nly // 2]
        ranges_three = [
            (0, 0, cuts[0], 0, 0, 0),
            (0, cuts[0], cuts[1], 0, 0, cuts[0] // 2),
            (1, 0, cuts[2], 0, 0, (cuts[0] + cuts[1]) // 2),
            (1, cuts[2], cuts[3], 0, 0, (cuts[0] + cuts[1] + cuts[2]) // 2),
        ]
        ((total, gz),) = halve_step(
            ranges_three, [AXIS_Z0], [(vx, vx_came), (vy, vy_came)], arrived
        )
        gw = tie(gw, total)
        total = add(total, swap(gz, *AXIS_Z0))
    gw = by_sequence(gw[:, 0].astype(F32))
    g_logits = sinkhorn_back(logits, picked, jnp.broadcast_to(gw[..., None], logits.shape)) * (
        1.0 / SOFTMAX_HEAT
    )
    precise = lax.Precision.HIGHEST
    flat_logits = g_logits.reshape(-1, blocks)
    flat_units = units_all.reshape(-1, width).astype(F32)
    g_sort = lax.dot_general(
        flat_logits, flat_units, TN, precision=precise, preferred_element_type=F32
    )
    g_unit = lax.dot_general(
        flat_logits, w_sort_t.astype(F32), NN, precision=precise, preferred_element_type=F32
    )
    g_own = own_rows(g_unit.reshape(g_logits.shape[:2] + (width,)))
    g_summary = rs * (
        g_own - summary * rs * rs * jnp.mean(g_own * summary, axis=-1, keepdims=True)
    )
    both = g_unit * flat_units
    both = both - flat_units * flat_units * jnp.mean(both, axis=-1, keepdims=True)
    small = jnp.concatenate([g_sort, jnp.sum(both, axis=0, keepdims=True) / gain1], axis=0)
    spread = to_units(
        jnp.concatenate([g_summary[:count_a] / len_a, g_summary[count_a:] / len_b], axis=0)
    )
    base = base_rows(xp, gmid, gn, jnp.take(spread, perm, axis=0), gain1)

    gx_a, gx_b = last(back_table, place, back, sizes, extra, sum(sizes), x, base, gain1, total_a)
    if fast:
        for bit in (0, 1):
            small = small + swap(small, "dp", bit)
        total = add(total, tie(swap(total, *AXIS_Z1), gx_a, small))
        vx, vy = double_step(ranges_three, [AXIS_Z0], [(total, swap(total, *AXIS_Z0))])
        ranges_back = [
            (0, 0, nbx, 0, 0, 0),
            (0, nbx, nlx, 0, 0, cuts[0]),
            (1, 0, nby, 1, 1, 0),
            (1, nby, nly, 1, 1, cuts[2]),
        ]
        vx, vy = double_step(
            ranges_back,
            [AXIS_Y, AXIS_X],
            [(vx, swap(vx, *AXIS_Y)), (vy, swap(vy, *AXIS_X))],
        )
        big_rows = keep.shape[0]
        ranges_all = [
            (0, 0, part_x, 0, 0, 0),
            (0, big_rows, part_late, 0, 0, nbx),
            (0, part_x, big_rows - part_x, 1, 1, 0),
            (0, big_rows + part_late, late_rows - part_late, 1, 1, nby),
        ]
        (sums_own,) = double_step(
            ranges_all,
            [AXIS_X, AXIS_Y],
            [(vx, swap(vx, *AXIS_X)), (vy, swap(vy, *AXIS_Y))],
        )
    else:
        across = [("dp", bit) for bit in range(1, bits_of(lax.axis_size("dp")))]
        along = [("blk", bit) for bit in range(bits_of(devices))]
        sums_own = jnp.concatenate(
            [
                reduce_any(add(keep, big_came), across + along),
                reduce_any(add(late_keep, late_came), along + across),
            ],
            axis=0,
        )
    sums_came = swap(sums_own, "dp", 0)

    if not fast:
        small = lax.psum(small, "dp")
    written = assemble(core, 0, sums_own, width, ff, None)
    sum_up, sum_down, sum_out, sum_qkv, gains = assemble(core, 1, sums_came, width, ff, written)

    return (
        out_a.reshape(x_a.shape),
        out_b.reshape(x_b.shape),
        gx_a.reshape(x_a.shape),
        gx_b.reshape(x_b.shape),
        gains[0] + small[blocks],
        sum_qkv,
        sum_out,
        small[:blocks].T,
        gains[1],
        sum_up,
        sum_down,
    )


def solution(mesh):
    rows_spec = P("dp", "blk", None)
    in_specs = (
        (rows_spec, rows_spec, P("dp", "blk"), P("dp", "blk")) + (P(),) * 7 + (rows_spec, rows_spec)
    )
    out_specs = (rows_spec,) * 4 + (P(),) * 7
    return jax.shard_map(
        per_device, mesh=mesh, in_specs=in_specs, out_specs=out_specs, check_vma=False
    )
```

```python
import functools

import jax
import jax.numpy as jnp
import numpy as np
from jax import lax
from jax.experimental import pallas as pl
from jax.experimental.pallas import tpu as pltpu
from jax.sharding import PartitionSpec as P

HEADS = 8
SINK_ITERS = 8
EPSILON = 1e-05
SOFTMAX_HEAT = 0.75
UNIT = 32
EXTRA = 256
GROUP = 64
TILE = 256
HALF = 256
PER_HALF = 4
VMEM_LIMIT = 62 * 1024 * 1024

F32 = jnp.float32
BF16 = jnp.bfloat16

NN = (((1,), (0,)), ((), ()))
NT = (((1,), (1,)), ((), ()))
TN = (((0,), (0,)), ((), ()))


def dot(a, b, dims=NN):
    return lax.dot_general(a, b, dims, preferred_element_type=F32)


def inverse_norm(values):
    return lax.rsqrt(jnp.mean(values * values, axis=-1, keepdims=True) + EPSILON)


def whole(shape):
    zeros = (0,) * len(shape)
    return pl.BlockSpec(shape, lambda *_: zeros, pipeline_mode=pl.Buffered(1))


def rows_of(tile, width):
    return pl.BlockSpec((tile, width), lambda i: (i, 0))


SMEM = pl.BlockSpec(memory_space=pltpu.SMEM)


def params():
    return pltpu.CompilerParams(
        dimension_semantics=("arbitrary",), vmem_limit_bytes=VMEM_LIMIT
    )


def cost(flops, nbytes):
    return pl.CostEstimate(flops=int(flops * 1e-3), bytes_accessed=int(nbytes * 1e-3), transcendentals=0)


ANY = pl.BlockSpec(memory_space=pl.ANY)
VMEM = pl.BlockSpec(memory_space=pltpu.VMEM)
HBM = pl.BlockSpec(memory_space=pltpu.HBM)


def limit(mib):
    return pltpu.CompilerParams(vmem_limit_bytes=mib * 1024 * 1024)


def request_kernel(
    npl, seqs_a, seqs_b, devices, capacity, first, early, sizes, extra, spare_rows,
    sela_ref, selb_ref, table_ref, back_ref, far_ref, ret_ref, perm_ref, place_ref, kinds_ref, fill, begin, used,
):
    count_a = seqs_a * npl
    count_b = seqs_b * npl
    units_a = 2 * count_a
    width = sum(sizes)
    shift = npl.bit_length() - 1 if npl & (npl - 1) == 0 else -1

    def choice(j):
        ref, at = (sela_ref, j) if j < count_a else (selb_ref, j - count_a)
        return ref[at // npl, at % npl]

    def split(chosen):
        if shift >= 0:
            return lax.shift_right_logical(chosen, shift), lax.bitwise_and(chosen, npl - 1)
        return lax.div(chosen, npl), lax.rem(chosen, npl)

    def clear(ref):
        def body(i, carry):
            ref[i] = -1
            return carry

        return body

    lax.fori_loop(0, devices * capacity, clear(table_ref), 0)
    lax.fori_loop(0, devices * width, clear(back_ref), 0)
    for s in range(devices):
        fill[s] = 0
        used[s] = 0
        used[devices + s] = 0
    one = lambda flag: jnp.where(flag, 1, 0)
    ready_a, ready_b, must_a, must_b = (jnp.int32(0) for _ in range(4))
    for j in range(count_a + count_b):
        source, inner = split(choice(j))
        slot = fill[source]
        begin[j] = slot
        size = 2 if j < count_a else 1
        fill[source] = slot + size
        if j < count_a:
            unit = inner * 2 + (j // npl) * npl * 2
            ready_a = ready_a + one(slot + 2 <= first)
            table_ref[source * capacity + slot + 1] = unit + 1
        else:
            unit = inner + (units_a + (j - count_a) // npl * npl)
            ready_b = ready_b + one(slot + 1 <= first)
        table_ref[source * capacity + slot] = unit

    two = early < count_a + count_b // 2

    def must(j):
        source, _ = split(choice(j))
        if not two:
            return begin[j] < 0
        return begin[j] < fill[source] - 6

    for j in range(count_a):
        must_a = must_a + one(must(j))
    for j in range(count_b):
        must_b = must_b + one(must(count_a + j))
    even = jnp.logical_or(lax.bitwise_and(must_b, 1) == 0, ready_b > must_b)
    pairs = lax.shift_right_logical(must_b + one(even), 1)
    take_a = jnp.minimum(ready_a, early - pairs)
    if not two:
        take_a = jnp.int32(count_a)
    take_b = 2 * (early - take_a)
    late_b = 2 * (early + count_a - take_a)
    kinds_ref[0] = take_a
    kinds_ref[1] = early + count_a - take_a
    second = devices * first * UNIT

    def ret_row(phase, source, slot):
        chunks = list(enumerate(sizes))
        if two:
            chunks = chunks[:1] if phase == 0 else chunks[1:]
        row = jnp.int32(0)
        begin_slot, begin_row = 0, 0
        for index, size in chunks:
            height = size * UNIT + (extra if index == len(sizes) - 1 else 0)
            here = begin_row + source * height + (slot - begin_slot) * UNIT
            row = jnp.where(slot >= begin_slot, here, row)
            begin_slot += size
            begin_row += devices * height
        return row

    def put(pos, unit, inner, source, slot, late):
        near = (source * first + slot) * UNIT
        rest = second + source * ((capacity - first) * UNIT + spare_rows) + (slot - first) * UNIT
        far_ref[pos] = jnp.where(slot < first, near, rest)
        at = late * devices + source
        back = used[at]
        used[at] = back + 1
        if two:
            ret_ref[pos] = jnp.where(late == 0, ret_row(0, source, back), ret_row(1, source, back))
            back_ref[source * width + back + late * sizes[0]] = inner
        else:
            ret_ref[pos] = ret_row(0, source, back)
            back_ref[source * width + back] = inner
        perm_ref[pos] = unit
        place_ref[unit] = pos

    spare = take_a - must_a
    taken, other, free = (jnp.int32(0) for _ in range(3))
    for j in range(count_a):
        source, inner = split(choice(j))
        slot = begin[j]
        need = must(j)
        pick = jnp.logical_and(jnp.logical_not(need), jnp.logical_and(slot + 2 <= first, free < spare))
        use = jnp.logical_or(need, pick)
        free = free + one(pick)
        pos = 2 * jnp.where(use, taken, early + other)
        inner = inner * 2 + (j // npl) * npl * 2
        put(pos, 2 * j, inner, source, slot, one(jnp.logical_not(use)))
        put(pos + 1, 2 * j + 1, inner + 1, source, slot + 1, one(jnp.logical_not(use)))
        taken = taken + one(use)
        other = other + one(jnp.logical_not(use))
    spare = take_b - must_b
    drop = one(spare < 0)
    taken, other, free = (jnp.int32(0) for _ in range(3))
    for j in range(count_b):
        source, inner = split(choice(count_a + j))
        slot = begin[count_a + j]
        need = must(count_a + j)
        skip = jnp.logical_and(need, drop > 0)
        drop = drop - one(skip)
        pick = jnp.logical_and(jnp.logical_not(need), jnp.logical_and(slot + 1 <= first, free < spare))
        use = jnp.logical_or(jnp.logical_and(need, jnp.logical_not(skip)), pick)
        free = free + one(pick)
        pos = jnp.where(use, 2 * take_a + taken, late_b + other)
        inner = inner + (units_a + (j // npl) * npl)
        put(pos, units_a + j, inner, source, slot, one(jnp.logical_not(use)))
        taken = taken + one(use)
        other = other + one(jnp.logical_not(use))


def digest_kernel(
    tiles_a, settings, sela_ref, selb_ref, xa_ref, xb_ref, gain_ref, avg_ref, wsort_ref,
    x_ref, means_ref, news_ref, far_ref, ret_ref, perm_ref, place_ref, kinds_ref,
    sums, table_ref, back_ref, fill, begin, used,
):
    step = pl.program_id(0)

    @pl.when(step == 0)
    def _():
        request_kernel(
            *settings, sela_ref, selb_ref, table_ref, back_ref, far_ref, ret_ref, perm_ref, place_ref,
            kinds_ref, fill, begin, used,
        )

    def take(src):
        x = src[...]
        x_ref[...] = x
        x = x.astype(F32)
        scaled = x * inverse_norm(x)
        units = x.shape[0] // UNIT
        at = pl.ds(pl.multiple_of(step * units, units), units)
        sums[at, :] = jnp.sum(scaled.reshape(units, UNIT, x.shape[1]), axis=1)

    pl.when(step < tiles_a)(lambda: take(xa_ref))
    pl.when(step >= tiles_a)(lambda: take(xb_ref))

    @pl.when(step == pl.num_programs(0) - 1)
    def _():
        means = lax.dot_general(
            avg_ref[...], sums[...], NN, precision=lax.Precision.HIGHEST, preferred_element_type=F32
        )
        means_ref[...] = means
        summary = means * gain_ref[...]
        unit = (summary * inverse_norm(summary)).astype(BF16)
        logits = dot(unit, wsort_ref[...], NT) * (1.0 / SOFTMAX_HEAT)
        picks, blocks = logits.shape
        devices, height, lanes = news_ref.shape
        line = lax.broadcasted_iota(jnp.int32, (picks, lanes - blocks), 0)
        lane = lax.broadcasted_iota(jnp.int32, (picks, lanes - blocks), 1)
        chosen = jnp.zeros((picks, lanes - blocks), jnp.int32)
        count_a = sela_ref.shape[0] * sela_ref.shape[1]
        for j in range(picks):
            ref, at = (sela_ref, j) if j < count_a else (selb_ref, j - count_a)
            npl = ref.shape[1]
            chosen = jnp.where(line == j, ref[at // npl, at % npl], chosen)
        chosen = jnp.where(lane == 0, chosen, 0).astype(F32)
        message = jnp.concatenate([logits, chosen], axis=1)
        lane = lax.broadcasted_iota(jnp.int32, (1, lanes), 1)
        wanted = table_ref.shape[0] // devices
        order = back_ref.shape[0] // devices
        rest = lax.broadcasted_iota(jnp.int32, (height - picks, lanes), 0)
        for d in range(devices):
            row = jnp.zeros((1, lanes), jnp.int32)
            for k in range(wanted):
                row = jnp.where(lane == k, table_ref[d * wanted + k], row)
            for k in range(order):
                row = jnp.where(lane == wanted + k, back_ref[d * order + k], row)
            news_ref[d, :picks, :] = message
            news_ref[d, picks:, :] = jnp.where(rest == 0, row.astype(F32), 0.0)


def digest(x_a, x_b, sel_a, sel_b, gain_row, average, w_sort_t, settings):
    npl, seqs_a, seqs_b, devices, capacity, _, _, sizes, _, _ = settings
    width = x_a.shape[1]
    tile = 2 * TILE if x_a.shape[0] % (2 * TILE) == 0 and x_b.shape[0] % (2 * TILE) == 0 else TILE
    tiles_a = x_a.shape[0] // tile
    tiles_b = x_b.shape[0] // tile
    rows = x_a.shape[0] + x_b.shape[0]
    picks = average.shape[0]
    height = -(-picks // 8) * 8 + 8
    units = rows // UNIT
    ints = lambda n: jax.ShapeDtypeStruct((n,), jnp.int32)
    return pl.pallas_call(
        functools.partial(digest_kernel, tiles_a, settings),
        grid=(tiles_a + tiles_b,),
        in_specs=[
            SMEM,
            SMEM,
            pl.BlockSpec((tile, width), lambda i: (jnp.minimum(i, tiles_a - 1), 0)),
            pl.BlockSpec((tile, width), lambda i: (jnp.maximum(i - tiles_a, 0), 0)),
            whole((1, width)),
            whole(average.shape),
            whole(w_sort_t.shape),
        ],
        out_specs=[rows_of(tile, width), whole((picks, width)), whole((devices, height, 128))]
        + [SMEM] * 5,
        out_shape=[
            jax.ShapeDtypeStruct((rows, width), BF16),
            jax.ShapeDtypeStruct((picks, width), F32),
            jax.ShapeDtypeStruct((devices, height, 128), F32),
        ]
        + [ints(n) for n in (units, units, units, units, 2)],
        scratch_shapes=[
            pltpu.VMEM((units, width), F32),
            pltpu.SMEM((devices * capacity,), jnp.int32),
            pltpu.SMEM((devices * sum(sizes),), jnp.int32),
            pltpu.SMEM((devices,), jnp.int32),
            pltpu.SMEM((picks,), jnp.int32),
            pltpu.SMEM((2 * devices,), jnp.int32),
        ],
        compiler_params=params(),
        cost_estimate=cost(rows * width * 10, rows * width * 4),
        name="digest",
    )(sel_a, sel_b, x_a, x_b, gain_row, average, w_sort_t)


def pack_kernel(devices, capacity, first, spare, table_ref, x_ref, *rest):
    outs = rest[: 1 if first == capacity else 2]
    held, sems = rest[len(outs) :]
    sizes = [first, capacity - first]
    copies = []
    for part, out_ref in enumerate(outs):
        size = sizes[part]
        base = part * devices * first
        for r in range(devices):
            for slot in range(size):
                unit = jnp.maximum(table_ref[r * capacity + part * first + slot], 0)
                src = pl.ds(pl.multiple_of(unit * UNIT, UNIT), UNIT)
                at = (base + r * size + slot) * UNIT
                held[at : at + UNIT, :] = x_ref[src, :]
            at = (base + r * size) * UNIT
            copy = pltpu.make_async_copy(
                held.at[pl.ds(at, size * UNIT)],
                out_ref.at[pl.ds(r * (size * UNIT + part * spare), size * UNIT)],
                sems.at[part * devices + r],
            )
            copy.start()
            copies.append(copy)
    for copy in copies:
        copy.wait()


def pack(table, x, devices, capacity, first, spare):
    width = x.shape[1]
    sizes = [first] if first == capacity else [first, capacity - first]
    return pl.pallas_call(
        functools.partial(pack_kernel, devices, capacity, first, spare),
        in_specs=[SMEM, VMEM],
        out_specs=[HBM] * len(sizes),
        out_shape=[
            jax.ShapeDtypeStruct((devices * (n * UNIT + i * spare), width), BF16)
            for i, n in enumerate(sizes)
        ],
        scratch_shapes=[
            pltpu.VMEM((devices * capacity * UNIT, width), BF16),
            pltpu.SemaphoreType.DMA((len(sizes) * devices,)),
        ],
        compiler_params=limit(62),
        cost_estimate=cost(0, x.size * 6),
        name="pack",
    )(table, x)


def arrange_kernel(units_a, perm_ref, x_ref, cota_ref, cotb_ref, xp_ref, cotp_ref):
    def body(pos, carry):
        unit = perm_ref[pos]
        at = pl.ds(pl.multiple_of(pos * UNIT, UNIT), UNIT)
        xp_ref[at, :] = x_ref[pl.ds(pl.multiple_of(unit * UNIT, UNIT), UNIT), :]

        @pl.when(unit < units_a)
        def _():
            cotp_ref[at, :] = cota_ref[pl.ds(pl.multiple_of(unit * UNIT, UNIT), UNIT), :]

        @pl.when(unit >= units_a)
        def _():
            src = pl.ds(pl.multiple_of((unit - units_a) * UNIT, UNIT), UNIT)
            cotp_ref[at, :] = cotb_ref[src, :]

        return carry

    lax.fori_loop(0, x_ref.shape[0] // UNIT, body, 0)


def arrange(perm, x, cot_a, cot_b):
    like = jax.ShapeDtypeStruct(x.shape, BF16)
    return pl.pallas_call(
        functools.partial(arrange_kernel, cot_a.shape[0] // UNIT),
        in_specs=[SMEM, VMEM, VMEM, VMEM],
        out_specs=[VMEM, VMEM],
        out_shape=[like, like],
        compiler_params=limit(16),
        cost_estimate=cost(0, x.size * 8),
        name="arrange",
    )(perm, x, cot_a, cot_b)


def restore_kernel(perm_ref, out_ref, outa_ref, outb_ref):
    units_a = outa_ref.shape[0] // UNIT

    def body(pos, carry):
        unit = perm_ref[pos]
        at = pl.ds(pl.multiple_of(pos * UNIT, UNIT), UNIT)

        @pl.when(unit < units_a)
        def _():
            outa_ref[pl.ds(pl.multiple_of(unit * UNIT, UNIT), UNIT), :] = out_ref[at, :]

        @pl.when(unit >= units_a)
        def _():
            dst = pl.ds(pl.multiple_of((unit - units_a) * UNIT, UNIT), UNIT)
            outb_ref[dst, :] = out_ref[at, :]

        return carry

    lax.fori_loop(0, out_ref.shape[0] // UNIT, body, 0)


def restore(perm, out, rows_a):
    rows, width = out.shape
    return pl.pallas_call(
        restore_kernel,
        in_specs=[SMEM, VMEM],
        out_specs=[VMEM, VMEM],
        out_shape=[
            jax.ShapeDtypeStruct((rows_a, width), BF16),
            jax.ShapeDtypeStruct((rows - rows_a, width), BF16),
        ],
        compiler_params=limit(16),
        cost_estimate=cost(0, out.size * 4),
        name="restore",
    )(perm, out)


def project_kernel(x_ref, gain_ref, w_ref, proj_ref):
    x = x_ref[...].astype(F32)
    proj_ref[...] = dot((x * inverse_norm(x) * gain_ref[...]).astype(BF16), w_ref[...]).astype(BF16)


def project(x, gain_row, w_qkv):
    rows, width = x.shape
    wide = w_qkv.shape[1]
    return pl.pallas_call(
        project_kernel,
        grid=(rows // TILE,),
        in_specs=[rows_of(TILE, width), whole((1, width)), whole((width, wide))],
        out_specs=rows_of(TILE, wide),
        out_shape=jax.ShapeDtypeStruct((rows, wide), BF16),
        compiler_params=params(),
        cost_estimate=cost(2 * rows * width * wide, rows * (width + wide) * 2),
        name="project",
    )(x, gain_row, w_qkv)


def log_sum(values, axis):
    top = jnp.max(values, axis=axis, keepdims=True)
    return top + jnp.log(jnp.sum(jnp.exp(values - top), axis=axis, keepdims=True))


def sinkhorn_kernel(logits_ref, picked_ref, weight_ref):
    state = logits_ref[...]
    for _ in range(SINK_ITERS):
        state = state - log_sum(state, 2)
        state = state - log_sum(state, 1)
    count = state.shape[1]
    weight = count * jnp.sum(jnp.exp(state) * picked_ref[...], axis=2, keepdims=True)
    weight_ref[...] = jnp.broadcast_to(weight, weight_ref.shape)


def sinkhorn(logits, picked):
    seqs, count, _ = logits.shape
    return pl.pallas_call(
        sinkhorn_kernel,
        out_shape=jax.ShapeDtypeStruct((seqs, count, 128), F32),
        cost_estimate=cost(logits.size * 100, logits.size * 32),
        name="sinkhorn",
    )(logits, picked)


def exact(a, b, dims=NN):
    return lax.dot_general(
        a, b, dims, precision=lax.Precision.HIGHEST, preferred_element_type=F32
    )


def sort_back_kernel(
    npl, seqs_a, lengths, tall, me_ref, perm_ref, logits_ref, picked_ref, units_ref, wsort_ref, gain_ref,
    means_ref, arrived, token_ref, small_ref, spread_ref, kept, letters, sems,
):
    seqs, blocks, _ = logits_ref.shape
    devices = blocks // npl
    picks = means_ref.shape[0]
    extra = letters.shape[1]
    height = arrived.shape[0] // devices
    copies = []
    for d in range(devices):
        source = arrived.at[pl.ds(d * height + tall, extra), pl.ds(0, 128)]
        copies.append(pltpu.make_async_copy(source, letters.at[d], sems.at[d]))
    for copy in copies:
        copy.start()
    state = logits_ref[...]
    for step in range(SINK_ITERS):
        state = state - log_sum(state, 2)
        kept[2 * step] = jnp.exp(state)
        state = state - log_sum(state, 1)
        kept[2 * step + 1] = jnp.exp(state)
    for copy in copies:
        copy.wait()
    rows = seqs * blocks
    line = lax.broadcasted_iota(jnp.int32, (rows, 128), 0)
    lane = lax.broadcasted_iota(jnp.int32, (rows, 128), 1)
    own_lane = line // blocks * npl + line % npl
    device = (line // npl) % devices
    table = jnp.zeros((rows, 128), F32)
    for d in range(devices):
        table = jnp.where(device == d, letters[d, 0:1, :].astype(F32), table)
    gw = jnp.sum(jnp.where(lane == own_lane, table, 0.0), axis=1, keepdims=True)
    grad = blocks * picked_ref[...] * gw.reshape(seqs, blocks, 1) * kept[2 * SINK_ITERS - 1]
    for step in reversed(range(SINK_ITERS)):
        grad = grad - kept[2 * step + 1] * jnp.sum(grad, axis=1, keepdims=True)
        grad = grad - kept[2 * step] * jnp.sum(grad, axis=2, keepdims=True)
    grad = (grad * (1.0 / SOFTMAX_HEAT)).reshape(rows, blocks)
    units = units_ref[...].astype(F32)
    small_ref[:blocks, :] = exact(grad, units, TN)
    g_unit = exact(grad, wsort_ref[...].astype(F32))
    both = g_unit * units
    both = both - units * units * jnp.mean(both, axis=-1, keepdims=True)
    row = jnp.sum(both, axis=0, keepdims=True) / gain_ref[...]
    first = lax.broadcasted_iota(jnp.int32, (small_ref.shape[0] - blocks, units.shape[1]), 0) == 0
    small_ref[blocks:, :] = jnp.where(first, row, 0.0)
    line = lax.broadcasted_iota(jnp.int32, (picks, rows), 0)
    lane = lax.broadcasted_iota(jnp.int32, (picks, rows), 1)
    mine = lane == line // npl * blocks + me_ref[0] * npl + line % npl
    g_own = exact(jnp.where(mine, 1.0, 0.0), g_unit)
    summary = means_ref[...] * gain_ref[...]
    rs = inverse_norm(summary)
    g_summary = rs * (
        g_own - summary * (rs * rs) * jnp.mean(g_own * summary, axis=-1, keepdims=True)
    )
    count_a = seqs_a * npl
    places = spread_ref.shape[0]
    line = lax.broadcasted_iota(jnp.int32, (places, picks), 0)
    lane = lax.broadcasted_iota(jnp.int32, (places, picks), 1)
    unit = jnp.zeros((places, picks), jnp.int32)
    for pos in range(places):
        unit = jnp.where(line == pos, perm_ref[pos], unit)
    block = jnp.where(unit < 2 * count_a, unit // 2, unit - count_a)
    share = jnp.where(lane < count_a, 1.0 / lengths[0], 1.0 / lengths[1])
    spread_ref[...] = exact(jnp.where(lane == block, share, 0.0), g_summary)


def sort_back(
    me, perm, logits, picked, units, w_sort_t, gain, means, arrived, npl, seqs_a, lengths, tall, extra, token
):
    seqs, blocks, _ = logits.shape
    width = means.shape[1]
    return pl.pallas_call(
        functools.partial(sort_back_kernel, npl, seqs_a, lengths, tall),
        in_specs=[SMEM, SMEM] + [VMEM] * 6 + [ANY, ANY],
        out_specs=[VMEM, VMEM],
        out_shape=[
            jax.ShapeDtypeStruct((blocks + 8, width), F32),
            jax.ShapeDtypeStruct((perm.shape[0], width), F32),
        ],
        scratch_shapes=[
            pltpu.VMEM((2 * SINK_ITERS,) + logits.shape, F32),
            pltpu.VMEM((blocks // npl, extra, 128), BF16),
            pltpu.SemaphoreType.DMA((blocks // npl,)),
        ],
        compiler_params=limit(24),
        cost_estimate=cost(logits.size * 200, logits.size * 32),
        name="sort_back",
    )(me, perm, logits, picked, units, w_sort_t, gain, means, arrived, token)


def head_masks(rows):
    lane = lax.broadcasted_iota(jnp.int32, (rows, HALF), 1) // (HALF // PER_HALF)
    return [lane == h for h in range(PER_HALF)]


def stack_heads(values, masks):
    zero = jnp.zeros_like(values)
    return jnp.concatenate([jnp.where(m, values, zero) for m in masks], axis=0)


def unstack_heads(values, masks):
    total = None
    for h, m in enumerate(masks):
        part = jnp.where(m, values[h * GROUP : (h + 1) * GROUP], 0.0)
        total = part if total is None else total + part
    return total


def repeat_heads(values):
    return jnp.concatenate([values] * PER_HALF, axis=0)


class Mover:
    def __init__(self, sems):
        self.sems, self.used, self.out = sems, 0, []

    def start(self, source, target):
        copy = pltpu.make_async_copy(source, target, self.sems.at[self.used])
        self.used += 1
        copy.start()
        return copy

    def store(self, source, target):
        self.out.append(self.start(source, target))

    def finish(self):
        for copy in self.out:
            copy.wait()


BATCH = 4


def forward_kernel(first_group, groups, recvs, prior, final, *refs):
    refs = list(refs)
    take = lambda n: [refs.pop(0) for _ in range(n)]
    far_ref, kinds_ref, core_ref = take(3)
    recv_hbm = take(recvs)
    x_hbm, cot_hbm, proj_hbm, wrow_hbm, mask_ref, gain1_ref, gain2_ref = take(7)
    wqkv_hbm, wout_hbm, wup_hbm, wdown_hbm, _ = take(5)
    prior_refs = take(3) if prior else []
    if prior:
        take(6)
    out_hbm, gmid_hbm, gatt_hbm, prob_hbm, farx_hbm, farkv_hbm = take(6)
    if final:
        keep_hbm, give_hbm, gain_ref = take(3)
    else:
        up_hbm, down_hbm, gain_ref = take(3)
    x_ref, cot_ref, proj_ref, wrow_ref, wqkv_ref, wout_ref, wup_ref, wdown_ref = take(8)
    out_ref, gmid_ref, gatt_ref, prob_ref, farx_ref, farkv_ref, attended = take(7)
    one_ref, two_ref = take(2)
    if prior:
        up_prior, down_prior = take(2)
    (sems,) = take(1)
    move = Mover(sems)
    rows = groups * GROUP
    width = x_ref.shape[1]
    ff = wup_ref.shape[1]
    base = first_group
    here = pl.ds(first_group * GROUP, rows)
    rows_one = recv_hbm[0].shape[0]
    far_sem = sems.at[sems.shape[0] - 1]
    for u in range(rows // UNIT):
        row = far_ref[2 * base + u]
        dst = farx_ref.at[pl.ds(u * UNIT, UNIT)]

        def bring(ref, row, dst=dst):
            src = ref.at[pl.ds(pl.multiple_of(row, 16), UNIT)]
            pltpu.make_async_copy(src, dst, far_sem).start()

        if recvs == 1:
            bring(recv_hbm[0], row)
        else:
            pl.when(row < rows_one)(lambda row=row, bring=bring: bring(recv_hbm[0], row))
            pl.when(row >= rows_one)(lambda row=row, bring=bring: bring(recv_hbm[1], row - rows_one))
    got_wqkv = move.start(wqkv_hbm, wqkv_ref)
    got_proj = move.start(proj_hbm.at[here], proj_ref)
    got_wrow = move.start(wrow_hbm.at[here], wrow_ref)
    got_x = move.start(x_hbm.at[here], x_ref)
    got_wout = move.start(wout_hbm, wout_ref)
    got_cot = move.start(cot_hbm.at[here], cot_ref)
    got_up = move.start(wup_hbm, wup_ref)
    got_down = move.start(wdown_hbm, wdown_ref)
    if prior:
        got_prior = [
            move.start(prior_refs[0], up_prior),
            move.start(prior_refs[1], down_prior),
        ]

    pltpu.make_async_copy(farx_ref, farx_ref, far_sem).wait()
    move.store(farx_ref, farx_hbm.at[here])
    far = farx_ref[...].astype(F32)
    far = (far * inverse_norm(far) * gain1_ref[...]).astype(BF16)
    got_wqkv.wait()
    farkv_ref[...] = dot(far, wqkv_ref[:, width:]).astype(BF16)
    move.store(farkv_ref, farkv_hbm.at[here])
    masks16 = head_masks(GROUP)
    head_scale = (width // HEADS) ** -0.5
    boundary = kinds_ref[1 if prior else 0]
    got_proj.wait()
    got_wrow.wait()
    for first in range(0, groups, BATCH):
        work = [
            (i, half) for i in range(first, min(first + BATCH, groups)) for half in range(width // HALF)
        ]
        scores, vals = [], []
        for i, half in work:
            at = slice(i * GROUP, (i + 1) * GROUP)
            lo = half * HALF
            q = proj_ref[at, lo : lo + HALF] * jnp.asarray(head_scale, BF16)
            keys = jnp.concatenate(
                [proj_ref[at, width + lo : width + lo + HALF], farkv_ref[at, lo : lo + HALF]], axis=0
            )
            vals.append(
                jnp.concatenate(
                    [
                        proj_ref[at, 2 * width + lo : 2 * width + lo + HALF],
                        farkv_ref[at, width + lo : width + lo + HALF],
                    ],
                    axis=0,
                )
            )
            which = jnp.where(base + i < boundary, 0, 1)
            scores.append(dot(stack_heads(q, masks16), keys, NT) + repeat_heads(mask_ref[which]))
        tops = [jnp.max(v, axis=1, keepdims=True) for v in scores]
        weights = [jnp.exp(v - t) for v, t in zip(scores, tops)]
        sums = [jnp.sum(v, axis=1, keepdims=True) for v in weights]
        probs = [v * (1.0 / t) for v, t in zip(weights, sums)]
        mixed = []
        for (i, half), prob, value in zip(work, probs, vals):
            at = slice(i * GROUP, (i + 1) * GROUP)
            prob_ref[i, half] = prob.astype(BF16)
            mixed.append(dot((prob * repeat_heads(wrow_ref[at, :])).astype(BF16), value))
        for (i, half), value in zip(work, mixed):
            at = slice(i * GROUP, (i + 1) * GROUP)
            lo = half * HALF
            attended[at, lo : lo + HALF] = unstack_heads(value, masks16).astype(BF16)
    move.store(prob_ref, prob_hbm.at[pl.ds(first_group, groups)])

    got_x.wait()
    got_wout.wait()
    att = attended[...]
    middle = x_ref[...].astype(F32) + dot(att, wout_ref[...])
    r2 = inverse_norm(middle)
    scaled = middle * r2
    second = (scaled * gain2_ref[...]).astype(BF16)
    got_cot.wait()
    cot = cot_ref[...]
    cot_t = cot.T
    second_t = second.T
    got_up.wait()
    got_down.wait()
    if prior:
        for copy in got_prior:
            copy.wait()

    def total(value, old, lanes):
        return value + old[:, lanes].astype(F32) if prior else value

    edge = ff // 2

    pending = []

    def send(ref, half, lines):
        sem = sems.at[move.used]
        move.used += 1
        for which, hbm in ((half, keep_hbm), (1 - half, give_hbm)):
            copy = pltpu.make_async_copy(ref.at[lines], hbm.at[lines], sem)
            pl.when(core_ref[0] == which)(copy.start)
        pending.append(copy)

    def put_up(c, value):
        lanes = slice(c, c + width)
        if not final:
            one_ref[:, lanes] = value.astype(BF16)
            at = (slice(None), pl.ds(c, width))
            move.store(one_ref.at[at], up_hbm.at[at])
            return
        ref, at = (one_ref, c) if c < edge else (two_ref, c - edge)
        ref[at : at + width, :] = total(value, up_prior if prior else None, lanes).astype(BF16)
        send(ref, 0 if c < edge else 1, pl.ds(at, width))

    def put_down(c, value):
        lanes = slice(c, c + width)
        if not final:
            two_ref[:, lanes] = value.astype(BF16)
            at = (slice(None), pl.ds(c, width))
            move.store(two_ref.at[at], down_hbm.at[at])
            return
        ref, at = (one_ref, c) if c < edge else (two_ref, c - edge)
        at += edge + width // 2
        ref[at : at + width, :] = total(value, down_prior if prior else None, lanes).T.astype(BF16)
        send(ref, 0 if c < edge else 1, pl.ds(at, width))

    def put_out(value):
        if not final:
            one_ref[:, ff:] = value.astype(BF16)
            at = (slice(None), pl.ds(ff, width))
            move.store(one_ref.at[at], up_hbm.at[at])
            return
        value = total(value, up_prior if prior else None, slice(ff, ff + width)).astype(BF16)
        lines = slice(edge, edge + width // 2)
        one_ref[lines, :] = value[: width // 2]
        two_ref[lines, :] = value[width // 2 :]
        send(one_ref, 0, pl.ds(edge, width // 2))
        send(two_ref, 1, pl.ds(edge, width // 2))

    result = middle
    back = jnp.zeros((rows, width), F32)
    c0 = 0.7978845608028654
    c1 = 0.044715
    for c in range(0, ff, width):
        hidden = dot(second, wup_ref[:, c : c + width])
        grad = dot(cot, wdown_ref[c : c + width, :], NT)
        square = hidden * hidden
        t = jnp.tanh(hidden * (c0 + (c0 * c1) * square))
        left = 0.5 + 0.5 * t
        active = (hidden * left).astype(BF16)
        slope = left + (0.5 * hidden) * (1.0 - t * t) * (c0 + (3.0 * c0 * c1) * square)
        grad = (grad * slope).astype(BF16)
        result = result + dot(active, wdown_ref[c : c + width, :])
        back = back + dot(grad, wup_ref[:, c : c + width], NT)
        put_down(c, dot(cot_t, active))
        put_up(c, dot(second_t, grad))
    out_ref[...] = result.astype(BF16)
    move.store(out_ref, out_hbm.at[here])
    gain = jnp.sum(back * scaled, axis=0, keepdims=True)
    gain_ref[...] = gain + prior_refs[2][...] if prior else gain
    e = back * gain2_ref[...]
    inner = jnp.mean(e * scaled, axis=-1, keepdims=True)
    grad_middle = cot.astype(F32) + r2 * (e - scaled * inner)
    branch = grad_middle.astype(BF16)
    gmid_ref[...] = branch
    move.store(gmid_ref, gmid_hbm.at[here])
    put_out(dot(att.T, branch))
    gatt_ref[...] = dot(branch, wout_ref[...], NT).astype(BF16)
    move.store(gatt_ref, gatt_hbm.at[here])
    for copy in pending:
        copy.wait()
    move.finish()


def forward(
    far_rows, kinds, core, recv, x, cot, proj, wrow, mask, gain1, gain2, w_qkv, w_out, w_up, w_down,
    first_group, groups, prior, final, token,
):
    rows, width = x.shape
    ff = w_up.shape[1]
    halves = width // HALF
    count = groups * GROUP
    like = lambda wide, kind=BF16: jax.ShapeDtypeStruct((rows, wide), kind)
    probs = jax.ShapeDtypeStruct((rows // GROUP, halves, PER_HALF * GROUP, 2 * GROUP), BF16)
    part = ff + width // 2
    if final:
        tails = [(part, width), (part, width)]
    else:
        tails = [(width, ff + width), (width, ff)]
    in_specs = [SMEM] * 3 + [ANY] * (len(recv) + 4) + [VMEM] * 3 + [ANY] * 5
    operands = [far_rows, kinds, core, *recv, x, cot, proj, wrow, mask, gain1, gain2]
    operands += [w_qkv, w_out, w_up, w_down, token]
    scratch = [
        pltpu.VMEM((count, width), BF16),
        pltpu.VMEM((count, width), BF16),
        pltpu.VMEM((count, 3 * width), BF16),
        pltpu.VMEM((count, 2 * GROUP), F32),
    ]
    scratch += [pltpu.VMEM(w.shape, BF16) for w in (w_qkv, w_out, w_up, w_down)]
    scratch += [pltpu.VMEM((count, width), BF16)] * 3
    scratch += [pltpu.VMEM((groups,) + probs.shape[1:], BF16)]
    scratch += [pltpu.VMEM((count, n * width), BF16) for n in (1, 2, 1)]
    scratch += [pltpu.VMEM(shape, BF16) for shape in tails]
    aliases = {}
    if prior is not None:
        streams, sums = prior
        in_specs += [ANY, ANY, VMEM] + [ANY] * 6
        operands += list(sums)
        aliases = {len(operands) + i: i for i in range(6)}
        operands += list(streams)
        scratch += [pltpu.VMEM((width, ff + width), BF16), pltpu.VMEM((width, ff), BF16)]
    scratch += [pltpu.SemaphoreType.DMA((40,))]
    out = pl.pallas_call(
        functools.partial(
            forward_kernel, first_group, groups, len(recv), prior is not None, final
        ),
        in_specs=in_specs,
        out_specs=[ANY] * 8 + [VMEM],
        out_shape=[like(width), like(width), like(width), probs, like(width), like(2 * width)]
        + [jax.ShapeDtypeStruct(shape, BF16) for shape in tails]
        + [jax.ShapeDtypeStruct((1, width), F32)],
        scratch_shapes=scratch,
        input_output_aliases=aliases,
        compiler_params=pltpu.CompilerParams(vmem_limit_bytes=VMEM_LIMIT),
        cost_estimate=cost(1.0e9 * groups, 1e6 * groups),
        name="forward",
    )(*operands)
    return out[:6], out[6:]


def backward_kernel(first_group, groups, prior, chunks, letter, *refs):
    refs = list(refs)
    take = lambda n: [refs.pop(0) for _ in range(n)]
    ret_rows, place_ref = take(2)
    proj_hbm, farx_hbm, farkv_hbm, gatt_hbm, prob_hbm, wrow_hbm, wqkv_hbm = take(7)
    if prior:
        prior_gain, prior_gw = take(2)
        take(2)
    take(1)
    dproj_hbm, dfar_hbm, gw_ref, gain_ref = take(4)
    ret_hbm = take(chunks)
    proj_ref, farx_ref, farkv_ref, gatt_ref, prob_ref, wrow_ref, wqkv_ref = take(7)
    dproj_ref, dfar_ref = take(2)
    ret_refs = take(chunks)
    (sems,) = take(1)
    move = Mover(sems)
    rows = groups * GROUP
    width = gatt_ref.shape[1]
    start = first_group * GROUP
    batches = [(first, min(first + BATCH, groups)) for first in range(0, groups, BATCH)]
    loads = []
    for low, high in batches:
        at = pl.ds(low * GROUP, (high - low) * GROUP)
        there = pl.ds(start + low * GROUP, (high - low) * GROUP)
        loads.append(
            [
                move.start(hbm.at[there], ref.at[at])
                for hbm, ref in (
                    (proj_hbm, proj_ref),
                    (farkv_hbm, farkv_ref),
                    (gatt_hbm, gatt_ref),
                    (wrow_hbm, wrow_ref),
                )
            ]
            + [
                move.start(
                    prob_hbm.at[pl.ds(first_group + low, high - low)],
                    prob_ref.at[pl.ds(low, high - low)],
                )
            ]
        )
    got_wqkv = move.start(wqkv_hbm, wqkv_ref)
    got_farx = move.start(farx_hbm.at[pl.ds(start, rows)], farx_ref)
    masks16 = head_masks(GROUP)
    head_scale = (width // HEADS) ** -0.5
    far_lane = lax.broadcasted_iota(jnp.int32, (GROUP // UNIT, 2 * GROUP), 1) >= GROUP
    for (low, high), copies in zip(batches, loads):
        for copy in copies:
            copy.wait()
        work = [(i, half) for i in range(low, high) for half in range(width // HALF)]
        stacks, products = [], []
        for i, half in work:
            at = slice(i * GROUP, (i + 1) * GROUP)
            lo = half * HALF
            vals = jnp.concatenate(
                [
                    proj_ref[at, 2 * width + lo : 2 * width + lo + HALF],
                    farkv_ref[at, width + lo : width + lo + HALF],
                ],
                axis=0,
            )
            up = stack_heads(gatt_ref[at, lo : lo + HALF], masks16)
            stacks.append(up)
            products.append(prob_ref[i, half].astype(F32) * dot(up, vals, NT))
        for i in range(low, high):
            summed = jnp.zeros((GROUP, 2 * GROUP), F32)
            for (j, _), prod in zip(work, products):
                if j == i:
                    for h in range(PER_HALF):
                        summed = summed + prod[h * GROUP : (h + 1) * GROUP]
            pair = jnp.sum(summed.reshape(GROUP // UNIT, UNIT, 2 * GROUP), axis=1)
            pair = jnp.sum(jnp.where(far_lane, pair, 0.0), axis=1, keepdims=True)
            gw_ref[i] = jnp.broadcast_to(pair, (GROUP // UNIT, 128))
        scales = [repeat_heads(wrow_ref[i * GROUP : (i + 1) * GROUP, :]) for i, _ in work]
        products = [v * s for v, s in zip(products, scales)]
        totals = [jnp.sum(v, axis=1, keepdims=True) for v in products]
        for (i, half), up, prod, scale, total in zip(work, stacks, products, scales, totals):
            at = slice(i * GROUP, (i + 1) * GROUP)
            lo = half * HALF
            prob = prob_ref[i, half].astype(F32)
            ds = (prod - prob * total).astype(BF16)
            mixed = (prob * scale).astype(BF16)
            q = stack_heads(
                proj_ref[at, lo : lo + HALF] * jnp.asarray(head_scale, BF16), masks16
            )
            keys = jnp.concatenate(
                [proj_ref[at, width + lo : width + lo + HALF], farkv_ref[at, lo : lo + HALF]], axis=0
            )
            dq = unstack_heads(dot(ds, keys), masks16) * head_scale
            dk = dot(ds, q, TN).astype(BF16)
            dv = dot(mixed, up, TN).astype(BF16)
            dproj_ref[at, lo : lo + HALF] = dq.astype(BF16)
            dproj_ref[at, width + lo : width + lo + HALF] = dk[:GROUP]
            dproj_ref[at, 2 * width + lo : 2 * width + lo + HALF] = dv[:GROUP]
            dfar_ref[at, lo : lo + HALF] = dk[GROUP:]
            dfar_ref[at, width + lo : width + lo + HALF] = dv[GROUP:]
        at = pl.ds(low * GROUP, (high - low) * GROUP)
        there = pl.ds(start + low * GROUP, (high - low) * GROUP)
        move.store(dproj_ref.at[at], dproj_hbm.at[there])
        move.store(dfar_ref.at[at], dfar_hbm.at[there])

    got_wqkv.wait()
    got_farx.wait()
    grad = dot(dfar_ref[...], wqkv_ref[:, width:], NT)
    far = farx_ref[...].astype(F32)
    gain = jnp.sum(grad * (far * inverse_norm(far)), axis=0, keepdims=True)
    gain_ref[...] = gain + prior_gain[...] if prior else gain
    grad = grad.astype(BF16)
    for u in range(rows // UNIT):
        row = ret_rows[2 * first_group + u]
        edge = 0
        for ret_ref in ret_refs:
            value = grad[u * UNIT : (u + 1) * UNIT]

            def put(ret_ref=ret_ref, edge=edge, value=value):
                ret_ref[pl.ds(pl.multiple_of(row - edge, 16), UNIT), :] = value

            if chunks == 1:
                put()
            else:
                pl.when(jnp.logical_and(row >= edge, row < edge + ret_ref.shape[0]))(put)
            edge += ret_ref.shape[0]
    if letter:
        count_a, count_b, devices, extra = letter
        lane = lax.broadcasted_iota(jnp.int32, (1, 128), 1)
        row = jnp.zeros((1, 128), F32)

        def pair_at(at):
            if not prior:
                return gw_ref[at]
            early = prior_gw.shape[0]
            one = prior_gw[jnp.minimum(at, early - 1)]
            two = gw_ref[jnp.maximum(at - early, 0)]
            return jnp.where(at < early, one, two)

        for j in range(count_a + count_b):
            if j < count_a:
                both = pair_at(lax.shift_right_logical(place_ref[2 * j], 1))
                value = both[0:1] + both[1:2]
            else:
                pos = place_ref[count_a + j]
                both = pair_at(lax.shift_right_logical(pos, 1))
                value = jnp.where(lax.bitwise_and(pos, 1) == 0, both[0:1], both[1:2])
            row = jnp.where(lane == j, value, row)
        page = jnp.concatenate([row, jnp.zeros((1, width - 128), F32)], axis=1)
        line = lax.broadcasted_iota(jnp.int32, (extra, width), 0)
        page = jnp.where(line == 0, page, 0.0).astype(BF16)
        ret_ref = ret_refs[-1]
        height = ret_ref.shape[0] // devices
        for d in range(devices):
            ret_ref[(d + 1) * height - extra : (d + 1) * height, :] = page
    for ret_ref, hbm in zip(ret_refs, ret_hbm):
        move.store(ret_ref, hbm)
    move.finish()


def backward(
    ret_rows, place, proj, farx, farkv, gatt, prob, wrow, w_qkv, sizes, first_group, groups, prior, letter,
    token,
):
    rows, width = gatt.shape
    count = groups * GROUP
    in_specs = [SMEM, SMEM] + [ANY] * 7
    operands = [ret_rows, place, proj, farx, farkv, gatt, prob, wrow, w_qkv]
    aliases = {}
    if prior is not None:
        dproj, dfar, gw, gain = prior
        in_specs += [VMEM, VMEM, ANY, ANY]
        aliases = {len(operands) + 2: 0, len(operands) + 3: 1}
        operands += [gain, gw, dproj, dfar]
    in_specs += [ANY]
    operands += [token]
    batches = -(-groups // BATCH)
    return pl.pallas_call(
        functools.partial(
            backward_kernel, first_group, groups, prior is not None, len(sizes), letter
        ),
        in_specs=in_specs,
        out_specs=[ANY, ANY, VMEM, VMEM] + [ANY] * len(sizes),
        out_shape=[
            jax.ShapeDtypeStruct((rows, 3 * width), BF16),
            jax.ShapeDtypeStruct((rows, 2 * width), BF16),
            jax.ShapeDtypeStruct((groups, GROUP // UNIT, 128), F32),
            jax.ShapeDtypeStruct((1, width), F32),
        ]
        + [jax.ShapeDtypeStruct((n, width), BF16) for n in sizes],
        scratch_shapes=[
            pltpu.VMEM((count, 3 * width), BF16),
            pltpu.VMEM((count, width), BF16),
            pltpu.VMEM((count, 2 * width), BF16),
            pltpu.VMEM((count, width), BF16),
            pltpu.VMEM((groups,) + prob.shape[1:], BF16),
            pltpu.VMEM((count, 2 * GROUP), F32),
            pltpu.VMEM(w_qkv.shape, BF16),
            pltpu.VMEM((count, 3 * width), BF16),
            pltpu.VMEM((count, 2 * width), BF16),
        ]
        + [pltpu.VMEM((n, width), BF16) for n in sizes]
        + [pltpu.SemaphoreType.DMA((7 * batches + 2 + len(sizes),))],
        input_output_aliases=aliases,
        compiler_params=pltpu.CompilerParams(vmem_limit_bytes=VMEM_LIMIT),
        cost_estimate=cost(0.4e9 * groups, 1e6 * groups),
        name="backward",
    )(*operands)


def qkv_kernel(
    extra, core_ref, x_hbm, farx_hbm, dproj_hbm, dfar_hbm, gain1_ref, wqkv_hbm, gains_ref, token_ref,
    gn_hbm, keep_ref, give_ref, x_ref, farx_ref, dproj_ref, dfar_ref, wqkv_ref, gn_ref, near_t, far_t, sems,
):
    move = Mover(sems)
    rows, width = x_ref.shape
    wide = wqkv_ref.shape[1]
    size = min(512, rows)
    got_w = move.start(wqkv_hbm, wqkv_ref)
    loads = []
    for low in range(0, rows, size):
        at = pl.ds(low, size)
        loads.append(
            [
                move.start(hbm.at[at], ref.at[at])
                for hbm, ref in (
                    (x_hbm, x_ref),
                    (dproj_hbm, dproj_ref),
                    (farx_hbm, farx_ref),
                    (dfar_hbm, dfar_ref),
                )
            ]
        )
    got_w.wait()
    gain = jnp.zeros((1, width), F32)
    for low, copies in zip(range(0, rows, size), loads):
        at = slice(low, low + size)
        for copy in copies:
            copy.wait()
        x = x_ref[at, :].astype(F32)
        scaled = x * inverse_norm(x)
        near_t[:, at] = (scaled * gain1_ref[...]).astype(BF16).T
        far = farx_ref[at, :].astype(F32)
        far_t[:, at] = (far * inverse_norm(far) * gain1_ref[...]).astype(BF16).T
        grad = dot(dproj_ref[at, :], wqkv_ref[...], NT)
        gn_ref[at, :] = grad.astype(BF16)
        move.store(gn_ref.at[pl.ds(low, size)], gn_hbm.at[pl.ds(low, size)])
        gain = gain + jnp.sum(grad * scaled, axis=0, keepdims=True)
    grads = []
    for c in range(0, wide, width):
        value = dot(near_t[...], dproj_ref[:, c : c + width])
        if c:
            value = value + dot(far_t[...], dfar_ref[:, c - width : c])
        grads.append(value)

    line = lax.broadcasted_iota(jnp.int32, (extra, width), 0)
    small = jnp.where(line == 0, gain + gains_ref[0:1, :], 0.0)
    small = jnp.where(line == 1, gains_ref[1:2, :], small)
    total = wide + extra
    half = total // 2

    def write(ref, which):
        at = which * half
        while at < (which + 1) * half:
            block, line = divmod(at, width)
            if at >= wide:
                count = extra
                value = small
            else:
                count = min(width - line, (which + 1) * half - at)
                value = grads[block][line : line + count]
            ref[at - which * half : at - which * half + count, :] = value.astype(BF16)
            at += count

    @pl.when(core_ref[0] == 0)
    def _():
        write(keep_ref, 0)
        write(give_ref, 1)

    @pl.when(core_ref[0] == 1)
    def _():
        write(keep_ref, 1)
        write(give_ref, 0)

    move.finish()


def qkv_grads(core, x, farx, dproj, dfar, gain1, w_qkv, gains, extra, token):
    rows, width = x.shape
    wide = w_qkv.shape[1]
    half = (wide + extra) // 2
    tall = lambda size: pltpu.VMEM((rows, size), BF16)
    return pl.pallas_call(
        functools.partial(qkv_kernel, extra),
        in_specs=[SMEM] + [ANY] * 4 + [VMEM, ANY, VMEM, ANY],
        out_specs=[ANY, VMEM, VMEM],
        out_shape=[
            jax.ShapeDtypeStruct((rows, width), BF16),
            jax.ShapeDtypeStruct((half, width), BF16),
            jax.ShapeDtypeStruct((half, width), BF16),
        ],
        scratch_shapes=[
            tall(width),
            tall(width),
            tall(wide),
            tall(2 * width),
            pltpu.VMEM(w_qkv.shape, BF16),
            tall(width),
            pltpu.VMEM((width, rows), BF16),
            pltpu.VMEM((width, rows), BF16),
            pltpu.SemaphoreType.DMA((5 * (rows // min(512, rows)) + 1,)),
        ],
        compiler_params=limit(62),
        cost_estimate=cost(10e9, 25e6),
        name="qkv_grads",
    )(core, x, farx, dproj, dfar, gain1, w_qkv, gains, token)


def row_gradient(f, x):
    r1 = inverse_norm(x)
    scaled = x * r1
    return r1 * (f - scaled * jnp.mean(f * scaled, axis=-1, keepdims=True))


def base_kernel(x_ref, gmid_ref, gn_ref, gs_ref, gain1_ref, out_ref):
    rows, width = x_ref.shape
    spread = jnp.broadcast_to(gs_ref[...][:, None, :], (rows // UNIT, UNIT, width))
    f = (gn_ref[...].astype(F32) + spread.reshape(rows, width)) * gain1_ref[...]
    grad = gmid_ref[...].astype(F32) + row_gradient(f, x_ref[...].astype(F32))
    out_ref[...] = grad.astype(BF16)


def base_rows(x, gmid, gn, gs, gain1):
    rows, width = x.shape
    return pl.pallas_call(
        base_kernel,
        grid=(rows // TILE,),
        in_specs=[
            rows_of(TILE, width),
            rows_of(TILE, width),
            rows_of(TILE, width),
            rows_of(TILE // UNIT, width),
            whole((1, width)),
        ],
        out_specs=rows_of(TILE, width),
        out_shape=jax.ShapeDtypeStruct((rows, width), BF16),
        compiler_params=params(),
        cost_estimate=cost(rows * width * 20, rows * width * 8),
        name="base",
    )(x, gmid, gn, gs, gain1)


def last_kernel(sizes, extra, capacity, table_ref, place_ref, *refs):
    ret_refs = refs[: len(sizes)]
    x_ref, base_ref, gain1_ref, outa_ref, outb_ref, acc = refs[len(sizes) :]
    rows_a = outa_ref.shape[0]
    acc[...] = jnp.zeros_like(acc)

    begin = 0
    for index, (size, ret_ref) in enumerate(zip(sizes, ret_refs)):
        height = size * UNIT + (extra if index == len(sizes) - 1 else 0)

        def add(r, carry, size=size, ret_ref=ret_ref, begin=begin, height=height):
            for slot in range(size):
                unit = table_ref[r * capacity + begin + slot]

                @pl.when(unit >= 0)
                def _():
                    at = pl.ds(pl.multiple_of(unit * UNIT, UNIT), UNIT)
                    src = pl.ds(pl.multiple_of(r * height + slot * UNIT, 16), UNIT)
                    acc[at, :] += ret_ref[src, :].astype(F32)

            return carry

        lax.fori_loop(0, ret_ref.shape[0] // height, add, 0)
        begin += size

    def finish(out_ref, first):
        def body(u, carry):
            at = pl.ds(pl.multiple_of(place_ref[first + u] * UNIT, UNIT), UNIT)
            own = pl.ds(pl.multiple_of((first + u) * UNIT, UNIT), UNIT)
            f = acc[own, :] * gain1_ref[...]
            grad = base_ref[at, :].astype(F32) + row_gradient(f, x_ref[own, :].astype(F32))
            out_ref[pl.ds(pl.multiple_of(u * UNIT, UNIT), UNIT), :] = grad.astype(BF16)
            return carry

        lax.fori_loop(0, out_ref.shape[0] // UNIT, body, 0, unroll=2)

    finish(outa_ref, 0)
    finish(outb_ref, rows_a // UNIT)


def last(table, place, ret, sizes, extra, capacity, x, base, gain1, rows_a):
    rows, width = x.shape
    return pl.pallas_call(
        functools.partial(last_kernel, sizes, extra, capacity),
        in_specs=[SMEM, SMEM] + [VMEM] * (len(ret) + 3),
        out_specs=[VMEM, VMEM],
        out_shape=[
            jax.ShapeDtypeStruct((rows_a, width), BF16),
            jax.ShapeDtypeStruct((rows - rows_a, width), BF16),
        ],
        scratch_shapes=[pltpu.VMEM((rows, width), F32)],
        compiler_params=limit(24),
        cost_estimate=cost(rows * width * 20, rows * width * 12),
        name="last",
    )(table, place, *ret, x, base, gain1)


def bits_of(size):
    count = 0
    while (1 << count) < size:
        count += 1
    return count


def bit_of(axis, bit):
    return (lax.axis_index(axis) >> bit) & 1


def swap(values, axis, bit):
    size = lax.axis_size(axis)
    return lax.ppermute(values, axis, [(i, i ^ (1 << bit)) for i in range(size)])


def halve(values, axis, bit):
    half = values.shape[0] // 2
    mine = bit_of(axis, bit)
    keep = lax.dynamic_slice_in_dim(values, mine * half, half, 0)
    give = lax.dynamic_slice_in_dim(values, (1 - mine) * half, half, 0)
    return keep, give


def double(values, axis, bit):
    got = swap(values, axis, bit)
    return jnp.where(
        bit_of(axis, bit) == 0,
        jnp.concatenate([values, got], axis=0),
        jnp.concatenate([got, values], axis=0),
    )


def add(one, two):
    return (one.astype(F32) + two.astype(F32)).astype(BF16)


def reduce_any(values, order):
    for axis, bit in order:
        keep, give = halve(values, axis, bit)
        values = add(keep, swap(give, axis, bit))
    for axis, bit in reversed(order):
        values = double(values, axis, bit)
    return values


def tie(values, *tokens):
    return pl.pallas_call(
        lambda *refs: None,
        in_specs=[ANY] * (1 + len(tokens)),
        out_specs=ANY,
        out_shape=jax.ShapeDtypeStruct(values.shape, values.dtype),
        input_output_aliases={0: 0},
        name="tie",
    )(values, *tokens)


def fetch(sources, targets, sems):
    copies = [
        pltpu.make_async_copy(source, target, sems.at[i])
        for i, (source, target) in enumerate(zip(sources, targets))
    ]
    for copy in copies:
        copy.start()
    for copy in copies:
        copy.wait()


def halve_kernel(ranges, sources, bits_ref, *refs):
    count = 2 * (1 + max(r[4] for r in ranges))
    sems = refs[-1]
    outs = refs[2 * sources + 1 : 2 * sources + 1 + count]
    held = refs[2 * sources + 1 + count : -2]
    made = held[2 * sources :]
    fetch(refs[: 2 * sources], held, refs[-2])
    refs = held
    for source, first, count, bit, out, there in ranges:
        own, came = refs[2 * source], refs[2 * source + 1]
        half = count // 2
        keep = pl.multiple_of(first + bits_ref[bit] * half, 16)
        give = pl.multiple_of(first + (1 - bits_ref[bit]) * half, 16)
        for ref, line in ((made[2 * out], keep), (made[2 * out + 1], give)):
            rows = pl.ds(line, half)
            total = own[rows, :].astype(F32) + came[rows, :].astype(F32)
            ref[there : there + half, :] = total.astype(BF16)
    fetch(made, outs, sems)


def halve_step(ranges, bits, pairs, token):
    width = pairs[0][0].shape[1]
    count = 1 + max(r[4] for r in ranges)
    heights = [max(r[5] + r[2] // 2 for r in ranges if r[4] == out) for out in range(count)]
    shapes = [jax.ShapeDtypeStruct((n, width), BF16) for n in heights for _ in range(2)]
    flat = [v for pair in pairs for v in pair]
    out = pl.pallas_call(
        functools.partial(halve_kernel, ranges, len(pairs)),
        in_specs=[SMEM] + [HBM] * len(flat) + [ANY],
        out_specs=[HBM] * len(shapes),
        out_shape=shapes,
        scratch_shapes=[pltpu.VMEM(v.shape, BF16) for v in flat + shapes]
        + [pltpu.SemaphoreType.DMA((len(flat),)), pltpu.SemaphoreType.DMA((len(shapes),))],
        compiler_params=limit(62),
        cost_estimate=cost(0, 8 * sum(heights) * width),
        name="halve_step",
    )(jnp.stack([bit_of(*b) for b in bits]).astype(jnp.int32), *flat, token)
    return [(out[2 * i], out[2 * i + 1]) for i in range(count)]


def double_kernel(ranges, sources, tokens, bits_ref, *refs):
    count = 1 + max(r[0] for r in ranges)
    outs = refs[2 * sources + tokens : 2 * sources + tokens + count]
    held = refs[2 * sources + tokens + count : -1]
    fetch(refs[: 2 * sources], held, refs[-1])
    refs = held
    for source, first, count, bit, out, there in ranges:
        own, came = refs[2 * out], refs[2 * out + 1]
        half = count // 2
        keep = pl.multiple_of(first + bits_ref[bit] * half, 16)
        give = pl.multiple_of(first + (1 - bits_ref[bit]) * half, 16)
        outs[source][pl.ds(keep, half), :] = own[there : there + half, :]
        outs[source][pl.ds(give, half), :] = came[there : there + half, :]


def double_step(ranges, bits, pairs, *tokens):
    width = pairs[0][0].shape[1]
    count = 1 + max(r[0] for r in ranges)
    heights = [max(r[1] + r[2] for r in ranges if r[0] == source) for source in range(count)]
    flat = [v for pair in pairs for v in pair]
    return pl.pallas_call(
        functools.partial(double_kernel, ranges, len(pairs), len(tokens)),
        in_specs=[SMEM] + [ANY] * len(flat) + [ANY] * len(tokens),
        out_specs=[VMEM] * count,
        out_shape=[jax.ShapeDtypeStruct((n, width), BF16) for n in heights],
        scratch_shapes=[pltpu.VMEM(v.shape, BF16) for v in flat]
        + [pltpu.SemaphoreType.DMA((len(flat),))],
        compiler_params=limit(24),
        cost_estimate=cost(0, 4 * sum(heights) * width),
        name="double_step",
    )(jnp.stack([bit_of(*b) for b in bits]).astype(jnp.int32), *flat, *tokens)


AXIS_X, AXIS_Y, AXIS_Z0, AXIS_Z1 = ("dp", 1), ("blk", 0), ("blk", 1), ("blk", 2)


def places(half, width, ff):
    up, down, out, qkv, gains = range(5)
    edge = ff // 2
    result = [
        (c, width, up, 0, half * edge + c) for c in range(0, edge, width)
    ]
    result.append((edge, width // 2, out, half * (width // 2), 0))
    result += [
        (edge + width // 2 + c, width, down, half * edge + c, 0) for c in range(0, edge, width)
    ]
    start = edge + width // 2 + edge
    total = 3 * width + EXTRA
    at = half * total // 2
    while at < (half + 1) * total // 2:
        block, line = divmod(at, width)
        if at >= 3 * width:
            result.append((start + at - half * total // 2, 16, gains, 0, 0))
            break
        count = min(width - line, (half + 1) * total // 2 - at)
        result.append((start + at - half * total // 2, count, qkv, line, block * width))
        at += count
    return result


def assemble_kernel(which, prior, width, ff, core_ref, values_ref, *refs):
    outs = refs[5 if prior else 0 :][:5]
    held, sems = refs[-2:]

    def write(half):
        copies = []
        for i, (first, count, out, line, column) in enumerate(places(half, width, ff)):
            held[first : first + count, :] = values_ref[first : first + count, :].astype(F32)
            copy = pltpu.make_async_copy(
                held.at[pl.ds(first, count)],
                outs[out].at[pl.ds(line, count), pl.ds(column, width)],
                sems.at[i],
            )
            copy.start()
            copies.append(copy)
        for copy in copies:
            copy.wait()

    @pl.when(core_ref[0] == which)
    def _():
        write(0)

    @pl.when(core_ref[0] != which)
    def _():
        write(1)


def assemble(core, which, values, width, ff, prior):
    shapes = [(width, ff), (ff, width), (width, width), (width, 3 * width), (16, width)]
    operands = [core, values] + (list(prior) if prior is not None else [])
    most = max(len(places(half, width, ff)) for half in (0, 1))
    return pl.pallas_call(
        functools.partial(assemble_kernel, which, prior is not None, width, ff),
        in_specs=[SMEM, VMEM] + [ANY] * (len(operands) - 2),
        out_specs=[ANY] * 5,
        out_shape=[jax.ShapeDtypeStruct(shape, F32) for shape in shapes],
        scratch_shapes=[pltpu.VMEM(values.shape, F32), pltpu.SemaphoreType.DMA((most,))],
        input_output_aliases={} if prior is None else {2 + i: i for i in range(5)},
        compiler_params=limit(16),
        cost_estimate=cost(0, values.size * 6),
        name="assemble",
    )(*operands)


def exchange(values, devices):
    shape = values.shape
    parts = values.reshape(devices, shape[0] // devices, *shape[1:])
    return lax.all_to_all(parts, "blk", split_axis=0, concat_axis=0, tiled=True).reshape(shape)


def per_device(
    x_a, x_b, sel_a, sel_b, gain_one, w_qkv, w_out, w_sort, gain_two, w_up, w_down, cot_a, cot_b
):
    devices = lax.axis_size("blk")
    me = lax.axis_index("blk")
    seqs_a, rows_a, width = x_a.shape
    seqs_b, rows_b, _ = x_b.shape
    npl = sel_a.shape[1]
    blocks = npl * devices
    len_a = rows_a // npl
    len_b = rows_b // npl
    total_a = seqs_a * rows_a
    total_b = seqs_b * rows_b
    rows = total_a + total_b
    units = rows // UNIT
    units_a = total_a // UNIT
    count_a = seqs_a * npl
    count_b = seqs_b * npl
    picks = count_a + count_b
    picks_up = -(-picks // 16) * 16
    groups = rows // GROUP
    per = TILE // GROUP
    capacity = 2 * max(1, (4 * units + 5 * devices - 1) // (5 * devices))
    send_rows = devices * capacity * UNIT
    ff = w_up.shape[1]
    gain1 = gain_one.astype(F32).reshape(1, width)
    gain2 = gain_two.astype(F32).reshape(1, width)

    first, early = capacity, groups
    if capacity > 8:
        full, left = divmod(units, capacity)
        sure = (full * 8 + min(left, 8)) // 2 // per * per
        if capacity == 14 and 0 < sure < groups:
            first, early = 8, sure

    sizes = [8, 7] if early < groups else [capacity]
    extra = 16
    average = np.zeros((picks, units), np.float32)
    for j in range(count_a):
        average[j, 2 * j : 2 * j + 2] = 1.0 / len_a
    for j in range(count_b):
        average[count_a + j, units_a + j] = 1.0 / len_b
    settings = (npl, seqs_a, seqs_b, devices, capacity, first, early, sizes, extra, picks_up)
    w_sort_t = w_sort.T
    x, means, news, far_rows, ret_rows, perm, place, kinds = digest(
        x_a.reshape(-1, width), x_b.reshape(-1, width), sel_a, sel_b, gain1, average, w_sort_t, settings
    )
    news = lax.all_to_all(news, "blk", split_axis=0, concat_axis=0, tiled=True)
    table = news[:, picks, :capacity].astype(jnp.int32).reshape(-1)
    back_table = news[:, picks, capacity : capacity + sum(sizes)].astype(jnp.int32).reshape(-1)
    news = news[:, :picks]
    parcels = pack(table, x, devices, capacity, first, picks_up)
    recv = [exchange(parcels[0], devices)]
    summary = means * gain1
    rs = inverse_norm(summary)
    unit_summary = (summary * rs).astype(BF16)
    all_summaries = jnp.broadcast_to(
        jnp.pad(unit_summary, ((0, picks_up - picks), (0, 0))), (devices, picks_up, width)
    )

    xp, cot = arrange(perm, x, cot_a.reshape(-1, width), cot_b.reshape(-1, width))
    proj = project(xp, gain1, w_qkv)

    def by_sequence(values):
        tail = values.shape[2:]
        one = values[:, :count_a].reshape((devices, seqs_a, npl) + tail)
        two = values[:, count_a:].reshape((devices, seqs_b, npl) + tail)
        both = jnp.concatenate([one, two], axis=1)
        return jnp.swapaxes(both, 0, 1).reshape((seqs_a + seqs_b, blocks) + tail)

    def own_rows(values):
        return lax.dynamic_slice_in_dim(values, me * npl, npl, 1).reshape((-1,) + values.shape[2:])

    def to_units(values):
        return jnp.concatenate(
            [jnp.repeat(values[:count_a], len_a // UNIT, axis=0), values[count_a:]], axis=0
        )

    news = by_sequence(news)
    logits = news[..., :blocks]
    picked = (news[..., blocks : blocks + 1] == jnp.arange(blocks, dtype=F32)).astype(F32)
    weights = jnp.take(to_units(own_rows(sinkhorn(logits, picked))), perm, axis=0)
    lane = jnp.arange(2 * GROUP) >= GROUP
    wrow = jnp.where(lane[None, :], jnp.repeat(weights, UNIT, axis=0), 1.0)
    if len(parcels) > 1:
        tall = (capacity - first) * UNIT
        parcel = lax.dynamic_update_slice(
            parcels[1].reshape(devices, -1, width), all_summaries, (0, tall, 0)
        )
        recv.append(exchange(tie(parcel.reshape(-1, width), wrow, proj), devices))
        units_all = recv[1].reshape(devices, -1, width)[:, tall:]
    else:
        units_all = exchange(all_summaries.reshape(-1, width), devices)
        units_all = units_all.reshape(devices, picks_up, width)
    units_all = by_sequence(units_all[:, :picks])
    block_of = np.arange(GROUP) // len_b
    cross = block_of[:, None] != block_of[None, :]
    mask = np.zeros((2, GROUP, 2 * GROUP), np.float32)
    mask[1] = np.where(np.concatenate([cross, cross], axis=1), -1e30, 0.0)

    core = bit_of("dp", 0).astype(jnp.int32).reshape(1)
    shared = (xp, cot, proj, wrow, mask, gain1, gain2, w_qkv, w_out, w_up, w_down)
    heights = [
        devices * (n * UNIT + (extra if i == len(sizes) - 1 else 0))
        for i, n in enumerate(sizes)
    ]

    letter = (count_a, count_b, devices, extra)

    def run_backward(streams, *rest):
        _, _, gatt, prob, farx, farkv = streams
        return backward(ret_rows, place, proj, farx, farkv, gatt, prob, wrow, w_qkv, *rest)

    fast = lax.axis_size("dp") == 4 and devices == 8 and early < groups
    part_x = ff // 2 + width // 2
    if early < groups:
        prior = forward(far_rows, kinds, core, recv[:1], *shared, 0, early, None, False, wrow)
        dproj, dfar, gw_one, gain, *ret = run_backward(
            prior[0], heights[:1], 0, early, None, None, prior[0][0]
        )
        back = [exchange(v, devices) for v in ret]
        streams, sums = forward(
            far_rows, kinds, core, recv, *shared, early, groups - early, prior, True, gain
        )
        keep, give, g_gain2 = sums
        out_a, out_b = restore(perm, streams[0], total_a)
        big_came = swap(give, "dp", 0)
        token = keep
        if fast:
            ranges_one = [(0, 0, part_x, 0, 0, 0), (0, part_x, keep.shape[0] - part_x, 1, 1, 0)]
            (bx, gx), (by, gy) = halve_step(
                ranges_one, [AXIS_X, AXIS_Y], [(keep, big_came)], out_a
            )
            bx_came, by_came = swap(gx, *AXIS_X), swap(gy, *AXIS_Y)
            token = bx
        dproj, dfar, _, g_gain1_far, *ret = run_backward(
            streams, heights[1:], early, groups - early, (dproj, dfar, gw_one, gain), letter, token
        )
    else:
        streams, sums = forward(far_rows, kinds, core, recv, *shared, 0, groups, None, True, wrow)
        keep, give, g_gain2 = sums
        out_a, out_b = restore(perm, streams[0], total_a)
        big_came = swap(give, "dp", 0)
        back = []
        dproj, dfar, _, g_gain1_far, *ret = run_backward(
            streams, heights, 0, groups, None, letter, keep
        )
    _, gmid, _, _, farx, _ = streams

    parcel = tie(ret[0], bx_came, by_came, back[0]) if fast else ret[0]
    tall = sizes[-1] * UNIT
    arrived = exchange(parcel, devices)
    back.append(arrived)
    gains = jnp.concatenate([g_gain1_far, g_gain2], axis=0)
    token = dproj
    gn, late_keep, late_give = qkv_grads(
        core, xp, farx, dproj, dfar, gain1, w_qkv, gains, EXTRA, token
    )
    late_came = swap(late_give, "dp", 0)
    part_late = 384
    if fast:
        late_rows = late_keep.shape[0]
        ranges_late = [(0, 0, part_late, 0, 0, 0), (0, part_late, late_rows - part_late, 1, 1, 0)]
        (lx, gx), (ly, gy) = halve_step(
            ranges_late, [AXIS_X, AXIS_Y], [(late_keep, late_came)], late_came
        )
        lx_came, ly_came = swap(gx, *AXIS_X), swap(gy, *AXIS_Y)
        nbx, nlx, nby, nly = (v.shape[0] for v in (bx, lx, by, ly))
        ranges_two = [
            (0, 0, nbx, 0, 0, 0),
            (1, 0, nlx, 0, 0, nbx // 2),
            (2, 0, nby, 1, 1, 0),
            (3, 0, nly, 1, 1, nby // 2),
        ]
        (vx, gx), (vy, gy) = halve_step(
            ranges_two,
            [AXIS_Y, AXIS_X],
            [(bx, bx_came), (lx, lx_came), (by, by_came), (ly, ly_came)],
            lx,
        )
        vx_came, vy_came = swap(gx, *AXIS_Y), swap(gy, *AXIS_X)
    small, spread = sort_back(
        me.reshape(1), perm, logits, picked, units_all.reshape(-1, width), w_sort_t, gain1, means,
        arrived, npl, seqs_a, (len_a, len_b), tall, extra, vx if fast else arrived,
    )
    if fast:
        cuts = [nbx // 2, nlx // 2, nby // 2, nly // 2]
        ranges_three = [
            (0, 0, cuts[0], 0, 0, 0),
            (0, cuts[0], cuts[1], 0, 0, cuts[0] // 2),
            (1, 0, cuts[2], 0, 0, (cuts[0] + cuts[1]) // 2),
            (1, cuts[2], cuts[3], 0, 0, (cuts[0] + cuts[1] + cuts[2]) // 2),
        ]
        ((total, gz),) = halve_step(
            ranges_three, [AXIS_Z0], [(vx, vx_came), (vy, vy_came)], spread
        )
    base = base_rows(xp, gmid, gn, spread, gain1)
    if fast:
        total = add(total, tie(swap(gz, *AXIS_Z0), base))

    gx_a, gx_b = last(back_table, place, back, sizes, extra, sum(sizes), x, base, gain1, total_a)
    if fast:
        for bit in (0, 1):
            small = small + swap(small, "dp", bit)
        total = add(total, tie(swap(total, *AXIS_Z1), gx_a, small))
        vx, vy = double_step(ranges_three, [AXIS_Z0], [(total, swap(total, *AXIS_Z0))])
        ranges_back = [
            (0, 0, nbx, 0, 0, 0),
            (0, nbx, nlx, 0, 0, cuts[0]),
            (1, 0, nby, 1, 1, 0),
            (1, nby, nly, 1, 1, cuts[2]),
        ]
        vx, vy = double_step(
            ranges_back,
            [AXIS_Y, AXIS_X],
            [(vx, swap(vx, *AXIS_Y)), (vy, swap(vy, *AXIS_X))],
        )
        big_rows = keep.shape[0]
        ranges_all = [
            (0, 0, part_x, 0, 0, 0),
            (0, big_rows, part_late, 0, 0, nbx),
            (0, part_x, big_rows - part_x, 1, 1, 0),
            (0, big_rows + part_late, late_rows - part_late, 1, 1, nby),
        ]
        (sums_own,) = double_step(
            ranges_all,
            [AXIS_X, AXIS_Y],
            [(vx, swap(vx, *AXIS_X)), (vy, swap(vy, *AXIS_Y))],
        )
    else:
        across = [("dp", bit) for bit in range(1, bits_of(lax.axis_size("dp")))]
        along = [("blk", bit) for bit in range(bits_of(devices))]
        sums_own = jnp.concatenate(
            [
                reduce_any(add(keep, big_came), across + along),
                reduce_any(add(late_keep, late_came), along + across),
            ],
            axis=0,
        )
    sums_came = swap(sums_own, "dp", 0)

    if not fast:
        small = lax.psum(small, "dp")
    written = assemble(core, 0, sums_own, width, ff, None)
    sum_up, sum_down, sum_out, sum_qkv, gains = assemble(core, 1, sums_came, width, ff, written)

    return (
        out_a.reshape(x_a.shape),
        out_b.reshape(x_b.shape),
        gx_a.reshape(x_a.shape),
        gx_b.reshape(x_b.shape),
        gains[0] + small[blocks],
        sum_qkv,
        sum_out,
        small[:blocks].T,
        gains[1],
        sum_up,
        sum_down,
    )


def solution(mesh):
    rows_spec = P("dp", "blk", None)
    in_specs = (
        (rows_spec, rows_spec, P("dp", "blk"), P("dp", "blk")) + (P(),) * 7 + (rows_spec, rows_spec)
    )
    out_specs = (rows_spec,) * 4 + (P(),) * 7
    return jax.shard_map(
        per_device, mesh=mesh, in_specs=in_specs, out_specs=out_specs, check_vma=False
    )
```

```python
import functools

import jax
import jax.numpy as jnp
import numpy as np
from jax import lax
from jax.experimental import pallas as pl
from jax.experimental.pallas import tpu as pltpu
from jax.sharding import PartitionSpec as P

HEADS = 8
SINK_ITERS = 8
EPSILON = 1e-05
SOFTMAX_HEAT = 0.75
UNIT = 32
GROUP = 64
TILE = 256
HALF = 256
PER_HALF = 4
VMEM_LIMIT = 62 * 1024 * 1024

F32 = jnp.float32
BF16 = jnp.bfloat16

NN = (((1,), (0,)), ((), ()))
NT = (((1,), (1,)), ((), ()))
TN = (((0,), (0,)), ((), ()))


def dot(a, b, dims=NN):
    return lax.dot_general(a, b, dims, preferred_element_type=F32)


def inverse_norm(values):
    return lax.rsqrt(jnp.mean(values * values, axis=-1, keepdims=True) + EPSILON)


def whole(shape):
    zeros = (0,) * len(shape)
    return pl.BlockSpec(shape, lambda *_: zeros, pipeline_mode=pl.Buffered(1))


def rows_of(tile, width):
    return pl.BlockSpec((tile, width), lambda i: (i, 0))


SMEM = pl.BlockSpec(memory_space=pltpu.SMEM)


def params():
    return pltpu.CompilerParams(
        dimension_semantics=("arbitrary",), vmem_limit_bytes=VMEM_LIMIT
    )


def cost(flops, nbytes):
    return pl.CostEstimate(flops=int(flops * 1e-3), bytes_accessed=int(nbytes * 1e-3), transcendentals=0)


ANY = pl.BlockSpec(memory_space=pl.ANY)
VMEM = pl.BlockSpec(memory_space=pltpu.VMEM)
HBM = pl.BlockSpec(memory_space=pltpu.HBM)


def limit(mib):
    return pltpu.CompilerParams(vmem_limit_bytes=mib * 1024 * 1024)


def request_kernel(
    npl, seqs_a, seqs_b, devices, capacity, first, early, sizes, extra, spare_rows,
    sela_ref, selb_ref, table_ref, back_ref, far_ref, ret_ref, perm_ref, place_ref, kinds_ref, fill, begin, used,
):
    count_a = seqs_a * npl
    count_b = seqs_b * npl
    units_a = 2 * count_a
    width = sum(sizes)
    shift = npl.bit_length() - 1 if npl & (npl - 1) == 0 else -1

    def choice(j):
        ref, at = (sela_ref, j) if j < count_a else (selb_ref, j - count_a)
        return ref[at // npl, at % npl]

    def split(chosen):
        if shift >= 0:
            return lax.shift_right_logical(chosen, shift), lax.bitwise_and(chosen, npl - 1)
        return lax.div(chosen, npl), lax.rem(chosen, npl)

    def clear(ref):
        def body(i, carry):
            ref[i] = -1
            return carry

        return body

    lax.fori_loop(0, devices * capacity, clear(table_ref), 0)
    lax.fori_loop(0, devices * width, clear(back_ref), 0)
    for s in range(devices):
        fill[s] = 0
        used[s] = 0
        used[devices + s] = 0
    one = lambda flag: jnp.where(flag, 1, 0)
    ready_a, ready_b, must_a, must_b = (jnp.int32(0) for _ in range(4))
    for j in range(count_a + count_b):
        source, inner = split(choice(j))
        slot = fill[source]
        begin[j] = slot
        size = 2 if j < count_a else 1
        fill[source] = slot + size
        if j < count_a:
            unit = inner * 2 + (j // npl) * npl * 2
            ready_a = ready_a + one(slot + 2 <= first)
            table_ref[source * capacity + slot + 1] = unit + 1
        else:
            unit = inner + (units_a + (j - count_a) // npl * npl)
            ready_b = ready_b + one(slot + 1 <= first)
        table_ref[source * capacity + slot] = unit

    two = early < count_a + count_b // 2

    def must(j):
        source, _ = split(choice(j))
        if not two:
            return begin[j] < 0
        return begin[j] < fill[source] - 6

    for j in range(count_a):
        must_a = must_a + one(must(j))
    for j in range(count_b):
        must_b = must_b + one(must(count_a + j))
    even = jnp.logical_or(lax.bitwise_and(must_b, 1) == 0, ready_b > must_b)
    pairs = lax.shift_right_logical(must_b + one(even), 1)
    take_a = jnp.minimum(ready_a, early - pairs)
    if not two:
        take_a = jnp.int32(count_a)
    take_b = 2 * (early - take_a)
    late_b = 2 * (early + count_a - take_a)
    kinds_ref[0] = take_a
    kinds_ref[1] = early + count_a - take_a
    second = devices * first * UNIT

    def ret_row(phase, source, slot):
        chunks = list(enumerate(sizes))
        if two:
            chunks = chunks[:1] if phase == 0 else chunks[1:]
        row = jnp.int32(0)
        begin_slot, begin_row = 0, 0
        for index, size in chunks:
            height = size * UNIT + (extra if index == len(sizes) - 1 else 0)
            here = begin_row + source * height + (slot - begin_slot) * UNIT
            row = jnp.where(slot >= begin_slot, here, row)
            begin_slot += size
            begin_row += devices * height
        return row

    def put(pos, unit, inner, source, slot, late):
        near = (source * first + slot) * UNIT
        rest = second + source * ((capacity - first) * UNIT + spare_rows) + (slot - first) * UNIT
        far_ref[pos] = jnp.where(slot < first, near, rest)
        at = late * devices + source
        back = used[at]
        used[at] = back + 1
        if two:
            ret_ref[pos] = jnp.where(late == 0, ret_row(0, source, back), ret_row(1, source, back))
            back_ref[source * width + back + late * sizes[0]] = inner
        else:
            ret_ref[pos] = ret_row(0, source, back)
            back_ref[source * width + back] = inner
        perm_ref[pos] = unit
        place_ref[unit] = pos

    spare = take_a - must_a
    taken, other, free = (jnp.int32(0) for _ in range(3))
    for j in range(count_a):
        source, inner = split(choice(j))
        slot = begin[j]
        need = must(j)
        pick = jnp.logical_and(jnp.logical_not(need), jnp.logical_and(slot + 2 <= first, free < spare))
        use = jnp.logical_or(need, pick)
        free = free + one(pick)
        pos = 2 * jnp.where(use, taken, early + other)
        inner = inner * 2 + (j // npl) * npl * 2
        put(pos, 2 * j, inner, source, slot, one(jnp.logical_not(use)))
        put(pos + 1, 2 * j + 1, inner + 1, source, slot + 1, one(jnp.logical_not(use)))
        taken = taken + one(use)
        other = other + one(jnp.logical_not(use))
    spare = take_b - must_b
    drop = one(spare < 0)
    taken, other, free = (jnp.int32(0) for _ in range(3))
    for j in range(count_b):
        source, inner = split(choice(count_a + j))
        slot = begin[count_a + j]
        need = must(count_a + j)
        skip = jnp.logical_and(need, drop > 0)
        drop = drop - one(skip)
        pick = jnp.logical_and(jnp.logical_not(need), jnp.logical_and(slot + 1 <= first, free < spare))
        use = jnp.logical_or(jnp.logical_and(need, jnp.logical_not(skip)), pick)
        free = free + one(pick)
        pos = jnp.where(use, 2 * take_a + taken, late_b + other)
        inner = inner + (units_a + (j // npl) * npl)
        put(pos, units_a + j, inner, source, slot, one(jnp.logical_not(use)))
        taken = taken + one(use)
        other = other + one(jnp.logical_not(use))


def digest_kernel(
    tiles_a, settings, sela_ref, selb_ref, xa_ref, xb_ref, gain_ref, avg_ref, wsort_ref,
    x_ref, means_ref, news_ref, far_ref, ret_ref, perm_ref, place_ref, kinds_ref,
    sums, table_ref, back_ref, fill, begin, used,
):
    step = pl.program_id(0)

    @pl.when(step == 0)
    def _():
        request_kernel(
            *settings, sela_ref, selb_ref, table_ref, back_ref, far_ref, ret_ref, perm_ref, place_ref,
            kinds_ref, fill, begin, used,
        )

    def take(src):
        x = src[...]
        x_ref[...] = x
        x = x.astype(F32)
        scaled = x * inverse_norm(x)
        units = x.shape[0] // UNIT
        at = pl.ds(pl.multiple_of(step * units, units), units)
        sums[at, :] = jnp.sum(scaled.reshape(units, UNIT, x.shape[1]), axis=1)

    pl.when(step < tiles_a)(lambda: take(xa_ref))
    pl.when(step >= tiles_a)(lambda: take(xb_ref))

    @pl.when(step == pl.num_programs(0) - 1)
    def _():
        means = lax.dot_general(
            avg_ref[...], sums[...], NN, precision=lax.Precision.HIGHEST, preferred_element_type=F32
        )
        means_ref[...] = means
        summary = means * gain_ref[...]
        unit = (summary * inverse_norm(summary)).astype(BF16)
        logits = dot(unit, wsort_ref[...], NT) * (1.0 / SOFTMAX_HEAT)
        picks, blocks = logits.shape
        devices, height, lanes = news_ref.shape
        line = lax.broadcasted_iota(jnp.int32, (picks, lanes - blocks), 0)
        lane = lax.broadcasted_iota(jnp.int32, (picks, lanes - blocks), 1)
        chosen = jnp.zeros((picks, lanes - blocks), jnp.int32)
        count_a = sela_ref.shape[0] * sela_ref.shape[1]
        for j in range(picks):
            ref, at = (sela_ref, j) if j < count_a else (selb_ref, j - count_a)
            npl = ref.shape[1]
            chosen = jnp.where(line == j, ref[at // npl, at % npl], chosen)
        chosen = jnp.where(lane == 0, chosen, 0).astype(F32)
        message = jnp.concatenate([logits, chosen], axis=1)
        lane = lax.broadcasted_iota(jnp.int32, (1, lanes), 1)
        wanted = table_ref.shape[0] // devices
        order = back_ref.shape[0] // devices
        rest = lax.broadcasted_iota(jnp.int32, (height - picks, lanes), 0)
        for d in range(devices):
            row = jnp.zeros((1, lanes), jnp.int32)
            for k in range(wanted):
                row = jnp.where(lane == k, table_ref[d * wanted + k], row)
            for k in range(order):
                row = jnp.where(lane == wanted + k, back_ref[d * order + k], row)
            news_ref[d, :picks, :] = message
            news_ref[d, picks:, :] = jnp.where(rest == 0, row.astype(F32), 0.0)


def digest(x_a, x_b, sel_a, sel_b, gain_row, average, w_sort_t, settings):
    npl, seqs_a, seqs_b, devices, capacity, _, _, sizes, _, _ = settings
    width = x_a.shape[1]
    tile = 2 * TILE if x_a.shape[0] % (2 * TILE) == 0 and x_b.shape[0] % (2 * TILE) == 0 else TILE
    tiles_a = x_a.shape[0] // tile
    tiles_b = x_b.shape[0] // tile
    rows = x_a.shape[0] + x_b.shape[0]
    picks = average.shape[0]
    height = -(-picks // 8) * 8 + 8
    units = rows // UNIT
    ints = lambda n: jax.ShapeDtypeStruct((n,), jnp.int32)
    return pl.pallas_call(
        functools.partial(digest_kernel, tiles_a, settings),
        grid=(tiles_a + tiles_b,),
        in_specs=[
            SMEM,
            SMEM,
            pl.BlockSpec((tile, width), lambda i: (jnp.minimum(i, tiles_a - 1), 0)),
            pl.BlockSpec((tile, width), lambda i: (jnp.maximum(i - tiles_a, 0), 0)),
            whole((1, width)),
            whole(average.shape),
            whole(w_sort_t.shape),
        ],
        out_specs=[rows_of(tile, width), whole((picks, width)), whole((devices, height, 128))]
        + [SMEM] * 5,
        out_shape=[
            jax.ShapeDtypeStruct((rows, width), BF16),
            jax.ShapeDtypeStruct((picks, width), F32),
            jax.ShapeDtypeStruct((devices, height, 128), F32),
        ]
        + [ints(n) for n in (units, units, units, units, 2)],
        scratch_shapes=[
            pltpu.VMEM((units, width), F32),
            pltpu.SMEM((devices * capacity,), jnp.int32),
            pltpu.SMEM((devices * sum(sizes),), jnp.int32),
            pltpu.SMEM((devices,), jnp.int32),
            pltpu.SMEM((picks,), jnp.int32),
            pltpu.SMEM((2 * devices,), jnp.int32),
        ],
        compiler_params=params(),
        cost_estimate=cost(rows * width * 10, rows * width * 4),
        name="digest",
    )(sel_a, sel_b, x_a, x_b, gain_row, average, w_sort_t)


def pack_kernel(devices, capacity, first, spare, table_ref, x_ref, *rest):
    outs = rest[: 1 if first == capacity else 2]
    held, sems = rest[len(outs) :]
    sizes = [first, capacity - first]
    copies = []
    for part, out_ref in enumerate(outs):
        size = sizes[part]
        base = part * devices * first
        for r in range(devices):
            for slot in range(size):
                unit = jnp.maximum(table_ref[r * capacity + part * first + slot], 0)
                src = pl.ds(pl.multiple_of(unit * UNIT, UNIT), UNIT)
                at = (base + r * size + slot) * UNIT
                held[at : at + UNIT, :] = x_ref[src, :]
            at = (base + r * size) * UNIT
            copy = pltpu.make_async_copy(
                held.at[pl.ds(at, size * UNIT)],
                out_ref.at[pl.ds(r * (size * UNIT + part * spare), size * UNIT)],
                sems.at[part * devices + r],
            )
            copy.start()
            copies.append(copy)
    for copy in copies:
        copy.wait()


def pack(table, x, devices, capacity, first, spare):
    width = x.shape[1]
    sizes = [first] if first == capacity else [first, capacity - first]
    return pl.pallas_call(
        functools.partial(pack_kernel, devices, capacity, first, spare),
        in_specs=[SMEM, VMEM],
        out_specs=[HBM] * len(sizes),
        out_shape=[
            jax.ShapeDtypeStruct((devices * (n * UNIT + i * spare), width), BF16)
            for i, n in enumerate(sizes)
        ],
        scratch_shapes=[
            pltpu.VMEM((devices * capacity * UNIT, width), BF16),
            pltpu.SemaphoreType.DMA((len(sizes) * devices,)),
        ],
        compiler_params=limit(62),
        cost_estimate=cost(0, x.size * 6),
        name="pack",
    )(table, x)


def arrange_kernel(units_a, perm_ref, x_ref, cota_ref, cotb_ref, xp_ref, cotp_ref):
    def body(pos, carry):
        unit = perm_ref[pos]
        at = pl.ds(pl.multiple_of(pos * UNIT, UNIT), UNIT)
        xp_ref[at, :] = x_ref[pl.ds(pl.multiple_of(unit * UNIT, UNIT), UNIT), :]

        @pl.when(unit < units_a)
        def _():
            cotp_ref[at, :] = cota_ref[pl.ds(pl.multiple_of(unit * UNIT, UNIT), UNIT), :]

        @pl.when(unit >= units_a)
        def _():
            src = pl.ds(pl.multiple_of((unit - units_a) * UNIT, UNIT), UNIT)
            cotp_ref[at, :] = cotb_ref[src, :]

        return carry

    lax.fori_loop(0, x_ref.shape[0] // UNIT, body, 0)


def arrange(perm, x, cot_a, cot_b):
    like = jax.ShapeDtypeStruct(x.shape, BF16)
    return pl.pallas_call(
        functools.partial(arrange_kernel, cot_a.shape[0] // UNIT),
        in_specs=[SMEM, VMEM, VMEM, VMEM],
        out_specs=[VMEM, VMEM],
        out_shape=[like, like],
        compiler_params=limit(16),
        cost_estimate=cost(0, x.size * 8),
        name="arrange",
    )(perm, x, cot_a, cot_b)


def restore_kernel(perm_ref, out_ref, outa_ref, outb_ref):
    units_a = outa_ref.shape[0] // UNIT

    def body(pos, carry):
        unit = perm_ref[pos]
        at = pl.ds(pl.multiple_of(pos * UNIT, UNIT), UNIT)

        @pl.when(unit < units_a)
        def _():
            outa_ref[pl.ds(pl.multiple_of(unit * UNIT, UNIT), UNIT), :] = out_ref[at, :]

        @pl.when(unit >= units_a)
        def _():
            dst = pl.ds(pl.multiple_of((unit - units_a) * UNIT, UNIT), UNIT)
            outb_ref[dst, :] = out_ref[at, :]

        return carry

    lax.fori_loop(0, out_ref.shape[0] // UNIT, body, 0)


def restore(perm, out, rows_a):
    rows, width = out.shape
    return pl.pallas_call(
        restore_kernel,
        in_specs=[SMEM, VMEM],
        out_specs=[VMEM, VMEM],
        out_shape=[
            jax.ShapeDtypeStruct((rows_a, width), BF16),
            jax.ShapeDtypeStruct((rows - rows_a, width), BF16),
        ],
        compiler_params=limit(16),
        cost_estimate=cost(0, out.size * 4),
        name="restore",
    )(perm, out)


def project_kernel(x_ref, gain_ref, w_ref, proj_ref):
    x = x_ref[...].astype(F32)
    proj_ref[...] = dot((x * inverse_norm(x) * gain_ref[...]).astype(BF16), w_ref[...]).astype(BF16)


def project(x, gain_row, w_qkv):
    rows, width = x.shape
    wide = w_qkv.shape[1]
    return pl.pallas_call(
        project_kernel,
        grid=(rows // TILE,),
        in_specs=[rows_of(TILE, width), whole((1, width)), whole((width, wide))],
        out_specs=rows_of(TILE, wide),
        out_shape=jax.ShapeDtypeStruct((rows, wide), BF16),
        compiler_params=params(),
        cost_estimate=cost(2 * rows * width * wide, rows * (width + wide) * 2),
        name="project",
    )(x, gain_row, w_qkv)


def log_sum(values, axis):
    top = jnp.max(values, axis=axis, keepdims=True)
    return top + jnp.log(jnp.sum(jnp.exp(values - top), axis=axis, keepdims=True))


def sinkhorn_kernel(logits_ref, picked_ref, weight_ref):
    state = logits_ref[...]
    for _ in range(SINK_ITERS):
        state = state - log_sum(state, 2)
        state = state - log_sum(state, 1)
    count = state.shape[1]
    weight = count * jnp.sum(jnp.exp(state) * picked_ref[...], axis=2, keepdims=True)
    weight_ref[...] = jnp.broadcast_to(weight, weight_ref.shape)


def sinkhorn(logits, picked):
    seqs, count, _ = logits.shape
    return pl.pallas_call(
        sinkhorn_kernel,
        out_shape=jax.ShapeDtypeStruct((seqs, count, 128), F32),
        cost_estimate=cost(logits.size * 100, logits.size * 32),
        name="sinkhorn",
    )(logits, picked)


def exact(a, b, dims=NN):
    return lax.dot_general(
        a, b, dims, precision=lax.Precision.HIGHEST, preferred_element_type=F32
    )


def sort_back_kernel(
    npl, seqs_a, lengths, tall, me_ref, perm_ref, logits_ref, picked_ref, units_ref, wsort_ref, gain_ref,
    means_ref, arrived, token_ref, small_ref, spread_ref, kept, letters, sems,
):
    seqs, blocks, _ = logits_ref.shape
    devices = blocks // npl
    picks = means_ref.shape[0]
    extra = letters.shape[1]
    height = arrived.shape[0] // devices
    copies = []
    for d in range(devices):
        source = arrived.at[pl.ds(d * height + tall, extra), pl.ds(0, 128)]
        copies.append(pltpu.make_async_copy(source, letters.at[d], sems.at[d]))
    for copy in copies:
        copy.start()
    state = logits_ref[...]
    for step in range(SINK_ITERS):
        state = state - log_sum(state, 2)
        kept[2 * step] = jnp.exp(state)
        state = state - log_sum(state, 1)
        kept[2 * step + 1] = jnp.exp(state)
    for copy in copies:
        copy.wait()
    rows = seqs * blocks
    line = lax.broadcasted_iota(jnp.int32, (rows, 128), 0)
    lane = lax.broadcasted_iota(jnp.int32, (rows, 128), 1)
    own_lane = line // blocks * npl + line % npl
    device = (line // npl) % devices
    table = jnp.zeros((rows, 128), F32)
    for d in range(devices):
        table = jnp.where(device == d, letters[d, 0:1, :].astype(F32), table)
    gw = jnp.sum(jnp.where(lane == own_lane, table, 0.0), axis=1, keepdims=True)
    grad = blocks * picked_ref[...] * gw.reshape(seqs, blocks, 1) * kept[2 * SINK_ITERS - 1]
    for step in reversed(range(SINK_ITERS)):
        grad = grad - kept[2 * step + 1] * jnp.sum(grad, axis=1, keepdims=True)
        grad = grad - kept[2 * step] * jnp.sum(grad, axis=2, keepdims=True)
    grad = (grad * (1.0 / SOFTMAX_HEAT)).reshape(rows, blocks)
    units = units_ref[...].astype(F32)
    small_ref[:blocks, :] = exact(grad, units, TN)
    g_unit = exact(grad, wsort_ref[...].astype(F32))
    both = g_unit * units
    both = both - units * units * jnp.mean(both, axis=-1, keepdims=True)
    row = jnp.sum(both, axis=0, keepdims=True) / gain_ref[...]
    first = lax.broadcasted_iota(jnp.int32, (small_ref.shape[0] - blocks, units.shape[1]), 0) == 0
    small_ref[blocks:, :] = jnp.where(first, row, 0.0)
    line = lax.broadcasted_iota(jnp.int32, (picks, rows), 0)
    lane = lax.broadcasted_iota(jnp.int32, (picks, rows), 1)
    mine = lane == line // npl * blocks + me_ref[0] * npl + line % npl
    g_own = exact(jnp.where(mine, 1.0, 0.0), g_unit)
    summary = means_ref[...] * gain_ref[...]
    rs = inverse_norm(summary)
    g_summary = rs * (
        g_own - summary * (rs * rs) * jnp.mean(g_own * summary, axis=-1, keepdims=True)
    )
    count_a = seqs_a * npl
    places = spread_ref.shape[0]
    line = lax.broadcasted_iota(jnp.int32, (places, picks), 0)
    lane = lax.broadcasted_iota(jnp.int32, (places, picks), 1)
    unit = jnp.zeros((places, picks), jnp.int32)
    for pos in range(places):
        unit = jnp.where(line == pos, perm_ref[pos], unit)
    block = jnp.where(unit < 2 * count_a, unit // 2, unit - count_a)
    share = jnp.where(lane < count_a, 1.0 / lengths[0], 1.0 / lengths[1])
    spread_ref[...] = exact(jnp.where(lane == block, share, 0.0), g_summary)


def sort_back(
    me, perm, logits, picked, units, w_sort_t, gain, means, arrived, npl, seqs_a, lengths, tall, extra, token
):
    seqs, blocks, _ = logits.shape
    width = means.shape[1]
    return pl.pallas_call(
        functools.partial(sort_back_kernel, npl, seqs_a, lengths, tall),
        in_specs=[SMEM, SMEM] + [VMEM] * 6 + [ANY, ANY],
        out_specs=[VMEM, VMEM],
        out_shape=[
            jax.ShapeDtypeStruct((blocks + 8, width), F32),
            jax.ShapeDtypeStruct((perm.shape[0], width), F32),
        ],
        scratch_shapes=[
            pltpu.VMEM((2 * SINK_ITERS,) + logits.shape, F32),
            pltpu.VMEM((blocks // npl, extra, 128), BF16),
            pltpu.SemaphoreType.DMA((blocks // npl,)),
        ],
        compiler_params=limit(24),
        cost_estimate=cost(logits.size * 200, logits.size * 32),
        name="sort_back",
    )(me, perm, logits, picked, units, w_sort_t, gain, means, arrived, token)


def head_masks(rows):
    lane = lax.broadcasted_iota(jnp.int32, (rows, HALF), 1) // (HALF // PER_HALF)
    return [lane == h for h in range(PER_HALF)]


def stack_heads(values, masks):
    zero = jnp.zeros_like(values)
    return jnp.concatenate([jnp.where(m, values, zero) for m in masks], axis=0)


def unstack_heads(values, masks):
    total = None
    for h, m in enumerate(masks):
        part = jnp.where(m, values[h * GROUP : (h + 1) * GROUP], 0.0)
        total = part if total is None else total + part
    return total


def repeat_heads(values):
    return jnp.concatenate([values] * PER_HALF, axis=0)


class Mover:
    def __init__(self, sems):
        self.sems, self.used, self.out = sems, 0, []

    def start(self, source, target):
        copy = pltpu.make_async_copy(source, target, self.sems.at[self.used])
        self.used += 1
        copy.start()
        return copy

    def store(self, source, target):
        self.out.append(self.start(source, target))

    def finish(self):
        for copy in self.out:
            copy.wait()


BATCH = 4


def forward_kernel(first_group, groups, recvs, prior, final, *refs):
    refs = list(refs)
    take = lambda n: [refs.pop(0) for _ in range(n)]
    far_ref, kinds_ref, core_ref = take(3)
    recv_hbm = take(recvs)
    x_hbm, cot_hbm, proj_hbm, wrow_hbm, mask_ref, gain1_ref, gain2_ref = take(7)
    wqkv_hbm, wout_hbm, wup_hbm, wdown_hbm, _ = take(5)
    prior_refs = take(2) if prior else []
    if prior:
        take(6)
    out_hbm, gmid_hbm, gatt_hbm, prob_hbm, farx_hbm, farkv_hbm = take(6)
    if final:
        keep_hbm, give_hbm = take(2)
    else:
        up_hbm, down_hbm = take(2)
    x_ref, cot_ref, proj_ref, wrow_ref, wqkv_ref, wout_ref, wup_ref, wdown_ref = take(8)
    out_ref, gmid_ref, gatt_ref, prob_ref, farx_ref, farkv_ref, attended = take(7)
    one_ref, two_ref = take(2)
    if prior:
        up_prior, down_prior = take(2)
    (sems,) = take(1)
    move = Mover(sems)
    rows = groups * GROUP
    width = x_ref.shape[1]
    ff = wup_ref.shape[1]
    base = first_group
    here = pl.ds(first_group * GROUP, rows)
    rows_one = recv_hbm[0].shape[0]
    far_sem = sems.at[sems.shape[0] - 1]
    for u in range(rows // UNIT):
        row = far_ref[2 * base + u]
        dst = farx_ref.at[pl.ds(u * UNIT, UNIT)]

        def bring(ref, row, dst=dst):
            src = ref.at[pl.ds(pl.multiple_of(row, 16), UNIT)]
            pltpu.make_async_copy(src, dst, far_sem).start()

        if recvs == 1:
            bring(recv_hbm[0], row)
        else:
            pl.when(row < rows_one)(lambda row=row, bring=bring: bring(recv_hbm[0], row))
            pl.when(row >= rows_one)(lambda row=row, bring=bring: bring(recv_hbm[1], row - rows_one))
    got_wqkv = move.start(wqkv_hbm, wqkv_ref)
    got_proj = move.start(proj_hbm.at[here], proj_ref)
    got_wrow = move.start(wrow_hbm.at[here], wrow_ref)
    got_x = move.start(x_hbm.at[here], x_ref)
    got_wout = move.start(wout_hbm, wout_ref)
    got_cot = move.start(cot_hbm.at[here], cot_ref)
    got_up = move.start(wup_hbm, wup_ref)
    got_down = move.start(wdown_hbm, wdown_ref)
    if prior:
        got_prior = [
            move.start(prior_refs[0], up_prior),
            move.start(prior_refs[1], down_prior),
        ]

    pltpu.make_async_copy(farx_ref, farx_ref, far_sem).wait()
    move.store(farx_ref, farx_hbm.at[here])
    far = farx_ref[...].astype(F32)
    far = (far * inverse_norm(far) * gain1_ref[...]).astype(BF16)
    got_wqkv.wait()
    farkv_ref[...] = dot(far, wqkv_ref[:, width:]).astype(BF16)
    move.store(farkv_ref, farkv_hbm.at[here])
    masks16 = head_masks(GROUP)
    head_scale = (width // HEADS) ** -0.5
    boundary = kinds_ref[1 if prior else 0]
    got_proj.wait()
    got_wrow.wait()
    for first in range(0, groups, BATCH):
        work = [
            (i, half) for i in range(first, min(first + BATCH, groups)) for half in range(width // HALF)
        ]
        scores, vals = [], []
        for i, half in work:
            at = slice(i * GROUP, (i + 1) * GROUP)
            lo = half * HALF
            q = proj_ref[at, lo : lo + HALF] * jnp.asarray(head_scale, BF16)
            keys = jnp.concatenate(
                [proj_ref[at, width + lo : width + lo + HALF], farkv_ref[at, lo : lo + HALF]], axis=0
            )
            vals.append(
                jnp.concatenate(
                    [
                        proj_ref[at, 2 * width + lo : 2 * width + lo + HALF],
                        farkv_ref[at, width + lo : width + lo + HALF],
                    ],
                    axis=0,
                )
            )
            which = jnp.where(base + i < boundary, 0, 1)
            scores.append(dot(stack_heads(q, masks16), keys, NT) + repeat_heads(mask_ref[which]))
        tops = [jnp.max(v, axis=1, keepdims=True) for v in scores]
        weights = [jnp.exp(v - t) for v, t in zip(scores, tops)]
        sums = [jnp.sum(v, axis=1, keepdims=True) for v in weights]
        probs = [v * (1.0 / t) for v, t in zip(weights, sums)]
        mixed = []
        for (i, half), prob, value in zip(work, probs, vals):
            at = slice(i * GROUP, (i + 1) * GROUP)
            prob_ref[i, half] = prob.astype(BF16)
            mixed.append(dot((prob * repeat_heads(wrow_ref[at, :])).astype(BF16), value))
        for (i, half), value in zip(work, mixed):
            at = slice(i * GROUP, (i + 1) * GROUP)
            lo = half * HALF
            attended[at, lo : lo + HALF] = unstack_heads(value, masks16).astype(BF16)
    move.store(prob_ref, prob_hbm.at[pl.ds(first_group, groups)])

    got_x.wait()
    got_wout.wait()
    att = attended[...]
    middle = x_ref[...].astype(F32) + dot(att, wout_ref[...])
    r2 = inverse_norm(middle)
    scaled = middle * r2
    second = (scaled * gain2_ref[...]).astype(BF16)
    got_cot.wait()
    cot = cot_ref[...]
    cot_t = cot.T
    second_t = second.T
    got_up.wait()
    got_down.wait()
    if prior:
        for copy in got_prior:
            copy.wait()

    def total(value, old, lanes):
        return value + old[:, lanes].astype(F32) if prior else value

    edge = ff // 2

    pending = []

    def send(ref, half, lines):
        sem = sems.at[move.used]
        move.used += 1
        for which, hbm in ((half, keep_hbm), (1 - half, give_hbm)):
            copy = pltpu.make_async_copy(ref.at[lines], hbm.at[lines], sem)
            pl.when(core_ref[0] == which)(copy.start)
        pending.append(copy)

    def put_up(c, value):
        lanes = slice(c, c + width)
        if not final:
            one_ref[:, lanes] = value.astype(BF16)
            at = (slice(None), pl.ds(c, width))
            move.store(one_ref.at[at], up_hbm.at[at])
            return
        ref, at = (one_ref, c) if c < edge else (two_ref, c - edge)
        ref[at : at + width, :] = total(value, up_prior if prior else None, lanes).astype(BF16)
        send(ref, 0 if c < edge else 1, pl.ds(at, width))

    def put_down(c, value):
        lanes = slice(c, c + width)
        if not final:
            two_ref[:, lanes] = value.astype(BF16)
            at = (slice(None), pl.ds(c, width))
            move.store(two_ref.at[at], down_hbm.at[at])
            return
        ref, at = (one_ref, c) if c < edge else (two_ref, c - edge)
        at += edge + width // 2
        ref[at : at + width, :] = total(value, down_prior if prior else None, lanes).T.astype(BF16)
        send(ref, 0 if c < edge else 1, pl.ds(at, width))

    def put_out(value):
        if not final:
            one_ref[:, ff:] = value.astype(BF16)
            at = (slice(None), pl.ds(ff, width))
            move.store(one_ref.at[at], up_hbm.at[at])
            return
        value = total(value, up_prior if prior else None, slice(ff, ff + width)).astype(BF16)
        lines = slice(edge, edge + width // 2)
        one_ref[lines, :] = value[: width // 2]
        two_ref[lines, :] = value[width // 2 :]
        send(one_ref, 0, pl.ds(edge, width // 2))
        send(two_ref, 1, pl.ds(edge, width // 2))

    result = middle
    back = jnp.zeros((rows, width), F32)
    c0 = 0.7978845608028654
    c1 = 0.044715
    for c in range(0, ff, width):
        hidden = dot(second, wup_ref[:, c : c + width])
        grad = dot(cot, wdown_ref[c : c + width, :], NT)
        square = hidden * hidden
        t = jnp.tanh(hidden * (c0 + (c0 * c1) * square))
        left = 0.5 + 0.5 * t
        active = (hidden * left).astype(BF16)
        slope = left + (0.5 * hidden) * (1.0 - t * t) * (c0 + (3.0 * c0 * c1) * square)
        grad = (grad * slope).astype(BF16)
        result = result + dot(active, wdown_ref[c : c + width, :])
        back = back + dot(grad, wup_ref[:, c : c + width], NT)
        put_down(c, dot(cot_t, active))
        put_up(c, dot(second_t, grad))
    out_ref[...] = result.astype(BF16)
    move.store(out_ref, out_hbm.at[here])
    e = back * gain2_ref[...]
    inner = jnp.mean(e * scaled, axis=-1, keepdims=True)
    grad_middle = cot.astype(F32) + r2 * (e - scaled * inner)
    branch = grad_middle.astype(BF16)
    gmid_ref[...] = branch
    move.store(gmid_ref, gmid_hbm.at[here])
    put_out(dot(att.T, branch))
    gatt_ref[...] = dot(branch, wout_ref[...], NT).astype(BF16)
    move.store(gatt_ref, gatt_hbm.at[here])
    for copy in pending:
        copy.wait()
    move.finish()


def forward(
    far_rows, kinds, core, recv, x, cot, proj, wrow, mask, gain1, gain2, w_qkv, w_out, w_up, w_down,
    first_group, groups, prior, final, token,
):
    rows, width = x.shape
    ff = w_up.shape[1]
    halves = width // HALF
    count = groups * GROUP
    like = lambda wide, kind=BF16: jax.ShapeDtypeStruct((rows, wide), kind)
    probs = jax.ShapeDtypeStruct((rows // GROUP, halves, PER_HALF * GROUP, 2 * GROUP), BF16)
    part = ff + width // 2
    if final:
        tails = [(part, width), (part, width)]
    else:
        tails = [(width, ff + width), (width, ff)]
    in_specs = [SMEM] * 3 + [ANY] * (len(recv) + 4) + [VMEM] * 3 + [ANY] * 5
    operands = [far_rows, kinds, core, *recv, x, cot, proj, wrow, mask, gain1, gain2]
    operands += [w_qkv, w_out, w_up, w_down, token]
    scratch = [
        pltpu.VMEM((count, width), BF16),
        pltpu.VMEM((count, width), BF16),
        pltpu.VMEM((count, 3 * width), BF16),
        pltpu.VMEM((count, 2 * GROUP), F32),
    ]
    scratch += [pltpu.VMEM(w.shape, BF16) for w in (w_qkv, w_out, w_up, w_down)]
    scratch += [pltpu.VMEM((count, width), BF16)] * 3
    scratch += [pltpu.VMEM((groups,) + probs.shape[1:], BF16)]
    scratch += [pltpu.VMEM((count, n * width), BF16) for n in (1, 2, 1)]
    scratch += [pltpu.VMEM(shape, BF16) for shape in tails]
    aliases = {}
    if prior is not None:
        streams, sums = prior
        in_specs += [ANY, ANY] + [ANY] * 6
        operands += list(sums)
        aliases = {len(operands) + i: i for i in range(6)}
        operands += list(streams)
        scratch += [pltpu.VMEM((width, ff + width), BF16), pltpu.VMEM((width, ff), BF16)]
    scratch += [pltpu.SemaphoreType.DMA((40,))]
    out = pl.pallas_call(
        functools.partial(
            forward_kernel, first_group, groups, len(recv), prior is not None, final
        ),
        in_specs=in_specs,
        out_specs=[ANY] * 8,
        out_shape=[like(width), like(width), like(width), probs, like(width), like(2 * width)]
        + [jax.ShapeDtypeStruct(shape, BF16) for shape in tails],
        scratch_shapes=scratch,
        input_output_aliases=aliases,
        compiler_params=pltpu.CompilerParams(vmem_limit_bytes=VMEM_LIMIT),
        cost_estimate=cost(1.0e9 * groups, 1e6 * groups),
        name="forward",
    )(*operands)
    return out[:6], out[6:]


def backward_kernel(first_group, groups, prior, chunks, letter, *refs):
    refs = list(refs)
    take = lambda n: [refs.pop(0) for _ in range(n)]
    ret_rows, place_ref = take(2)
    proj_hbm, farkv_hbm, gatt_hbm, prob_hbm, wrow_hbm, wqkv_hbm = take(6)
    if prior:
        (prior_gw,) = take(1)
        take(2)
    take(1)
    dproj_hbm, dfar_hbm, gw_ref = take(3)
    ret_hbm = take(chunks)
    proj_ref, farkv_ref, gatt_ref, prob_ref, wrow_ref, wqkv_ref = take(6)
    dproj_ref, dfar_ref = take(2)
    ret_refs = take(chunks)
    (sems,) = take(1)
    move = Mover(sems)
    rows = groups * GROUP
    width = gatt_ref.shape[1]
    start = first_group * GROUP
    batches = [(first, min(first + BATCH, groups)) for first in range(0, groups, BATCH)]
    loads = []
    for low, high in batches:
        at = pl.ds(low * GROUP, (high - low) * GROUP)
        there = pl.ds(start + low * GROUP, (high - low) * GROUP)
        loads.append(
            [
                move.start(hbm.at[there], ref.at[at])
                for hbm, ref in (
                    (proj_hbm, proj_ref),
                    (farkv_hbm, farkv_ref),
                    (gatt_hbm, gatt_ref),
                    (wrow_hbm, wrow_ref),
                )
            ]
            + [
                move.start(
                    prob_hbm.at[pl.ds(first_group + low, high - low)],
                    prob_ref.at[pl.ds(low, high - low)],
                )
            ]
        )
    got_wqkv = move.start(wqkv_hbm, wqkv_ref)
    masks16 = head_masks(GROUP)
    head_scale = (width // HEADS) ** -0.5
    far_lane = lax.broadcasted_iota(jnp.int32, (GROUP // UNIT, 2 * GROUP), 1) >= GROUP
    for (low, high), copies in zip(batches, loads):
        for copy in copies:
            copy.wait()
        work = [(i, half) for i in range(low, high) for half in range(width // HALF)]
        stacks, products = [], []
        for i, half in work:
            at = slice(i * GROUP, (i + 1) * GROUP)
            lo = half * HALF
            vals = jnp.concatenate(
                [
                    proj_ref[at, 2 * width + lo : 2 * width + lo + HALF],
                    farkv_ref[at, width + lo : width + lo + HALF],
                ],
                axis=0,
            )
            up = stack_heads(gatt_ref[at, lo : lo + HALF], masks16)
            stacks.append(up)
            products.append(prob_ref[i, half].astype(F32) * dot(up, vals, NT))
        for i in range(low, high):
            summed = jnp.zeros((GROUP, 2 * GROUP), F32)
            for (j, _), prod in zip(work, products):
                if j == i:
                    for h in range(PER_HALF):
                        summed = summed + prod[h * GROUP : (h + 1) * GROUP]
            pair = jnp.sum(summed.reshape(GROUP // UNIT, UNIT, 2 * GROUP), axis=1)
            pair = jnp.sum(jnp.where(far_lane, pair, 0.0), axis=1, keepdims=True)
            gw_ref[i] = jnp.broadcast_to(pair, (GROUP // UNIT, 128))
        scales = [repeat_heads(wrow_ref[i * GROUP : (i + 1) * GROUP, :]) for i, _ in work]
        products = [v * s for v, s in zip(products, scales)]
        totals = [jnp.sum(v, axis=1, keepdims=True) for v in products]
        for (i, half), up, prod, scale, total in zip(work, stacks, products, scales, totals):
            at = slice(i * GROUP, (i + 1) * GROUP)
            lo = half * HALF
            prob = prob_ref[i, half].astype(F32)
            ds = (prod - prob * total).astype(BF16)
            mixed = (prob * scale).astype(BF16)
            q = stack_heads(
                proj_ref[at, lo : lo + HALF] * jnp.asarray(head_scale, BF16), masks16
            )
            keys = jnp.concatenate(
                [proj_ref[at, width + lo : width + lo + HALF], farkv_ref[at, lo : lo + HALF]], axis=0
            )
            dq = unstack_heads(dot(ds, keys), masks16) * head_scale
            dk = dot(ds, q, TN).astype(BF16)
            dv = dot(mixed, up, TN).astype(BF16)
            dproj_ref[at, lo : lo + HALF] = dq.astype(BF16)
            dproj_ref[at, width + lo : width + lo + HALF] = dk[:GROUP]
            dproj_ref[at, 2 * width + lo : 2 * width + lo + HALF] = dv[:GROUP]
            dfar_ref[at, lo : lo + HALF] = dk[GROUP:]
            dfar_ref[at, width + lo : width + lo + HALF] = dv[GROUP:]
        at = pl.ds(low * GROUP, (high - low) * GROUP)
        there = pl.ds(start + low * GROUP, (high - low) * GROUP)
        move.store(dproj_ref.at[at], dproj_hbm.at[there])
        move.store(dfar_ref.at[at], dfar_hbm.at[there])

    got_wqkv.wait()
    grad = dot(dfar_ref[...], wqkv_ref[:, width:], NT).astype(BF16)
    for u in range(rows // UNIT):
        row = ret_rows[2 * first_group + u]
        edge = 0
        for ret_ref in ret_refs:
            value = grad[u * UNIT : (u + 1) * UNIT]

            def put(ret_ref=ret_ref, edge=edge, value=value):
                ret_ref[pl.ds(pl.multiple_of(row - edge, 16), UNIT), :] = value

            if chunks == 1:
                put()
            else:
                pl.when(jnp.logical_and(row >= edge, row < edge + ret_ref.shape[0]))(put)
            edge += ret_ref.shape[0]
    if letter:
        count_a, count_b, devices, extra = letter
        lane = lax.broadcasted_iota(jnp.int32, (1, 128), 1)
        row = jnp.zeros((1, 128), F32)

        def pair_at(at):
            if not prior:
                return gw_ref[at]
            early = prior_gw.shape[0]
            one = prior_gw[jnp.minimum(at, early - 1)]
            two = gw_ref[jnp.maximum(at - early, 0)]
            return jnp.where(at < early, one, two)

        for j in range(count_a + count_b):
            if j < count_a:
                both = pair_at(lax.shift_right_logical(place_ref[2 * j], 1))
                value = both[0:1] + both[1:2]
            else:
                pos = place_ref[count_a + j]
                both = pair_at(lax.shift_right_logical(pos, 1))
                value = jnp.where(lax.bitwise_and(pos, 1) == 0, both[0:1], both[1:2])
            row = jnp.where(lane == j, value, row)
        page = jnp.concatenate([row, jnp.zeros((1, width - 128), F32)], axis=1)
        line = lax.broadcasted_iota(jnp.int32, (extra, width), 0)
        page = jnp.where(line == 0, page, 0.0).astype(BF16)
        ret_ref = ret_refs[-1]
        height = ret_ref.shape[0] // devices
        for d in range(devices):
            ret_ref[(d + 1) * height - extra : (d + 1) * height, :] = page
    for ret_ref, hbm in zip(ret_refs, ret_hbm):
        move.store(ret_ref, hbm)
    move.finish()


def backward(
    ret_rows, place, proj, farkv, gatt, prob, wrow, w_qkv, sizes, first_group, groups, prior, letter,
    token,
):
    rows, width = gatt.shape
    count = groups * GROUP
    in_specs = [SMEM, SMEM] + [ANY] * 6
    operands = [ret_rows, place, proj, farkv, gatt, prob, wrow, w_qkv]
    aliases = {}
    if prior is not None:
        dproj, dfar, gw = prior
        in_specs += [VMEM, ANY, ANY]
        aliases = {len(operands) + 1: 0, len(operands) + 2: 1}
        operands += [gw, dproj, dfar]
    in_specs += [ANY]
    operands += [token]
    batches = -(-groups // BATCH)
    return pl.pallas_call(
        functools.partial(
            backward_kernel, first_group, groups, prior is not None, len(sizes), letter
        ),
        in_specs=in_specs,
        out_specs=[ANY, ANY, VMEM] + [ANY] * len(sizes),
        out_shape=[
            jax.ShapeDtypeStruct((rows, 3 * width), BF16),
            jax.ShapeDtypeStruct((rows, 2 * width), BF16),
            jax.ShapeDtypeStruct((groups, GROUP // UNIT, 128), F32),
        ]
        + [jax.ShapeDtypeStruct((n, width), BF16) for n in sizes],
        scratch_shapes=[
            pltpu.VMEM((count, 3 * width), BF16),
            pltpu.VMEM((count, 2 * width), BF16),
            pltpu.VMEM((count, width), BF16),
            pltpu.VMEM((groups,) + prob.shape[1:], BF16),
            pltpu.VMEM((count, 2 * GROUP), F32),
            pltpu.VMEM(w_qkv.shape, BF16),
            pltpu.VMEM((count, 3 * width), BF16),
            pltpu.VMEM((count, 2 * width), BF16),
        ]
        + [pltpu.VMEM((n, width), BF16) for n in sizes]
        + [pltpu.SemaphoreType.DMA((7 * batches + 2 + len(sizes),))],
        input_output_aliases=aliases,
        compiler_params=pltpu.CompilerParams(vmem_limit_bytes=VMEM_LIMIT),
        cost_estimate=cost(0.4e9 * groups, 1e6 * groups),
        name="backward",
    )(*operands)


def qkv_kernel(
    core_ref, x_hbm, farx_hbm, dproj_hbm, dfar_hbm, gain1_ref, wqkv_hbm, token_ref,
    gn_hbm, keep_ref, give_ref, x_ref, farx_ref, dproj_ref, dfar_ref, wqkv_ref, gn_ref, near_t, far_t, sems,
):
    move = Mover(sems)
    rows, width = x_ref.shape
    wide = wqkv_ref.shape[1]
    size = min(512, rows)
    got_w = move.start(wqkv_hbm, wqkv_ref)
    loads = []
    for low in range(0, rows, size):
        at = pl.ds(low, size)
        loads.append(
            [
                move.start(hbm.at[at], ref.at[at])
                for hbm, ref in (
                    (x_hbm, x_ref),
                    (dproj_hbm, dproj_ref),
                    (farx_hbm, farx_ref),
                    (dfar_hbm, dfar_ref),
                )
            ]
        )
    got_w.wait()
    for low, copies in zip(range(0, rows, size), loads):
        at = slice(low, low + size)
        for copy in copies:
            copy.wait()
        x = x_ref[at, :].astype(F32)
        scaled = x * inverse_norm(x)
        near_t[:, at] = (scaled * gain1_ref[...]).astype(BF16).T
        far = farx_ref[at, :].astype(F32)
        far_t[:, at] = (far * inverse_norm(far) * gain1_ref[...]).astype(BF16).T
        grad = dot(dproj_ref[at, :], wqkv_ref[...], NT)
        gn_ref[at, :] = grad.astype(BF16)
        move.store(gn_ref.at[pl.ds(low, size)], gn_hbm.at[pl.ds(low, size)])
    grads = []
    for c in range(0, wide, width):
        value = dot(near_t[...], dproj_ref[:, c : c + width])
        if c:
            value = value + dot(far_t[...], dfar_ref[:, c - width : c])
        grads.append(value)

    half = wide // 2

    def write(ref, which):
        at = which * half
        while at < (which + 1) * half:
            block, line = divmod(at, width)
            count = min(width - line, (which + 1) * half - at)
            value = grads[block][line : line + count]
            ref[at - which * half : at - which * half + count, :] = value.astype(BF16)
            at += count

    @pl.when(core_ref[0] == 0)
    def _():
        write(keep_ref, 0)
        write(give_ref, 1)

    @pl.when(core_ref[0] == 1)
    def _():
        write(keep_ref, 1)
        write(give_ref, 0)

    move.finish()


def qkv_grads(core, x, farx, dproj, dfar, gain1, w_qkv, token):
    rows, width = x.shape
    wide = w_qkv.shape[1]
    half = wide // 2
    tall = lambda size: pltpu.VMEM((rows, size), BF16)
    return pl.pallas_call(
        qkv_kernel,
        in_specs=[SMEM] + [ANY] * 4 + [VMEM, ANY, ANY],
        out_specs=[ANY, VMEM, VMEM],
        out_shape=[
            jax.ShapeDtypeStruct((rows, width), BF16),
            jax.ShapeDtypeStruct((half, width), BF16),
            jax.ShapeDtypeStruct((half, width), BF16),
        ],
        scratch_shapes=[
            tall(width),
            tall(width),
            tall(wide),
            tall(2 * width),
            pltpu.VMEM(w_qkv.shape, BF16),
            tall(width),
            pltpu.VMEM((width, rows), BF16),
            pltpu.VMEM((width, rows), BF16),
            pltpu.SemaphoreType.DMA((5 * (rows // min(512, rows)) + 1,)),
        ],
        compiler_params=limit(62),
        cost_estimate=cost(10e9, 25e6),
        name="qkv_grads",
    )(core, x, farx, dproj, dfar, gain1, w_qkv, token)


def row_gradient(f, x):
    r1 = inverse_norm(x)
    scaled = x * r1
    return r1 * (f - scaled * jnp.mean(f * scaled, axis=-1, keepdims=True))


def base_kernel(x_ref, gmid_ref, gn_ref, gs_ref, gain1_ref, out_ref):
    rows, width = x_ref.shape
    spread = jnp.broadcast_to(gs_ref[...][:, None, :], (rows // UNIT, UNIT, width))
    f = (gn_ref[...].astype(F32) + spread.reshape(rows, width)) * gain1_ref[...]
    grad = gmid_ref[...].astype(F32) + row_gradient(f, x_ref[...].astype(F32))
    out_ref[...] = grad.astype(BF16)


def base_rows(x, gmid, gn, gs, gain1):
    rows, width = x.shape
    tile = 2 * TILE
    return pl.pallas_call(
        base_kernel,
        grid=(rows // tile,),
        in_specs=[
            rows_of(tile, width),
            rows_of(tile, width),
            rows_of(tile, width),
            rows_of(tile // UNIT, width),
            whole((1, width)),
        ],
        out_specs=rows_of(tile, width),
        out_shape=jax.ShapeDtypeStruct((rows, width), BF16),
        compiler_params=params(),
        cost_estimate=cost(rows * width * 20, rows * width * 8),
        name="base",
    )(x, gmid, gn, gs, gain1)


def last_kernel(sizes, extra, capacity, table_ref, place_ref, *refs):
    ret_refs = refs[: len(sizes)]
    x_ref, base_ref, gain1_ref, outa_ref, outb_ref, acc = refs[len(sizes) :]
    rows_a = outa_ref.shape[0]
    acc[...] = jnp.zeros_like(acc)

    begin = 0
    for index, (size, ret_ref) in enumerate(zip(sizes, ret_refs)):
        height = size * UNIT + (extra if index == len(sizes) - 1 else 0)

        def add(r, carry, size=size, ret_ref=ret_ref, begin=begin, height=height):
            for slot in range(size):
                unit = table_ref[r * capacity + begin + slot]

                @pl.when(unit >= 0)
                def _():
                    at = pl.ds(pl.multiple_of(unit * UNIT, UNIT), UNIT)
                    src = pl.ds(pl.multiple_of(r * height + slot * UNIT, 16), UNIT)
                    acc[at, :] += ret_ref[src, :].astype(F32)

            return carry

        lax.fori_loop(0, ret_ref.shape[0] // height, add, 0)
        begin += size

    def finish(out_ref, first):
        def body(u, carry):
            at = pl.ds(pl.multiple_of(place_ref[first + u] * UNIT, UNIT), UNIT)
            own = pl.ds(pl.multiple_of((first + u) * UNIT, UNIT), UNIT)
            f = acc[own, :] * gain1_ref[...]
            grad = base_ref[at, :].astype(F32) + row_gradient(f, x_ref[own, :].astype(F32))
            out_ref[pl.ds(pl.multiple_of(u * UNIT, UNIT), UNIT), :] = grad.astype(BF16)
            return carry

        lax.fori_loop(0, out_ref.shape[0] // UNIT, body, 0, unroll=2)

    finish(outa_ref, 0)
    finish(outb_ref, rows_a // UNIT)


def last(table, place, ret, sizes, extra, capacity, x, base, gain1, rows_a):
    rows, width = x.shape
    return pl.pallas_call(
        functools.partial(last_kernel, sizes, extra, capacity),
        in_specs=[SMEM, SMEM] + [VMEM] * (len(ret) + 3),
        out_specs=[VMEM, VMEM],
        out_shape=[
            jax.ShapeDtypeStruct((rows_a, width), BF16),
            jax.ShapeDtypeStruct((rows - rows_a, width), BF16),
        ],
        scratch_shapes=[pltpu.VMEM((rows, width), F32)],
        compiler_params=limit(24),
        cost_estimate=cost(rows * width * 20, rows * width * 12),
        name="last",
    )(table, place, *ret, x, base, gain1)


def bits_of(size):
    count = 0
    while (1 << count) < size:
        count += 1
    return count


def bit_of(axis, bit):
    return (lax.axis_index(axis) >> bit) & 1


def swap(values, axis, bit):
    size = lax.axis_size(axis)
    return lax.ppermute(values, axis, [(i, i ^ (1 << bit)) for i in range(size)])


def halve(values, axis, bit):
    half = values.shape[0] // 2
    mine = bit_of(axis, bit)
    keep = lax.dynamic_slice_in_dim(values, mine * half, half, 0)
    give = lax.dynamic_slice_in_dim(values, (1 - mine) * half, half, 0)
    return keep, give


def double(values, axis, bit):
    got = swap(values, axis, bit)
    return jnp.where(
        bit_of(axis, bit) == 0,
        jnp.concatenate([values, got], axis=0),
        jnp.concatenate([got, values], axis=0),
    )


def add(one, two):
    return (one.astype(F32) + two.astype(F32)).astype(BF16)


def reduce_any(values, order):
    for axis, bit in order:
        keep, give = halve(values, axis, bit)
        values = add(keep, swap(give, axis, bit))
    for axis, bit in reversed(order):
        values = double(values, axis, bit)
    return values


def tie(values, *tokens):
    return pl.pallas_call(
        lambda *refs: None,
        in_specs=[ANY] * (1 + len(tokens)),
        out_specs=ANY,
        out_shape=jax.ShapeDtypeStruct(values.shape, values.dtype),
        input_output_aliases={0: 0},
        name="tie",
    )(values, *tokens)


def fetch(sources, targets, sems):
    copies = [
        pltpu.make_async_copy(source, target, sems.at[i])
        for i, (source, target) in enumerate(zip(sources, targets))
    ]
    for copy in copies:
        copy.start()
    for copy in copies:
        copy.wait()


def halve_kernel(ranges, sources, bits_ref, *refs):
    count = 2 * (1 + max(r[4] for r in ranges))
    sems = refs[-1]
    outs = refs[2 * sources + 1 : 2 * sources + 1 + count]
    held = refs[2 * sources + 1 + count : -2]
    made = held[2 * sources :]
    fetch(refs[: 2 * sources], held, refs[-2])
    refs = held
    for source, first, count, bit, out, there in ranges:
        own, came = refs[2 * source], refs[2 * source + 1]
        half = count // 2
        keep = pl.multiple_of(first + bits_ref[bit] * half, 16)
        give = pl.multiple_of(first + (1 - bits_ref[bit]) * half, 16)
        for ref, line in ((made[2 * out], keep), (made[2 * out + 1], give)):
            rows = pl.ds(line, half)
            total = own[rows, :].astype(F32) + came[rows, :].astype(F32)
            ref[there : there + half, :] = total.astype(BF16)
    fetch(made, outs, sems)


def halve_step(ranges, bits, pairs, token):
    width = pairs[0][0].shape[1]
    count = 1 + max(r[4] for r in ranges)
    heights = [max(r[5] + r[2] // 2 for r in ranges if r[4] == out) for out in range(count)]
    shapes = [jax.ShapeDtypeStruct((n, width), BF16) for n in heights for _ in range(2)]
    flat = [v for pair in pairs for v in pair]
    out = pl.pallas_call(
        functools.partial(halve_kernel, ranges, len(pairs)),
        in_specs=[SMEM] + [HBM] * len(flat) + [ANY],
        out_specs=[HBM] * len(shapes),
        out_shape=shapes,
        scratch_shapes=[pltpu.VMEM(v.shape, BF16) for v in flat + shapes]
        + [pltpu.SemaphoreType.DMA((len(flat),)), pltpu.SemaphoreType.DMA((len(shapes),))],
        compiler_params=limit(62),
        cost_estimate=cost(0, 8 * sum(heights) * width),
        name="halve_step",
    )(jnp.stack([bit_of(*b) for b in bits]).astype(jnp.int32), *flat, token)
    return [(out[2 * i], out[2 * i + 1]) for i in range(count)]


def double_kernel(ranges, sources, tokens, bits_ref, *refs):
    count = 1 + max(r[0] for r in ranges)
    outs = refs[2 * sources + tokens : 2 * sources + tokens + count]
    held = refs[2 * sources + tokens + count : -1]
    fetch(refs[: 2 * sources], held, refs[-1])
    refs = held
    for source, first, count, bit, out, there in ranges:
        own, came = refs[2 * out], refs[2 * out + 1]
        half = count // 2
        keep = pl.multiple_of(first + bits_ref[bit] * half, 16)
        give = pl.multiple_of(first + (1 - bits_ref[bit]) * half, 16)
        outs[source][pl.ds(keep, half), :] = own[there : there + half, :]
        outs[source][pl.ds(give, half), :] = came[there : there + half, :]


def double_step(ranges, bits, pairs, *tokens):
    width = pairs[0][0].shape[1]
    count = 1 + max(r[0] for r in ranges)
    heights = [max(r[1] + r[2] for r in ranges if r[0] == source) for source in range(count)]
    flat = [v for pair in pairs for v in pair]
    return pl.pallas_call(
        functools.partial(double_kernel, ranges, len(pairs), len(tokens)),
        in_specs=[SMEM] + [ANY] * len(flat) + [ANY] * len(tokens),
        out_specs=[VMEM] * count,
        out_shape=[jax.ShapeDtypeStruct((n, width), BF16) for n in heights],
        scratch_shapes=[pltpu.VMEM(v.shape, BF16) for v in flat]
        + [pltpu.SemaphoreType.DMA((len(flat),))],
        compiler_params=limit(24),
        cost_estimate=cost(0, 4 * sum(heights) * width),
        name="double_step",
    )(jnp.stack([bit_of(*b) for b in bits]).astype(jnp.int32), *flat, *tokens)


AXIS_X, AXIS_Y, AXIS_Z0, AXIS_Z1 = ("dp", 1), ("blk", 0), ("blk", 1), ("blk", 2)


def places(half, width, ff):
    up, down, out, qkv = range(4)
    edge = ff // 2
    result = [
        (c, width, up, 0, half * edge + c) for c in range(0, edge, width)
    ]
    result.append((edge, width // 2, out, half * (width // 2), 0))
    result += [
        (edge + width // 2 + c, width, down, half * edge + c, 0) for c in range(0, edge, width)
    ]
    start = edge + width // 2 + edge
    total = 3 * width
    at = half * total // 2
    while at < (half + 1) * total // 2:
        block, line = divmod(at, width)
        count = min(width - line, (half + 1) * total // 2 - at)
        result.append((start + at - half * total // 2, count, qkv, line, block * width))
        at += count
    return result


def assemble_kernel(which, prior, width, ff, core_ref, values_ref, wup_ref, wqkv_ref, *refs):
    outs = refs[5 if prior else 0 :][:5]
    held, products, sems = refs[-3:]
    ones = jnp.ones((8, width), BF16)

    def write(half):
        copies = []
        seen = set()
        for i, (first, count, out, line, column) in enumerate(places(half, width, ff)):
            value = values_ref[first : first + count, :].astype(F32)
            held[first : first + count, :] = value
            copy = pltpu.make_async_copy(
                held.at[pl.ds(first, count)],
                outs[out].at[pl.ds(line, count), pl.ds(column, width)],
                sems.at[i],
            )
            copy.start()
            copies.append(copy)
            if out in (0, 3):
                weights = (wup_ref if out == 0 else wqkv_ref)[line : line + count, column : column + width]
                part = weights.astype(F32) * value
                if out in seen:
                    products[out // 3, line : line + count, :] += part
                else:
                    products[out // 3, line : line + count, :] = part
                    if count < width:
                        rest = slice(0, line) if line else slice(count, width)
                        products[out // 3, rest, :] = jnp.zeros((width - count, width), F32)
                    seen.add(out)
        for out, at in ((3, 0), (0, 1)):
            value = products[out // 3]
            high = value.astype(BF16)
            low = (value - high.astype(F32)).astype(BF16)
            row = (dot(ones, high, NT) + dot(ones, low, NT))[0:1]
            outs[4][at : at + 1, :] = row + refs[0][at : at + 1, :] if prior else row
        for copy in copies:
            copy.wait()

    outs[4][...] = jnp.zeros_like(outs[4])

    @pl.when(core_ref[0] == which)
    def _():
        write(0)

    @pl.when(core_ref[0] != which)
    def _():
        write(1)


def assemble(core, which, values, w_up, w_qkv, width, ff, prior):
    shapes = [(width, ff), (ff, width), (width, width), (width, 3 * width), (8, width)]
    operands = [core, values, w_up, w_qkv]
    if prior is not None:
        operands += [prior[4], *prior[:4]]
    most = max(len(places(half, width, ff)) for half in (0, 1))
    return pl.pallas_call(
        functools.partial(assemble_kernel, which, prior is not None, width, ff),
        in_specs=[SMEM] + [VMEM] * (3 if prior is None else 4) + [ANY] * (0 if prior is None else 4),
        out_specs=[ANY] * 4 + [VMEM],
        out_shape=[jax.ShapeDtypeStruct(shape, F32) for shape in shapes],
        scratch_shapes=[
            pltpu.VMEM(values.shape, F32),
            pltpu.VMEM((2, width, width), F32),
            pltpu.SemaphoreType.DMA((most,)),
        ],
        input_output_aliases={} if prior is None else {5 + i: i for i in range(4)},
        compiler_params=limit(20),
        cost_estimate=cost(0, values.size * 6),
        name="assemble",
    )(*operands)


def exchange(values, devices):
    shape = values.shape
    parts = values.reshape(devices, shape[0] // devices, *shape[1:])
    return lax.all_to_all(parts, "blk", split_axis=0, concat_axis=0, tiled=True).reshape(shape)


def per_device(
    x_a, x_b, sel_a, sel_b, gain_one, w_qkv, w_out, w_sort, gain_two, w_up, w_down, cot_a, cot_b
):
    devices = lax.axis_size("blk")
    me = lax.axis_index("blk")
    seqs_a, rows_a, width = x_a.shape
    seqs_b, rows_b, _ = x_b.shape
    npl = sel_a.shape[1]
    blocks = npl * devices
    len_a = rows_a // npl
    len_b = rows_b // npl
    total_a = seqs_a * rows_a
    total_b = seqs_b * rows_b
    rows = total_a + total_b
    units = rows // UNIT
    units_a = total_a // UNIT
    count_a = seqs_a * npl
    count_b = seqs_b * npl
    picks = count_a + count_b
    picks_up = -(-picks // 16) * 16
    groups = rows // GROUP
    per = TILE // GROUP
    capacity = 2 * max(1, (4 * units + 5 * devices - 1) // (5 * devices))
    send_rows = devices * capacity * UNIT
    ff = w_up.shape[1]
    gain1 = gain_one.astype(F32).reshape(1, width)
    gain2 = gain_two.astype(F32).reshape(1, width)

    first, early = capacity, groups
    if capacity > 8:
        full, left = divmod(units, capacity)
        sure = (full * 8 + min(left, 8)) // 2 // per * per
        if capacity == 14 and 0 < sure < groups:
            first, early = 8, sure

    sizes = [8, 7] if early < groups else [capacity]
    extra = 16
    average = np.zeros((picks, units), np.float32)
    for j in range(count_a):
        average[j, 2 * j : 2 * j + 2] = 1.0 / len_a
    for j in range(count_b):
        average[count_a + j, units_a + j] = 1.0 / len_b
    settings = (npl, seqs_a, seqs_b, devices, capacity, first, early, sizes, extra, picks_up)
    w_sort_t = w_sort.T
    x, means, news, far_rows, ret_rows, perm, place, kinds = digest(
        x_a.reshape(-1, width), x_b.reshape(-1, width), sel_a, sel_b, gain1, average, w_sort_t, settings
    )
    news = lax.all_to_all(news, "blk", split_axis=0, concat_axis=0, tiled=True)
    table = news[:, picks, :capacity].astype(jnp.int32).reshape(-1)
    back_table = news[:, picks, capacity : capacity + sum(sizes)].astype(jnp.int32).reshape(-1)
    news = news[:, :picks]
    parcels = pack(table, x, devices, capacity, first, picks_up)
    recv = [exchange(parcels[0], devices)]
    summary = means * gain1
    rs = inverse_norm(summary)
    unit_summary = (summary * rs).astype(BF16)
    all_summaries = jnp.broadcast_to(
        jnp.pad(unit_summary, ((0, picks_up - picks), (0, 0))), (devices, picks_up, width)
    )

    xp, cot = arrange(perm, x, cot_a.reshape(-1, width), cot_b.reshape(-1, width))
    proj = project(xp, gain1, w_qkv)

    def by_sequence(values):
        tail = values.shape[2:]
        one = values[:, :count_a].reshape((devices, seqs_a, npl) + tail)
        two = values[:, count_a:].reshape((devices, seqs_b, npl) + tail)
        both = jnp.concatenate([one, two], axis=1)
        return jnp.swapaxes(both, 0, 1).reshape((seqs_a + seqs_b, blocks) + tail)

    def own_rows(values):
        return lax.dynamic_slice_in_dim(values, me * npl, npl, 1).reshape((-1,) + values.shape[2:])

    def to_units(values):
        return jnp.concatenate(
            [jnp.repeat(values[:count_a], len_a // UNIT, axis=0), values[count_a:]], axis=0
        )

    news = by_sequence(news)
    logits = news[..., :blocks]
    picked = (news[..., blocks : blocks + 1] == jnp.arange(blocks, dtype=F32)).astype(F32)
    weights = jnp.take(to_units(own_rows(sinkhorn(logits, picked))), perm, axis=0)
    lane = jnp.arange(2 * GROUP) >= GROUP
    wrow = jnp.where(lane[None, :], jnp.repeat(weights, UNIT, axis=0), 1.0)
    if len(parcels) > 1:
        tall = (capacity - first) * UNIT
        parcel = lax.dynamic_update_slice(
            parcels[1].reshape(devices, -1, width), all_summaries, (0, tall, 0)
        )
        recv.append(exchange(tie(parcel.reshape(-1, width), wrow, proj), devices))
        units_all = recv[1].reshape(devices, -1, width)[:, tall:]
    else:
        units_all = exchange(all_summaries.reshape(-1, width), devices)
        units_all = units_all.reshape(devices, picks_up, width)
    units_all = by_sequence(units_all[:, :picks])
    block_of = np.arange(GROUP) // len_b
    cross = block_of[:, None] != block_of[None, :]
    mask = np.zeros((2, GROUP, 2 * GROUP), np.float32)
    mask[1] = np.where(np.concatenate([cross, cross], axis=1), -1e30, 0.0)

    core = bit_of("dp", 0).astype(jnp.int32).reshape(1)
    shared = (xp, cot, proj, wrow, mask, gain1, gain2, w_qkv, w_out, w_up, w_down)
    heights = [
        devices * (n * UNIT + (extra if i == len(sizes) - 1 else 0))
        for i, n in enumerate(sizes)
    ]

    letter = (count_a, count_b, devices, extra)

    def run_backward(streams, *rest):
        _, _, gatt, prob, _, farkv = streams
        return backward(ret_rows, place, proj, farkv, gatt, prob, wrow, w_qkv, *rest)

    fast = lax.axis_size("dp") == 4 and devices == 8 and early < groups
    part_x = ff // 2 + width // 2
    if early < groups:
        prior = forward(far_rows, kinds, core, recv[:1], *shared, 0, early, None, False, wrow)
        dproj, dfar, gw_one, *ret = run_backward(
            prior[0], heights[:1], 0, early, None, None, prior[0][0]
        )
        back = [exchange(v, devices) for v in ret]
        streams, sums = forward(
            far_rows, kinds, core, recv, *shared, early, groups - early, prior, True, dproj
        )
        keep, give = sums
        out_a, out_b = restore(perm, streams[0], total_a)
        big_came = swap(give, "dp", 0)
        token = keep
        if fast:
            ranges_one = [(0, 0, part_x, 0, 0, 0), (0, part_x, keep.shape[0] - part_x, 1, 1, 0)]
            (bx, gx), (by, gy) = halve_step(
                ranges_one, [AXIS_X, AXIS_Y], [(keep, big_came)], out_a
            )
            bx_came, by_came = swap(gx, *AXIS_X), swap(gy, *AXIS_Y)
            token = bx
        dproj, dfar, _, *ret = run_backward(
            streams, heights[1:], early, groups - early, (dproj, dfar, gw_one), letter, token
        )
    else:
        streams, sums = forward(far_rows, kinds, core, recv, *shared, 0, groups, None, True, wrow)
        keep, give = sums
        out_a, out_b = restore(perm, streams[0], total_a)
        big_came = swap(give, "dp", 0)
        back = []
        dproj, dfar, _, *ret = run_backward(
            streams, heights, 0, groups, None, letter, keep
        )
    _, gmid, _, _, farx, _ = streams

    parcel = tie(ret[0], bx_came, by_came, back[0]) if fast else ret[0]
    tall = sizes[-1] * UNIT
    arrived = exchange(parcel, devices)
    back.append(arrived)
    token = dproj
    gn, late_keep, late_give = qkv_grads(
        core, xp, farx, dproj, dfar, gain1, w_qkv, token
    )
    late_came = swap(late_give, "dp", 0)
    part_late = 256
    if fast:
        late_rows = late_keep.shape[0]
        ranges_late = [(0, 0, part_late, 0, 0, 0), (0, part_late, late_rows - part_late, 1, 1, 0)]
        (lx, gx), (ly, gy) = halve_step(
            ranges_late, [AXIS_X, AXIS_Y], [(late_keep, late_came)], late_came
        )
        lx_came, ly_came = swap(gx, *AXIS_X), swap(gy, *AXIS_Y)
        nbx, nlx, nby, nly = (v.shape[0] for v in (bx, lx, by, ly))
        ranges_two = [
            (0, 0, nbx, 0, 0, 0),
            (1, 0, nlx, 0, 0, nbx // 2),
            (2, 0, nby, 1, 1, 0),
            (3, 0, nly, 1, 1, nby // 2),
        ]
        (vx, gx), (vy, gy) = halve_step(
            ranges_two,
            [AXIS_Y, AXIS_X],
            [(bx, bx_came), (lx, lx_came), (by, by_came), (ly, ly_came)],
            lx,
        )
        vx_came, vy_came = swap(gx, *AXIS_Y), swap(gy, *AXIS_X)
    small, spread = sort_back(
        me.reshape(1), perm, logits, picked, units_all.reshape(-1, width), w_sort_t, gain1, means,
        arrived, npl, seqs_a, (len_a, len_b), tall, extra, vx if fast else arrived,
    )
    if fast:
        cuts = [nbx // 2, nlx // 2, nby // 2, nly // 2]
        ranges_three = [
            (0, 0, cuts[0], 0, 0, 0),
            (0, cuts[0], cuts[1], 0, 0, cuts[0] // 2),
            (1, 0, cuts[2], 0, 0, (cuts[0] + cuts[1]) // 2),
            (1, cuts[2], cuts[3], 0, 0, (cuts[0] + cuts[1] + cuts[2]) // 2),
        ]
        ((total, gz),) = halve_step(
            ranges_three, [AXIS_Z0], [(vx, vx_came), (vy, vy_came)], spread
        )
    base = base_rows(xp, gmid, gn, spread, gain1)
    if fast:
        total = add(total, tie(swap(gz, *AXIS_Z0), base))

    gx_a, gx_b = last(back_table, place, back, sizes, extra, sum(sizes), x, base, gain1, total_a)
    if fast:
        for bit in (0, 1):
            small = small + swap(small, "dp", bit)
        total = add(total, tie(swap(total, *AXIS_Z1), gx_a, small))
        vx, vy = double_step(ranges_three, [AXIS_Z0], [(total, swap(total, *AXIS_Z0))])
        ranges_back = [
            (0, 0, nbx, 0, 0, 0),
            (0, nbx, nlx, 0, 0, cuts[0]),
            (1, 0, nby, 1, 1, 0),
            (1, nby, nly, 1, 1, cuts[2]),
        ]
        vx, vy = double_step(
            ranges_back,
            [AXIS_Y, AXIS_X],
            [(vx, swap(vx, *AXIS_Y)), (vy, swap(vy, *AXIS_X))],
        )
        big_rows = keep.shape[0]
        ranges_all = [
            (0, 0, part_x, 0, 0, 0),
            (0, big_rows, part_late, 0, 0, nbx),
            (0, part_x, big_rows - part_x, 1, 1, 0),
            (0, big_rows + part_late, late_rows - part_late, 1, 1, nby),
        ]
        (sums_own,) = double_step(
            ranges_all,
            [AXIS_X, AXIS_Y],
            [(vx, swap(vx, *AXIS_X)), (vy, swap(vy, *AXIS_Y))],
        )
    else:
        across = [("dp", bit) for bit in range(1, bits_of(lax.axis_size("dp")))]
        along = [("blk", bit) for bit in range(bits_of(devices))]
        sums_own = jnp.concatenate(
            [
                reduce_any(add(keep, big_came), across + along),
                reduce_any(add(late_keep, late_came), along + across),
            ],
            axis=0,
        )
    sums_came = swap(sums_own, "dp", 0)

    if not fast:
        small = lax.psum(small, "dp")
    written = assemble(core, 0, sums_own, w_up, w_qkv, width, ff, None)
    sum_up, sum_down, sum_out, sum_qkv, gains = assemble(
        core, 1, sums_came, w_up, w_qkv, width, ff, written
    )

    return (
        out_a.reshape(x_a.shape),
        out_b.reshape(x_b.shape),
        gx_a.reshape(x_a.shape),
        gx_b.reshape(x_b.shape),
        gains[0] / gain1[0] + small[blocks],
        sum_qkv,
        sum_out,
        small[:blocks].T,
        gains[1] / gain2[0],
        sum_up,
        sum_down,
    )


def solution(mesh):
    rows_spec = P("dp", "blk", None)
    in_specs = (
        (rows_spec, rows_spec, P("dp", "blk"), P("dp", "blk")) + (P(),) * 7 + (rows_spec, rows_spec)
    )
    out_specs = (rows_spec,) * 4 + (P(),) * 7
    return jax.shard_map(
        per_device, mesh=mesh, in_specs=in_specs, out_specs=out_specs, check_vma=False
    )
```

```python
import functools

import jax
import jax.numpy as jnp
import numpy as np
from jax import lax
from jax.experimental import pallas as pl
from jax.experimental.pallas import tpu as pltpu
from jax.sharding import PartitionSpec as P

HEADS = 8
SINK_ITERS = 8
EPSILON = 1e-05
SOFTMAX_HEAT = 0.75
UNIT = 32
GROUP = 64
TILE = 256
HALF = 256
PER_HALF = 4
VMEM_LIMIT = 62 * 1024 * 1024

F32 = jnp.float32
BF16 = jnp.bfloat16

NN = (((1,), (0,)), ((), ()))
NT = (((1,), (1,)), ((), ()))
TN = (((0,), (0,)), ((), ()))


def dot(a, b, dims=NN):
    return lax.dot_general(a, b, dims, preferred_element_type=F32)


def inverse_norm(values):
    return lax.rsqrt(jnp.mean(values * values, axis=-1, keepdims=True) + EPSILON)


def whole(shape):
    zeros = (0,) * len(shape)
    return pl.BlockSpec(shape, lambda *_: zeros, pipeline_mode=pl.Buffered(1))


def rows_of(tile, width):
    return pl.BlockSpec((tile, width), lambda i: (i, 0))


SMEM = pl.BlockSpec(memory_space=pltpu.SMEM)


def params():
    return pltpu.CompilerParams(
        dimension_semantics=("arbitrary",), vmem_limit_bytes=VMEM_LIMIT
    )


def cost(flops, nbytes):
    return pl.CostEstimate(flops=int(flops * 1e-3), bytes_accessed=int(nbytes * 1e-3), transcendentals=0)


ANY = pl.BlockSpec(memory_space=pl.ANY)
VMEM = pl.BlockSpec(memory_space=pltpu.VMEM)
HBM = pl.BlockSpec(memory_space=pltpu.HBM)


def limit(mib):
    return pltpu.CompilerParams(vmem_limit_bytes=mib * 1024 * 1024)


def request_kernel(
    npl, seqs_a, seqs_b, devices, capacity, first, early, sizes, extra, spare_rows,
    sela_ref, selb_ref, table_ref, back_ref, far_ref, ret_ref, perm_ref, place_ref, kinds_ref, fill, begin, used,
):
    count_a = seqs_a * npl
    count_b = seqs_b * npl
    units_a = 2 * count_a
    width = sum(sizes)
    shift = npl.bit_length() - 1 if npl & (npl - 1) == 0 else -1

    def choice(j):
        ref, at = (sela_ref, j) if j < count_a else (selb_ref, j - count_a)
        return ref[at // npl, at % npl]

    def split(chosen):
        if shift >= 0:
            return lax.shift_right_logical(chosen, shift), lax.bitwise_and(chosen, npl - 1)
        return lax.div(chosen, npl), lax.rem(chosen, npl)

    def clear(ref):
        def body(i, carry):
            ref[i] = -1
            return carry

        return body

    lax.fori_loop(0, devices * capacity, clear(table_ref), 0)
    lax.fori_loop(0, devices * width, clear(back_ref), 0)
    for s in range(devices):
        fill[s] = 0
        used[s] = 0
        used[devices + s] = 0
    one = lambda flag: jnp.where(flag, 1, 0)
    ready_a, ready_b, must_a, must_b = (jnp.int32(0) for _ in range(4))
    for j in range(count_a + count_b):
        source, inner = split(choice(j))
        slot = fill[source]
        begin[j] = slot
        size = 2 if j < count_a else 1
        fill[source] = slot + size
        if j < count_a:
            unit = inner * 2 + (j // npl) * npl * 2
            ready_a = ready_a + one(slot + 2 <= first)
            table_ref[source * capacity + slot + 1] = unit + 1
        else:
            unit = inner + (units_a + (j - count_a) // npl * npl)
            ready_b = ready_b + one(slot + 1 <= first)
        table_ref[source * capacity + slot] = unit

    two = early < count_a + count_b // 2

    def must(j):
        source, _ = split(choice(j))
        if not two:
            return begin[j] < 0
        return begin[j] < fill[source] - 6

    for j in range(count_a):
        must_a = must_a + one(must(j))
    for j in range(count_b):
        must_b = must_b + one(must(count_a + j))
    even = jnp.logical_or(lax.bitwise_and(must_b, 1) == 0, ready_b > must_b)
    pairs = lax.shift_right_logical(must_b + one(even), 1)
    take_a = jnp.minimum(ready_a, early - pairs)
    if not two:
        take_a = jnp.int32(count_a)
    take_b = 2 * (early - take_a)
    late_b = 2 * (early + count_a - take_a)
    kinds_ref[0] = take_a
    kinds_ref[1] = early + count_a - take_a
    second = devices * first * UNIT

    def ret_row(phase, source, slot):
        chunks = list(enumerate(sizes))
        if two:
            chunks = chunks[:1] if phase == 0 else chunks[1:]
        row = jnp.int32(0)
        begin_slot, begin_row = 0, 0
        for index, size in chunks:
            height = size * UNIT + (extra if index == len(sizes) - 1 else 0)
            here = begin_row + source * height + (slot - begin_slot) * UNIT
            row = jnp.where(slot >= begin_slot, here, row)
            begin_slot += size
            begin_row += devices * height
        return row

    def put(pos, unit, inner, source, slot, late):
        near = (source * first + slot) * UNIT
        rest = second + source * ((capacity - first) * UNIT + spare_rows) + (slot - first) * UNIT
        far_ref[pos] = jnp.where(slot < first, near, rest)
        at = late * devices + source
        back = used[at]
        used[at] = back + 1
        if two:
            ret_ref[pos] = jnp.where(late == 0, ret_row(0, source, back), ret_row(1, source, back))
            back_ref[source * width + back + late * sizes[0]] = inner
        else:
            ret_ref[pos] = ret_row(0, source, back)
            back_ref[source * width + back] = inner
        perm_ref[pos] = unit
        place_ref[unit] = pos

    spare = take_a - must_a
    taken, other, free = (jnp.int32(0) for _ in range(3))
    for j in range(count_a):
        source, inner = split(choice(j))
        slot = begin[j]
        need = must(j)
        pick = jnp.logical_and(jnp.logical_not(need), jnp.logical_and(slot + 2 <= first, free < spare))
        use = jnp.logical_or(need, pick)
        free = free + one(pick)
        pos = 2 * jnp.where(use, taken, early + other)
        inner = inner * 2 + (j // npl) * npl * 2
        put(pos, 2 * j, inner, source, slot, one(jnp.logical_not(use)))
        put(pos + 1, 2 * j + 1, inner + 1, source, slot + 1, one(jnp.logical_not(use)))
        taken = taken + one(use)
        other = other + one(jnp.logical_not(use))
    spare = take_b - must_b
    drop = one(spare < 0)
    taken, other, free = (jnp.int32(0) for _ in range(3))
    for j in range(count_b):
        source, inner = split(choice(count_a + j))
        slot = begin[count_a + j]
        need = must(count_a + j)
        skip = jnp.logical_and(need, drop > 0)
        drop = drop - one(skip)
        pick = jnp.logical_and(jnp.logical_not(need), jnp.logical_and(slot + 1 <= first, free < spare))
        use = jnp.logical_or(jnp.logical_and(need, jnp.logical_not(skip)), pick)
        free = free + one(pick)
        pos = jnp.where(use, 2 * take_a + taken, late_b + other)
        inner = inner + (units_a + (j // npl) * npl)
        put(pos, units_a + j, inner, source, slot, one(jnp.logical_not(use)))
        taken = taken + one(use)
        other = other + one(jnp.logical_not(use))


def digest_kernel(
    tiles_a, settings, sela_ref, selb_ref, xa_ref, xb_ref, gain_ref, avg_ref, wsort_ref,
    x_ref, means_ref, news_ref, far_ref, ret_ref, perm_ref, place_ref, kinds_ref,
    sums, table_ref, back_ref, fill, begin, used,
):
    step = pl.program_id(0)

    @pl.when(step == 0)
    def _():
        request_kernel(
            *settings, sela_ref, selb_ref, table_ref, back_ref, far_ref, ret_ref, perm_ref, place_ref,
            kinds_ref, fill, begin, used,
        )

    def take(src):
        x = src[...]
        x_ref[...] = x
        x = x.astype(F32)
        scaled = x * inverse_norm(x)
        units = x.shape[0] // UNIT
        at = pl.ds(pl.multiple_of(step * units, units), units)
        sums[at, :] = jnp.sum(scaled.reshape(units, UNIT, x.shape[1]), axis=1)

    pl.when(step < tiles_a)(lambda: take(xa_ref))
    pl.when(step >= tiles_a)(lambda: take(xb_ref))

    @pl.when(step == pl.num_programs(0) - 1)
    def _():
        means = lax.dot_general(
            avg_ref[...], sums[...], NN, precision=lax.Precision.HIGHEST, preferred_element_type=F32
        )
        means_ref[...] = means
        summary = means * gain_ref[...]
        unit = (summary * inverse_norm(summary)).astype(BF16)
        logits = dot(unit, wsort_ref[...], NT) * (1.0 / SOFTMAX_HEAT)
        picks, blocks = logits.shape
        devices, height, lanes = news_ref.shape
        line = lax.broadcasted_iota(jnp.int32, (picks, lanes - blocks), 0)
        lane = lax.broadcasted_iota(jnp.int32, (picks, lanes - blocks), 1)
        chosen = jnp.zeros((picks, lanes - blocks), jnp.int32)
        count_a = sela_ref.shape[0] * sela_ref.shape[1]
        for j in range(picks):
            ref, at = (sela_ref, j) if j < count_a else (selb_ref, j - count_a)
            npl = ref.shape[1]
            chosen = jnp.where(line == j, ref[at // npl, at % npl], chosen)
        chosen = jnp.where(lane == 0, chosen, 0).astype(F32)
        message = jnp.concatenate([logits, chosen], axis=1)
        lane = lax.broadcasted_iota(jnp.int32, (1, lanes), 1)
        wanted = table_ref.shape[0] // devices
        order = back_ref.shape[0] // devices
        rest = lax.broadcasted_iota(jnp.int32, (height - picks, lanes), 0)
        for d in range(devices):
            row = jnp.zeros((1, lanes), jnp.int32)
            for k in range(wanted):
                row = jnp.where(lane == k, table_ref[d * wanted + k], row)
            for k in range(order):
                row = jnp.where(lane == wanted + k, back_ref[d * order + k], row)
            news_ref[d, :picks, :] = message
            news_ref[d, picks:, :] = jnp.where(rest == 0, row.astype(F32), 0.0)


def digest(x_a, x_b, sel_a, sel_b, gain_row, average, w_sort_t, settings):
    npl, seqs_a, seqs_b, devices, capacity, _, _, sizes, _, _ = settings
    width = x_a.shape[1]
    tile = 2 * TILE if x_a.shape[0] % (2 * TILE) == 0 and x_b.shape[0] % (2 * TILE) == 0 else TILE
    tiles_a = x_a.shape[0] // tile
    tiles_b = x_b.shape[0] // tile
    rows = x_a.shape[0] + x_b.shape[0]
    picks = average.shape[0]
    height = -(-picks // 8) * 8 + 8
    units = rows // UNIT
    ints = lambda n: jax.ShapeDtypeStruct((n,), jnp.int32)
    return pl.pallas_call(
        functools.partial(digest_kernel, tiles_a, settings),
        grid=(tiles_a + tiles_b,),
        in_specs=[
            SMEM,
            SMEM,
            pl.BlockSpec((tile, width), lambda i: (jnp.minimum(i, tiles_a - 1), 0)),
            pl.BlockSpec((tile, width), lambda i: (jnp.maximum(i - tiles_a, 0), 0)),
            whole((1, width)),
            whole(average.shape),
            whole(w_sort_t.shape),
        ],
        out_specs=[rows_of(tile, width), whole((picks, width)), whole((devices, height, 128))]
        + [SMEM] * 5,
        out_shape=[
            jax.ShapeDtypeStruct((rows, width), BF16),
            jax.ShapeDtypeStruct((picks, width), F32),
            jax.ShapeDtypeStruct((devices, height, 128), F32),
        ]
        + [ints(n) for n in (units, units, units, units, 2)],
        scratch_shapes=[
            pltpu.VMEM((units, width), F32),
            pltpu.SMEM((devices * capacity,), jnp.int32),
            pltpu.SMEM((devices * sum(sizes),), jnp.int32),
            pltpu.SMEM((devices,), jnp.int32),
            pltpu.SMEM((picks,), jnp.int32),
            pltpu.SMEM((2 * devices,), jnp.int32),
        ],
        compiler_params=params(),
        cost_estimate=cost(rows * width * 10, rows * width * 4),
        name="digest",
    )(sel_a, sel_b, x_a, x_b, gain_row, average, w_sort_t)


def pack_kernel(devices, capacity, first, spare, table_ref, x_ref, *rest):
    outs = rest[: 1 if first == capacity else 2]
    held, sems = rest[len(outs) :]
    sizes = [first, capacity - first]
    copies = []
    for part, out_ref in enumerate(outs):
        size = sizes[part]
        base = part * devices * first
        for r in range(devices):
            for slot in range(size):
                unit = jnp.maximum(table_ref[r * capacity + part * first + slot], 0)
                src = pl.ds(pl.multiple_of(unit * UNIT, UNIT), UNIT)
                at = (base + r * size + slot) * UNIT
                held[at : at + UNIT, :] = x_ref[src, :]
            at = (base + r * size) * UNIT
            copy = pltpu.make_async_copy(
                held.at[pl.ds(at, size * UNIT)],
                out_ref.at[pl.ds(r * (size * UNIT + part * spare), size * UNIT)],
                sems.at[part * devices + r],
            )
            copy.start()
            copies.append(copy)
    for copy in copies:
        copy.wait()


def pack(table, x, devices, capacity, first, spare):
    width = x.shape[1]
    sizes = [first] if first == capacity else [first, capacity - first]
    return pl.pallas_call(
        functools.partial(pack_kernel, devices, capacity, first, spare),
        in_specs=[SMEM, VMEM],
        out_specs=[HBM] * len(sizes),
        out_shape=[
            jax.ShapeDtypeStruct((devices * (n * UNIT + i * spare), width), BF16)
            for i, n in enumerate(sizes)
        ],
        scratch_shapes=[
            pltpu.VMEM((devices * capacity * UNIT, width), BF16),
            pltpu.SemaphoreType.DMA((len(sizes) * devices,)),
        ],
        compiler_params=limit(62),
        cost_estimate=cost(0, x.size * 6),
        name="pack",
    )(table, x)


def arrange_kernel(units_a, perm_ref, x_ref, cota_ref, cotb_ref, xp_ref, cotp_ref):
    def body(pos, carry):
        unit = perm_ref[pos]
        at = pl.ds(pl.multiple_of(pos * UNIT, UNIT), UNIT)
        xp_ref[at, :] = x_ref[pl.ds(pl.multiple_of(unit * UNIT, UNIT), UNIT), :]

        @pl.when(unit < units_a)
        def _():
            cotp_ref[at, :] = cota_ref[pl.ds(pl.multiple_of(unit * UNIT, UNIT), UNIT), :]

        @pl.when(unit >= units_a)
        def _():
            src = pl.ds(pl.multiple_of((unit - units_a) * UNIT, UNIT), UNIT)
            cotp_ref[at, :] = cotb_ref[src, :]

        return carry

    lax.fori_loop(0, x_ref.shape[0] // UNIT, body, 0)


def arrange(perm, x, cot_a, cot_b):
    like = jax.ShapeDtypeStruct(x.shape, BF16)
    return pl.pallas_call(
        functools.partial(arrange_kernel, cot_a.shape[0] // UNIT),
        in_specs=[SMEM, VMEM, VMEM, VMEM],
        out_specs=[VMEM, VMEM],
        out_shape=[like, like],
        compiler_params=limit(16),
        cost_estimate=cost(0, x.size * 8),
        name="arrange",
    )(perm, x, cot_a, cot_b)


def restore_kernel(perm_ref, out_ref, outa_ref, outb_ref):
    units_a = outa_ref.shape[0] // UNIT

    def body(pos, carry):
        unit = perm_ref[pos]
        at = pl.ds(pl.multiple_of(pos * UNIT, UNIT), UNIT)

        @pl.when(unit < units_a)
        def _():
            outa_ref[pl.ds(pl.multiple_of(unit * UNIT, UNIT), UNIT), :] = out_ref[at, :]

        @pl.when(unit >= units_a)
        def _():
            dst = pl.ds(pl.multiple_of((unit - units_a) * UNIT, UNIT), UNIT)
            outb_ref[dst, :] = out_ref[at, :]

        return carry

    lax.fori_loop(0, out_ref.shape[0] // UNIT, body, 0)


def restore(perm, out, rows_a):
    rows, width = out.shape
    return pl.pallas_call(
        restore_kernel,
        in_specs=[SMEM, VMEM],
        out_specs=[VMEM, VMEM],
        out_shape=[
            jax.ShapeDtypeStruct((rows_a, width), BF16),
            jax.ShapeDtypeStruct((rows - rows_a, width), BF16),
        ],
        compiler_params=limit(16),
        cost_estimate=cost(0, out.size * 4),
        name="restore",
    )(perm, out)


def project_kernel(x_ref, gain_ref, w_ref, proj_ref):
    x = x_ref[...].astype(F32)
    proj_ref[...] = dot((x * inverse_norm(x) * gain_ref[...]).astype(BF16), w_ref[...]).astype(BF16)


def project(x, gain_row, w_qkv):
    rows, width = x.shape
    wide = w_qkv.shape[1]
    return pl.pallas_call(
        project_kernel,
        grid=(rows // TILE,),
        in_specs=[rows_of(TILE, width), whole((1, width)), whole((width, wide))],
        out_specs=rows_of(TILE, wide),
        out_shape=jax.ShapeDtypeStruct((rows, wide), BF16),
        compiler_params=params(),
        cost_estimate=cost(2 * rows * width * wide, rows * (width + wide) * 2),
        name="project",
    )(x, gain_row, w_qkv)


def log_sum(values, axis):
    top = jnp.max(values, axis=axis, keepdims=True)
    return top + jnp.log(jnp.sum(jnp.exp(values - top), axis=axis, keepdims=True))


def sinkhorn_kernel(logits_ref, picked_ref, weight_ref):
    state = logits_ref[...]
    for _ in range(SINK_ITERS):
        state = state - log_sum(state, 2)
        state = state - log_sum(state, 1)
    count = state.shape[1]
    weight = count * jnp.sum(jnp.exp(state) * picked_ref[...], axis=2, keepdims=True)
    weight_ref[...] = jnp.broadcast_to(weight, weight_ref.shape)


def sinkhorn(logits, picked):
    seqs, count, _ = logits.shape
    return pl.pallas_call(
        sinkhorn_kernel,
        out_shape=jax.ShapeDtypeStruct((seqs, count, 128), F32),
        cost_estimate=cost(logits.size * 100, logits.size * 32),
        name="sinkhorn",
    )(logits, picked)


def exact(a, b, dims=NN):
    return lax.dot_general(
        a, b, dims, precision=lax.Precision.HIGHEST, preferred_element_type=F32
    )


def sort_back_kernel(
    npl, seqs_a, lengths, tall, me_ref, perm_ref, logits_ref, picked_ref, units_ref, wsort_ref, gain_ref,
    means_ref, arrived, token_ref, small_ref, spread_ref, kept, letters, sems,
):
    seqs, blocks, _ = logits_ref.shape
    devices = blocks // npl
    picks = means_ref.shape[0]
    extra = letters.shape[1]
    height = arrived.shape[0] // devices
    copies = []
    for d in range(devices):
        source = arrived.at[pl.ds(d * height + tall, extra), pl.ds(0, 128)]
        copies.append(pltpu.make_async_copy(source, letters.at[d], sems.at[d]))
    for copy in copies:
        copy.start()
    state = logits_ref[...]
    for step in range(SINK_ITERS):
        state = state - log_sum(state, 2)
        kept[2 * step] = jnp.exp(state)
        state = state - log_sum(state, 1)
        kept[2 * step + 1] = jnp.exp(state)
    for copy in copies:
        copy.wait()
    rows = seqs * blocks
    line = lax.broadcasted_iota(jnp.int32, (rows, 128), 0)
    lane = lax.broadcasted_iota(jnp.int32, (rows, 128), 1)
    own_lane = line // blocks * npl + line % npl
    device = (line // npl) % devices
    table = jnp.zeros((rows, 128), F32)
    for d in range(devices):
        table = jnp.where(device == d, letters[d, 0:1, :].astype(F32), table)
    gw = jnp.sum(jnp.where(lane == own_lane, table, 0.0), axis=1, keepdims=True)
    grad = blocks * picked_ref[...] * gw.reshape(seqs, blocks, 1) * kept[2 * SINK_ITERS - 1]
    for step in reversed(range(SINK_ITERS)):
        grad = grad - kept[2 * step + 1] * jnp.sum(grad, axis=1, keepdims=True)
        grad = grad - kept[2 * step] * jnp.sum(grad, axis=2, keepdims=True)
    grad = (grad * (1.0 / SOFTMAX_HEAT)).reshape(rows, blocks)
    units = units_ref[...].astype(F32)
    small_ref[:blocks, :] = exact(grad, units, TN)
    g_unit = exact(grad, wsort_ref[...].astype(F32))
    both = g_unit * units
    both = both - units * units * jnp.mean(both, axis=-1, keepdims=True)
    row = jnp.sum(both, axis=0, keepdims=True) / gain_ref[...]
    first = lax.broadcasted_iota(jnp.int32, (small_ref.shape[0] - blocks, units.shape[1]), 0) == 0
    small_ref[blocks:, :] = jnp.where(first, row, 0.0)
    line = lax.broadcasted_iota(jnp.int32, (picks, rows), 0)
    lane = lax.broadcasted_iota(jnp.int32, (picks, rows), 1)
    mine = lane == line // npl * blocks + me_ref[0] * npl + line % npl
    g_own = exact(jnp.where(mine, 1.0, 0.0), g_unit)
    summary = means_ref[...] * gain_ref[...]
    rs = inverse_norm(summary)
    g_summary = rs * (
        g_own - summary * (rs * rs) * jnp.mean(g_own * summary, axis=-1, keepdims=True)
    )
    count_a = seqs_a * npl
    places = spread_ref.shape[0]
    line = lax.broadcasted_iota(jnp.int32, (places, picks), 0)
    lane = lax.broadcasted_iota(jnp.int32, (places, picks), 1)
    unit = jnp.zeros((places, picks), jnp.int32)
    for pos in range(places):
        unit = jnp.where(line == pos, perm_ref[pos], unit)
    block = jnp.where(unit < 2 * count_a, unit // 2, unit - count_a)
    share = jnp.where(lane < count_a, 1.0 / lengths[0], 1.0 / lengths[1])
    spread_ref[...] = exact(jnp.where(lane == block, share, 0.0), g_summary)


def sort_back(
    me, perm, logits, picked, units, w_sort_t, gain, means, arrived, npl, seqs_a, lengths, tall, extra, token
):
    seqs, blocks, _ = logits.shape
    width = means.shape[1]
    return pl.pallas_call(
        functools.partial(sort_back_kernel, npl, seqs_a, lengths, tall),
        in_specs=[SMEM, SMEM] + [VMEM] * 6 + [ANY, ANY],
        out_specs=[VMEM, VMEM],
        out_shape=[
            jax.ShapeDtypeStruct((blocks + 8, width), F32),
            jax.ShapeDtypeStruct((perm.shape[0], width), F32),
        ],
        scratch_shapes=[
            pltpu.VMEM((2 * SINK_ITERS,) + logits.shape, F32),
            pltpu.VMEM((blocks // npl, extra, 128), BF16),
            pltpu.SemaphoreType.DMA((blocks // npl,)),
        ],
        compiler_params=limit(24),
        cost_estimate=cost(logits.size * 200, logits.size * 32),
        name="sort_back",
    )(me, perm, logits, picked, units, w_sort_t, gain, means, arrived, token)


def head_masks(rows):
    lane = lax.broadcasted_iota(jnp.int32, (rows, HALF), 1) // (HALF // PER_HALF)
    return [lane == h for h in range(PER_HALF)]


def stack_heads(values, masks):
    zero = jnp.zeros_like(values)
    return jnp.concatenate([jnp.where(m, values, zero) for m in masks], axis=0)


def unstack_heads(values, masks):
    total = None
    for h, m in enumerate(masks):
        part = jnp.where(m, values[h * GROUP : (h + 1) * GROUP], 0.0)
        total = part if total is None else total + part
    return total


def repeat_heads(values):
    return jnp.concatenate([values] * PER_HALF, axis=0)


class Mover:
    def __init__(self, sems):
        self.sems, self.used, self.out = sems, 0, []

    def start(self, source, target):
        copy = pltpu.make_async_copy(source, target, self.sems.at[self.used])
        self.used += 1
        copy.start()
        return copy

    def store(self, source, target):
        self.out.append(self.start(source, target))

    def finish(self):
        for copy in self.out:
            copy.wait()


BATCH = 4


def forward_kernel(first_group, groups, recvs, prior, final, *refs):
    refs = list(refs)
    take = lambda n: [refs.pop(0) for _ in range(n)]
    far_ref, kinds_ref, core_ref = take(3)
    recv_hbm = take(recvs)
    x_hbm, cot_hbm, proj_hbm, wrow_hbm, mask_ref, gain1_ref, gain2_ref = take(7)
    wqkv_hbm, wout_hbm, wup_hbm, wdown_hbm, _ = take(5)
    prior_refs = take(2) if prior else []
    if prior:
        take(6)
    out_hbm, gmid_hbm, gatt_hbm, prob_hbm, farx_hbm, farkv_hbm = take(6)
    if final:
        keep_hbm, give_hbm = take(2)
    else:
        up_hbm, down_hbm = take(2)
    x_ref, cot_ref, proj_ref, wrow_ref, wqkv_ref, wout_ref, wup_ref, wdown_ref = take(8)
    out_ref, gmid_ref, gatt_ref, prob_ref, farx_ref, farkv_ref, attended = take(7)
    one_ref, two_ref = take(2)
    if prior:
        up_prior, down_prior = take(2)
    (sems,) = take(1)
    move = Mover(sems)
    rows = groups * GROUP
    width = x_ref.shape[1]
    ff = wup_ref.shape[1]
    base = first_group
    here = pl.ds(first_group * GROUP, rows)
    rows_one = recv_hbm[0].shape[0]
    far_sem = sems.at[sems.shape[0] - 1]
    for u in range(rows // UNIT):
        row = far_ref[2 * base + u]
        dst = farx_ref.at[pl.ds(u * UNIT, UNIT)]

        def bring(ref, row, dst=dst):
            src = ref.at[pl.ds(pl.multiple_of(row, 16), UNIT)]
            pltpu.make_async_copy(src, dst, far_sem).start()

        if recvs == 1:
            bring(recv_hbm[0], row)
        else:
            pl.when(row < rows_one)(lambda row=row, bring=bring: bring(recv_hbm[0], row))
            pl.when(row >= rows_one)(lambda row=row, bring=bring: bring(recv_hbm[1], row - rows_one))
    got_wqkv = move.start(wqkv_hbm, wqkv_ref)
    got_proj = move.start(proj_hbm.at[here], proj_ref)
    got_wrow = move.start(wrow_hbm.at[here], wrow_ref)
    got_x = move.start(x_hbm.at[here], x_ref)
    got_wout = move.start(wout_hbm, wout_ref)
    got_cot = move.start(cot_hbm.at[here], cot_ref)
    got_up = move.start(wup_hbm, wup_ref)
    got_down = move.start(wdown_hbm, wdown_ref)
    if prior:
        got_prior = [
            move.start(prior_refs[0], up_prior),
            move.start(prior_refs[1], down_prior),
        ]

    pltpu.make_async_copy(farx_ref, farx_ref, far_sem).wait()
    move.store(farx_ref, farx_hbm.at[here])
    far = farx_ref[...].astype(F32)
    far = (far * inverse_norm(far) * gain1_ref[...]).astype(BF16)
    got_wqkv.wait()
    farkv_ref[...] = dot(far, wqkv_ref[:, width:]).astype(BF16)
    move.store(farkv_ref, farkv_hbm.at[here])
    masks16 = head_masks(GROUP)
    head_scale = (width // HEADS) ** -0.5
    boundary = kinds_ref[1 if prior else 0]
    got_proj.wait()
    got_wrow.wait()
    for first in range(0, groups, BATCH):
        work = [
            (i, half) for i in range(first, min(first + BATCH, groups)) for half in range(width // HALF)
        ]
        scores, vals = [], []
        for i, half in work:
            at = slice(i * GROUP, (i + 1) * GROUP)
            lo = half * HALF
            q = proj_ref[at, lo : lo + HALF] * jnp.asarray(head_scale, BF16)
            keys = jnp.concatenate(
                [proj_ref[at, width + lo : width + lo + HALF], farkv_ref[at, lo : lo + HALF]], axis=0
            )
            vals.append(
                jnp.concatenate(
                    [
                        proj_ref[at, 2 * width + lo : 2 * width + lo + HALF],
                        farkv_ref[at, width + lo : width + lo + HALF],
                    ],
                    axis=0,
                )
            )
            which = jnp.where(base + i < boundary, 0, 1)
            scores.append(dot(stack_heads(q, masks16), keys, NT) + repeat_heads(mask_ref[which]))
        tops = [jnp.max(v, axis=1, keepdims=True) for v in scores]
        weights = [jnp.exp(v - t) for v, t in zip(scores, tops)]
        sums = [jnp.sum(v, axis=1, keepdims=True) for v in weights]
        probs = [v * (1.0 / t) for v, t in zip(weights, sums)]
        mixed = []
        for (i, half), prob, value in zip(work, probs, vals):
            at = slice(i * GROUP, (i + 1) * GROUP)
            prob_ref[i, half] = prob.astype(BF16)
            mixed.append(dot((prob * repeat_heads(wrow_ref[at, :])).astype(BF16), value))
        for (i, half), value in zip(work, mixed):
            at = slice(i * GROUP, (i + 1) * GROUP)
            lo = half * HALF
            attended[at, lo : lo + HALF] = unstack_heads(value, masks16).astype(BF16)
    move.store(prob_ref, prob_hbm.at[pl.ds(first_group, groups)])

    got_x.wait()
    got_wout.wait()
    att = attended[...]
    middle = x_ref[...].astype(F32) + dot(att, wout_ref[...])
    r2 = inverse_norm(middle)
    scaled = middle * r2
    second = (scaled * gain2_ref[...]).astype(BF16)
    got_cot.wait()
    cot = cot_ref[...]
    cot_t = cot.T
    second_t = second.T
    got_up.wait()
    got_down.wait()
    if prior:
        for copy in got_prior:
            copy.wait()

    def total(value, old, lanes):
        return value + old[:, lanes].astype(F32) if prior else value

    edge = ff // 2

    pending = []

    def send(ref, half, lines):
        sem = sems.at[move.used]
        move.used += 1
        for which, hbm in ((half, keep_hbm), (1 - half, give_hbm)):
            copy = pltpu.make_async_copy(ref.at[lines], hbm.at[lines], sem)
            pl.when(core_ref[0] == which)(copy.start)
        pending.append(copy)

    def put_up(c, value):
        lanes = slice(c, c + width)
        if not final:
            one_ref[:, lanes] = value.astype(BF16)
            at = (slice(None), pl.ds(c, width))
            move.store(one_ref.at[at], up_hbm.at[at])
            return
        ref, at = (one_ref, c) if c < edge else (two_ref, c - edge)
        ref[at : at + width, :] = total(value, up_prior if prior else None, lanes).astype(BF16)
        send(ref, 0 if c < edge else 1, pl.ds(at, width))

    def put_down(c, value):
        lanes = slice(c, c + width)
        if not final:
            two_ref[:, lanes] = value.astype(BF16)
            at = (slice(None), pl.ds(c, width))
            move.store(two_ref.at[at], down_hbm.at[at])
            return
        ref, at = (one_ref, c) if c < edge else (two_ref, c - edge)
        at += edge + width // 2
        ref[at : at + width, :] = total(value, down_prior if prior else None, lanes).T.astype(BF16)
        send(ref, 0 if c < edge else 1, pl.ds(at, width))

    def put_out(value):
        if not final:
            one_ref[:, ff:] = value.astype(BF16)
            at = (slice(None), pl.ds(ff, width))
            move.store(one_ref.at[at], up_hbm.at[at])
            return
        value = total(value, up_prior if prior else None, slice(ff, ff + width)).astype(BF16)
        lines = slice(edge, edge + width // 2)
        one_ref[lines, :] = value[: width // 2]
        two_ref[lines, :] = value[width // 2 :]
        send(one_ref, 0, pl.ds(edge, width // 2))
        send(two_ref, 1, pl.ds(edge, width // 2))

    result = middle
    back = jnp.zeros((rows, width), F32)
    c0 = 0.7978845608028654
    c1 = 0.044715
    for c in range(0, ff, width):
        hidden = dot(second, wup_ref[:, c : c + width])
        grad = dot(cot, wdown_ref[c : c + width, :], NT)
        square = hidden * hidden
        t = jnp.tanh(hidden * (c0 + (c0 * c1) * square))
        left = 0.5 + 0.5 * t
        active = (hidden * left).astype(BF16)
        slope = left + (0.5 * hidden) * (1.0 - t * t) * (c0 + (3.0 * c0 * c1) * square)
        grad = (grad * slope).astype(BF16)
        result = result + dot(active, wdown_ref[c : c + width, :])
        back = back + dot(grad, wup_ref[:, c : c + width], NT)
        put_down(c, dot(cot_t, active))
        put_up(c, dot(second_t, grad))
    out_ref[...] = result.astype(BF16)
    move.store(out_ref, out_hbm.at[here])
    e = back * gain2_ref[...]
    inner = jnp.mean(e * scaled, axis=-1, keepdims=True)
    grad_middle = cot.astype(F32) + r2 * (e - scaled * inner)
    branch = grad_middle.astype(BF16)
    gmid_ref[...] = branch
    move.store(gmid_ref, gmid_hbm.at[here])
    put_out(dot(att.T, branch))
    gatt_ref[...] = dot(branch, wout_ref[...], NT).astype(BF16)
    move.store(gatt_ref, gatt_hbm.at[here])
    for copy in pending:
        copy.wait()
    move.finish()


def forward(
    far_rows, kinds, core, recv, x, cot, proj, wrow, mask, gain1, gain2, w_qkv, w_out, w_up, w_down,
    first_group, groups, prior, final, token,
):
    rows, width = x.shape
    ff = w_up.shape[1]
    halves = width // HALF
    count = groups * GROUP
    like = lambda wide, kind=BF16: jax.ShapeDtypeStruct((rows, wide), kind)
    probs = jax.ShapeDtypeStruct((rows // GROUP, halves, PER_HALF * GROUP, 2 * GROUP), BF16)
    part = ff + width // 2
    if final:
        tails = [(part, width), (part, width)]
    else:
        tails = [(width, ff + width), (width, ff)]
    in_specs = [SMEM] * 3 + [ANY] * (len(recv) + 4) + [VMEM] * 3 + [ANY] * 5
    operands = [far_rows, kinds, core, *recv, x, cot, proj, wrow, mask, gain1, gain2]
    operands += [w_qkv, w_out, w_up, w_down, token]
    scratch = [
        pltpu.VMEM((count, width), BF16),
        pltpu.VMEM((count, width), BF16),
        pltpu.VMEM((count, 3 * width), BF16),
        pltpu.VMEM((count, 2 * GROUP), F32),
    ]
    scratch += [pltpu.VMEM(w.shape, BF16) for w in (w_qkv, w_out, w_up, w_down)]
    scratch += [pltpu.VMEM((count, width), BF16)] * 3
    scratch += [pltpu.VMEM((groups,) + probs.shape[1:], BF16)]
    scratch += [pltpu.VMEM((count, n * width), BF16) for n in (1, 2, 1)]
    scratch += [pltpu.VMEM(shape, BF16) for shape in tails]
    aliases = {}
    if prior is not None:
        streams, sums = prior
        in_specs += [ANY, ANY] + [ANY] * 6
        operands += list(sums)
        aliases = {len(operands) + i: i for i in range(6)}
        operands += list(streams)
        scratch += [pltpu.VMEM((width, ff + width), BF16), pltpu.VMEM((width, ff), BF16)]
    scratch += [pltpu.SemaphoreType.DMA((40,))]
    out = pl.pallas_call(
        functools.partial(
            forward_kernel, first_group, groups, len(recv), prior is not None, final
        ),
        in_specs=in_specs,
        out_specs=[ANY] * 8,
        out_shape=[like(width), like(width), like(width), probs, like(width), like(2 * width)]
        + [jax.ShapeDtypeStruct(shape, BF16) for shape in tails],
        scratch_shapes=scratch,
        input_output_aliases=aliases,
        compiler_params=pltpu.CompilerParams(vmem_limit_bytes=VMEM_LIMIT),
        cost_estimate=cost(1.0e9 * groups, 1e6 * groups),
        name="forward",
    )(*operands)
    return out[:6], out[6:]


def backward_kernel(first_group, groups, prior, chunks, letter, *refs):
    refs = list(refs)
    take = lambda n: [refs.pop(0) for _ in range(n)]
    ret_rows, place_ref = take(2)
    proj_hbm, farkv_hbm, gatt_hbm, prob_hbm, wrow_hbm, wqkv_hbm = take(6)
    if prior:
        (prior_gw,) = take(1)
        take(2)
    take(1)
    dproj_hbm, dfar_hbm, gw_ref = take(3)
    ret_hbm = take(chunks)
    proj_ref, farkv_ref, gatt_ref, prob_ref, wrow_ref, wqkv_ref = take(6)
    dproj_ref, dfar_ref = take(2)
    ret_refs = take(chunks)
    (sems,) = take(1)
    move = Mover(sems)
    rows = groups * GROUP
    width = gatt_ref.shape[1]
    start = first_group * GROUP
    batches = [(first, min(first + BATCH, groups)) for first in range(0, groups, BATCH)]
    loads = []
    for low, high in batches:
        at = pl.ds(low * GROUP, (high - low) * GROUP)
        there = pl.ds(start + low * GROUP, (high - low) * GROUP)
        loads.append(
            [
                move.start(hbm.at[there], ref.at[at])
                for hbm, ref in (
                    (proj_hbm, proj_ref),
                    (farkv_hbm, farkv_ref),
                    (gatt_hbm, gatt_ref),
                    (wrow_hbm, wrow_ref),
                )
            ]
            + [
                move.start(
                    prob_hbm.at[pl.ds(first_group + low, high - low)],
                    prob_ref.at[pl.ds(low, high - low)],
                )
            ]
        )
    got_wqkv = move.start(wqkv_hbm, wqkv_ref)
    masks16 = head_masks(GROUP)
    head_scale = (width // HEADS) ** -0.5
    far_lane = lax.broadcasted_iota(jnp.int32, (GROUP // UNIT, 2 * GROUP), 1) >= GROUP
    for (low, high), copies in zip(batches, loads):
        for copy in copies:
            copy.wait()
        work = [(i, half) for i in range(low, high) for half in range(width // HALF)]
        stacks, products = [], []
        for i, half in work:
            at = slice(i * GROUP, (i + 1) * GROUP)
            lo = half * HALF
            vals = jnp.concatenate(
                [
                    proj_ref[at, 2 * width + lo : 2 * width + lo + HALF],
                    farkv_ref[at, width + lo : width + lo + HALF],
                ],
                axis=0,
            )
            up = stack_heads(gatt_ref[at, lo : lo + HALF], masks16)
            stacks.append(up)
            products.append(prob_ref[i, half].astype(F32) * dot(up, vals, NT))
        for i in range(low, high):
            summed = jnp.zeros((GROUP, 2 * GROUP), F32)
            for (j, _), prod in zip(work, products):
                if j == i:
                    for h in range(PER_HALF):
                        summed = summed + prod[h * GROUP : (h + 1) * GROUP]
            pair = jnp.sum(summed.reshape(GROUP // UNIT, UNIT, 2 * GROUP), axis=1)
            pair = jnp.sum(jnp.where(far_lane, pair, 0.0), axis=1, keepdims=True)
            gw_ref[i] = jnp.broadcast_to(pair, (GROUP // UNIT, 128))
        scales = [repeat_heads(wrow_ref[i * GROUP : (i + 1) * GROUP, :]) for i, _ in work]
        products = [v * s for v, s in zip(products, scales)]
        totals = [jnp.sum(v, axis=1, keepdims=True) for v in products]
        for (i, half), up, prod, scale, total in zip(work, stacks, products, scales, totals):
            at = slice(i * GROUP, (i + 1) * GROUP)
            lo = half * HALF
            prob = prob_ref[i, half].astype(F32)
            ds = (prod - prob * total).astype(BF16)
            mixed = (prob * scale).astype(BF16)
            q = stack_heads(
                proj_ref[at, lo : lo + HALF] * jnp.asarray(head_scale, BF16), masks16
            )
            keys = jnp.concatenate(
                [proj_ref[at, width + lo : width + lo + HALF], farkv_ref[at, lo : lo + HALF]], axis=0
            )
            dq = unstack_heads(dot(ds, keys), masks16) * head_scale
            dk = dot(ds, q, TN).astype(BF16)
            dv = dot(mixed, up, TN).astype(BF16)
            dproj_ref[at, lo : lo + HALF] = dq.astype(BF16)
            dproj_ref[at, width + lo : width + lo + HALF] = dk[:GROUP]
            dproj_ref[at, 2 * width + lo : 2 * width + lo + HALF] = dv[:GROUP]
            dfar_ref[at, lo : lo + HALF] = dk[GROUP:]
            dfar_ref[at, width + lo : width + lo + HALF] = dv[GROUP:]
        at = pl.ds(low * GROUP, (high - low) * GROUP)
        there = pl.ds(start + low * GROUP, (high - low) * GROUP)
        move.store(dproj_ref.at[at], dproj_hbm.at[there])
        move.store(dfar_ref.at[at], dfar_hbm.at[there])

    got_wqkv.wait()
    grad = dot(dfar_ref[...], wqkv_ref[:, width:], NT).astype(BF16)
    for u in range(rows // UNIT):
        row = ret_rows[2 * first_group + u]
        edge = 0
        for ret_ref in ret_refs:
            value = grad[u * UNIT : (u + 1) * UNIT]

            def put(ret_ref=ret_ref, edge=edge, value=value):
                ret_ref[pl.ds(pl.multiple_of(row - edge, 16), UNIT), :] = value

            if chunks == 1:
                put()
            else:
                pl.when(jnp.logical_and(row >= edge, row < edge + ret_ref.shape[0]))(put)
            edge += ret_ref.shape[0]
    if letter:
        count_a, count_b, devices, extra = letter
        lane = lax.broadcasted_iota(jnp.int32, (1, 128), 1)
        row = jnp.zeros((1, 128), F32)

        def pair_at(at):
            if not prior:
                return gw_ref[at]
            early = prior_gw.shape[0]
            one = prior_gw[jnp.minimum(at, early - 1)]
            two = gw_ref[jnp.maximum(at - early, 0)]
            return jnp.where(at < early, one, two)

        for j in range(count_a + count_b):
            if j < count_a:
                both = pair_at(lax.shift_right_logical(place_ref[2 * j], 1))
                value = both[0:1] + both[1:2]
            else:
                pos = place_ref[count_a + j]
                both = pair_at(lax.shift_right_logical(pos, 1))
                value = jnp.where(lax.bitwise_and(pos, 1) == 0, both[0:1], both[1:2])
            row = jnp.where(lane == j, value, row)
        page = jnp.concatenate([row, jnp.zeros((1, width - 128), F32)], axis=1)
        line = lax.broadcasted_iota(jnp.int32, (extra, width), 0)
        page = jnp.where(line == 0, page, 0.0).astype(BF16)
        ret_ref = ret_refs[-1]
        height = ret_ref.shape[0] // devices
        for d in range(devices):
            ret_ref[(d + 1) * height - extra : (d + 1) * height, :] = page
    for ret_ref, hbm in zip(ret_refs, ret_hbm):
        move.store(ret_ref, hbm)
    move.finish()


def backward(
    ret_rows, place, proj, farkv, gatt, prob, wrow, w_qkv, sizes, first_group, groups, prior, letter,
    token,
):
    rows, width = gatt.shape
    count = groups * GROUP
    in_specs = [SMEM, SMEM] + [ANY] * 6
    operands = [ret_rows, place, proj, farkv, gatt, prob, wrow, w_qkv]
    aliases = {}
    if prior is not None:
        dproj, dfar, gw = prior
        in_specs += [VMEM, ANY, ANY]
        aliases = {len(operands) + 1: 0, len(operands) + 2: 1}
        operands += [gw, dproj, dfar]
    in_specs += [ANY]
    operands += [token]
    batches = -(-groups // BATCH)
    return pl.pallas_call(
        functools.partial(
            backward_kernel, first_group, groups, prior is not None, len(sizes), letter
        ),
        in_specs=in_specs,
        out_specs=[ANY, ANY, VMEM] + [ANY] * len(sizes),
        out_shape=[
            jax.ShapeDtypeStruct((rows, 3 * width), BF16),
            jax.ShapeDtypeStruct((rows, 2 * width), BF16),
            jax.ShapeDtypeStruct((groups, GROUP // UNIT, 128), F32),
        ]
        + [jax.ShapeDtypeStruct((n, width), BF16) for n in sizes],
        scratch_shapes=[
            pltpu.VMEM((count, 3 * width), BF16),
            pltpu.VMEM((count, 2 * width), BF16),
            pltpu.VMEM((count, width), BF16),
            pltpu.VMEM((groups,) + prob.shape[1:], BF16),
            pltpu.VMEM((count, 2 * GROUP), F32),
            pltpu.VMEM(w_qkv.shape, BF16),
            pltpu.VMEM((count, 3 * width), BF16),
            pltpu.VMEM((count, 2 * width), BF16),
        ]
        + [pltpu.VMEM((n, width), BF16) for n in sizes]
        + [pltpu.SemaphoreType.DMA((7 * batches + 2 + len(sizes),))],
        input_output_aliases=aliases,
        compiler_params=pltpu.CompilerParams(vmem_limit_bytes=VMEM_LIMIT),
        cost_estimate=cost(0.4e9 * groups, 1e6 * groups),
        name="backward",
    )(*operands)


def qkv_kernel(
    core_ref, x_hbm, farx_hbm, dproj_hbm, dfar_hbm, gain1_ref, wqkv_hbm, token_ref,
    gn_hbm, keep_ref, give_ref, x_ref, farx_ref, dproj_ref, dfar_ref, wqkv_ref, gn_ref, near_t, far_t, sems,
):
    move = Mover(sems)
    rows, width = x_ref.shape
    wide = wqkv_ref.shape[1]
    size = min(512, rows)
    got_w = move.start(wqkv_hbm, wqkv_ref)
    loads = []
    for low in range(0, rows, size):
        at = pl.ds(low, size)
        loads.append(
            [
                move.start(hbm.at[at], ref.at[at])
                for hbm, ref in (
                    (x_hbm, x_ref),
                    (dproj_hbm, dproj_ref),
                    (farx_hbm, farx_ref),
                    (dfar_hbm, dfar_ref),
                )
            ]
        )
    got_w.wait()
    for low, copies in zip(range(0, rows, size), loads):
        at = slice(low, low + size)
        for copy in copies:
            copy.wait()
        x = x_ref[at, :].astype(F32)
        scaled = x * inverse_norm(x)
        near_t[:, at] = (scaled * gain1_ref[...]).astype(BF16).T
        far = farx_ref[at, :].astype(F32)
        far_t[:, at] = (far * inverse_norm(far) * gain1_ref[...]).astype(BF16).T
        grad = dot(dproj_ref[at, :], wqkv_ref[...], NT)
        gn_ref[at, :] = grad.astype(BF16)
        move.store(gn_ref.at[pl.ds(low, size)], gn_hbm.at[pl.ds(low, size)])
    grads = []
    for c in range(0, wide, width):
        value = dot(near_t[...], dproj_ref[:, c : c + width])
        if c:
            value = value + dot(far_t[...], dfar_ref[:, c - width : c])
        grads.append(value)

    half = wide // 2

    def write(ref, which):
        at = which * half
        while at < (which + 1) * half:
            block, line = divmod(at, width)
            count = min(width - line, (which + 1) * half - at)
            value = grads[block][line : line + count]
            ref[at - which * half : at - which * half + count, :] = value.astype(BF16)
            at += count

    @pl.when(core_ref[0] == 0)
    def _():
        write(keep_ref, 0)
        write(give_ref, 1)

    @pl.when(core_ref[0] == 1)
    def _():
        write(keep_ref, 1)
        write(give_ref, 0)

    move.finish()


def qkv_grads(core, x, farx, dproj, dfar, gain1, w_qkv, token):
    rows, width = x.shape
    wide = w_qkv.shape[1]
    half = wide // 2
    tall = lambda size: pltpu.VMEM((rows, size), BF16)
    return pl.pallas_call(
        qkv_kernel,
        in_specs=[SMEM] + [ANY] * 4 + [VMEM, ANY, ANY],
        out_specs=[ANY, VMEM, VMEM],
        out_shape=[
            jax.ShapeDtypeStruct((rows, width), BF16),
            jax.ShapeDtypeStruct((half, width), BF16),
            jax.ShapeDtypeStruct((half, width), BF16),
        ],
        scratch_shapes=[
            tall(width),
            tall(width),
            tall(wide),
            tall(2 * width),
            pltpu.VMEM(w_qkv.shape, BF16),
            tall(width),
            pltpu.VMEM((width, rows), BF16),
            pltpu.VMEM((width, rows), BF16),
            pltpu.SemaphoreType.DMA((5 * (rows // min(512, rows)) + 1,)),
        ],
        compiler_params=limit(62),
        cost_estimate=cost(10e9, 25e6),
        name="qkv_grads",
    )(core, x, farx, dproj, dfar, gain1, w_qkv, token)


def row_gradient(f, x):
    r1 = inverse_norm(x)
    scaled = x * r1
    return r1 * (f - scaled * jnp.mean(f * scaled, axis=-1, keepdims=True))


def base_kernel(x_ref, gmid_ref, gn_ref, gs_ref, gain1_ref, out_ref):
    rows, width = x_ref.shape
    spread = jnp.broadcast_to(gs_ref[...][:, None, :], (rows // UNIT, UNIT, width))
    f = (gn_ref[...].astype(F32) + spread.reshape(rows, width)) * gain1_ref[...]
    grad = gmid_ref[...].astype(F32) + row_gradient(f, x_ref[...].astype(F32))
    out_ref[...] = grad.astype(BF16)


def base_rows(x, gmid, gn, gs, gain1):
    rows, width = x.shape
    tile = 2 * TILE
    return pl.pallas_call(
        base_kernel,
        grid=(rows // tile,),
        in_specs=[
            rows_of(tile, width),
            rows_of(tile, width),
            rows_of(tile, width),
            rows_of(tile // UNIT, width),
            whole((1, width)),
        ],
        out_specs=rows_of(tile, width),
        out_shape=jax.ShapeDtypeStruct((rows, width), BF16),
        compiler_params=params(),
        cost_estimate=cost(rows * width * 20, rows * width * 8),
        name="base",
    )(x, gmid, gn, gs, gain1)


def last_kernel(sizes, extra, capacity, table_ref, place_ref, *refs):
    ret_refs = refs[: len(sizes)]
    x_ref, base_ref, gain1_ref, outa_ref, outb_ref, acc = refs[len(sizes) :]
    rows_a = outa_ref.shape[0]
    acc[...] = jnp.zeros_like(acc)

    begin = 0
    for index, (size, ret_ref) in enumerate(zip(sizes, ret_refs)):
        height = size * UNIT + (extra if index == len(sizes) - 1 else 0)

        def add(r, carry, size=size, ret_ref=ret_ref, begin=begin, height=height):
            for slot in range(size):
                unit = table_ref[r * capacity + begin + slot]

                @pl.when(unit >= 0)
                def _():
                    at = pl.ds(pl.multiple_of(unit * UNIT, UNIT), UNIT)
                    src = pl.ds(pl.multiple_of(r * height + slot * UNIT, 16), UNIT)
                    acc[at, :] += ret_ref[src, :].astype(F32)

            return carry

        lax.fori_loop(0, ret_ref.shape[0] // height, add, 0)
        begin += size

    def finish(out_ref, first):
        def body(u, carry):
            at = pl.ds(pl.multiple_of(place_ref[first + u] * UNIT, UNIT), UNIT)
            own = pl.ds(pl.multiple_of((first + u) * UNIT, UNIT), UNIT)
            f = acc[own, :] * gain1_ref[...]
            grad = base_ref[at, :].astype(F32) + row_gradient(f, x_ref[own, :].astype(F32))
            out_ref[pl.ds(pl.multiple_of(u * UNIT, UNIT), UNIT), :] = grad.astype(BF16)
            return carry

        lax.fori_loop(0, out_ref.shape[0] // UNIT, body, 0, unroll=2)

    finish(outa_ref, 0)
    finish(outb_ref, rows_a // UNIT)


def last(table, place, ret, sizes, extra, capacity, x, base, gain1, rows_a):
    rows, width = x.shape
    return pl.pallas_call(
        functools.partial(last_kernel, sizes, extra, capacity),
        in_specs=[SMEM, SMEM] + [VMEM] * (len(ret) + 3),
        out_specs=[VMEM, VMEM],
        out_shape=[
            jax.ShapeDtypeStruct((rows_a, width), BF16),
            jax.ShapeDtypeStruct((rows - rows_a, width), BF16),
        ],
        scratch_shapes=[pltpu.VMEM((rows, width), F32)],
        compiler_params=limit(24),
        cost_estimate=cost(rows * width * 20, rows * width * 12),
        name="last",
    )(table, place, *ret, x, base, gain1)


def bits_of(size):
    count = 0
    while (1 << count) < size:
        count += 1
    return count


def bit_of(axis, bit):
    return (lax.axis_index(axis) >> bit) & 1


def swap(values, axis, bit):
    size = lax.axis_size(axis)
    return lax.ppermute(values, axis, [(i, i ^ (1 << bit)) for i in range(size)])


def halve(values, axis, bit):
    half = values.shape[0] // 2
    mine = bit_of(axis, bit)
    keep = lax.dynamic_slice_in_dim(values, mine * half, half, 0)
    give = lax.dynamic_slice_in_dim(values, (1 - mine) * half, half, 0)
    return keep, give


def double(values, axis, bit):
    got = swap(values, axis, bit)
    return jnp.where(
        bit_of(axis, bit) == 0,
        jnp.concatenate([values, got], axis=0),
        jnp.concatenate([got, values], axis=0),
    )


def add(one, two):
    return (one.astype(F32) + two.astype(F32)).astype(BF16)


def reduce_any(values, order):
    for axis, bit in order:
        keep, give = halve(values, axis, bit)
        values = add(keep, swap(give, axis, bit))
    for axis, bit in reversed(order):
        values = double(values, axis, bit)
    return values


def tie(values, *tokens):
    return pl.pallas_call(
        lambda *refs: None,
        in_specs=[ANY] * (1 + len(tokens)),
        out_specs=ANY,
        out_shape=jax.ShapeDtypeStruct(values.shape, values.dtype),
        input_output_aliases={0: 0},
        name="tie",
    )(values, *tokens)


def fetch(sources, targets, sems):
    copies = [
        pltpu.make_async_copy(source, target, sems.at[i])
        for i, (source, target) in enumerate(zip(sources, targets))
    ]
    for copy in copies:
        copy.start()
    for copy in copies:
        copy.wait()


def halve_kernel(ranges, sources, bits_ref, *refs):
    count = 2 * (1 + max(r[4] for r in ranges))
    sems = refs[-1]
    outs = refs[2 * sources + 1 : 2 * sources + 1 + count]
    held = refs[2 * sources + 1 + count : -2]
    made = held[2 * sources :]
    fetch(refs[: 2 * sources], held, refs[-2])
    refs = held
    for source, first, count, bit, out, there in ranges:
        own, came = refs[2 * source], refs[2 * source + 1]
        half = count // 2
        keep = pl.multiple_of(first + bits_ref[bit] * half, 16)
        give = pl.multiple_of(first + (1 - bits_ref[bit]) * half, 16)
        for ref, line in ((made[2 * out], keep), (made[2 * out + 1], give)):
            rows = pl.ds(line, half)
            total = own[rows, :].astype(F32) + came[rows, :].astype(F32)
            ref[there : there + half, :] = total.astype(BF16)
    fetch(made, outs, sems)


def halve_step(ranges, bits, pairs, token):
    width = pairs[0][0].shape[1]
    count = 1 + max(r[4] for r in ranges)
    heights = [max(r[5] + r[2] // 2 for r in ranges if r[4] == out) for out in range(count)]
    shapes = [jax.ShapeDtypeStruct((n, width), BF16) for n in heights for _ in range(2)]
    flat = [v for pair in pairs for v in pair]
    out = pl.pallas_call(
        functools.partial(halve_kernel, ranges, len(pairs)),
        in_specs=[SMEM] + [HBM] * len(flat) + [ANY],
        out_specs=[HBM] * len(shapes),
        out_shape=shapes,
        scratch_shapes=[pltpu.VMEM(v.shape, BF16) for v in flat + shapes]
        + [pltpu.SemaphoreType.DMA((len(flat),)), pltpu.SemaphoreType.DMA((len(shapes),))],
        compiler_params=limit(62),
        cost_estimate=cost(0, 8 * sum(heights) * width),
        name="halve_step",
    )(jnp.stack([bit_of(*b) for b in bits]).astype(jnp.int32), *flat, token)
    return [(out[2 * i], out[2 * i + 1]) for i in range(count)]


def double_kernel(ranges, sources, tokens, bits_ref, *refs):
    count = 1 + max(r[0] for r in ranges)
    outs = refs[2 * sources + tokens : 2 * sources + tokens + count]
    held = refs[2 * sources + tokens + count : -1]
    fetch(refs[: 2 * sources], held, refs[-1])
    refs = held
    for source, first, count, bit, out, there in ranges:
        own, came = refs[2 * out], refs[2 * out + 1]
        half = count // 2
        keep = pl.multiple_of(first + bits_ref[bit] * half, 16)
        give = pl.multiple_of(first + (1 - bits_ref[bit]) * half, 16)
        outs[source][pl.ds(keep, half), :] = own[there : there + half, :]
        outs[source][pl.ds(give, half), :] = came[there : there + half, :]


def double_step(ranges, bits, pairs, *tokens):
    width = pairs[0][0].shape[1]
    count = 1 + max(r[0] for r in ranges)
    heights = [max(r[1] + r[2] for r in ranges if r[0] == source) for source in range(count)]
    flat = [v for pair in pairs for v in pair]
    return pl.pallas_call(
        functools.partial(double_kernel, ranges, len(pairs), len(tokens)),
        in_specs=[SMEM] + [ANY] * len(flat) + [ANY] * len(tokens),
        out_specs=[VMEM] * count,
        out_shape=[jax.ShapeDtypeStruct((n, width), BF16) for n in heights],
        scratch_shapes=[pltpu.VMEM(v.shape, BF16) for v in flat]
        + [pltpu.SemaphoreType.DMA((len(flat),))],
        compiler_params=limit(24),
        cost_estimate=cost(0, 4 * sum(heights) * width),
        name="double_step",
    )(jnp.stack([bit_of(*b) for b in bits]).astype(jnp.int32), *flat, *tokens)


AXIS_X, AXIS_Y, AXIS_Z0, AXIS_Z1 = ("dp", 1), ("blk", 0), ("blk", 1), ("blk", 2)


def places(half, width, ff):
    up, down, out, qkv = range(4)
    edge = ff // 2
    result = [
        (c, width, up, 0, half * edge + c) for c in range(0, edge, width)
    ]
    result.append((edge, width // 2, out, half * (width // 2), 0))
    result += [
        (edge + width // 2 + c, width, down, half * edge + c, 0) for c in range(0, edge, width)
    ]
    start = edge + width // 2 + edge
    total = 3 * width
    at = half * total // 2
    while at < (half + 1) * total // 2:
        block, line = divmod(at, width)
        count = min(width - line, (half + 1) * total // 2 - at)
        result.append((start + at - half * total // 2, count, qkv, line, block * width))
        at += count
    return result


def assemble_kernel(which, prior, width, ff, core_ref, values_ref, wup_ref, wqkv_ref, *refs):
    outs = refs[5 if prior else 0 :][:5]
    held, products, sems = refs[-3:]
    ones = jnp.ones((8, width), BF16)

    def write(half):
        copies = []
        seen = set()
        for i, (first, count, out, line, column) in enumerate(places(half, width, ff)):
            value = values_ref[first : first + count, :].astype(F32)
            held[first : first + count, :] = value
            copy = pltpu.make_async_copy(
                held.at[pl.ds(first, count)],
                outs[out].at[pl.ds(line, count), pl.ds(column, width)],
                sems.at[i],
            )
            copy.start()
            copies.append(copy)
            if out in (0, 3):
                weights = (wup_ref if out == 0 else wqkv_ref)[line : line + count, column : column + width]
                part = weights.astype(F32) * value
                if out in seen:
                    products[out // 3, line : line + count, :] += part
                else:
                    products[out // 3, line : line + count, :] = part
                    if count < width:
                        rest = slice(0, line) if line else slice(count, width)
                        products[out // 3, rest, :] = jnp.zeros((width - count, width), F32)
                    seen.add(out)
        for out, at in ((3, 0), (0, 1)):
            value = products[out // 3]
            high = value.astype(BF16)
            low = (value - high.astype(F32)).astype(BF16)
            row = (dot(ones, high, NT) + dot(ones, low, NT))[0:1]
            outs[4][at : at + 1, :] = row + refs[0][at : at + 1, :] if prior else row
        for copy in copies:
            copy.wait()

    outs[4][...] = jnp.zeros_like(outs[4])

    @pl.when(core_ref[0] == which)
    def _():
        write(0)

    @pl.when(core_ref[0] != which)
    def _():
        write(1)


def assemble(core, which, values, w_up, w_qkv, width, ff, prior):
    shapes = [(width, ff), (ff, width), (width, width), (width, 3 * width), (8, width)]
    operands = [core, values, w_up, w_qkv]
    if prior is not None:
        operands += [prior[4], *prior[:4]]
    most = max(len(places(half, width, ff)) for half in (0, 1))
    return pl.pallas_call(
        functools.partial(assemble_kernel, which, prior is not None, width, ff),
        in_specs=[SMEM] + [VMEM] * (3 if prior is None else 4) + [ANY] * (0 if prior is None else 4),
        out_specs=[ANY] * 4 + [VMEM],
        out_shape=[jax.ShapeDtypeStruct(shape, F32) for shape in shapes],
        scratch_shapes=[
            pltpu.VMEM(values.shape, F32),
            pltpu.VMEM((2, width, width), F32),
            pltpu.SemaphoreType.DMA((most,)),
        ],
        input_output_aliases={} if prior is None else {5 + i: i for i in range(4)},
        compiler_params=limit(20),
        cost_estimate=cost(0, values.size * 6),
        name="assemble",
    )(*operands)


def exchange(values, devices):
    shape = values.shape
    parts = values.reshape(devices, shape[0] // devices, *shape[1:])
    return lax.all_to_all(parts, "blk", split_axis=0, concat_axis=0, tiled=True).reshape(shape)


def per_device(
    x_a, x_b, sel_a, sel_b, gain_one, w_qkv, w_out, w_sort, gain_two, w_up, w_down, cot_a, cot_b
):
    devices = lax.axis_size("blk")
    me = lax.axis_index("blk")
    seqs_a, rows_a, width = x_a.shape
    seqs_b, rows_b, _ = x_b.shape
    npl = sel_a.shape[1]
    blocks = npl * devices
    len_a = rows_a // npl
    len_b = rows_b // npl
    total_a = seqs_a * rows_a
    total_b = seqs_b * rows_b
    rows = total_a + total_b
    units = rows // UNIT
    units_a = total_a // UNIT
    count_a = seqs_a * npl
    count_b = seqs_b * npl
    picks = count_a + count_b
    picks_up = -(-picks // 16) * 16
    groups = rows // GROUP
    per = TILE // GROUP
    capacity = 2 * max(1, (4 * units + 5 * devices - 1) // (5 * devices))
    send_rows = devices * capacity * UNIT
    ff = w_up.shape[1]
    gain1 = gain_one.astype(F32).reshape(1, width)
    gain2 = gain_two.astype(F32).reshape(1, width)

    first, early = capacity, groups
    if capacity > 8:
        full, left = divmod(units, capacity)
        sure = (full * 8 + min(left, 8)) // 2 // per * per
        if capacity == 14 and 0 < sure < groups:
            first, early = 8, sure

    sizes = [8, 7] if early < groups else [capacity]
    extra = 16
    average = np.zeros((picks, units), np.float32)
    for j in range(count_a):
        average[j, 2 * j : 2 * j + 2] = 1.0 / len_a
    for j in range(count_b):
        average[count_a + j, units_a + j] = 1.0 / len_b
    settings = (npl, seqs_a, seqs_b, devices, capacity, first, early, sizes, extra, picks_up)
    w_sort_t = w_sort.T
    x, means, news, far_rows, ret_rows, perm, place, kinds = digest(
        x_a.reshape(-1, width), x_b.reshape(-1, width), sel_a, sel_b, gain1, average, w_sort_t, settings
    )
    news = lax.all_to_all(news, "blk", split_axis=0, concat_axis=0, tiled=True)
    table = news[:, picks, :capacity].astype(jnp.int32).reshape(-1)
    back_table = news[:, picks, capacity : capacity + sum(sizes)].astype(jnp.int32).reshape(-1)
    news = news[:, :picks]
    parcels = pack(table, x, devices, capacity, first, picks_up)
    recv = [exchange(parcels[0], devices)]
    summary = means * gain1
    rs = inverse_norm(summary)
    unit_summary = (summary * rs).astype(BF16)
    all_summaries = jnp.broadcast_to(
        jnp.pad(unit_summary, ((0, picks_up - picks), (0, 0))), (devices, picks_up, width)
    )

    xp, cot = arrange(perm, x, cot_a.reshape(-1, width), cot_b.reshape(-1, width))
    proj = project(xp, gain1, w_qkv)

    def by_sequence(values):
        tail = values.shape[2:]
        one = values[:, :count_a].reshape((devices, seqs_a, npl) + tail)
        two = values[:, count_a:].reshape((devices, seqs_b, npl) + tail)
        both = jnp.concatenate([one, two], axis=1)
        return jnp.swapaxes(both, 0, 1).reshape((seqs_a + seqs_b, blocks) + tail)

    def own_rows(values):
        return lax.dynamic_slice_in_dim(values, me * npl, npl, 1).reshape((-1,) + values.shape[2:])

    def to_units(values):
        return jnp.concatenate(
            [jnp.repeat(values[:count_a], len_a // UNIT, axis=0), values[count_a:]], axis=0
        )

    news = by_sequence(news)
    logits = news[..., :blocks]
    picked = (news[..., blocks : blocks + 1] == jnp.arange(blocks, dtype=F32)).astype(F32)
    weights = jnp.take(to_units(own_rows(sinkhorn(logits, picked))), perm, axis=0)
    lane = jnp.arange(2 * GROUP) >= GROUP
    wrow = jnp.where(lane[None, :], jnp.repeat(weights, UNIT, axis=0), 1.0)
    if len(parcels) > 1:
        tall = (capacity - first) * UNIT
        parcel = lax.dynamic_update_slice(
            parcels[1].reshape(devices, -1, width), all_summaries, (0, tall, 0)
        )
        recv.append(exchange(tie(parcel.reshape(-1, width), wrow, proj), devices))
        units_all = recv[1].reshape(devices, -1, width)[:, tall:]
    else:
        units_all = exchange(all_summaries.reshape(-1, width), devices)
        units_all = units_all.reshape(devices, picks_up, width)
    units_all = by_sequence(units_all[:, :picks])
    block_of = np.arange(GROUP) // len_b
    cross = block_of[:, None] != block_of[None, :]
    mask = np.zeros((2, GROUP, 2 * GROUP), np.float32)
    mask[1] = np.where(np.concatenate([cross, cross], axis=1), -1e30, 0.0)

    core = bit_of("dp", 0).astype(jnp.int32).reshape(1)
    shared = (xp, cot, proj, wrow, mask, gain1, gain2, w_qkv, w_out, w_up, w_down)
    heights = [
        devices * (n * UNIT + (extra if i == len(sizes) - 1 else 0))
        for i, n in enumerate(sizes)
    ]

    letter = (count_a, count_b, devices, extra)

    def run_backward(streams, *rest):
        _, _, gatt, prob, _, farkv = streams
        return backward(ret_rows, place, proj, farkv, gatt, prob, wrow, w_qkv, *rest)

    fast = lax.axis_size("dp") == 4 and devices == 8 and early < groups
    part_x = ff // 2 + width // 2
    if early < groups:
        prior = forward(far_rows, kinds, core, recv[:1], *shared, 0, early, None, False, wrow)
        dproj, dfar, gw_one, *ret = run_backward(
            prior[0], heights[:1], 0, early, None, None, prior[0][0]
        )
        back = [exchange(v, devices) for v in ret]
        streams, sums = forward(
            far_rows, kinds, core, recv, *shared, early, groups - early, prior, True, dproj
        )
        keep, give = sums
        out_a, out_b = restore(perm, streams[0], total_a)
        big_came = swap(give, "dp", 0)
        token = keep
        if fast:
            ranges_one = [(0, 0, part_x, 0, 0, 0), (0, part_x, keep.shape[0] - part_x, 1, 1, 0)]
            (bx, gx), (by, gy) = halve_step(
                ranges_one, [AXIS_X, AXIS_Y], [(keep, big_came)], out_a
            )
            bx_came, by_came = swap(gx, *AXIS_X), swap(gy, *AXIS_Y)
            token = bx
        dproj, dfar, _, *ret = run_backward(
            streams, heights[1:], early, groups - early, (dproj, dfar, gw_one), letter, token
        )
    else:
        streams, sums = forward(far_rows, kinds, core, recv, *shared, 0, groups, None, True, wrow)
        keep, give = sums
        out_a, out_b = restore(perm, streams[0], total_a)
        big_came = swap(give, "dp", 0)
        back = []
        dproj, dfar, _, *ret = run_backward(
            streams, heights, 0, groups, None, letter, keep
        )
    _, gmid, _, _, farx, _ = streams

    parcel = tie(ret[0], bx_came, by_came, back[0]) if fast else ret[0]
    tall = sizes[-1] * UNIT
    arrived = exchange(parcel, devices)
    back.append(arrived)
    token = dproj
    gn, late_keep, late_give = qkv_grads(
        core, xp, farx, dproj, dfar, gain1, w_qkv, token
    )
    late_came = swap(late_give, "dp", 0)
    part_late = 256
    if fast:
        late_rows = late_keep.shape[0]
        ranges_late = [(0, 0, part_late, 0, 0, 0), (0, part_late, late_rows - part_late, 1, 1, 0)]
        (lx, gx), (ly, gy) = halve_step(
            ranges_late, [AXIS_X, AXIS_Y], [(late_keep, late_came)], late_came
        )
        lx_came, ly_came = swap(gx, *AXIS_X), swap(gy, *AXIS_Y)
        nbx, nlx, nby, nly = (v.shape[0] for v in (bx, lx, by, ly))
        ranges_two = [
            (0, 0, nbx, 0, 0, 0),
            (1, 0, nlx, 0, 0, nbx // 2),
            (2, 0, nby, 1, 1, 0),
            (3, 0, nly, 1, 1, nby // 2),
        ]
        (vx, gx), (vy, gy) = halve_step(
            ranges_two,
            [AXIS_Y, AXIS_X],
            [(bx, bx_came), (lx, lx_came), (by, by_came), (ly, ly_came)],
            lx,
        )
        vx_came, vy_came = swap(gx, *AXIS_Y), swap(gy, *AXIS_X)
    small, spread = sort_back(
        me.reshape(1), perm, logits, picked, units_all.reshape(-1, width), w_sort_t, gain1, means,
        arrived, npl, seqs_a, (len_a, len_b), tall, extra, vx if fast else arrived,
    )
    if fast:
        cuts = [nbx // 2, nlx // 2, nby // 2, nly // 2]
        ranges_three = [
            (0, 0, cuts[0], 0, 0, 0),
            (0, cuts[0], cuts[1], 0, 0, cuts[0] // 2),
            (1, 0, cuts[2], 0, 1, 0),
            (1, cuts[2], cuts[3], 0, 1, cuts[2] // 2),
        ]
        (zx, gx), (zy, gy) = halve_step(
            ranges_three, [AXIS_Z0], [(vx, vx_came), (vy, vy_came)], spread
        )
    base = base_rows(xp, gmid, gn, spread, gain1)
    if fast:
        zx_came, zy_came = swap(gx, *AXIS_Z0), swap(gy, *AXIS_Z0)
        zx = add(zx, tie(zx_came, base, zy_came))
        zx_came = swap(zx, *AXIS_Z1)
        zy = add(zy, zy_came)
        zy_came = swap(zy, *AXIS_Z1)

    gx_a, gx_b = last(back_table, place, back, sizes, extra, sum(sizes), x, base, gain1, total_a)
    if fast:
        for bit in (0, 1):
            small = small + swap(small, "dp", bit)
        zx, zy = add(zx, tie(zx_came, small)), add(zy, zy_came)
        vx, vy = double_step(
            ranges_three,
            [AXIS_Z0],
            [(zx, swap(zx, *AXIS_Z0)), (zy, swap(zy, *AXIS_Z0))],
        )
        ranges_back = [
            (0, 0, nbx, 0, 0, 0),
            (0, nbx, nlx, 0, 0, cuts[0]),
            (1, 0, nby, 1, 1, 0),
            (1, nby, nly, 1, 1, cuts[2]),
        ]
        vx, vy = double_step(
            ranges_back,
            [AXIS_Y, AXIS_X],
            [(vx, swap(vx, *AXIS_Y)), (vy, swap(vy, *AXIS_X))],
        )
        big_rows = keep.shape[0]
        ranges_all = [
            (0, 0, part_x, 0, 0, 0),
            (0, big_rows, part_late, 0, 0, nbx),
            (0, part_x, big_rows - part_x, 1, 1, 0),
            (0, big_rows + part_late, late_rows - part_late, 1, 1, nby),
        ]
        (sums_own,) = double_step(
            ranges_all,
            [AXIS_X, AXIS_Y],
            [(vx, swap(vx, *AXIS_X)), (vy, swap(vy, *AXIS_Y))],
            gx_a,
        )
    else:
        across = [("dp", bit) for bit in range(1, bits_of(lax.axis_size("dp")))]
        along = [("blk", bit) for bit in range(bits_of(devices))]
        sums_own = jnp.concatenate(
            [
                reduce_any(add(keep, big_came), across + along),
                reduce_any(add(late_keep, late_came), along + across),
            ],
            axis=0,
        )
    sums_came = swap(sums_own, "dp", 0)

    if not fast:
        small = lax.psum(small, "dp")
    written = assemble(core, 0, sums_own, w_up, w_qkv, width, ff, None)
    sum_up, sum_down, sum_out, sum_qkv, gains = assemble(
        core, 1, sums_came, w_up, w_qkv, width, ff, written
    )

    return (
        out_a.reshape(x_a.shape),
        out_b.reshape(x_b.shape),
        gx_a.reshape(x_a.shape),
        gx_b.reshape(x_b.shape),
        gains[0] / gain1[0] + small[blocks],
        sum_qkv,
        sum_out,
        small[:blocks].T,
        gains[1] / gain2[0],
        sum_up,
        sum_down,
    )


def solution(mesh):
    rows_spec = P("dp", "blk", None)
    in_specs = (
        (rows_spec, rows_spec, P("dp", "blk"), P("dp", "blk")) + (P(),) * 7 + (rows_spec, rows_spec)
    )
    out_specs = (rows_spec,) * 4 + (P(),) * 7
    return jax.shard_map(
        per_device, mesh=mesh, in_specs=in_specs, out_specs=out_specs, check_vma=False
    )
```

```python
import functools

import jax
import jax.numpy as jnp
import numpy as np
from jax import lax
from jax.experimental import pallas as pl
from jax.experimental.pallas import tpu as pltpu
from jax.sharding import PartitionSpec as P

HEADS = 8
SINK_ITERS = 8
EPSILON = 1e-05
SOFTMAX_HEAT = 0.75
UNIT = 32
GROUP = 64
TILE = 256
HALF = 256
PER_HALF = 4
VMEM_LIMIT = 62 * 1024 * 1024

F32 = jnp.float32
BF16 = jnp.bfloat16

NN = (((1,), (0,)), ((), ()))
NT = (((1,), (1,)), ((), ()))
TN = (((0,), (0,)), ((), ()))


def dot(a, b, dims=NN):
    return lax.dot_general(a, b, dims, preferred_element_type=F32)


def inverse_norm(values):
    return lax.rsqrt(jnp.mean(values * values, axis=-1, keepdims=True) + EPSILON)


def whole(shape):
    zeros = (0,) * len(shape)
    return pl.BlockSpec(shape, lambda *_: zeros, pipeline_mode=pl.Buffered(1))


def rows_of(tile, width):
    return pl.BlockSpec((tile, width), lambda i: (i, 0))


SMEM = pl.BlockSpec(memory_space=pltpu.SMEM)


def params():
    return pltpu.CompilerParams(
        dimension_semantics=("arbitrary",), vmem_limit_bytes=VMEM_LIMIT
    )


def cost(flops, nbytes):
    return pl.CostEstimate(flops=int(flops * 1e-3), bytes_accessed=int(nbytes * 1e-3), transcendentals=0)


ANY = pl.BlockSpec(memory_space=pl.ANY)
VMEM = pl.BlockSpec(memory_space=pltpu.VMEM)
HBM = pl.BlockSpec(memory_space=pltpu.HBM)


def limit(mib):
    return pltpu.CompilerParams(vmem_limit_bytes=mib * 1024 * 1024)


def request_kernel(
    npl, seqs_a, seqs_b, devices, capacity, first, early, sizes, extra, spare_rows,
    sela_ref, selb_ref, table_ref, back_ref, far_ref, ret_ref, perm_ref, place_ref, kinds_ref, fill, begin, used,
):
    count_a = seqs_a * npl
    count_b = seqs_b * npl
    units_a = 2 * count_a
    width = sum(sizes)
    shift = npl.bit_length() - 1 if npl & (npl - 1) == 0 else -1

    def choice(j):
        ref, at = (sela_ref, j) if j < count_a else (selb_ref, j - count_a)
        return ref[at // npl, at % npl]

    def split(chosen):
        if shift >= 0:
            return lax.shift_right_logical(chosen, shift), lax.bitwise_and(chosen, npl - 1)
        return lax.div(chosen, npl), lax.rem(chosen, npl)

    def clear(ref):
        def body(i, carry):
            ref[i] = -1
            return carry

        return body

    lax.fori_loop(0, devices * capacity, clear(table_ref), 0)
    lax.fori_loop(0, devices * width, clear(back_ref), 0)
    for s in range(devices):
        fill[s] = 0
        used[s] = 0
        used[devices + s] = 0
    one = lambda flag: jnp.where(flag, 1, 0)
    ready_a, ready_b, must_a, must_b = (jnp.int32(0) for _ in range(4))
    for j in range(count_a + count_b):
        source, inner = split(choice(j))
        slot = fill[source]
        begin[j] = slot
        size = 2 if j < count_a else 1
        fill[source] = slot + size
        if j < count_a:
            unit = inner * 2 + (j // npl) * npl * 2
            ready_a = ready_a + one(slot + 2 <= first)
            table_ref[source * capacity + slot + 1] = unit + 1
        else:
            unit = inner + (units_a + (j - count_a) // npl * npl)
            ready_b = ready_b + one(slot + 1 <= first)
        table_ref[source * capacity + slot] = unit

    two = early < count_a + count_b // 2

    def must(j):
        source, _ = split(choice(j))
        if not two:
            return begin[j] < 0
        return begin[j] < fill[source] - 6

    for j in range(count_a):
        must_a = must_a + one(must(j))
    for j in range(count_b):
        must_b = must_b + one(must(count_a + j))
    even = jnp.logical_or(lax.bitwise_and(must_b, 1) == 0, ready_b > must_b)
    pairs = lax.shift_right_logical(must_b + one(even), 1)
    take_a = jnp.minimum(ready_a, early - pairs)
    if not two:
        take_a = jnp.int32(count_a)
    take_b = 2 * (early - take_a)
    late_b = 2 * (early + count_a - take_a)
    kinds_ref[0] = take_a
    kinds_ref[1] = early + count_a - take_a
    second = devices * first * UNIT

    def ret_row(phase, source, slot):
        chunks = list(enumerate(sizes))
        if two:
            chunks = chunks[:1] if phase == 0 else chunks[1:]
        row = jnp.int32(0)
        begin_slot, begin_row = 0, 0
        for index, size in chunks:
            height = size * UNIT + (extra if index == len(sizes) - 1 else 0)
            here = begin_row + source * height + (slot - begin_slot) * UNIT
            row = jnp.where(slot >= begin_slot, here, row)
            begin_slot += size
            begin_row += devices * height
        return row

    def put(pos, unit, inner, source, slot, late):
        near = (source * first + slot) * UNIT
        rest = second + source * ((capacity - first) * UNIT + spare_rows) + (slot - first) * UNIT
        far_ref[pos] = jnp.where(slot < first, near, rest)
        at = late * devices + source
        back = used[at]
        used[at] = back + 1
        if two:
            ret_ref[pos] = jnp.where(late == 0, ret_row(0, source, back), ret_row(1, source, back))
            back_ref[source * width + back + late * sizes[0]] = inner
        else:
            ret_ref[pos] = ret_row(0, source, back)
            back_ref[source * width + back] = inner
        perm_ref[pos] = unit
        place_ref[unit] = pos

    spare = take_a - must_a
    taken, other, free = (jnp.int32(0) for _ in range(3))
    for j in range(count_a):
        source, inner = split(choice(j))
        slot = begin[j]
        need = must(j)
        pick = jnp.logical_and(jnp.logical_not(need), jnp.logical_and(slot + 2 <= first, free < spare))
        use = jnp.logical_or(need, pick)
        free = free + one(pick)
        pos = 2 * jnp.where(use, taken, early + other)
        inner = inner * 2 + (j // npl) * npl * 2
        put(pos, 2 * j, inner, source, slot, one(jnp.logical_not(use)))
        put(pos + 1, 2 * j + 1, inner + 1, source, slot + 1, one(jnp.logical_not(use)))
        taken = taken + one(use)
        other = other + one(jnp.logical_not(use))
    spare = take_b - must_b
    drop = one(spare < 0)
    taken, other, free = (jnp.int32(0) for _ in range(3))
    for j in range(count_b):
        source, inner = split(choice(count_a + j))
        slot = begin[count_a + j]
        need = must(count_a + j)
        skip = jnp.logical_and(need, drop > 0)
        drop = drop - one(skip)
        pick = jnp.logical_and(jnp.logical_not(need), jnp.logical_and(slot + 1 <= first, free < spare))
        use = jnp.logical_or(jnp.logical_and(need, jnp.logical_not(skip)), pick)
        free = free + one(pick)
        pos = jnp.where(use, 2 * take_a + taken, late_b + other)
        inner = inner + (units_a + (j // npl) * npl)
        put(pos, units_a + j, inner, source, slot, one(jnp.logical_not(use)))
        taken = taken + one(use)
        other = other + one(jnp.logical_not(use))


def digest_kernel(
    tiles_a, settings, sela_ref, selb_ref, xa_ref, xb_ref, gain_ref, avg_ref, wsort_ref,
    x_ref, means_ref, news_ref, far_ref, ret_ref, perm_ref, place_ref, kinds_ref,
    sums, table_ref, back_ref, fill, begin, used,
):
    step = pl.program_id(0)

    @pl.when(step == 0)
    def _():
        request_kernel(
            *settings, sela_ref, selb_ref, table_ref, back_ref, far_ref, ret_ref, perm_ref, place_ref,
            kinds_ref, fill, begin, used,
        )

    def take(src):
        x = src[...]
        x_ref[...] = x
        x = x.astype(F32)
        scaled = x * inverse_norm(x)
        units = x.shape[0] // UNIT
        at = pl.ds(pl.multiple_of(step * units, units), units)
        sums[at, :] = jnp.sum(scaled.reshape(units, UNIT, x.shape[1]), axis=1)

    pl.when(step < tiles_a)(lambda: take(xa_ref))
    pl.when(step >= tiles_a)(lambda: take(xb_ref))

    @pl.when(step == pl.num_programs(0) - 1)
    def _():
        means = lax.dot_general(
            avg_ref[...], sums[...], NN, precision=lax.Precision.HIGHEST, preferred_element_type=F32
        )
        means_ref[...] = means
        summary = means * gain_ref[...]
        unit = (summary * inverse_norm(summary)).astype(BF16)
        logits = dot(unit, wsort_ref[...], NT) * (1.0 / SOFTMAX_HEAT)
        picks, blocks = logits.shape
        devices, height, lanes = news_ref.shape
        line = lax.broadcasted_iota(jnp.int32, (picks, lanes - blocks), 0)
        lane = lax.broadcasted_iota(jnp.int32, (picks, lanes - blocks), 1)
        chosen = jnp.zeros((picks, lanes - blocks), jnp.int32)
        count_a = sela_ref.shape[0] * sela_ref.shape[1]
        for j in range(picks):
            ref, at = (sela_ref, j) if j < count_a else (selb_ref, j - count_a)
            npl = ref.shape[1]
            chosen = jnp.where(line == j, ref[at // npl, at % npl], chosen)
        chosen = jnp.where(lane == 0, chosen, 0).astype(F32)
        message = jnp.concatenate([logits, chosen], axis=1)
        lane = lax.broadcasted_iota(jnp.int32, (1, lanes), 1)
        wanted = table_ref.shape[0] // devices
        order = back_ref.shape[0] // devices
        rest = lax.broadcasted_iota(jnp.int32, (height - picks, lanes), 0)
        for d in range(devices):
            row = jnp.zeros((1, lanes), jnp.int32)
            for k in range(wanted):
                row = jnp.where(lane == k, table_ref[d * wanted + k], row)
            for k in range(order):
                row = jnp.where(lane == wanted + k, back_ref[d * order + k], row)
            news_ref[d, :picks, :] = message
            news_ref[d, picks:, :] = jnp.where(rest == 0, row.astype(F32), 0.0)


def digest(x_a, x_b, sel_a, sel_b, gain_row, average, w_sort_t, settings):
    npl, seqs_a, seqs_b, devices, capacity, _, _, sizes, _, _ = settings
    width = x_a.shape[1]
    tile = 2 * TILE if x_a.shape[0] % (2 * TILE) == 0 and x_b.shape[0] % (2 * TILE) == 0 else TILE
    tiles_a = x_a.shape[0] // tile
    tiles_b = x_b.shape[0] // tile
    rows = x_a.shape[0] + x_b.shape[0]
    picks = average.shape[0]
    height = -(-picks // 8) * 8 + 8
    units = rows // UNIT
    ints = lambda n: jax.ShapeDtypeStruct((n,), jnp.int32)
    return pl.pallas_call(
        functools.partial(digest_kernel, tiles_a, settings),
        grid=(tiles_a + tiles_b,),
        in_specs=[
            SMEM,
            SMEM,
            pl.BlockSpec((tile, width), lambda i: (jnp.minimum(i, tiles_a - 1), 0)),
            pl.BlockSpec((tile, width), lambda i: (jnp.maximum(i - tiles_a, 0), 0)),
            whole((1, width)),
            whole(average.shape),
            whole(w_sort_t.shape),
        ],
        out_specs=[rows_of(tile, width), whole((picks, width)), whole((devices, height, 128))]
        + [SMEM] * 5,
        out_shape=[
            jax.ShapeDtypeStruct((rows, width), BF16),
            jax.ShapeDtypeStruct((picks, width), F32),
            jax.ShapeDtypeStruct((devices, height, 128), F32),
        ]
        + [ints(n) for n in (units, units, units, units, 2)],
        scratch_shapes=[
            pltpu.VMEM((units, width), F32),
            pltpu.SMEM((devices * capacity,), jnp.int32),
            pltpu.SMEM((devices * sum(sizes),), jnp.int32),
            pltpu.SMEM((devices,), jnp.int32),
            pltpu.SMEM((picks,), jnp.int32),
            pltpu.SMEM((2 * devices,), jnp.int32),
        ],
        compiler_params=params(),
        cost_estimate=cost(rows * width * 10, rows * width * 4),
        name="digest",
    )(sel_a, sel_b, x_a, x_b, gain_row, average, w_sort_t)


def pack_kernel(devices, capacity, first, spare, table_ref, x_ref, *rest):
    outs = rest[: 1 if first == capacity else 2]
    held, sems = rest[len(outs) :]
    sizes = [first, capacity - first]
    copies = []
    for part, out_ref in enumerate(outs):
        size = sizes[part]
        base = part * devices * first
        for r in range(devices):
            for slot in range(size):
                unit = jnp.maximum(table_ref[r * capacity + part * first + slot], 0)
                src = pl.ds(pl.multiple_of(unit * UNIT, UNIT), UNIT)
                at = (base + r * size + slot) * UNIT
                held[at : at + UNIT, :] = x_ref[src, :]
            at = (base + r * size) * UNIT
            copy = pltpu.make_async_copy(
                held.at[pl.ds(at, size * UNIT)],
                out_ref.at[pl.ds(r * (size * UNIT + part * spare), size * UNIT)],
                sems.at[part * devices + r],
            )
            copy.start()
            copies.append(copy)
    for copy in copies:
        copy.wait()


def pack(table, x, devices, capacity, first, spare):
    width = x.shape[1]
    sizes = [first] if first == capacity else [first, capacity - first]
    return pl.pallas_call(
        functools.partial(pack_kernel, devices, capacity, first, spare),
        in_specs=[SMEM, VMEM],
        out_specs=[HBM] * len(sizes),
        out_shape=[
            jax.ShapeDtypeStruct((devices * (n * UNIT + i * spare), width), BF16)
            for i, n in enumerate(sizes)
        ],
        scratch_shapes=[
            pltpu.VMEM((devices * capacity * UNIT, width), BF16),
            pltpu.SemaphoreType.DMA((len(sizes) * devices,)),
        ],
        compiler_params=limit(62),
        cost_estimate=cost(0, x.size * 6),
        name="pack",
    )(table, x)


def arrange_kernel(units_a, perm_ref, x_ref, cota_ref, cotb_ref, xp_ref, cotp_ref):
    def body(pos, carry):
        unit = perm_ref[pos]
        at = pl.ds(pl.multiple_of(pos * UNIT, UNIT), UNIT)
        xp_ref[at, :] = x_ref[pl.ds(pl.multiple_of(unit * UNIT, UNIT), UNIT), :]

        @pl.when(unit < units_a)
        def _():
            cotp_ref[at, :] = cota_ref[pl.ds(pl.multiple_of(unit * UNIT, UNIT), UNIT), :]

        @pl.when(unit >= units_a)
        def _():
            src = pl.ds(pl.multiple_of((unit - units_a) * UNIT, UNIT), UNIT)
            cotp_ref[at, :] = cotb_ref[src, :]

        return carry

    lax.fori_loop(0, x_ref.shape[0] // UNIT, body, 0)


def arrange(perm, x, cot_a, cot_b):
    like = jax.ShapeDtypeStruct(x.shape, BF16)
    return pl.pallas_call(
        functools.partial(arrange_kernel, cot_a.shape[0] // UNIT),
        in_specs=[SMEM, VMEM, VMEM, VMEM],
        out_specs=[VMEM, VMEM],
        out_shape=[like, like],
        compiler_params=limit(16),
        cost_estimate=cost(0, x.size * 8),
        name="arrange",
    )(perm, x, cot_a, cot_b)


def restore_kernel(perm_ref, out_ref, outa_ref, outb_ref):
    units_a = outa_ref.shape[0] // UNIT

    def body(pos, carry):
        unit = perm_ref[pos]
        at = pl.ds(pl.multiple_of(pos * UNIT, UNIT), UNIT)

        @pl.when(unit < units_a)
        def _():
            outa_ref[pl.ds(pl.multiple_of(unit * UNIT, UNIT), UNIT), :] = out_ref[at, :]

        @pl.when(unit >= units_a)
        def _():
            dst = pl.ds(pl.multiple_of((unit - units_a) * UNIT, UNIT), UNIT)
            outb_ref[dst, :] = out_ref[at, :]

        return carry

    lax.fori_loop(0, out_ref.shape[0] // UNIT, body, 0)


def restore(perm, out, rows_a):
    rows, width = out.shape
    return pl.pallas_call(
        restore_kernel,
        in_specs=[SMEM, VMEM],
        out_specs=[VMEM, VMEM],
        out_shape=[
            jax.ShapeDtypeStruct((rows_a, width), BF16),
            jax.ShapeDtypeStruct((rows - rows_a, width), BF16),
        ],
        compiler_params=limit(16),
        cost_estimate=cost(0, out.size * 4),
        name="restore",
    )(perm, out)


def project_kernel(x_ref, gain_ref, w_ref, proj_ref):
    x = x_ref[...].astype(F32)
    proj_ref[...] = dot((x * inverse_norm(x) * gain_ref[...]).astype(BF16), w_ref[...]).astype(BF16)


def project(x, gain_row, w_qkv):
    rows, width = x.shape
    wide = w_qkv.shape[1]
    return pl.pallas_call(
        project_kernel,
        grid=(rows // TILE,),
        in_specs=[rows_of(TILE, width), whole((1, width)), whole((width, wide))],
        out_specs=rows_of(TILE, wide),
        out_shape=jax.ShapeDtypeStruct((rows, wide), BF16),
        compiler_params=params(),
        cost_estimate=cost(2 * rows * width * wide, rows * (width + wide) * 2),
        name="project",
    )(x, gain_row, w_qkv)


def log_sum(values, axis):
    top = jnp.max(values, axis=axis, keepdims=True)
    return top + jnp.log(jnp.sum(jnp.exp(values - top), axis=axis, keepdims=True))


def sinkhorn_kernel(logits_ref, picked_ref, weight_ref):
    state = logits_ref[...]
    for _ in range(SINK_ITERS):
        state = state - log_sum(state, 2)
        state = state - log_sum(state, 1)
    count = state.shape[1]
    weight = count * jnp.sum(jnp.exp(state) * picked_ref[...], axis=2, keepdims=True)
    weight_ref[...] = jnp.broadcast_to(weight, weight_ref.shape)


def sinkhorn(logits, picked):
    seqs, count, _ = logits.shape
    return pl.pallas_call(
        sinkhorn_kernel,
        out_shape=jax.ShapeDtypeStruct((seqs, count, 128), F32),
        cost_estimate=cost(logits.size * 100, logits.size * 32),
        name="sinkhorn",
    )(logits, picked)


def exact(a, b, dims=NN):
    return lax.dot_general(
        a, b, dims, precision=lax.Precision.HIGHEST, preferred_element_type=F32
    )


def sort_back_kernel(
    npl, seqs_a, lengths, tall, me_ref, perm_ref, logits_ref, picked_ref, units_ref, wsort_ref, gain_ref,
    means_ref, arrived, token_ref, small_ref, spread_ref, kept, letters, sems,
):
    seqs, blocks, _ = logits_ref.shape
    devices = blocks // npl
    picks = means_ref.shape[0]
    extra = letters.shape[1]
    height = arrived.shape[0] // devices
    copies = []
    for d in range(devices):
        source = arrived.at[pl.ds(d * height + tall, extra), pl.ds(0, 128)]
        copies.append(pltpu.make_async_copy(source, letters.at[d], sems.at[d]))
    for copy in copies:
        copy.start()
    state = logits_ref[...]
    for step in range(SINK_ITERS):
        state = state - log_sum(state, 2)
        kept[2 * step] = jnp.exp(state)
        state = state - log_sum(state, 1)
        kept[2 * step + 1] = jnp.exp(state)
    for copy in copies:
        copy.wait()
    rows = seqs * blocks
    line = lax.broadcasted_iota(jnp.int32, (rows, 128), 0)
    lane = lax.broadcasted_iota(jnp.int32, (rows, 128), 1)
    own_lane = line // blocks * npl + line % npl
    device = (line // npl) % devices
    table = jnp.zeros((rows, 128), F32)
    for d in range(devices):
        table = jnp.where(device == d, letters[d, 0:1, :].astype(F32), table)
    gw = jnp.sum(jnp.where(lane == own_lane, table, 0.0), axis=1, keepdims=True)
    grad = blocks * picked_ref[...] * gw.reshape(seqs, blocks, 1) * kept[2 * SINK_ITERS - 1]
    for step in reversed(range(SINK_ITERS)):
        grad = grad - kept[2 * step + 1] * jnp.sum(grad, axis=1, keepdims=True)
        grad = grad - kept[2 * step] * jnp.sum(grad, axis=2, keepdims=True)
    grad = (grad * (1.0 / SOFTMAX_HEAT)).reshape(rows, blocks)
    units = units_ref[...].astype(F32)
    small_ref[:blocks, :] = exact(grad, units, TN)
    g_unit = exact(grad, wsort_ref[...].astype(F32))
    both = g_unit * units
    both = both - units * units * jnp.mean(both, axis=-1, keepdims=True)
    row = jnp.sum(both, axis=0, keepdims=True) / gain_ref[...]
    first = lax.broadcasted_iota(jnp.int32, (small_ref.shape[0] - blocks, units.shape[1]), 0) == 0
    small_ref[blocks:, :] = jnp.where(first, row, 0.0)
    line = lax.broadcasted_iota(jnp.int32, (picks, rows), 0)
    lane = lax.broadcasted_iota(jnp.int32, (picks, rows), 1)
    mine = lane == line // npl * blocks + me_ref[0] * npl + line % npl
    g_own = exact(jnp.where(mine, 1.0, 0.0), g_unit)
    summary = means_ref[...] * gain_ref[...]
    rs = inverse_norm(summary)
    g_summary = rs * (
        g_own - summary * (rs * rs) * jnp.mean(g_own * summary, axis=-1, keepdims=True)
    )
    count_a = seqs_a * npl
    places = spread_ref.shape[0]
    line = lax.broadcasted_iota(jnp.int32, (places, picks), 0)
    lane = lax.broadcasted_iota(jnp.int32, (places, picks), 1)
    unit = jnp.zeros((places, picks), jnp.int32)
    for pos in range(places):
        unit = jnp.where(line == pos, perm_ref[pos], unit)
    block = jnp.where(unit < 2 * count_a, unit // 2, unit - count_a)
    share = jnp.where(lane < count_a, 1.0 / lengths[0], 1.0 / lengths[1])
    spread_ref[...] = exact(jnp.where(lane == block, share, 0.0), g_summary)


def sort_back(
    me, perm, logits, picked, units, w_sort_t, gain, means, arrived, npl, seqs_a, lengths, tall, extra, token
):
    seqs, blocks, _ = logits.shape
    width = means.shape[1]
    return pl.pallas_call(
        functools.partial(sort_back_kernel, npl, seqs_a, lengths, tall),
        in_specs=[SMEM, SMEM] + [VMEM] * 6 + [ANY, ANY],
        out_specs=[VMEM, VMEM],
        out_shape=[
            jax.ShapeDtypeStruct((blocks + 8, width), F32),
            jax.ShapeDtypeStruct((perm.shape[0], width), F32),
        ],
        scratch_shapes=[
            pltpu.VMEM((2 * SINK_ITERS,) + logits.shape, F32),
            pltpu.VMEM((blocks // npl, extra, 128), BF16),
            pltpu.SemaphoreType.DMA((blocks // npl,)),
        ],
        compiler_params=limit(24),
        cost_estimate=cost(logits.size * 200, logits.size * 32),
        name="sort_back",
    )(me, perm, logits, picked, units, w_sort_t, gain, means, arrived, token)


def head_masks(rows):
    lane = lax.broadcasted_iota(jnp.int32, (rows, HALF), 1) // (HALF // PER_HALF)
    return [lane == h for h in range(PER_HALF)]


def stack_heads(values, masks):
    zero = jnp.zeros_like(values)
    return jnp.concatenate([jnp.where(m, values, zero) for m in masks], axis=0)


def unstack_heads(values, masks):
    total = None
    for h, m in enumerate(masks):
        part = jnp.where(m, values[h * GROUP : (h + 1) * GROUP], 0.0)
        total = part if total is None else total + part
    return total


def repeat_heads(values):
    return jnp.concatenate([values] * PER_HALF, axis=0)


class Mover:
    def __init__(self, sems):
        self.sems, self.used, self.out = sems, 0, []

    def start(self, source, target):
        copy = pltpu.make_async_copy(source, target, self.sems.at[self.used])
        self.used += 1
        copy.start()
        return copy

    def store(self, source, target):
        self.out.append(self.start(source, target))

    def finish(self):
        for copy in self.out:
            copy.wait()


BATCH = 4


def forward_kernel(first_group, groups, recvs, prior, final, *refs):
    refs = list(refs)
    take = lambda n: [refs.pop(0) for _ in range(n)]
    far_ref, kinds_ref, core_ref = take(3)
    recv_hbm = take(recvs)
    x_hbm, cot_hbm, proj_hbm, wrow_hbm, mask_ref, gain1_ref, gain2_ref = take(7)
    wqkv_hbm, wout_hbm, wup_hbm, wdown_hbm, _ = take(5)
    prior_refs = take(2) if prior else []
    if prior:
        take(6)
    out_hbm, gmid_hbm, gatt_hbm, prob_hbm, farx_hbm, farkv_hbm = take(6)
    if final:
        keep_hbm, give_hbm = take(2)
    else:
        up_hbm, down_hbm = take(2)
    x_ref, cot_ref, proj_ref, wrow_ref, wqkv_ref, wout_ref, wup_ref, wdown_ref = take(8)
    out_ref, gmid_ref, gatt_ref, prob_ref, farx_ref, farkv_ref, attended = take(7)
    one_ref, two_ref = take(2)
    if prior:
        up_prior, down_prior = take(2)
    (sems,) = take(1)
    move = Mover(sems)
    rows = groups * GROUP
    width = x_ref.shape[1]
    ff = wup_ref.shape[1]
    base = first_group
    here = pl.ds(first_group * GROUP, rows)
    rows_one = recv_hbm[0].shape[0]
    far_sem = sems.at[sems.shape[0] - 1]
    for u in range(rows // UNIT):
        row = far_ref[2 * base + u]
        dst = farx_ref.at[pl.ds(u * UNIT, UNIT)]

        def bring(ref, row, dst=dst):
            src = ref.at[pl.ds(pl.multiple_of(row, 16), UNIT)]
            pltpu.make_async_copy(src, dst, far_sem).start()

        if recvs == 1:
            bring(recv_hbm[0], row)
        else:
            pl.when(row < rows_one)(lambda row=row, bring=bring: bring(recv_hbm[0], row))
            pl.when(row >= rows_one)(lambda row=row, bring=bring: bring(recv_hbm[1], row - rows_one))
    got_wqkv = move.start(wqkv_hbm, wqkv_ref)
    got_proj = move.start(proj_hbm.at[here], proj_ref)
    got_wrow = move.start(wrow_hbm.at[here], wrow_ref)
    got_x = move.start(x_hbm.at[here], x_ref)
    got_wout = move.start(wout_hbm, wout_ref)
    got_cot = move.start(cot_hbm.at[here], cot_ref)
    got_up = move.start(wup_hbm, wup_ref)
    got_down = move.start(wdown_hbm, wdown_ref)
    if prior:
        got_prior = [
            move.start(prior_refs[0], up_prior),
            move.start(prior_refs[1], down_prior),
        ]

    pltpu.make_async_copy(farx_ref, farx_ref, far_sem).wait()
    move.store(farx_ref, farx_hbm.at[here])
    far = farx_ref[...].astype(F32)
    far = (far * inverse_norm(far) * gain1_ref[...]).astype(BF16)
    got_wqkv.wait()
    farkv_ref[...] = dot(far, wqkv_ref[:, width:]).astype(BF16)
    move.store(farkv_ref, farkv_hbm.at[here])
    masks16 = head_masks(GROUP)
    head_scale = (width // HEADS) ** -0.5
    boundary = kinds_ref[1 if prior else 0]
    got_proj.wait()
    got_wrow.wait()
    for first in range(0, groups, BATCH):
        work = [
            (i, half) for i in range(first, min(first + BATCH, groups)) for half in range(width // HALF)
        ]
        scores, vals = [], []
        for i, half in work:
            at = slice(i * GROUP, (i + 1) * GROUP)
            lo = half * HALF
            q = proj_ref[at, lo : lo + HALF] * jnp.asarray(head_scale, BF16)
            keys = jnp.concatenate(
                [proj_ref[at, width + lo : width + lo + HALF], farkv_ref[at, lo : lo + HALF]], axis=0
            )
            vals.append(
                jnp.concatenate(
                    [
                        proj_ref[at, 2 * width + lo : 2 * width + lo + HALF],
                        farkv_ref[at, width + lo : width + lo + HALF],
                    ],
                    axis=0,
                )
            )
            which = jnp.where(base + i < boundary, 0, 1)
            scores.append(dot(stack_heads(q, masks16), keys, NT) + repeat_heads(mask_ref[which]))
        tops = [jnp.max(v, axis=1, keepdims=True) for v in scores]
        weights = [jnp.exp(v - t) for v, t in zip(scores, tops)]
        sums = [jnp.sum(v, axis=1, keepdims=True) for v in weights]
        probs = [v * (1.0 / t) for v, t in zip(weights, sums)]
        mixed = []
        for (i, half), prob, value in zip(work, probs, vals):
            at = slice(i * GROUP, (i + 1) * GROUP)
            prob_ref[i, half] = prob.astype(BF16)
            mixed.append(dot((prob * repeat_heads(wrow_ref[at, :])).astype(BF16), value))
        for (i, half), value in zip(work, mixed):
            at = slice(i * GROUP, (i + 1) * GROUP)
            lo = half * HALF
            attended[at, lo : lo + HALF] = unstack_heads(value, masks16).astype(BF16)
    move.store(prob_ref, prob_hbm.at[pl.ds(first_group, groups)])

    got_x.wait()
    got_wout.wait()
    att = attended[...]
    middle = x_ref[...].astype(F32) + dot(att, wout_ref[...])
    r2 = inverse_norm(middle)
    scaled = middle * r2
    second = (scaled * gain2_ref[...]).astype(BF16)
    got_cot.wait()
    cot = cot_ref[...]
    cot_t = cot.T
    second_t = second.T
    got_up.wait()
    got_down.wait()
    if prior:
        for copy in got_prior:
            copy.wait()

    def total(value, old, lanes):
        return value + old[:, lanes].astype(F32) if prior else value

    edge = ff // 2

    pending = []

    def send(ref, half, lines):
        sem = sems.at[move.used]
        move.used += 1
        for which, hbm in ((half, keep_hbm), (1 - half, give_hbm)):
            copy = pltpu.make_async_copy(ref.at[lines], hbm.at[lines], sem)
            pl.when(core_ref[0] == which)(copy.start)
        pending.append(copy)

    def put_up(c, value):
        lanes = slice(c, c + width)
        if not final:
            one_ref[:, lanes] = value.astype(BF16)
            at = (slice(None), pl.ds(c, width))
            move.store(one_ref.at[at], up_hbm.at[at])
            return
        ref, at = (one_ref, c) if c < edge else (two_ref, c - edge)
        ref[at : at + width, :] = total(value, up_prior if prior else None, lanes).astype(BF16)
        send(ref, 0 if c < edge else 1, pl.ds(at, width))

    def put_down(c, value):
        lanes = slice(c, c + width)
        if not final:
            two_ref[:, lanes] = value.astype(BF16)
            at = (slice(None), pl.ds(c, width))
            move.store(two_ref.at[at], down_hbm.at[at])
            return
        ref, at = (one_ref, c) if c < edge else (two_ref, c - edge)
        at += edge + width // 2
        ref[at : at + width, :] = total(value, down_prior if prior else None, lanes).T.astype(BF16)
        send(ref, 0 if c < edge else 1, pl.ds(at, width))

    def put_out(value):
        if not final:
            one_ref[:, ff:] = value.astype(BF16)
            at = (slice(None), pl.ds(ff, width))
            move.store(one_ref.at[at], up_hbm.at[at])
            return
        value = total(value, up_prior if prior else None, slice(ff, ff + width)).astype(BF16)
        lines = slice(edge, edge + width // 2)
        one_ref[lines, :] = value[: width // 2]
        two_ref[lines, :] = value[width // 2 :]
        send(one_ref, 0, pl.ds(edge, width // 2))
        send(two_ref, 1, pl.ds(edge, width // 2))

    result = middle
    back = jnp.zeros((rows, width), F32)
    c0 = 0.7978845608028654
    c1 = 0.044715
    for c in range(0, ff, width):
        hidden = dot(second, wup_ref[:, c : c + width])
        grad = dot(cot, wdown_ref[c : c + width, :], NT)
        square = hidden * hidden
        t = jnp.tanh(hidden * (c0 + (c0 * c1) * square))
        left = 0.5 + 0.5 * t
        active = (hidden * left).astype(BF16)
        slope = left + (0.5 * hidden) * (1.0 - t * t) * (c0 + (3.0 * c0 * c1) * square)
        grad = (grad * slope).astype(BF16)
        result = result + dot(active, wdown_ref[c : c + width, :])
        back = back + dot(grad, wup_ref[:, c : c + width], NT)
        put_down(c, dot(cot_t, active))
        put_up(c, dot(second_t, grad))
    out_ref[...] = result.astype(BF16)
    move.store(out_ref, out_hbm.at[here])
    e = back * gain2_ref[...]
    inner = jnp.mean(e * scaled, axis=-1, keepdims=True)
    grad_middle = cot.astype(F32) + r2 * (e - scaled * inner)
    branch = grad_middle.astype(BF16)
    gmid_ref[...] = branch
    move.store(gmid_ref, gmid_hbm.at[here])
    put_out(dot(att.T, branch))
    gatt_ref[...] = dot(branch, wout_ref[...], NT).astype(BF16)
    move.store(gatt_ref, gatt_hbm.at[here])
    for copy in pending:
        copy.wait()
    move.finish()


def forward(
    far_rows, kinds, core, recv, x, cot, proj, wrow, mask, gain1, gain2, w_qkv, w_out, w_up, w_down,
    first_group, groups, prior, final, token,
):
    rows, width = x.shape
    ff = w_up.shape[1]
    halves = width // HALF
    count = groups * GROUP
    like = lambda wide, kind=BF16: jax.ShapeDtypeStruct((rows, wide), kind)
    probs = jax.ShapeDtypeStruct((rows // GROUP, halves, PER_HALF * GROUP, 2 * GROUP), BF16)
    part = ff + width // 2
    if final:
        tails = [(part, width), (part, width)]
    else:
        tails = [(width, ff + width), (width, ff)]
    in_specs = [SMEM] * 3 + [ANY] * (len(recv) + 4) + [VMEM] * 3 + [ANY] * 5
    operands = [far_rows, kinds, core, *recv, x, cot, proj, wrow, mask, gain1, gain2]
    operands += [w_qkv, w_out, w_up, w_down, token]
    scratch = [
        pltpu.VMEM((count, width), BF16),
        pltpu.VMEM((count, width), BF16),
        pltpu.VMEM((count, 3 * width), BF16),
        pltpu.VMEM((count, 2 * GROUP), F32),
    ]
    scratch += [pltpu.VMEM(w.shape, BF16) for w in (w_qkv, w_out, w_up, w_down)]
    scratch += [pltpu.VMEM((count, width), BF16)] * 3
    scratch += [pltpu.VMEM((groups,) + probs.shape[1:], BF16)]
    scratch += [pltpu.VMEM((count, n * width), BF16) for n in (1, 2, 1)]
    scratch += [pltpu.VMEM(shape, BF16) for shape in tails]
    aliases = {}
    if prior is not None:
        streams, sums = prior
        in_specs += [ANY, ANY] + [ANY] * 6
        operands += list(sums)
        aliases = {len(operands) + i: i for i in range(6)}
        operands += list(streams)
        scratch += [pltpu.VMEM((width, ff + width), BF16), pltpu.VMEM((width, ff), BF16)]
    scratch += [pltpu.SemaphoreType.DMA((40,))]
    out = pl.pallas_call(
        functools.partial(
            forward_kernel, first_group, groups, len(recv), prior is not None, final
        ),
        in_specs=in_specs,
        out_specs=[ANY] * 8,
        out_shape=[like(width), like(width), like(width), probs, like(width), like(2 * width)]
        + [jax.ShapeDtypeStruct(shape, BF16) for shape in tails],
        scratch_shapes=scratch,
        input_output_aliases=aliases,
        compiler_params=pltpu.CompilerParams(vmem_limit_bytes=VMEM_LIMIT),
        cost_estimate=cost(1.0e9 * groups, 1e6 * groups),
        name="forward",
    )(*operands)
    return out[:6], out[6:]


def backward_kernel(first_group, groups, prior, chunks, letter, *refs):
    refs = list(refs)
    take = lambda n: [refs.pop(0) for _ in range(n)]
    ret_rows, place_ref = take(2)
    proj_hbm, farkv_hbm, gatt_hbm, prob_hbm, wrow_hbm, wqkv_hbm = take(6)
    if prior:
        (prior_gw,) = take(1)
        take(2)
    take(1)
    dproj_hbm, dfar_hbm, gw_ref = take(3)
    ret_hbm = take(chunks)
    proj_ref, farkv_ref, gatt_ref, prob_ref, wrow_ref, wqkv_ref = take(6)
    dproj_ref, dfar_ref = take(2)
    ret_refs = take(chunks)
    (sems,) = take(1)
    move = Mover(sems)
    rows = groups * GROUP
    width = gatt_ref.shape[1]
    start = first_group * GROUP
    batches = [(first, min(first + BATCH, groups)) for first in range(0, groups, BATCH)]
    loads = []
    for low, high in batches:
        at = pl.ds(low * GROUP, (high - low) * GROUP)
        there = pl.ds(start + low * GROUP, (high - low) * GROUP)
        loads.append(
            [
                move.start(hbm.at[there], ref.at[at])
                for hbm, ref in (
                    (proj_hbm, proj_ref),
                    (farkv_hbm, farkv_ref),
                    (gatt_hbm, gatt_ref),
                    (wrow_hbm, wrow_ref),
                )
            ]
            + [
                move.start(
                    prob_hbm.at[pl.ds(first_group + low, high - low)],
                    prob_ref.at[pl.ds(low, high - low)],
                )
            ]
        )
    got_wqkv = move.start(wqkv_hbm, wqkv_ref)
    masks16 = head_masks(GROUP)
    head_scale = (width // HEADS) ** -0.5
    far_lane = lax.broadcasted_iota(jnp.int32, (GROUP // UNIT, 2 * GROUP), 1) >= GROUP
    for (low, high), copies in zip(batches, loads):
        for copy in copies:
            copy.wait()
        work = [(i, half) for i in range(low, high) for half in range(width // HALF)]
        stacks, products = [], []
        for i, half in work:
            at = slice(i * GROUP, (i + 1) * GROUP)
            lo = half * HALF
            vals = jnp.concatenate(
                [
                    proj_ref[at, 2 * width + lo : 2 * width + lo + HALF],
                    farkv_ref[at, width + lo : width + lo + HALF],
                ],
                axis=0,
            )
            up = stack_heads(gatt_ref[at, lo : lo + HALF], masks16)
            stacks.append(up)
            products.append(prob_ref[i, half].astype(F32) * dot(up, vals, NT))
        for i in range(low, high):
            summed = jnp.zeros((GROUP, 2 * GROUP), F32)
            for (j, _), prod in zip(work, products):
                if j == i:
                    for h in range(PER_HALF):
                        summed = summed + prod[h * GROUP : (h + 1) * GROUP]
            pair = jnp.sum(summed.reshape(GROUP // UNIT, UNIT, 2 * GROUP), axis=1)
            pair = jnp.sum(jnp.where(far_lane, pair, 0.0), axis=1, keepdims=True)
            gw_ref[i] = jnp.broadcast_to(pair, (GROUP // UNIT, 128))
        scales = [repeat_heads(wrow_ref[i * GROUP : (i + 1) * GROUP, :]) for i, _ in work]
        products = [v * s for v, s in zip(products, scales)]
        totals = [jnp.sum(v, axis=1, keepdims=True) for v in products]
        for (i, half), up, prod, scale, total in zip(work, stacks, products, scales, totals):
            at = slice(i * GROUP, (i + 1) * GROUP)
            lo = half * HALF
            prob = prob_ref[i, half].astype(F32)
            ds = (prod - prob * total).astype(BF16)
            mixed = (prob * scale).astype(BF16)
            q = stack_heads(
                proj_ref[at, lo : lo + HALF] * jnp.asarray(head_scale, BF16), masks16
            )
            keys = jnp.concatenate(
                [proj_ref[at, width + lo : width + lo + HALF], farkv_ref[at, lo : lo + HALF]], axis=0
            )
            dq = unstack_heads(dot(ds, keys), masks16) * head_scale
            dk = dot(ds, q, TN).astype(BF16)
            dv = dot(mixed, up, TN).astype(BF16)
            dproj_ref[at, lo : lo + HALF] = dq.astype(BF16)
            dproj_ref[at, width + lo : width + lo + HALF] = dk[:GROUP]
            dproj_ref[at, 2 * width + lo : 2 * width + lo + HALF] = dv[:GROUP]
            dfar_ref[at, lo : lo + HALF] = dk[GROUP:]
            dfar_ref[at, width + lo : width + lo + HALF] = dv[GROUP:]
        at = pl.ds(low * GROUP, (high - low) * GROUP)
        there = pl.ds(start + low * GROUP, (high - low) * GROUP)
        move.store(dproj_ref.at[at], dproj_hbm.at[there])
        move.store(dfar_ref.at[at], dfar_hbm.at[there])

    got_wqkv.wait()
    grad = dot(dfar_ref[...], wqkv_ref[:, width:], NT).astype(BF16)
    for u in range(rows // UNIT):
        row = ret_rows[2 * first_group + u]
        edge = 0
        for ret_ref in ret_refs:
            value = grad[u * UNIT : (u + 1) * UNIT]

            def put(ret_ref=ret_ref, edge=edge, value=value):
                ret_ref[pl.ds(pl.multiple_of(row - edge, 16), UNIT), :] = value

            if chunks == 1:
                put()
            else:
                pl.when(jnp.logical_and(row >= edge, row < edge + ret_ref.shape[0]))(put)
            edge += ret_ref.shape[0]
    if letter:
        count_a, count_b, devices, extra = letter
        lane = lax.broadcasted_iota(jnp.int32, (1, 128), 1)
        row = jnp.zeros((1, 128), F32)

        def pair_at(at):
            if not prior:
                return gw_ref[at]
            early = prior_gw.shape[0]
            one = prior_gw[jnp.minimum(at, early - 1)]
            two = gw_ref[jnp.maximum(at - early, 0)]
            return jnp.where(at < early, one, two)

        for j in range(count_a + count_b):
            if j < count_a:
                both = pair_at(lax.shift_right_logical(place_ref[2 * j], 1))
                value = both[0:1] + both[1:2]
            else:
                pos = place_ref[count_a + j]
                both = pair_at(lax.shift_right_logical(pos, 1))
                value = jnp.where(lax.bitwise_and(pos, 1) == 0, both[0:1], both[1:2])
            row = jnp.where(lane == j, value, row)
        page = jnp.concatenate([row, jnp.zeros((1, width - 128), F32)], axis=1)
        line = lax.broadcasted_iota(jnp.int32, (extra, width), 0)
        page = jnp.where(line == 0, page, 0.0).astype(BF16)
        ret_ref = ret_refs[-1]
        height = ret_ref.shape[0] // devices
        for d in range(devices):
            ret_ref[(d + 1) * height - extra : (d + 1) * height, :] = page
    for ret_ref, hbm in zip(ret_refs, ret_hbm):
        move.store(ret_ref, hbm)
    move.finish()


def backward(
    ret_rows, place, proj, farkv, gatt, prob, wrow, w_qkv, sizes, first_group, groups, prior, letter,
    token,
):
    rows, width = gatt.shape
    count = groups * GROUP
    in_specs = [SMEM, SMEM] + [ANY] * 6
    operands = [ret_rows, place, proj, farkv, gatt, prob, wrow, w_qkv]
    aliases = {}
    if prior is not None:
        dproj, dfar, gw = prior
        in_specs += [VMEM, ANY, ANY]
        aliases = {len(operands) + 1: 0, len(operands) + 2: 1}
        operands += [gw, dproj, dfar]
    in_specs += [ANY]
    operands += [token]
    batches = -(-groups // BATCH)
    return pl.pallas_call(
        functools.partial(
            backward_kernel, first_group, groups, prior is not None, len(sizes), letter
        ),
        in_specs=in_specs,
        out_specs=[ANY, ANY, VMEM] + [ANY] * len(sizes),
        out_shape=[
            jax.ShapeDtypeStruct((rows, 3 * width), BF16),
            jax.ShapeDtypeStruct((rows, 2 * width), BF16),
            jax.ShapeDtypeStruct((groups, GROUP // UNIT, 128), F32),
        ]
        + [jax.ShapeDtypeStruct((n, width), BF16) for n in sizes],
        scratch_shapes=[
            pltpu.VMEM((count, 3 * width), BF16),
            pltpu.VMEM((count, 2 * width), BF16),
            pltpu.VMEM((count, width), BF16),
            pltpu.VMEM((groups,) + prob.shape[1:], BF16),
            pltpu.VMEM((count, 2 * GROUP), F32),
            pltpu.VMEM(w_qkv.shape, BF16),
            pltpu.VMEM((count, 3 * width), BF16),
            pltpu.VMEM((count, 2 * width), BF16),
        ]
        + [pltpu.VMEM((n, width), BF16) for n in sizes]
        + [pltpu.SemaphoreType.DMA((7 * batches + 2 + len(sizes),))],
        input_output_aliases=aliases,
        compiler_params=pltpu.CompilerParams(vmem_limit_bytes=VMEM_LIMIT),
        cost_estimate=cost(0.4e9 * groups, 1e6 * groups),
        name="backward",
    )(*operands)


def qkv_kernel(
    core_ref, x_hbm, farx_hbm, dproj_hbm, dfar_hbm, gain1_ref, wqkv_hbm, token_ref,
    gn_hbm, keep_ref, give_ref, x_ref, farx_ref, dproj_ref, dfar_ref, wqkv_ref, gn_ref, near_t, far_t, sems,
):
    move = Mover(sems)
    rows, width = x_ref.shape
    wide = wqkv_ref.shape[1]
    size = min(512, rows)
    got_w = move.start(wqkv_hbm, wqkv_ref)
    loads = []
    for low in range(0, rows, size):
        at = pl.ds(low, size)
        loads.append(
            [
                move.start(hbm.at[at], ref.at[at])
                for hbm, ref in (
                    (x_hbm, x_ref),
                    (dproj_hbm, dproj_ref),
                    (farx_hbm, farx_ref),
                    (dfar_hbm, dfar_ref),
                )
            ]
        )
    got_w.wait()
    for low, copies in zip(range(0, rows, size), loads):
        at = slice(low, low + size)
        for copy in copies:
            copy.wait()
        x = x_ref[at, :].astype(F32)
        scaled = x * inverse_norm(x)
        near_t[:, at] = (scaled * gain1_ref[...]).astype(BF16).T
        far = farx_ref[at, :].astype(F32)
        far_t[:, at] = (far * inverse_norm(far) * gain1_ref[...]).astype(BF16).T
        grad = dot(dproj_ref[at, :], wqkv_ref[...], NT)
        gn_ref[at, :] = grad.astype(BF16)
        move.store(gn_ref.at[pl.ds(low, size)], gn_hbm.at[pl.ds(low, size)])
    grads = []
    for c in range(0, wide, width):
        value = dot(near_t[...], dproj_ref[:, c : c + width])
        if c:
            value = value + dot(far_t[...], dfar_ref[:, c - width : c])
        grads.append(value)

    half = wide // 2

    def write(ref, which):
        at = which * half
        while at < (which + 1) * half:
            block, line = divmod(at, width)
            count = min(width - line, (which + 1) * half - at)
            value = grads[block][line : line + count]
            ref[at - which * half : at - which * half + count, :] = value.astype(BF16)
            at += count

    @pl.when(core_ref[0] == 0)
    def _():
        write(keep_ref, 0)
        write(give_ref, 1)

    @pl.when(core_ref[0] == 1)
    def _():
        write(keep_ref, 1)
        write(give_ref, 0)

    move.finish()


def qkv_grads(core, x, farx, dproj, dfar, gain1, w_qkv, token):
    rows, width = x.shape
    wide = w_qkv.shape[1]
    half = wide // 2
    tall = lambda size: pltpu.VMEM((rows, size), BF16)
    return pl.pallas_call(
        qkv_kernel,
        in_specs=[SMEM] + [ANY] * 4 + [VMEM, ANY, ANY],
        out_specs=[ANY, VMEM, VMEM],
        out_shape=[
            jax.ShapeDtypeStruct((rows, width), BF16),
            jax.ShapeDtypeStruct((half, width), BF16),
            jax.ShapeDtypeStruct((half, width), BF16),
        ],
        scratch_shapes=[
            tall(width),
            tall(width),
            tall(wide),
            tall(2 * width),
            pltpu.VMEM(w_qkv.shape, BF16),
            tall(width),
            pltpu.VMEM((width, rows), BF16),
            pltpu.VMEM((width, rows), BF16),
            pltpu.SemaphoreType.DMA((5 * (rows // min(512, rows)) + 1,)),
        ],
        compiler_params=limit(62),
        cost_estimate=cost(10e9, 25e6),
        name="qkv_grads",
    )(core, x, farx, dproj, dfar, gain1, w_qkv, token)


def row_gradient(f, x):
    r1 = inverse_norm(x)
    scaled = x * r1
    return r1 * (f - scaled * jnp.mean(f * scaled, axis=-1, keepdims=True))


def base_kernel(x_ref, gmid_ref, gn_ref, gs_ref, gain1_ref, out_ref):
    rows, width = x_ref.shape
    spread = jnp.broadcast_to(gs_ref[...][:, None, :], (rows // UNIT, UNIT, width))
    f = (gn_ref[...].astype(F32) + spread.reshape(rows, width)) * gain1_ref[...]
    grad = gmid_ref[...].astype(F32) + row_gradient(f, x_ref[...].astype(F32))
    out_ref[...] = grad.astype(BF16)


def base_rows(x, gmid, gn, gs, gain1):
    rows, width = x.shape
    tile = 2 * TILE
    return pl.pallas_call(
        base_kernel,
        grid=(rows // tile,),
        in_specs=[
            rows_of(tile, width),
            rows_of(tile, width),
            rows_of(tile, width),
            rows_of(tile // UNIT, width),
            whole((1, width)),
        ],
        out_specs=rows_of(tile, width),
        out_shape=jax.ShapeDtypeStruct((rows, width), BF16),
        compiler_params=params(),
        cost_estimate=cost(rows * width * 20, rows * width * 8),
        name="base",
    )(x, gmid, gn, gs, gain1)


def last_kernel(sizes, extra, capacity, table_ref, place_ref, *refs):
    ret_refs = refs[: len(sizes)]
    x_ref, base_ref, gain1_ref, outa_ref, outb_ref, acc = refs[len(sizes) :]
    rows_a = outa_ref.shape[0]
    acc[...] = jnp.zeros_like(acc)

    begin = 0
    for index, (size, ret_ref) in enumerate(zip(sizes, ret_refs)):
        height = size * UNIT + (extra if index == len(sizes) - 1 else 0)

        def add(r, carry, size=size, ret_ref=ret_ref, begin=begin, height=height):
            for slot in range(size):
                unit = table_ref[r * capacity + begin + slot]

                @pl.when(unit >= 0)
                def _():
                    at = pl.ds(pl.multiple_of(unit * UNIT, UNIT), UNIT)
                    src = pl.ds(pl.multiple_of(r * height + slot * UNIT, 16), UNIT)
                    acc[at, :] += ret_ref[src, :].astype(F32)

            return carry

        lax.fori_loop(0, ret_ref.shape[0] // height, add, 0)
        begin += size

    def finish(out_ref, first):
        def body(u, carry):
            at = pl.ds(pl.multiple_of(place_ref[first + u] * UNIT, UNIT), UNIT)
            own = pl.ds(pl.multiple_of((first + u) * UNIT, UNIT), UNIT)
            f = acc[own, :] * gain1_ref[...]
            grad = base_ref[at, :].astype(F32) + row_gradient(f, x_ref[own, :].astype(F32))
            out_ref[pl.ds(pl.multiple_of(u * UNIT, UNIT), UNIT), :] = grad.astype(BF16)
            return carry

        lax.fori_loop(0, out_ref.shape[0] // UNIT, body, 0, unroll=2)

    finish(outa_ref, 0)
    finish(outb_ref, rows_a // UNIT)


def last(table, place, ret, sizes, extra, capacity, x, base, gain1, rows_a):
    rows, width = x.shape
    return pl.pallas_call(
        functools.partial(last_kernel, sizes, extra, capacity),
        in_specs=[SMEM, SMEM] + [VMEM] * (len(ret) + 3),
        out_specs=[VMEM, VMEM],
        out_shape=[
            jax.ShapeDtypeStruct((rows_a, width), BF16),
            jax.ShapeDtypeStruct((rows - rows_a, width), BF16),
        ],
        scratch_shapes=[pltpu.VMEM((rows, width), F32)],
        compiler_params=limit(62),
        cost_estimate=cost(rows * width * 20, rows * width * 12),
        name="last",
    )(table, place, *ret, x, base, gain1)


def bits_of(size):
    count = 0
    while (1 << count) < size:
        count += 1
    return count


def bit_of(axis, bit):
    return (lax.axis_index(axis) >> bit) & 1


def swap(values, axis, bit):
    size = lax.axis_size(axis)
    return lax.ppermute(values, axis, [(i, i ^ (1 << bit)) for i in range(size)])


def halve(values, axis, bit):
    half = values.shape[0] // 2
    mine = bit_of(axis, bit)
    keep = lax.dynamic_slice_in_dim(values, mine * half, half, 0)
    give = lax.dynamic_slice_in_dim(values, (1 - mine) * half, half, 0)
    return keep, give


def double(values, axis, bit):
    got = swap(values, axis, bit)
    return jnp.where(
        bit_of(axis, bit) == 0,
        jnp.concatenate([values, got], axis=0),
        jnp.concatenate([got, values], axis=0),
    )


def add(one, two):
    return (one.astype(F32) + two.astype(F32)).astype(BF16)


def reduce_any(values, order):
    for axis, bit in order:
        keep, give = halve(values, axis, bit)
        values = add(keep, swap(give, axis, bit))
    for axis, bit in reversed(order):
        values = double(values, axis, bit)
    return values


def tie(values, *tokens):
    return pl.pallas_call(
        lambda *refs: None,
        in_specs=[ANY] * (1 + len(tokens)),
        out_specs=ANY,
        out_shape=jax.ShapeDtypeStruct(values.shape, values.dtype),
        input_output_aliases={0: 0},
        name="tie",
    )(values, *tokens)


def fetch(sources, targets, sems):
    copies = [
        pltpu.make_async_copy(source, target, sems.at[i])
        for i, (source, target) in enumerate(zip(sources, targets))
    ]
    for copy in copies:
        copy.start()
    for copy in copies:
        copy.wait()


def halve_kernel(ranges, sources, bits_ref, *refs):
    count = 2 * (1 + max(r[4] for r in ranges))
    sems = refs[-1]
    outs = refs[2 * sources + 1 : 2 * sources + 1 + count]
    held = refs[2 * sources + 1 + count : -2]
    made = held[2 * sources :]
    fetch(refs[: 2 * sources], held, refs[-2])
    refs = held
    for source, first, count, bit, out, there in ranges:
        own, came = refs[2 * source], refs[2 * source + 1]
        half = count // 2
        keep = pl.multiple_of(first + bits_ref[bit] * half, 16)
        give = pl.multiple_of(first + (1 - bits_ref[bit]) * half, 16)
        for ref, line in ((made[2 * out], keep), (made[2 * out + 1], give)):
            rows = pl.ds(line, half)
            total = own[rows, :].astype(F32) + came[rows, :].astype(F32)
            ref[there : there + half, :] = total.astype(BF16)
    fetch(made, outs, sems)


def halve_step(ranges, bits, pairs, token):
    width = pairs[0][0].shape[1]
    count = 1 + max(r[4] for r in ranges)
    heights = [max(r[5] + r[2] // 2 for r in ranges if r[4] == out) for out in range(count)]
    shapes = [jax.ShapeDtypeStruct((n, width), BF16) for n in heights for _ in range(2)]
    flat = [v for pair in pairs for v in pair]
    out = pl.pallas_call(
        functools.partial(halve_kernel, ranges, len(pairs)),
        in_specs=[SMEM] + [HBM] * len(flat) + [ANY],
        out_specs=[HBM] * len(shapes),
        out_shape=shapes,
        scratch_shapes=[pltpu.VMEM(v.shape, BF16) for v in flat + shapes]
        + [pltpu.SemaphoreType.DMA((len(flat),)), pltpu.SemaphoreType.DMA((len(shapes),))],
        compiler_params=limit(62),
        cost_estimate=cost(0, 8 * sum(heights) * width),
        name="halve_step",
    )(jnp.stack([bit_of(*b) for b in bits]).astype(jnp.int32), *flat, token)
    return [(out[2 * i], out[2 * i + 1]) for i in range(count)]


def double_kernel(ranges, sources, tokens, bits_ref, *refs):
    count = 1 + max(r[0] for r in ranges)
    outs = refs[2 * sources + tokens : 2 * sources + tokens + count]
    held = refs[2 * sources + tokens + count : -1]
    fetch(refs[: 2 * sources], held, refs[-1])
    refs = held
    for source, first, count, bit, out, there in ranges:
        own, came = refs[2 * out], refs[2 * out + 1]
        half = count // 2
        keep = pl.multiple_of(first + bits_ref[bit] * half, 16)
        give = pl.multiple_of(first + (1 - bits_ref[bit]) * half, 16)
        outs[source][pl.ds(keep, half), :] = own[there : there + half, :]
        outs[source][pl.ds(give, half), :] = came[there : there + half, :]


def double_step(ranges, bits, pairs, *tokens):
    width = pairs[0][0].shape[1]
    count = 1 + max(r[0] for r in ranges)
    heights = [max(r[1] + r[2] for r in ranges if r[0] == source) for source in range(count)]
    flat = [v for pair in pairs for v in pair]
    return pl.pallas_call(
        functools.partial(double_kernel, ranges, len(pairs), len(tokens)),
        in_specs=[SMEM] + [ANY] * len(flat) + [ANY] * len(tokens),
        out_specs=[VMEM] * count,
        out_shape=[jax.ShapeDtypeStruct((n, width), BF16) for n in heights],
        scratch_shapes=[pltpu.VMEM(v.shape, BF16) for v in flat]
        + [pltpu.SemaphoreType.DMA((len(flat),))],
        compiler_params=limit(24),
        cost_estimate=cost(0, 4 * sum(heights) * width),
        name="double_step",
    )(jnp.stack([bit_of(*b) for b in bits]).astype(jnp.int32), *flat, *tokens)


AXIS_X, AXIS_Y, AXIS_Z0, AXIS_Z1 = ("dp", 1), ("blk", 0), ("blk", 1), ("blk", 2)


def places(half, width, ff):
    up, down, out, qkv = range(4)
    edge = ff // 2
    result = [
        (c, width, up, 0, half * edge + c) for c in range(0, edge, width)
    ]
    result.append((edge, width // 2, out, half * (width // 2), 0))
    result += [
        (edge + width // 2 + c, width, down, half * edge + c, 0) for c in range(0, edge, width)
    ]
    start = edge + width // 2 + edge
    total = 3 * width
    at = half * total // 2
    while at < (half + 1) * total // 2:
        block, line = divmod(at, width)
        count = min(width - line, (half + 1) * total // 2 - at)
        result.append((start + at - half * total // 2, count, qkv, line, block * width))
        at += count
    return result


def assemble_kernel(which, prior, width, ff, core_ref, values_ref, wup_ref, wqkv_ref, *refs):
    outs = refs[5 if prior else 0 :][:5]
    held, products, sems = refs[-3:]
    ones = jnp.ones((8, width), BF16)

    def write(half):
        copies = []
        seen = set()
        for i, (first, count, out, line, column) in enumerate(places(half, width, ff)):
            value = values_ref[first : first + count, :].astype(F32)
            held[first : first + count, :] = value
            copy = pltpu.make_async_copy(
                held.at[pl.ds(first, count)],
                outs[out].at[pl.ds(line, count), pl.ds(column, width)],
                sems.at[i],
            )
            copy.start()
            copies.append(copy)
            if out in (0, 3):
                weights = (wup_ref if out == 0 else wqkv_ref)[line : line + count, column : column + width]
                part = weights.astype(F32) * value
                if out in seen:
                    products[out // 3, line : line + count, :] += part
                else:
                    products[out // 3, line : line + count, :] = part
                    if count < width:
                        rest = slice(0, line) if line else slice(count, width)
                        products[out // 3, rest, :] = jnp.zeros((width - count, width), F32)
                    seen.add(out)
        for out, at in ((3, 0), (0, 1)):
            value = products[out // 3]
            high = value.astype(BF16)
            low = (value - high.astype(F32)).astype(BF16)
            row = (dot(ones, high, NT) + dot(ones, low, NT))[0:1]
            outs[4][at : at + 1, :] = row + refs[0][at : at + 1, :] if prior else row
        for copy in copies:
            copy.wait()

    outs[4][...] = jnp.zeros_like(outs[4])

    @pl.when(core_ref[0] == which)
    def _():
        write(0)

    @pl.when(core_ref[0] != which)
    def _():
        write(1)


def assemble(core, which, values, w_up, w_qkv, width, ff, prior):
    shapes = [(width, ff), (ff, width), (width, width), (width, 3 * width), (8, width)]
    operands = [core, values, w_up, w_qkv]
    if prior is not None:
        operands += [prior[4], *prior[:4]]
    most = max(len(places(half, width, ff)) for half in (0, 1))
    return pl.pallas_call(
        functools.partial(assemble_kernel, which, prior is not None, width, ff),
        in_specs=[SMEM] + [VMEM] * (3 if prior is None else 4) + [ANY] * (0 if prior is None else 4),
        out_specs=[ANY] * 4 + [VMEM],
        out_shape=[jax.ShapeDtypeStruct(shape, F32) for shape in shapes],
        scratch_shapes=[
            pltpu.VMEM(values.shape, F32),
            pltpu.VMEM((2, width, width), F32),
            pltpu.SemaphoreType.DMA((most,)),
        ],
        input_output_aliases={} if prior is None else {5 + i: i for i in range(4)},
        compiler_params=limit(20),
        cost_estimate=cost(0, values.size * 6),
        name="assemble",
    )(*operands)


def exchange(values, devices):
    shape = values.shape
    parts = values.reshape(devices, shape[0] // devices, *shape[1:])
    return lax.all_to_all(parts, "blk", split_axis=0, concat_axis=0, tiled=True).reshape(shape)


def per_device(
    x_a, x_b, sel_a, sel_b, gain_one, w_qkv, w_out, w_sort, gain_two, w_up, w_down, cot_a, cot_b
):
    devices = lax.axis_size("blk")
    me = lax.axis_index("blk")
    seqs_a, rows_a, width = x_a.shape
    seqs_b, rows_b, _ = x_b.shape
    npl = sel_a.shape[1]
    blocks = npl * devices
    len_a = rows_a // npl
    len_b = rows_b // npl
    total_a = seqs_a * rows_a
    total_b = seqs_b * rows_b
    rows = total_a + total_b
    units = rows // UNIT
    units_a = total_a // UNIT
    count_a = seqs_a * npl
    count_b = seqs_b * npl
    picks = count_a + count_b
    picks_up = -(-picks // 16) * 16
    groups = rows // GROUP
    per = TILE // GROUP
    capacity = 2 * max(1, (4 * units + 5 * devices - 1) // (5 * devices))
    send_rows = devices * capacity * UNIT
    ff = w_up.shape[1]
    gain1 = gain_one.astype(F32).reshape(1, width)
    gain2 = gain_two.astype(F32).reshape(1, width)

    first, early = capacity, groups
    if capacity > 8:
        full, left = divmod(units, capacity)
        sure = (full * 8 + min(left, 8)) // 2 // per * per
        if capacity == 14 and 0 < sure < groups:
            first, early = 8, sure

    sizes = [8, 7] if early < groups else [capacity]
    extra = 16
    average = np.zeros((picks, units), np.float32)
    for j in range(count_a):
        average[j, 2 * j : 2 * j + 2] = 1.0 / len_a
    for j in range(count_b):
        average[count_a + j, units_a + j] = 1.0 / len_b
    settings = (npl, seqs_a, seqs_b, devices, capacity, first, early, sizes, extra, picks_up)
    w_sort_t = w_sort.T
    x, means, news, far_rows, ret_rows, perm, place, kinds = digest(
        x_a.reshape(-1, width), x_b.reshape(-1, width), sel_a, sel_b, gain1, average, w_sort_t, settings
    )
    news = lax.all_to_all(news, "blk", split_axis=0, concat_axis=0, tiled=True)
    table = news[:, picks, :capacity].astype(jnp.int32).reshape(-1)
    back_table = news[:, picks, capacity : capacity + sum(sizes)].astype(jnp.int32).reshape(-1)
    news = news[:, :picks]
    parcels = pack(table, x, devices, capacity, first, picks_up)
    recv = [exchange(parcels[0], devices)]
    summary = means * gain1
    rs = inverse_norm(summary)
    unit_summary = (summary * rs).astype(BF16)
    all_summaries = jnp.broadcast_to(
        jnp.pad(unit_summary, ((0, picks_up - picks), (0, 0))), (devices, picks_up, width)
    )

    xp, cot = arrange(perm, x, cot_a.reshape(-1, width), cot_b.reshape(-1, width))
    proj = project(xp, gain1, w_qkv)

    def by_sequence(values):
        tail = values.shape[2:]
        one = values[:, :count_a].reshape((devices, seqs_a, npl) + tail)
        two = values[:, count_a:].reshape((devices, seqs_b, npl) + tail)
        both = jnp.concatenate([one, two], axis=1)
        return jnp.swapaxes(both, 0, 1).reshape((seqs_a + seqs_b, blocks) + tail)

    def own_rows(values):
        return lax.dynamic_slice_in_dim(values, me * npl, npl, 1).reshape((-1,) + values.shape[2:])

    def to_units(values):
        return jnp.concatenate(
            [jnp.repeat(values[:count_a], len_a // UNIT, axis=0), values[count_a:]], axis=0
        )

    news = by_sequence(news)
    logits = news[..., :blocks]
    picked = (news[..., blocks : blocks + 1] == jnp.arange(blocks, dtype=F32)).astype(F32)
    weights = jnp.take(to_units(own_rows(sinkhorn(logits, picked))), perm, axis=0)
    lane = jnp.arange(2 * GROUP) >= GROUP
    wrow = jnp.where(lane[None, :], jnp.repeat(weights, UNIT, axis=0), 1.0)
    if len(parcels) > 1:
        tall = (capacity - first) * UNIT
        parcel = lax.dynamic_update_slice(
            parcels[1].reshape(devices, -1, width), all_summaries, (0, tall, 0)
        )
        recv.append(exchange(tie(parcel.reshape(-1, width), wrow, proj), devices))
        units_all = recv[1].reshape(devices, -1, width)[:, tall:]
    else:
        units_all = exchange(all_summaries.reshape(-1, width), devices)
        units_all = units_all.reshape(devices, picks_up, width)
    units_all = by_sequence(units_all[:, :picks])
    block_of = np.arange(GROUP) // len_b
    cross = block_of[:, None] != block_of[None, :]
    mask = np.zeros((2, GROUP, 2 * GROUP), np.float32)
    mask[1] = np.where(np.concatenate([cross, cross], axis=1), -1e30, 0.0)

    core = bit_of("dp", 0).astype(jnp.int32).reshape(1)
    shared = (xp, cot, proj, wrow, mask, gain1, gain2, w_qkv, w_out, w_up, w_down)
    heights = [
        devices * (n * UNIT + (extra if i == len(sizes) - 1 else 0))
        for i, n in enumerate(sizes)
    ]

    letter = (count_a, count_b, devices, extra)

    def run_backward(streams, *rest):
        _, _, gatt, prob, _, farkv = streams
        return backward(ret_rows, place, proj, farkv, gatt, prob, wrow, w_qkv, *rest)

    fast = lax.axis_size("dp") == 4 and devices == 8 and early < groups
    part_x = ff // 2 + width // 2
    if early < groups:
        prior = forward(far_rows, kinds, core, recv[:1], *shared, 0, early, None, False, wrow)
        dproj, dfar, gw_one, *ret = run_backward(
            prior[0], heights[:1], 0, early, None, None, prior[0][0]
        )
        back = [exchange(v, devices) for v in ret]
        streams, sums = forward(
            far_rows, kinds, core, recv, *shared, early, groups - early, prior, True, dproj
        )
        keep, give = sums
        out_a, out_b = restore(perm, streams[0], total_a)
        big_came = swap(give, "dp", 0)
        token = keep
        if fast:
            ranges_one = [(0, 0, part_x, 0, 0, 0), (0, part_x, keep.shape[0] - part_x, 1, 1, 0)]
            (bx, gx), (by, gy) = halve_step(
                ranges_one, [AXIS_X, AXIS_Y], [(keep, big_came)], out_a
            )
            bx_came, by_came = swap(gx, *AXIS_X), swap(gy, *AXIS_Y)
            token = bx
        dproj, dfar, _, *ret = run_backward(
            streams, heights[1:], early, groups - early, (dproj, dfar, gw_one), letter, token
        )
    else:
        streams, sums = forward(far_rows, kinds, core, recv, *shared, 0, groups, None, True, wrow)
        keep, give = sums
        out_a, out_b = restore(perm, streams[0], total_a)
        big_came = swap(give, "dp", 0)
        back = []
        dproj, dfar, _, *ret = run_backward(
            streams, heights, 0, groups, None, letter, keep
        )
    _, gmid, _, _, farx, _ = streams

    parcel = tie(ret[0], bx_came, by_came, back[0]) if fast else ret[0]
    tall = sizes[-1] * UNIT
    arrived = exchange(parcel, devices)
    back.append(arrived)
    token = dproj
    gn, late_keep, late_give = qkv_grads(
        core, xp, farx, dproj, dfar, gain1, w_qkv, token
    )
    late_came = swap(late_give, "dp", 0)
    part_late = 256
    if fast:
        late_rows = late_keep.shape[0]
        ranges_late = [(0, 0, part_late, 0, 0, 0), (0, part_late, late_rows - part_late, 1, 1, 0)]
        (lx, gx), (ly, gy) = halve_step(
            ranges_late, [AXIS_X, AXIS_Y], [(late_keep, late_came)], late_came
        )
        lx_came, ly_came = swap(gx, *AXIS_X), swap(gy, *AXIS_Y)
        nbx, nlx, nby, nly = (v.shape[0] for v in (bx, lx, by, ly))
        ranges_two = [
            (0, 0, nbx, 0, 0, 0),
            (1, 0, nlx, 0, 0, nbx // 2),
            (2, 0, nby, 1, 1, 0),
            (3, 0, nly, 1, 1, nby // 2),
        ]
        (vx, gx), (vy, gy) = halve_step(
            ranges_two,
            [AXIS_Y, AXIS_X],
            [(bx, bx_came), (lx, lx_came), (by, by_came), (ly, ly_came)],
            lx,
        )
        vx_came, vy_came = swap(gx, *AXIS_Y), swap(gy, *AXIS_X)
    small, spread = sort_back(
        me.reshape(1), perm, logits, picked, units_all.reshape(-1, width), w_sort_t, gain1, means,
        arrived, npl, seqs_a, (len_a, len_b), tall, extra, vx if fast else arrived,
    )
    if fast:
        cuts = [nbx // 2, nlx // 2, nby // 2, nly // 2]
        ranges_three = [
            (0, 0, cuts[0], 0, 0, 0),
            (0, cuts[0], cuts[1], 0, 0, cuts[0] // 2),
            (1, 0, cuts[2], 0, 1, 0),
            (1, cuts[2], cuts[3], 0, 1, cuts[2] // 2),
        ]
        (zx, gx), (zy, gy) = halve_step(
            ranges_three, [AXIS_Z0], [(vx, vx_came), (vy, vy_came)], spread
        )
    base = base_rows(xp, gmid, gn, spread, gain1)
    if fast:
        zx_came, zy_came = swap(gx, *AXIS_Z0), swap(gy, *AXIS_Z0)
        zx = add(zx, tie(zx_came, base, zy_came))
        zx_came = swap(zx, *AXIS_Z1)
        zy = add(zy, zy_came)
        zy_came = swap(zy, *AXIS_Z1)

    gx_a, gx_b = last(back_table, place, back, sizes, extra, sum(sizes), x, base, gain1, total_a)
    if fast:
        for bit in (0, 1):
            small = small + swap(small, "dp", bit)
        zx, zy = add(zx, tie(zx_came, small)), add(zy, zy_came)
        vx, vy = double_step(
            ranges_three,
            [AXIS_Z0],
            [(zx, swap(zx, *AXIS_Z0)), (zy, swap(zy, *AXIS_Z0))],
        )
        ranges_back = [
            (0, 0, nbx, 0, 0, 0),
            (0, nbx, nlx, 0, 0, cuts[0]),
            (1, 0, nby, 1, 1, 0),
            (1, nby, nly, 1, 1, cuts[2]),
        ]
        vx, vy = double_step(
            ranges_back,
            [AXIS_Y, AXIS_X],
            [(vx, swap(vx, *AXIS_Y)), (vy, swap(vy, *AXIS_X))],
        )
        big_rows = keep.shape[0]
        ranges_all = [
            (0, 0, part_x, 0, 0, 0),
            (0, big_rows, part_late, 0, 0, nbx),
            (0, part_x, big_rows - part_x, 1, 1, 0),
            (0, big_rows + part_late, late_rows - part_late, 1, 1, nby),
        ]
        (sums_own,) = double_step(
            ranges_all,
            [AXIS_X, AXIS_Y],
            [(vx, swap(vx, *AXIS_X)), (vy, swap(vy, *AXIS_Y))],
            gx_a,
        )
    else:
        across = [("dp", bit) for bit in range(1, bits_of(lax.axis_size("dp")))]
        along = [("blk", bit) for bit in range(bits_of(devices))]
        sums_own = jnp.concatenate(
            [
                reduce_any(add(keep, big_came), across + along),
                reduce_any(add(late_keep, late_came), along + across),
            ],
            axis=0,
        )
    sums_came = swap(sums_own, "dp", 0)

    if not fast:
        small = lax.psum(small, "dp")
    written = assemble(core, 0, sums_own, w_up, w_qkv, width, ff, None)
    sum_up, sum_down, sum_out, sum_qkv, gains = assemble(
        core, 1, sums_came, w_up, w_qkv, width, ff, written
    )

    return (
        out_a.reshape(x_a.shape),
        out_b.reshape(x_b.shape),
        gx_a.reshape(x_a.shape),
        gx_b.reshape(x_b.shape),
        gains[0] / gain1[0] + small[blocks],
        sum_qkv,
        sum_out,
        small[:blocks].T,
        gains[1] / gain2[0],
        sum_up,
        sum_down,
    )


def solution(mesh):
    rows_spec = P("dp", "blk", None)
    in_specs = (
        (rows_spec, rows_spec, P("dp", "blk"), P("dp", "blk")) + (P(),) * 7 + (rows_spec, rows_spec)
    )
    out_specs = (rows_spec,) * 4 + (P(),) * 7
    return jax.shard_map(
        per_device, mesh=mesh, in_specs=in_specs, out_specs=out_specs, check_vma=False
    )
```
